32 devices in a mesh: rows: 4 (over y, x), blk: 8 (over z, core).
Axes of the slice: x: 2, y: 2, z: 4, core: 2. Of those that a mesh axis runs over, the one named last changes fastest.
Arguments:
- tokens: bfloat16 [4, 1024, 2048], P('rows', 'blk'), may hold values from -6 to 6
- cotangent: bfloat16 [4, 1024, 2048], P('rows', 'blk'), may hold values from -6 to 6
- lengths: int32 [4], P('rows'), may hold values from 512 to 1024, as said below
- block_map: int32 [4, 16], P('rows'), may hold values from 0 to 15, as said below
- gain_attend: float32 [2048], replicated, may hold values from 0.5 to 1.5
- gain_expand: float32 [2048], replicated, may hold values from 0.5 to 1.5
- attend_in: float32 [2048, 6144], P(('rows', 'blk')), may hold values from -0.125 to 0.125
- attend_out: float32 [2048, 2048], P(None, ('rows', 'blk')), may hold values from -2 to 2
- expand_in: float32 [2048, 16384], P(('rows', 'blk')), may hold values from -0.125 to 0.125
- reduce_out: float32 [8192, 2048], P(None, ('rows', 'blk')), may hold values from -0.0625 to 0.0625
- attend_in_first: float32 [2048, 6144], P(('rows', 'blk')), may hold values from -72 to 72
- attend_out_first: float32 [2048, 2048], P(None, ('rows', 'blk')), may hold values from -0.6 to 0.6
- expand_in_first: float32 [2048, 16384], P(('rows', 'blk')), may hold values from -0.6 to 0.6
- reduce_out_first: float32 [8192, 2048], P(None, ('rows', 'blk')), may hold values from -0.6 to 0.6
- attend_in_second: float32 [2048, 6144], P(('rows', 'blk')), may hold values from 12.288 to 1228.8
- attend_out_second: float32 [2048, 2048], P(None, ('rows', 'blk')), may hold values from 0.24576 to 24.576
- expand_in_second: float32 [2048, 16384], P(('rows', 'blk')), may hold values from 0.001 to 1
- reduce_out_second: float32 [8192, 2048], P(None, ('rows', 'blk')), may hold values from 0.01 to 100
Outputs:
- layer_out: bfloat16 [4, 1024, 2048], P('rows', 'blk')
- grad_input: float32 [4, 1024, 2048], P('rows', 'blk')
- grad_gain_attend: float32 [2048], replicated
- grad_gain_expand: float32 [2048], replicated
- attend_in_next: float32 [2048, 6144], P(('rows', 'blk'))
- attend_in_first_next: float32 [2048, 6144], P(('rows', 'blk'))
- attend_in_second_next: float32 [2048, 6144], P(('rows', 'blk'))
- attend_out_first_next: float32 [2048, 2048], P(None, ('rows', 'blk'))
- attend_out_second_next: float32 [2048, 2048], P(None, ('rows', 'blk'))
- expand_in_next: float32 [2048, 16384], P(('rows', 'blk'))
- expand_in_first_next: float32 [2048, 16384], P(('rows', 'blk'))
- expand_in_second_next: float32 [2048, 16384], P(('rows', 'blk'))
- reduce_out_next: float32 [8192, 2048], P(None, ('rows', 'blk'))
- reduce_out_first_next: float32 [8192, 2048], P(None, ('rows', 'blk'))
- reduce_out_second_next: float32 [8192, 2048], P(None, ('rows', 'blk'))
The draws below stay inside these ranges and needn't reach their ends.
Inputs may be any that keep to these rules, and one draw needn't show every extreme that they name: `lengths`: one row of every draw has length exactly 1024. `block_map`: in each row, the blocks stored at indices 2 j and 2 j + 1 are b and 15 - b for some b < 8; every block of the row is stored once.
All inputs are finite; a program needn't handle non-finite values.
Results may differ from the reference program's by a relative error of at most 0.033.
Values may be sent and summed in bfloat16 or wider, within the bound.
A program may use at most 896 MiB of HBM per device.

```python
import math
import jax
import jax.numpy as jnp
from jax import lax

D = 2048
HEADS = 32
HEAD_DIM = 64
FF = 8192
BLOCK = 64
NBLOCKS = 16
LEN = 1024
ROWS = 4


def draw_lengths(key, part):
    key = jax.random.fold_in(key, 11)
    key_rows, key_pick = jax.random.split(key)
    drawn_lengths = jax.random.randint(key_rows, (ROWS,), LEN // 2, LEN + 1)
    chosen = jax.random.randint(key_pick, (), 0, ROWS)
    return jnp.where(jnp.arange(ROWS) == chosen, LEN, drawn_lengths).astype(jnp.int32)


def draw_block_map(key, part):
    key = jax.random.fold_in(key, 23)
    halves = NBLOCKS // 2
    row_keys = jax.random.split(key, ROWS)
    orders = jax.vmap(lambda row_key: jax.random.permutation(row_key, halves))(row_keys)
    return jnp.stack([orders, NBLOCKS - 1 - orders], axis=-1).reshape(ROWS, NBLOCKS).astype(jnp.int32)


def shard_levels(key, extent, pieces, low, top_value):
    def one(axis_at, parts):
        heights = jax.random.uniform(jax.random.fold_in(jax.random.fold_in(key, 6), axis_at), (parts,), jnp.float32, low / len(pieces), top_value / len(pieces))
        return jnp.repeat(jnp.exp(heights), extent[axis_at] // parts).reshape((-1,) + (1,) * (len(extent) - axis_at - 1))

    factor_of = one(*pieces[0])
    for cut in pieces[1:]:
        factor_of = factor_of * one(*cut)
    return factor_of


def normal_values(own_key, shape, scale, reach, shards=(), held_as=jnp.bfloat16):
    values = scale * jax.random.normal(own_key, shape, jnp.float32)
    if shards:
        values = values * shard_levels(own_key, shape, shards, -0.22, 0.18)
    return jnp.clip(values, -reach, reach).astype(held_as)


def setup_inputs(seed: int = 0) -> dict:
    streams_of = jax.random.split(jax.random.key(seed), 19)
    tokens = normal_values(streams_of[0], (ROWS, LEN, D), 1.0, 6.0, ((0, 4), (1, 8)))
    cotangent = normal_values(streams_of[1], (ROWS, LEN, D), 1.0, 6.0, ((0, 4), (1, 8)))
    lengths = draw_lengths(jax.random.fold_in(streams_of[18], 71), 0)
    block_map = draw_block_map(jax.random.fold_in(streams_of[18], 71), 0)
    gain_attend = jnp.clip(1.0 + 0.1 * jax.random.normal(streams_of[4], (D,), jnp.float32), 0.5, 1.5)
    gain_expand = jnp.clip(1.0 + 0.1 * jax.random.normal(streams_of[5], (D,), jnp.float32), 0.5, 1.5)
    attend_in = normal_values(streams_of[6], (D, 3 * D), D ** -0.5, 0.125, ((0, 32),), jnp.float32)
    attend_out = normal_values(streams_of[7], (D, D), (D // (4 * BLOCK)) ** -0.5, 2.0, ((1, 32),), jnp.float32)
    expand_in = normal_values(streams_of[8], (D, 2 * FF), D ** -0.5, 0.125, ((0, 32),), jnp.float32)
    reduce_out = normal_values(streams_of[9], (FF, D), FF ** -0.5, 0.0625, ((1, 32),), jnp.float32)
    attend_in_first = normal_values(streams_of[10], (D, 3 * D), 12.0, 72.0, ((0, 32),), jnp.float32)
    attend_out_first = normal_values(streams_of[11], (D, D), 0.1, 0.6, ((1, 32),), jnp.float32)
    expand_in_first = normal_values(streams_of[12], (D, 2 * FF), 0.1, 0.6, ((0, 32),), jnp.float32)
    reduce_out_first = normal_values(streams_of[13], (FF, D), 0.1, 0.6, ((1, 32),), jnp.float32)
    attend_in_second = jnp.clip(jnp.exp(math.log(1228.8) - 4.6051702 * jax.random.uniform(streams_of[14], (D, 3 * D), jnp.float32) ** shard_levels(streams_of[14], (D, 3 * D), ((0, 32),), -0.2, 0.2)), 12.288, 1228.8)
    attend_out_second = jnp.clip(jnp.exp(math.log(24.576) - 4.6051702 * jax.random.uniform(streams_of[15], (D, D), jnp.float32) ** shard_levels(streams_of[15], (D, D), ((1, 32),), -0.2, 0.2)), 0.24576, 24.576)
    expand_in_second = jnp.clip(jnp.exp(math.log(1.0) - 6.9077552 * jax.random.uniform(streams_of[16], (D, 2 * FF), jnp.float32) ** shard_levels(streams_of[16], (D, 2 * FF), ((0, 32),), -0.2, 0.2)), 0.001, 1.0)
    reduce_out_second = jnp.clip(jnp.exp(math.log(100.0) - 9.2103404 * jax.random.uniform(streams_of[17], (FF, D), jnp.float32) ** shard_levels(streams_of[17], (FF, D), ((1, 32),), -0.2, 0.2)), 0.01, 100.0)
    return dict(tokens=tokens, cotangent=cotangent, lengths=lengths, block_map=block_map, gain_attend=gain_attend, gain_expand=gain_expand, attend_in=attend_in, attend_out=attend_out, expand_in=expand_in, reduce_out=reduce_out, attend_in_first=attend_in_first, attend_out_first=attend_out_first, expand_in_first=expand_in_first, reduce_out_first=reduce_out_first, attend_in_second=attend_in_second, attend_out_second=attend_out_second, expand_in_second=expand_in_second, reduce_out_second=reduce_out_second)


@jax.custom_vjp
def low(v):
    return lax.optimization_barrier(v.astype(jnp.bfloat16)).astype(jnp.float32)

@jax.custom_vjp
def low_back(v):
    return v

def low_keep(v):
    return (low(v), None)

def low_pass(kept, grad):
    return (grad,)

def back_keep(v):
    return (v, None)

def back_low(kept, grad):
    return (low(grad),)
low.defvjp(low_keep, low_pass)
low_back.defvjp(back_keep, back_low)
theta_base = 130000.0
norm_eps = 1e-05
neg_large = -1e+30
beta_one = 0.9
beta_two = 0.95
learn_rate = 0.01
decay_rate = 0.1
adam_eps = 1e-08
step_count = 10
highest = lax.Precision.HIGHEST

def rope_tables(positions, head_size):
    halfway = head_size // 2
    frequency = jnp.exp(-jnp.arange(halfway, dtype=jnp.float32) * (2.0 / head_size) * math.log(theta_base))
    angles = positions.astype(jnp.float32)[:, None] * frequency[None, :]
    return (jnp.cos(angles)[:, None, :], jnp.sin(angles)[:, None, :])

def rotate(values, cosine, sine_table):
    halfway = values.shape[-1] // 2
    front_half = values[..., :halfway]
    back_half = values[..., halfway:]
    return jnp.concatenate([front_half * cosine - back_half * sine_table, back_half * cosine + front_half * sine_table], axis=-1)

def normalize(values, gain_vector):
    return low(values * lax.rsqrt(lax.optimization_barrier(jnp.mean(values * values, axis=-1, keepdims=True)) + norm_eps) * gain_vector)

def attend_row(queries, keys_row, values_row, positions, length):
    seq_len = positions.shape[0]
    width_rows = math.gcd(seq_len, 512)
    factor = 1.0 / math.sqrt(HEAD_DIM)
    key_live = positions < length

    def one_block(inputs):
        query_block, place_block = inputs
        scores = low_back(jnp.einsum('qhe,khe->hqk', query_block, keys_row, precision=highest) * factor)
        allowed = (positions[None, None, :] <= place_block[None, :, None]) & key_live[None, None, :]
        scores = jnp.where(allowed, scores, neg_large)
        weights = low(jax.nn.softmax(scores, axis=-1))
        summed = jnp.einsum('hqk,khe->qhe', weights, values_row, precision=highest)
        return jnp.where((place_block < length)[:, None, None], summed, 0.0)
    outputs = lax.map(jax.checkpoint(one_block), (queries.reshape(seq_len // width_rows, width_rows, HEADS, HEAD_DIM), positions.reshape(seq_len // width_rows, width_rows)))
    return outputs.reshape(seq_len, HEADS * HEAD_DIM)

def layer_row(inputs, gain_pair, lowered):
    row_values, positions, length = inputs
    gain_attend, gain_expand = gain_pair
    attend_in, attend_out, expand_in, reduce_out = lowered
    seq_len = positions.shape[0]
    normed_one = normalize(row_values, gain_attend)
    mixed_qkv = low_back(jnp.dot(normed_one, attend_in, precision=highest)).reshape(seq_len, 3, HEADS, HEAD_DIM)
    cosine, sine_table = rope_tables(positions, HEAD_DIM)
    queries = low(low_back(rotate(mixed_qkv[:, 0], cosine, sine_table)))
    keys_row = low(low_back(rotate(mixed_qkv[:, 1], cosine, sine_table)))
    values_row = low(low_back(mixed_qkv[:, 2]))
    attended = low(low_back(attend_row(queries, keys_row, values_row, positions, length)))
    residual = row_values + low_back(jnp.dot(attended, attend_out, precision=highest))
    normed_two = normalize(residual, gain_expand)
    gate_up = jnp.dot(normed_two, expand_in, precision=highest)
    gate_part = low_back(gate_up[:, :FF])
    up_part = low_back(gate_up[:, FF:])
    hidden = low(jax.nn.silu(gate_part) * up_part)
    return residual + low_back(jnp.dot(hidden, reduce_out, precision=highest))

def adam_step(master, moment_one, moment_two, gradient):
    moment_one = beta_one * moment_one + (1.0 - beta_one) * gradient
    moment_two = beta_two * moment_two + (1.0 - beta_two) * gradient * gradient
    update = moment_one / (1.0 - beta_one ** step_count) / (jnp.sqrt(moment_two / (1.0 - beta_two ** step_count)) + adam_eps)
    return (master - learn_rate * (update + decay_rate * master), moment_one, moment_two)

def reference(tokens, cotangent, lengths, block_map, gain_attend, gain_expand, attend_in, attend_out, expand_in, reduce_out, attend_in_first, attend_out_first, expand_in_first, reduce_out_first, attend_in_second, attend_out_second, expand_in_second, reduce_out_second):
    offsets = jnp.arange(BLOCK, dtype=jnp.int32)
    positions = (block_map[:, :, None] * BLOCK + offsets[None, None, :]).reshape(ROWS, LEN).astype(jnp.int32)

    def whole_layer(values, gain_one, gain_two, weight_a, weight_b, weight_c, weight_d):
        lowered = (low(weight_a), low(weight_b), low(weight_c), low(weight_d))

        def one_row(inputs):
            return layer_row(inputs, (gain_one, gain_two), lowered)
        return lax.map(jax.checkpoint(one_row), (values, positions, lengths))
    result, pullback = jax.vjp(whole_layer, tokens.astype(jnp.float32), gain_attend, gain_expand, attend_in, attend_out, expand_in, reduce_out)
    gradients = pullback(cotangent.astype(jnp.float32))
    set_one = adam_step(attend_in, attend_in_first, attend_in_second, gradients[3])
    set_two = adam_step(attend_out, attend_out_first, attend_out_second, gradients[4])
    set_three = adam_step(expand_in, expand_in_first, expand_in_second, gradients[5])
    set_four = adam_step(reduce_out, reduce_out_first, reduce_out_second, gradients[6])
    return (result.astype(jnp.bfloat16), gradients[0], gradients[1], gradients[2], set_one[0], set_one[1], set_one[2], set_two[1], set_two[2], set_three[0], set_three[1], set_three[2], set_four[0], set_four[1], set_four[2])
```

```python
import functools
import math

import jax
import jax.numpy as jnp
from jax import lax
from jax.experimental import pallas as pl
from jax.experimental.pallas import tpu as pltpu
from jax.sharding import PartitionSpec as P

HEADS = 32
HEAD_DIM = 64
MESH = pl.DeviceIdType.MESH
MIB = 1 << 20

theta_base = 130000.0
norm_eps = 1e-05
neg_large = -1e30
beta_one = 0.9
beta_two = 0.95
learn_rate = 0.01
decay_rate = 0.1
adam_eps = 1e-08
step_count = 10


def line_place():
    b = lax.axis_index("blk")
    return lax.axis_index("rows"), b // 2, b % 2

def greet(neighbours):
    barrier = pltpu.get_barrier_semaphore()
    for cond, dev in neighbours:
        def sig(dev=dev):
            pl.semaphore_signal(barrier, inc=1, device_id=dev, device_id_type=MESH)
        if cond is None: sig()
        else: pl.when(cond)(sig)
    count = 0
    for cond, dev in neighbours:
        count = count + (1 if cond is None else cond.astype(jnp.int32))
    pl.semaphore_wait(barrier, count)

def gather_kernel(chips, x_ref, o_ref, copy_sem, send_up, send_down, send_side, recv):
    r, z, c = line_place()
    t = x_ref.shape[0]
    up, down, side = (r, 2 * (z + 1) + c), (r, 2 * (z - 1) + c), (r, 2 * z + 1 - c)
    has_up, has_down = z < chips - 1, z > 0
    greet([(None, side), (has_up, up), (has_down, down)])
    def piece(j): return o_ref.at[pl.ds(pl.multiple_of(j * t, t), t)]
    def remote(src, j, sem, dev):
        return pltpu.make_async_remote_copy(src_ref=src, dst_ref=piece(j), send_sem=sem.at[j], recv_sem=recv.at[j], device_id=dev, device_id_type=MESH)
    mine = 2 * z + c
    pl.when(has_up)(lambda: remote(x_ref, mine, send_up, up).start())
    pl.when(has_down)(lambda: remote(x_ref, mine, send_down, down).start())
    remote(x_ref, mine, send_side, side).start()
    local = pltpu.make_async_copy(x_ref, piece(mine), copy_sem)
    local.start()
    for k in range(1, chips):
        @pl.when(z - k >= 0)
        def _():
            j = 2 * (z - k) + c
            remote(piece(j), j, send_up, up).wait_recv()
            pl.when(has_up)(lambda: remote(piece(j), j, send_up, up).start())
            remote(piece(j), j, send_side, side).start()
        @pl.when(z + k < chips)
        def _():
            j = 2 * (z + k) + c
            remote(piece(j), j, send_down, down).wait_recv()
            pl.when(has_down)(lambda: remote(piece(j), j, send_down, down).start())
            remote(piece(j), j, send_side, side).start()
    for y in range(chips):
        j = 2 * y + (1 - c)
        remote(piece(j), j, send_side, side).wait_recv()
    for y in range(chips):
        j = 2 * y + c
        pl.when(has_up & (z >= y))(lambda: remote(piece(j), j, send_up, up).wait_send())
        pl.when(has_down & (z <= y))(lambda: remote(piece(j), j, send_down, down).wait_send())
        remote(piece(j), j, send_side, side).wait_send()
    local.wait()

def line_gather(x, cid, mem=pl.ANY):
    nb = lax.axis_size("blk")
    return pl.pallas_call(
        functools.partial(gather_kernel, nb // 2),
        out_shape=jax.ShapeDtypeStruct((nb * x.shape[0],) + x.shape[1:], x.dtype),
        in_specs=[pl.BlockSpec(memory_space=mem)],
        out_specs=pl.BlockSpec(memory_space=mem),
        scratch_shapes=[pltpu.SemaphoreType.DMA] + [pltpu.SemaphoreType.DMA((nb,))] * 4,
        compiler_params=pltpu.CompilerParams(collective_id=cid, has_side_effects=True, vmem_limit_bytes=60*2**20),
        cost_estimate=pl.CostEstimate(flops=0, bytes_accessed=150000000, transcendentals=0),
    )(x)

def scatter_kernel(chips, x_ref, o_ref, side_buf, up_buf, down_buf, out_buf, send_side, recv_side, send_up, recv_up, send_down, recv_down):
    r, z, c = line_place()
    t = o_ref.shape[0]
    up, down, side = (r, 2 * (z + 1) + c), (r, 2 * (z - 1) + c), (r, 2 * z + 1 - c)
    has_up, has_down = z < chips - 1, z > 0
    greet([(None, side), (has_up, up), (has_down, down)])
    def piece(j): return x_ref.at[pl.ds(pl.multiple_of(j * t, t), t)]
    def to_side(y):
        return pltpu.make_async_remote_copy(src_ref=piece(2 * y + 1 - c), dst_ref=side_buf.at[y], send_sem=send_side.at[y], recv_sem=recv_side.at[y], device_id=side, device_id_type=MESH)
    def to_up(y):
        return pltpu.make_async_remote_copy(src_ref=out_buf.at[y], dst_ref=up_buf.at[y], send_sem=send_up.at[y], recv_sem=recv_up.at[y], device_id=up, device_id_type=MESH)
    def to_down(y):
        return pltpu.make_async_remote_copy(src_ref=out_buf.at[y], dst_ref=down_buf.at[y], send_sem=send_down.at[y], recv_sem=recv_down.at[y], device_id=down, device_id_type=MESH)
    order = []
    lo, hi = 0, chips - 1
    while lo <= hi:
        order.append(hi)
        if lo != hi: order.append(lo)
        lo += 1; hi -= 1
    for y in order:
        to_side(y).start()
    f32 = jnp.float32
    def total(y):
        return piece(2 * y + c)[...].astype(f32) + side_buf[y].astype(f32)
    for step in range(chips - 1):
        y = chips - 1 - step
        @pl.when(y > z)
        def _():
            to_side(y).wait_recv()
            @pl.when(has_down)
            def _():
                to_up(y).wait_recv()
                out_buf[y] = (total(y) + up_buf[y].astype(f32)).astype(out_buf.dtype)
            @pl.when(z == 0)
            def _():
                out_buf[y] = total(y).astype(out_buf.dtype)
            to_up(y).start()
        w = step
        @pl.when(w < z)
        def _():
            to_side(w).wait_recv()
            @pl.when(has_up)
            def _():
                to_down(w).wait_recv()
                out_buf[w] = (total(w) + down_buf[w].astype(f32)).astype(out_buf.dtype)
            @pl.when(z == chips - 1)
            def _():
                out_buf[w] = total(w).astype(out_buf.dtype)
            to_down(w).start()
    for y in range(chips):
        @pl.when(z == y)
        def _():
            to_side(y).wait_recv()
            o_ref[...] = total(y)
            @pl.when(has_down)
            def _():
                to_up(y).wait_recv()
                o_ref[...] += up_buf[y].astype(f32)
            @pl.when(has_up)
            def _():
                to_down(y).wait_recv()
                o_ref[...] += down_buf[y].astype(f32)
    for y in range(chips):
        to_side(y).wait_send()
        pl.when(y > z)(lambda: to_up(y).wait_send())
        pl.when(y < z)(lambda: to_down(y).wait_send())

def line_scatter(x, cid):
    nb = lax.axis_size("blk")
    t = x.shape[0] // nb
    w = x.shape[1]
    V = pl.BlockSpec(memory_space=pltpu.VMEM)
    D = pltpu.SemaphoreType.DMA((nb // 2,))
    return pl.pallas_call(
        functools.partial(scatter_kernel, nb // 2),
        out_shape=jax.ShapeDtypeStruct((t, w), jnp.float32),
        in_specs=[V], out_specs=V,
        scratch_shapes=[pltpu.VMEM((nb // 2, t, w), x.dtype)] * 4 + [D] * 6,
        compiler_params=pltpu.CompilerParams(collective_id=cid, has_side_effects=True, vmem_limit_bytes=60*2**20),
        cost_estimate=pl.CostEstimate(flops=0, bytes_accessed=150000000, transcendentals=0),
    )(x)


def rope_tables(positions, head_size):
    halfway = head_size // 2
    frequency = jnp.exp(
        -jnp.arange(halfway, dtype=jnp.float32) * (2.0 / head_size) * math.log(theta_base)
    )
    angles = positions.astype(jnp.float32)[:, None] * frequency[None, :]
    return (jnp.cos(angles)[:, None, :], jnp.sin(angles)[:, None, :])


def rotate(values, cosine, sine_table):
    halfway = values.shape[-1] // 2
    front_half = values[..., :halfway]
    back_half = values[..., halfway:]
    return jnp.concatenate(
        [
            front_half * cosine - back_half * sine_table,
            back_half * cosine + front_half * sine_table,
        ],
        axis=-1,
    )


def rotate_back(values, cosine, sine_table):
    halfway = values.shape[-1] // 2
    front_half = values[..., :halfway]
    back_half = values[..., halfway:]
    return jnp.concatenate(
        [
            front_half * cosine + back_half * sine_table,
            back_half * cosine - front_half * sine_table,
        ],
        axis=-1,
    )


def norm_forward(values, gain_vector):
    inverse = lax.rsqrt(jnp.mean(values * values, axis=-1, keepdims=True) + norm_eps)
    unit_values = values * inverse
    return (unit_values, inverse, (unit_values * gain_vector).astype(jnp.bfloat16))


def norm_backward(grad_normed, unit_values, inverse, gain_vector):
    grad_unit = grad_normed * gain_vector
    grad_values = inverse * (
        grad_unit - unit_values * jnp.mean(grad_unit * unit_values, axis=-1, keepdims=True)
    )
    return (grad_values, jnp.sum(grad_normed * unit_values, axis=0))


def contract_last(left, right):
    return lax.dot_general(
        left, right, (((1,), (1,)), ((), ())), preferred_element_type=jnp.float32
    )


def adam_step(master, moment_one, moment_two, gradient):
    moment_one = beta_one * moment_one + (1.0 - beta_one) * gradient
    moment_two = beta_two * moment_two + (1.0 - beta_two) * gradient * gradient
    update = (
        moment_one
        / (1.0 - beta_one**step_count)
        / (jnp.sqrt(moment_two / (1.0 - beta_two**step_count)) + adam_eps)
    )
    return (master - learn_rate * (update + decay_rate * master), moment_one, moment_two)


def moment_step(moment_one, moment_two, gradient):
    moment_one = beta_one * moment_one + (1.0 - beta_one) * gradient
    moment_two = beta_two * moment_two + (1.0 - beta_two) * gradient * gradient
    return (moment_one, moment_two)


def attend_kernel(q_ref, k_ref, v_ref, q_place, k_place, length_ref, o_ref, p_ref):
    scores = lax.dot_general(
        q_ref[0], k_ref[0], (((1,), (1,)), ((), ())), preferred_element_type=jnp.float32
    ) * (1.0 / math.sqrt(HEAD_DIM))
    place = q_place[...]
    scores = jnp.where(k_place[...] <= place, scores, neg_large)
    top = jnp.max(scores, axis=-1, keepdims=True)
    weights = jnp.exp(scores - top)
    weights = weights * (1.0 / jnp.sum(weights, axis=-1, keepdims=True))
    low = weights.astype(jnp.bfloat16)
    p_ref[0] = low
    out = jnp.dot(low, v_ref[0], preferred_element_type=jnp.float32)
    o_ref[0] = jnp.where(place < length_ref[0], out, 0.0).astype(jnp.bfloat16)


def attend(q, k, v, place, live_place, length):
    heads, seq, size = q.shape
    tile = 256
    whole = pl.BlockSpec((1, seq, size), lambda h, i: (h, 0, 0))
    part = pl.BlockSpec((1, tile, size), lambda h, i: (h, i, 0))
    return pl.pallas_call(
        attend_kernel,
        grid=(heads, seq // tile),
        in_specs=[
            part,
            whole,
            whole,
            pl.BlockSpec((tile, 1), lambda h, i: (i, 0)),
            pl.BlockSpec((1, seq), lambda h, i: (0, 0)),
            pl.BlockSpec(memory_space=pltpu.SMEM),
        ],
        out_specs=[part, pl.BlockSpec((1, tile, seq), lambda h, i: (h, i, 0))],
        out_shape=[
            jax.ShapeDtypeStruct((heads, seq, size), jnp.bfloat16),
            jax.ShapeDtypeStruct((heads, seq, seq), jnp.bfloat16),
        ],
        compiler_params=pltpu.CompilerParams(vmem_limit_bytes=56 * MIB),
        cost_estimate=pl.CostEstimate(
            flops=4 * heads * seq * seq * size, bytes_accessed=2 * heads * seq * seq,
            transcendentals=heads * seq * seq,
        ),
    )(q, k, v, place[:, None], live_place[None, :], length.reshape(1))


def attend_back_kernel(
    q_ref, k_ref, v_ref, o_ref, g_ref, p_ref, dq_ref, dk_ref, dv_ref, dk_acc, dv_acc
):
    step = pl.program_id(1)

    @pl.when(step == 0)
    def _():
        dk_acc[...] = jnp.zeros_like(dk_acc)
        dv_acc[...] = jnp.zeros_like(dv_acc)

    f32 = jnp.float32
    low = p_ref[0]
    grad = g_ref[0]
    over_rows = (((0,), (0,)), ((), ()))
    dv_acc[...] += lax.dot_general(low, grad, over_rows, preferred_element_type=f32)
    delta = jnp.sum(grad.astype(f32) * o_ref[0].astype(f32), axis=-1, keepdims=True)
    grad_p = lax.dot_general(
        grad, v_ref[0], (((1,), (1,)), ((), ())), preferred_element_type=f32
    )
    grad_s = (low.astype(f32) * (grad_p - delta)).astype(jnp.bfloat16)
    factor = 1.0 / math.sqrt(HEAD_DIM)
    dq_ref[0] = jnp.dot(grad_s, k_ref[0], preferred_element_type=f32) * factor
    dk_acc[...] += lax.dot_general(grad_s, q_ref[0], over_rows, preferred_element_type=f32)

    @pl.when(step == pl.num_programs(1) - 1)
    def _():
        dk_ref[0] = dk_acc[...] * factor
        dv_ref[0] = dv_acc[...]


def attend_back(q, k, v, o, g, p):
    heads, seq, size = q.shape
    tile = 256
    whole = pl.BlockSpec((1, seq, size), lambda h, i: (h, 0, 0))
    part = pl.BlockSpec((1, tile, size), lambda h, i: (h, i, 0))
    shape = jax.ShapeDtypeStruct((heads, seq, size), jnp.float32)
    return pl.pallas_call(
        attend_back_kernel,
        grid=(heads, seq // tile),
        in_specs=[
            part, whole, whole, part, part, pl.BlockSpec((1, tile, seq), lambda h, i: (h, i, 0)),
        ],
        out_specs=[part, whole, whole],
        out_shape=[shape] * 3,
        scratch_shapes=[pltpu.VMEM((seq, size), jnp.float32)] * 2,
        compiler_params=pltpu.CompilerParams(vmem_limit_bytes=56 * MIB),
        cost_estimate=pl.CostEstimate(
            flops=10 * heads * seq * seq * size, bytes_accessed=2 * heads * seq * seq,
            transcendentals=0,
        ),
    )(q, k, v, o, g, p)


def spread(weight, parts):
    rows, columns = weight.shape
    nb = lax.axis_size("blk")
    pieces = weight.astype(jnp.bfloat16).reshape(rows, parts, nb, columns // (parts * nb))
    pieces = pieces.transpose(2, 0, 1, 3).reshape(nb * rows, columns // nb)
    mine = lax.all_to_all(pieces, "blk", 0, 0, tiled=True)
    return lax.all_gather(mine, "rows", axis=0, tiled=True)


def collect(gradient, parts):
    nb = lax.axis_size("blk")
    mine = lax.psum_scatter(
        gradient.astype(jnp.bfloat16), "rows", scatter_dimension=0, tiled=True
    )
    pieces = lax.all_to_all(mine, "blk", 0, 0, tiled=True)
    rows, width = pieces.shape[0] // nb, pieces.shape[1]
    pieces = pieces.reshape(nb, rows, parts, width // parts).transpose(1, 2, 0, 3)
    return pieces.reshape(rows, nb * width).astype(jnp.float32)


def over_tokens(left, right):
    return lax.dot_general(
        left, right, (((0,), (0,)), ((), ())), preferred_element_type=jnp.float32
    )


def shards(
    tokens, cotangent, lengths, block_map, gain_attend, gain_expand,
    attend_in, attend_out, expand_in, reduce_out,
    attend_in_first, attend_out_first, expand_in_first, reduce_out_first,
    attend_in_second, attend_out_second, expand_in_second, reduce_out_second,
):
    f32, bf16 = jnp.float32, jnp.bfloat16
    nb = lax.axis_size("blk")
    near = tokens.shape[1]
    seq = near * nb
    heads = HEADS // nb
    block_rows = near // 2
    length = lengths[0]
    offsets = jnp.arange(block_rows, dtype=jnp.int32)
    place = (block_map[0][:, None] * block_rows + offsets[None, :]).reshape(-1)
    live_place = jnp.where(place < length, place, jnp.int32(1 << 30))
    cosine, sine = rope_tables(place, HEAD_DIM)

    x = tokens[0].astype(f32)
    unit_one, inverse_one, h1 = norm_forward(x, gain_attend)
    w_in = spread(attend_in, 3)
    h1_all = line_gather(h1, 0)
    w_out = spread(attend_out.T, 1)
    w_gu = spread(expand_in, 2)
    w_red = spread(reduce_out.T, 1)
    g_all = line_gather(cotangent[0], 0)

    mixed = jnp.dot(h1_all, w_in, preferred_element_type=f32).reshape(seq, 3, heads, HEAD_DIM)
    q = rotate(mixed[:, 0], cosine, sine).astype(bf16).transpose(1, 0, 2)
    k = rotate(mixed[:, 1], cosine, sine).astype(bf16).transpose(1, 0, 2)
    v = mixed[:, 2].astype(bf16).transpose(1, 0, 2)
    o, p = attend(q, k, v, place, live_place, length)
    attended = o.transpose(1, 0, 2).reshape(seq, heads * HEAD_DIM)
    x1 = x + line_scatter(contract_last(attended, w_out).astype(bf16), 1)
    unit_two, inverse_two, h2 = norm_forward(x1, gain_expand)
    h2_all = line_gather(h2, 0)
    gate_up = jnp.dot(h2_all, w_gu, preferred_element_type=f32)
    units = gate_up.shape[1] // 2
    gate, up = gate_up[:, :units], gate_up[:, units:]
    sigmoid = jax.nn.sigmoid(gate)
    silu = gate * sigmoid
    hidden = (silu * up).astype(bf16)
    grad_hidden = jnp.dot(g_all, w_red, preferred_element_type=f32)
    grad_gate = grad_hidden * up * (sigmoid * (1.0 + gate * (1.0 - sigmoid)))
    grad_up = grad_hidden * silu
    grad_gu = jnp.concatenate([grad_gate, grad_up], axis=1).astype(bf16)
    grad_h2 = line_scatter(contract_last(grad_gu, w_gu).astype(bf16), 1)
    y = x1 + line_scatter(contract_last(hidden, w_red).astype(bf16), 1)
    grad_expand = collect(over_tokens(h2_all, grad_gu), 2)
    grad_reduce = collect(over_tokens(g_all, hidden), 1)
    middle, gain_two = norm_backward(grad_h2, unit_two, inverse_two, gain_expand)
    grad_x1 = cotangent[0].astype(f32) + middle
    branch_all = line_gather(grad_x1.astype(bf16), 0)
    grad_o = jnp.dot(branch_all, w_out, preferred_element_type=f32).astype(bf16)
    grad_o = jnp.where((place < length)[:, None], grad_o, jnp.zeros((), bf16))
    grad_o = grad_o.reshape(seq, heads, HEAD_DIM).transpose(1, 0, 2)
    grad_q, grad_k, grad_v = attend_back(q, k, v, o, grad_o, p)
    grad_out = collect(over_tokens(branch_all, attended), 1)

    def by_token(value):
        return value.astype(bf16).astype(f32).transpose(1, 0, 2)

    grad_mixed = jnp.stack(
        [
            rotate_back(by_token(grad_q), cosine, sine),
            rotate_back(by_token(grad_k), cosine, sine),
            by_token(grad_v),
        ],
        axis=1,
    ).reshape(seq, -1).astype(bf16)
    grad_h1 = line_scatter(contract_last(grad_mixed, w_in).astype(bf16), 1)
    grad_in = collect(over_tokens(h1_all, grad_mixed), 3)
    first, gain_one = norm_backward(grad_h1, unit_one, inverse_one, gain_attend)
    grad_input = grad_x1 + first
    gain_one, gain_two = lax.psum((gain_one, gain_two), ("rows", "blk"))
    set_one = adam_step(attend_in, attend_in_first, attend_in_second, grad_in)
    set_two = moment_step(attend_out_first, attend_out_second, grad_out.T)
    set_three = adam_step(expand_in, expand_in_first, expand_in_second, grad_expand)
    set_four = adam_step(reduce_out, reduce_out_first, reduce_out_second, grad_reduce.T)
    return (
        (y.astype(bf16).reshape(tokens.shape), grad_input.reshape(tokens.shape), gain_one, gain_two)
        + set_one + set_two + set_three + set_four
    )


def solution(mesh):
    placed = (
        P("rows", "blk", None),
        P("rows", "blk", None),
        P("rows"),
        P("rows", None),
        P(),
        P(),
        P(("rows", "blk"), None),
        P(None, ("rows", "blk")),
        P(("rows", "blk"), None),
        P(None, ("rows", "blk")),
        P(("rows", "blk"), None),
        P(None, ("rows", "blk")),
        P(("rows", "blk"), None),
        P(None, ("rows", "blk")),
        P(("rows", "blk"), None),
        P(None, ("rows", "blk")),
        P(("rows", "blk"), None),
        P(None, ("rows", "blk")),
    )
    return jax.shard_map(
        shards,
        mesh=mesh,
        in_specs=placed,
        out_specs=(
            P("rows", "blk", None),
            P("rows", "blk", None),
            P(),
            P(),
            P(("rows", "blk"), None),
            P(("rows", "blk"), None),
            P(("rows", "blk"), None),
            P(None, ("rows", "blk")),
            P(None, ("rows", "blk")),
            P(("rows", "blk"), None),
            P(("rows", "blk"), None),
            P(("rows", "blk"), None),
            P(None, ("rows", "blk")),
            P(None, ("rows", "blk")),
            P(None, ("rows", "blk")),
        ),
        check_vma=False,
    )
```

```python
import functools
import math

import jax
import jax.numpy as jnp
from jax import lax
from jax.experimental import pallas as pl
from jax.experimental.pallas import tpu as pltpu
from jax.sharding import PartitionSpec as P

HEADS = 32
HEAD_DIM = 64
MESH = pl.DeviceIdType.MESH
MIB = 1 << 20

theta_base = 130000.0
norm_eps = 1e-05
neg_large = -1e30
beta_one = 0.9
beta_two = 0.95
learn_rate = 0.01
decay_rate = 0.1
adam_eps = 1e-08
step_count = 10


def line_place():
    b = lax.axis_index("blk")
    return lax.axis_index("rows"), b // 2, b % 2


def greet(chips, swaps):
    r, z, c = line_place()
    barrier = pltpu.get_barrier_semaphore()

    def signal(b):
        pl.semaphore_signal(barrier, inc=1, device_id=(r, b), device_id_type=MESH)

    if swaps:
        b, nb = 2 * z + c, 2 * chips
        for k in range(1, nb):
            signal(lax.rem(b + k, nb))
        pl.semaphore_wait(barrier, nb - 1)
        return
    signal(2 * z + 1 - c)
    pl.when(z < chips - 1)(lambda: signal(2 * (z + 1) + c))
    pl.when(z > 0)(lambda: signal(2 * (z - 1) + c))
    pl.semaphore_wait(barrier, 1 + (z < chips - 1).astype(jnp.int32) + (z > 0).astype(jnp.int32))


def swap_copies(src, dst, local, send, recv):
    r, b = lax.axis_index("rows"), lax.axis_index("blk")
    nb = src.shape[0]
    others = [lax.rem(b + k, nb) for k in range(1, nb)]

    def remote(other, slot):
        return pltpu.make_async_remote_copy(
            src_ref=src.at[other], dst_ref=dst.at[slot], send_sem=send.at[other],
            recv_sem=recv.at[slot], device_id=(r, other), device_id_type=MESH,
        )

    def start():
        for other in others:
            remote(other, b).start()
        pltpu.make_async_copy(src.at[b], dst.at[b], local).start()

    def wait():
        for other in others:
            remote(other, other).wait_recv()
        for other in others:
            remote(other, b).wait_send()
        pltpu.make_async_copy(src.at[b], dst.at[b], local).wait()

    return start, wait


def swap_sems(swaps):
    sems = []
    for pieces in swaps:
        sems += [pltpu.SemaphoreType.DMA] + [pltpu.SemaphoreType.DMA((pieces.shape[0],))] * 2
    return sems


def swap_list(srcs, dsts, sems):
    made = [swap_copies(s, d, *sems[3 * i : 3 * i + 3]) for i, (s, d) in enumerate(zip(srcs, dsts))]
    return [one[0] for one in made], [one[1] for one in made]


def swap_kernel(n, *refs):
    starts, waits = swap_list(refs[:n], refs[n : 2 * n], refs[2 * n :])
    greet(refs[0].shape[0] // 2, True)
    for start in starts:
        start()
    for wait in waits:
        wait()


def like(value):
    return jax.ShapeDtypeStruct(value.shape, value.dtype)


ANY = pl.BlockSpec(memory_space=pl.ANY)
VMEM = pl.BlockSpec(memory_space=pltpu.VMEM)


def params(cid):
    return pltpu.CompilerParams(
        collective_id=cid, has_side_effects=True, vmem_limit_bytes=60 * MIB
    )


def cost(flops):
    return pl.CostEstimate(flops=flops, bytes_accessed=150_000_000, transcendentals=0)


def swap(cid, *pieces):
    n = len(pieces)
    return pl.pallas_call(
        functools.partial(swap_kernel, n),
        out_shape=[like(value) for value in pieces],
        in_specs=[ANY] * n,
        out_specs=[ANY] * n,
        scratch_shapes=swap_sems(pieces),
        compiler_params=params(cid),
        cost_estimate=cost(0),
    )(*pieces)


def gather_kernel(chips, cuts, tile, with_dot, n, *refs):
    refs = list(refs)
    x_ref = refs.pop(0)
    w_ref = refs.pop(0) if with_dot else None
    srcs = [refs.pop(0) for _ in range(n)]
    o_ref = refs.pop(0)
    prod_ref = refs.pop(0) if with_dot else None
    dsts = [refs.pop(0) for _ in range(n)]
    copy_sem, send_up, send_down, send_side, recv = refs[:5]
    starts, waits = swap_list(srcs, dsts, refs[5:])
    r, z, c = line_place()
    t = x_ref.shape[0]
    h = t // cuts
    up, down, side = (r, 2 * (z + 1) + c), (r, 2 * (z - 1) + c), (r, 2 * z + 1 - c)
    has_up, has_down = z < chips - 1, z > 0
    greet(chips, n > 0)

    def piece(j, q):
        return o_ref.at[pl.ds(pl.multiple_of(j * t + q * h, h), h)]

    def remote(src, j, q, sem, dev):
        return pltpu.make_async_remote_copy(
            src_ref=src, dst_ref=piece(j, q), send_sem=sem.at[j, q], recv_sem=recv.at[j, q],
            device_id=dev, device_id_type=MESH,
        )

    def dot(y):
        if not with_dot:
            return
        rows = pl.ds(pl.multiple_of(y * 2 * t, 2 * t), 2 * t)

        def one(i, _):
            cols = pl.ds(pl.multiple_of(i * tile, tile), tile)
            prod_ref[rows, cols] = jnp.dot(
                o_ref[rows, :], w_ref[:, cols], preferred_element_type=jnp.float32
            ).astype(prod_ref.dtype)
            return 0

        lax.fori_loop(0, w_ref.shape[1] // tile, one, 0)

    mine = 2 * z + c
    for q in range(cuts):
        from_here = x_ref.at[pl.ds(q * h, h)]
        pl.when(has_up)(lambda: remote(from_here, mine, q, send_up, up).start())
        pl.when(has_down)(lambda: remote(from_here, mine, q, send_down, down).start())
        remote(from_here, mine, q, send_side, side).start()
    whole = o_ref.at[pl.ds(pl.multiple_of(mine * t, t), t)]
    local = pltpu.make_async_copy(x_ref, whole, copy_sem)
    local.start()
    for start in starts:
        start()

    def from_side(y):
        for q in range(cuts):
            j = 2 * y + 1 - c
            remote(piece(j, q), j, q, send_side, side).wait_recv()

    from_side(z)
    local.wait()
    dot(z)
    for k in range(1, chips):
        for q in range(cuts):
            @pl.when(z - k >= 0)
            def _():
                j = 2 * (z - k) + c
                remote(piece(j, q), j, q, send_up, up).wait_recv()
                pl.when(has_up)(lambda: remote(piece(j, q), j, q, send_up, up).start())
                remote(piece(j, q), j, q, send_side, side).start()

            @pl.when(z + k < chips)
            def _():
                j = 2 * (z + k) + c
                remote(piece(j, q), j, q, send_down, down).wait_recv()
                pl.when(has_down)(lambda: remote(piece(j, q), j, q, send_down, down).start())
                remote(piece(j, q), j, q, send_side, side).start()

        @pl.when(z - k >= 0)
        def _():
            from_side(z - k)
            dot(z - k)

        @pl.when(z + k < chips)
        def _():
            from_side(z + k)
            dot(z + k)

    for y in range(chips):
        j = 2 * y + c
        for q in range(cuts):
            pl.when(has_up & (z >= y))(lambda: remote(piece(j, q), j, q, send_up, up).wait_send())
            pl.when(has_down & (z <= y))(
                lambda: remote(piece(j, q), j, q, send_down, down).wait_send()
            )
            remote(piece(j, q), j, q, send_side, side).wait_send()
    for wait in waits:
        wait()


def line_gather(cid, x, w=None, swaps=(), cuts=2, tile=512):
    nb = lax.axis_size("blk")
    all_rows = nb * x.shape[0]
    with_dot = w is not None
    place = VMEM if with_dot else ANY
    outs = [jax.ShapeDtypeStruct((all_rows, x.shape[1]), x.dtype)]
    flops = 0
    if with_dot:
        outs.append(jax.ShapeDtypeStruct((all_rows, w.shape[1]), jnp.bfloat16))
        flops = 2 * all_rows * w.shape[0] * w.shape[1]
        tile = min(tile, w.shape[1])
    return pl.pallas_call(
        functools.partial(gather_kernel, nb // 2, cuts, tile, with_dot, len(swaps)),
        out_shape=outs + [like(value) for value in swaps],
        in_specs=[place] * (1 + with_dot) + [ANY] * len(swaps),
        out_specs=[place] * (1 + with_dot) + [ANY] * len(swaps),
        scratch_shapes=[pltpu.SemaphoreType.DMA]
        + [pltpu.SemaphoreType.DMA((nb, cuts))] * 4
        + swap_sems(swaps),
        compiler_params=params(cid),
        cost_estimate=cost(flops),
    )(*([x, w] if with_dot else [x]), *swaps)


def need_order(chips):
    table = []
    for z in range(chips):
        need = {
            y: (chips - 1 + z - y) if y > z else (chips - 1 - z + y)
            for y in range(chips) if y != z
        }
        table.append(sorted(need, key=lambda y: need[y]) + [z])
    return table


def pick(table, z, k):
    out = 0
    for at, row in enumerate(table):
        out = out + jnp.where(z == at, row[k], 0)
    return out


def scatter_kernel(chips, cuts, tile, n, *refs):
    refs = list(refs)
    a_ref, w_ref = refs.pop(0), refs.pop(0)
    srcs = [refs.pop(0) for _ in range(n)]
    o_ref = refs.pop(0)
    dsts = [refs.pop(0) for _ in range(n)]
    mine, away, side_buf, up_buf, down_buf, out_buf = refs[:6]
    send_side, recv_side, send_up, recv_up, send_down, recv_down = refs[6:12]
    starts, waits = swap_list(srcs, dsts, refs[12:])
    r, z, c = line_place()
    t, width = o_ref.shape
    low, f32 = away.dtype, jnp.float32
    up, down, side = (r, 2 * (z + 1) + c), (r, 2 * (z - 1) + c), (r, 2 * z + 1 - c)
    has_up, has_down = z < chips - 1, z > 0
    greet(chips, n > 0)
    h = t // cuts

    def remote(src, dst, y, q, send, recv, dev):
        return pltpu.make_async_remote_copy(
            src_ref=src.at[y, pl.ds(q * h, h)], dst_ref=dst.at[y, pl.ds(q * h, h)],
            send_sem=send.at[y, q], recv_sem=recv.at[y, q], device_id=dev, device_id_type=MESH,
        )

    def to_side(y, q):
        return remote(away, side_buf, y, q, send_side, recv_side, side)

    def to_up(y, q):
        return remote(out_buf, up_buf, y, q, send_up, recv_up, up)

    def to_down(y, q):
        return remote(out_buf, down_buf, y, q, send_down, recv_down, down)

    def rows(q):
        return pl.ds(q * h, h)

    def total(y, q):
        to_side(y, q).wait_recv()
        return mine[y, rows(q)].astype(f32) + side_buf[y, rows(q)].astype(f32)

    def make(y):
        a = a_ref[pl.ds(pl.multiple_of(2 * y * t, 2 * t), 2 * t)]

        def one(i, _):
            cols = pl.ds(pl.multiple_of(i * tile, tile), tile)
            got = lax.dot_general(
                a, w_ref[cols], (((1,), (1,)), ((), ())), preferred_element_type=f32
            ).astype(low)

            @pl.when(c == 0)
            def _():
                mine[y, :, cols] = got[:t]
                away[y, :, cols] = got[t:]

            @pl.when(c == 1)
            def _():
                mine[y, :, cols] = got[t:]
                away[y, :, cols] = got[:t]

            return 0

        lax.fori_loop(0, width // tile, one, 0)
        for q in range(cuts):
            to_side(y, q).start()

    table = need_order(chips)
    for s in range(chips):
        make(pick(table, z, s))
        if s == chips - 1:
            break
        y = chips - 1 + z - s
        w = s - (chips - 1) + z
        for q in range(cuts):
            @pl.when(y <= chips - 1)
            def _():
                now = total(y, q)

                @pl.when(has_down)
                def _():
                    to_up(y, q).wait_recv()
                    out_buf[y, rows(q)] = (now + up_buf[y, rows(q)].astype(f32)).astype(low)

                @pl.when(z == 0)
                def _():
                    out_buf[y, rows(q)] = now.astype(low)

                to_up(y, q).start()

            @pl.when(w >= 0)
            def _():
                now = total(w, q)

                @pl.when(has_up)
                def _():
                    to_down(w, q).wait_recv()
                    out_buf[w, rows(q)] = (now + down_buf[w, rows(q)].astype(f32)).astype(low)

                @pl.when(z == chips - 1)
                def _():
                    out_buf[w, rows(q)] = now.astype(low)

                to_down(w, q).start()

        if s == 0:
            for start in starts:
                start()
    for q in range(cuts):
        o_ref[rows(q)] = total(z, q)
    for q in range(cuts):
        @pl.when(has_down)
        def _():
            to_up(z, q).wait_recv()
            o_ref[rows(q)] += up_buf[z, rows(q)].astype(f32)

        @pl.when(has_up)
        def _():
            to_down(z, q).wait_recv()
            o_ref[rows(q)] += down_buf[z, rows(q)].astype(f32)

    for y in range(chips):
        for q in range(cuts):
            to_side(y, q).wait_send()
            pl.when(y > z)(lambda: to_up(y, q).wait_send())
            pl.when(y < z)(lambda: to_down(y, q).wait_send())
    for wait in waits:
        wait()


def dot_scatter(cid, a, w, swaps=(), cuts=2, tile=1024):
    nb = lax.axis_size("blk")
    t, width = a.shape[0] // nb, w.shape[0]
    n = len(swaps)
    sems = pltpu.SemaphoreType.DMA((nb // 2, cuts))
    return pl.pallas_call(
        functools.partial(scatter_kernel, nb // 2, cuts, tile, n),
        out_shape=[jax.ShapeDtypeStruct((t, width), jnp.float32)] + [like(s) for s in swaps],
        in_specs=[VMEM, VMEM] + [ANY] * n,
        out_specs=[VMEM] + [ANY] * n,
        scratch_shapes=[pltpu.VMEM((nb // 2, t, width), jnp.bfloat16)] * 6
        + [sems] * 6
        + swap_sems(swaps),
        compiler_params=params(cid),
        cost_estimate=cost(2 * a.shape[0] * width * w.shape[1]),
    )(a, w, *swaps)


def rope_tables(positions, head_size):
    halfway = head_size // 2
    frequency = jnp.exp(
        -jnp.arange(halfway, dtype=jnp.float32) * (2.0 / head_size) * math.log(theta_base)
    )
    angles = positions.astype(jnp.float32)[:, None] * frequency[None, :]
    return (jnp.cos(angles)[:, None, :], jnp.sin(angles)[:, None, :])


def rotate(values, cosine, sine_table):
    halfway = values.shape[-1] // 2
    front_half = values[..., :halfway]
    back_half = values[..., halfway:]
    return jnp.concatenate(
        [
            front_half * cosine - back_half * sine_table,
            back_half * cosine + front_half * sine_table,
        ],
        axis=-1,
    )


def rotate_back(values, cosine, sine_table):
    halfway = values.shape[-1] // 2
    front_half = values[..., :halfway]
    back_half = values[..., halfway:]
    return jnp.concatenate(
        [
            front_half * cosine + back_half * sine_table,
            back_half * cosine - front_half * sine_table,
        ],
        axis=-1,
    )


def norm_forward(values, gain_vector):
    inverse = lax.rsqrt(jnp.mean(values * values, axis=-1, keepdims=True) + norm_eps)
    unit_values = values * inverse
    return (unit_values, inverse, (unit_values * gain_vector).astype(jnp.bfloat16))


def norm_backward(grad_normed, unit_values, inverse, gain_vector):
    grad_unit = grad_normed * gain_vector
    grad_values = inverse * (
        grad_unit - unit_values * jnp.mean(grad_unit * unit_values, axis=-1, keepdims=True)
    )
    return (grad_values, jnp.sum(grad_normed * unit_values, axis=0))


def contract_last(left, right):
    return lax.dot_general(
        left, right, (((1,), (1,)), ((), ())), preferred_element_type=jnp.float32
    )


def adam_step(master, moment_one, moment_two, gradient):
    moment_one = beta_one * moment_one + (1.0 - beta_one) * gradient
    moment_two = beta_two * moment_two + (1.0 - beta_two) * gradient * gradient
    update = (
        moment_one
        / (1.0 - beta_one**step_count)
        / (jnp.sqrt(moment_two / (1.0 - beta_two**step_count)) + adam_eps)
    )
    return (master - learn_rate * (update + decay_rate * master), moment_one, moment_two)


def moment_step(moment_one, moment_two, gradient):
    moment_one = beta_one * moment_one + (1.0 - beta_one) * gradient
    moment_two = beta_two * moment_two + (1.0 - beta_two) * gradient * gradient
    return (moment_one, moment_two)


def beside_grid(n, starts, waits, chips):
    if not n:
        return lambda: None
    first = (pl.program_id(0) == 0) & (pl.program_id(1) == 0)
    last = (pl.program_id(0) == pl.num_programs(0) - 1) & (
        pl.program_id(1) == pl.num_programs(1) - 1
    )

    @pl.when(first)
    def _():
        greet(chips, True)
        for start in starts:
            start()

    def finish():
        @pl.when(last)
        def _():
            for wait in waits:
                wait()

    return finish


def attend_kernel(chips, n, *refs):
    q_ref, k_ref, v_ref, q_place, k_place, length_ref = refs[:6]
    o_ref, p_ref = refs[6 + n : 8 + n]
    starts, waits = swap_list(refs[6 : 6 + n], refs[8 + n : 8 + 2 * n], refs[8 + 2 * n :])
    finish = beside_grid(n, starts, waits, chips)
    scores = lax.dot_general(
        q_ref[0], k_ref[0], (((1,), (1,)), ((), ())), preferred_element_type=jnp.float32
    ) * (1.0 / math.sqrt(HEAD_DIM))
    place = q_place[...]
    scores = jnp.where(k_place[...] <= place, scores, neg_large)
    top = jnp.max(scores, axis=-1, keepdims=True)
    weights = jnp.exp(scores - top)
    weights = weights * (1.0 / jnp.sum(weights, axis=-1, keepdims=True))
    low = weights.astype(jnp.bfloat16)
    p_ref[0] = low
    out = jnp.dot(low, v_ref[0], preferred_element_type=jnp.float32)
    o_ref[0] = jnp.where(place < length_ref[0], out, 0.0).astype(jnp.bfloat16)
    finish()


def attend(cid, q, k, v, place, live_place, length, swaps=()):
    heads, seq, size = q.shape
    tile = 256
    n = len(swaps)
    whole = pl.BlockSpec((1, seq, size), lambda h, i: (h, 0, 0))
    part = pl.BlockSpec((1, tile, size), lambda h, i: (h, i, 0))
    return pl.pallas_call(
        functools.partial(attend_kernel, lax.axis_size("blk") // 2, n),
        grid=(heads, seq // tile),
        in_specs=[
            part,
            whole,
            whole,
            pl.BlockSpec((tile, 1), lambda h, i: (i, 0)),
            pl.BlockSpec((1, seq), lambda h, i: (0, 0)),
            pl.BlockSpec(memory_space=pltpu.SMEM),
        ]
        + [ANY] * n,
        out_specs=[part, pl.BlockSpec((1, tile, seq), lambda h, i: (h, i, 0))] + [ANY] * n,
        out_shape=[
            jax.ShapeDtypeStruct((heads, seq, size), jnp.bfloat16),
            jax.ShapeDtypeStruct((heads, seq, seq), jnp.bfloat16),
        ]
        + [like(value) for value in swaps],
        scratch_shapes=swap_sems(swaps),
        compiler_params=params(cid),
        cost_estimate=cost(4 * heads * seq * seq * size),
    )(q, k, v, place[:, None], live_place[None, :], length.reshape(1), *swaps)


def attend_back_kernel(chips, n, *refs):
    q_ref, k_ref, v_ref, o_ref, g_ref, p_ref = refs[:6]
    dq_ref, dk_ref, dv_ref = refs[6 + n : 9 + n]
    dk_acc, dv_acc = refs[9 + 2 * n : 11 + 2 * n]
    starts, waits = swap_list(refs[6 : 6 + n], refs[9 + n : 9 + 2 * n], refs[11 + 2 * n :])
    finish = beside_grid(n, starts, waits, chips)
    step = pl.program_id(1)

    @pl.when(step == 0)
    def _():
        dk_acc[...] = jnp.zeros_like(dk_acc)
        dv_acc[...] = jnp.zeros_like(dv_acc)

    f32 = jnp.float32
    low = p_ref[0]
    grad = g_ref[0]
    over_rows = (((0,), (0,)), ((), ()))
    dv_acc[...] += lax.dot_general(low, grad, over_rows, preferred_element_type=f32)
    delta = jnp.sum(grad.astype(f32) * o_ref[0].astype(f32), axis=-1, keepdims=True)
    grad_p = lax.dot_general(
        grad, v_ref[0], (((1,), (1,)), ((), ())), preferred_element_type=f32
    )
    grad_s = (low.astype(f32) * (grad_p - delta)).astype(jnp.bfloat16)
    factor = 1.0 / math.sqrt(HEAD_DIM)
    dq_ref[0] = jnp.dot(grad_s, k_ref[0], preferred_element_type=f32) * factor
    dk_acc[...] += lax.dot_general(grad_s, q_ref[0], over_rows, preferred_element_type=f32)

    @pl.when(step == pl.num_programs(1) - 1)
    def _():
        dk_ref[0] = dk_acc[...] * factor
        dv_ref[0] = dv_acc[...]

    finish()


def attend_back(cid, q, k, v, o, g, p, swaps=()):
    heads, seq, size = q.shape
    tile = 256
    n = len(swaps)
    whole = pl.BlockSpec((1, seq, size), lambda h, i: (h, 0, 0))
    part = pl.BlockSpec((1, tile, size), lambda h, i: (h, i, 0))
    shape = jax.ShapeDtypeStruct((heads, seq, size), jnp.float32)
    return pl.pallas_call(
        functools.partial(attend_back_kernel, lax.axis_size("blk") // 2, n),
        grid=(heads, seq // tile),
        in_specs=[
            part, whole, whole, part, part, pl.BlockSpec((1, tile, seq), lambda h, i: (h, i, 0)),
        ]
        + [ANY] * n,
        out_specs=[part, whole, whole] + [ANY] * n,
        out_shape=[shape] * 3 + [like(value) for value in swaps],
        scratch_shapes=[pltpu.VMEM((seq, size), jnp.float32)] * 2 + swap_sems(swaps),
        compiler_params=params(cid),
        cost_estimate=cost(10 * heads * seq * seq * size),
    )(q, k, v, o, g, p, *swaps)


def arrange_kernel(*refs):
    wide = refs[0].shape[1]
    out = refs[-1]
    for part, ref in enumerate(refs[:-1]):
        out[0, :, part * wide : (part + 1) * wide] = ref[...].astype(out.dtype)


def arrange(weight, parts):
    rows, columns = weight.shape
    nb = lax.axis_size("blk")
    wide = columns // (parts * nb)
    return pl.pallas_call(
        arrange_kernel,
        grid=(nb,),
        in_specs=[
            pl.BlockSpec((rows, wide), lambda j, part=part: (0, part * nb + j))
            for part in range(parts)
        ],
        out_specs=pl.BlockSpec((1, rows, parts * wide), lambda j: (j, 0, 0)),
        out_shape=jax.ShapeDtypeStruct((nb, rows, parts * wide), jnp.bfloat16),
        cost_estimate=pl.CostEstimate(
            flops=0, bytes_accessed=6 * rows * columns, transcendentals=0
        ),
    )(*([weight] * parts))


def over_rows(pieces):
    nb, rows, wide = pieces.shape
    return lax.all_gather(pieces.reshape(nb * rows, wide), "rows", axis=0, tiled=True)


def sum_rows(gradient):
    nb = lax.axis_size("blk")
    mine = lax.psum_scatter(
        gradient.astype(jnp.bfloat16), "rows", scatter_dimension=0, tiled=True
    )
    return mine.reshape(nb, mine.shape[0] // nb, mine.shape[1])


def step_kernel(with_master, grad, *refs):
    gradient = grad[0].astype(jnp.float32)
    if with_master:
        master, one, two, master_next, one_next, two_next = refs
        master_next[...], one_next[...], two_next[...] = adam_step(
            master[...], one[...], two[...], gradient
        )
    else:
        one, two, one_next, two_next = refs
        one_next[...], two_next[...] = moment_step(one[...], two[...], gradient)


def step(pieces, parts, states):
    nb = pieces.shape[0]
    rows, columns = states[0].shape
    wide = columns // (parts * nb)
    at = pl.BlockSpec((rows, wide), lambda j, part: (0, part * nb + j))
    outs = len(states)
    return pl.pallas_call(
        functools.partial(step_kernel, outs == 3),
        grid=(nb, parts),
        in_specs=[pl.BlockSpec((1, rows, wide), lambda j, part: (j, 0, part))] + [at] * outs,
        out_specs=[at] * outs,
        out_shape=[jax.ShapeDtypeStruct((rows, columns), jnp.float32)] * outs,
        cost_estimate=pl.CostEstimate(
            flops=0, bytes_accessed=(8 * outs + 2) * rows * columns, transcendentals=0
        ),
    )(pieces, *states)


def total_kernel(nr, nb, x_ref, o_ref, held, rows_held, send_one, recv_one, send_two, recv_two):
    r, b = lax.axis_index("rows"), lax.axis_index("blk")
    barrier = pltpu.get_barrier_semaphore()
    across = [lax.rem(b + k, nb) for k in range(1, nb)]
    along = [lax.rem(r + k, nr) for k in range(1, nr)]
    for other in across:
        pl.semaphore_signal(barrier, inc=1, device_id=(r, other), device_id_type=MESH)
    for other in along:
        pl.semaphore_signal(barrier, inc=1, device_id=(other, b), device_id_type=MESH)
    pl.semaphore_wait(barrier, nb + nr - 2)
    held[b] = x_ref[...]

    def first(other, slot):
        return pltpu.make_async_remote_copy(
            src_ref=held.at[b], dst_ref=held.at[slot], send_sem=send_one.at[other],
            recv_sem=recv_one.at[slot], device_id=(r, other), device_id_type=MESH,
        )

    def second(other, slot):
        return pltpu.make_async_remote_copy(
            src_ref=rows_held.at[r], dst_ref=rows_held.at[slot], send_sem=send_two.at[other],
            recv_sem=recv_two.at[slot], device_id=(other, b), device_id_type=MESH,
        )

    for other in across:
        first(other, b).start()
    for other in across:
        first(other, other).wait_recv()
    rows_held[r] = jnp.sum(held[...], axis=0)
    for other in along:
        second(other, r).start()
    for other in along:
        second(other, other).wait_recv()
    o_ref[...] = jnp.sum(rows_held[...], axis=0)
    for other in across:
        first(other, b).wait_send()
    for other in along:
        second(other, r).wait_send()


def total_of(x, cid):
    nr, nb = lax.axis_size("rows"), lax.axis_size("blk")
    return pl.pallas_call(
        functools.partial(total_kernel, nr, nb),
        out_shape=jax.ShapeDtypeStruct(x.shape, x.dtype),
        in_specs=[pl.BlockSpec(memory_space=pltpu.VMEM)],
        out_specs=pl.BlockSpec(memory_space=pltpu.VMEM),
        scratch_shapes=[pltpu.VMEM((nb,) + x.shape, x.dtype), pltpu.VMEM((nr,) + x.shape, x.dtype)]
        + [pltpu.SemaphoreType.DMA((nb,))] * 2 + [pltpu.SemaphoreType.DMA((nr,))] * 2,
        compiler_params=pltpu.CompilerParams(collective_id=cid, has_side_effects=True),
    )(x)


def after(value, *others):
    return lax.optimization_barrier((value,) + others)[0]


def over_tokens(left, right):
    return lax.dot_general(
        left, right, (((0,), (0,)), ((), ())), preferred_element_type=jnp.float32
    )


def shards(
    tokens, cotangent, lengths, block_map, gain_attend, gain_expand,
    attend_in, attend_out, expand_in, reduce_out,
    attend_in_first, attend_out_first, expand_in_first, reduce_out_first,
    attend_in_second, attend_out_second, expand_in_second, reduce_out_second,
):
    f32, bf16 = jnp.float32, jnp.bfloat16
    nb = lax.axis_size("blk")
    near = tokens.shape[1]
    seq = near * nb
    heads = HEADS // nb
    block_rows = near // 2
    length = lengths[0]
    offsets = jnp.arange(block_rows, dtype=jnp.int32)
    place = (block_map[0][:, None] * block_rows + offsets[None, :]).reshape(-1)
    live_place = jnp.where(place < length, place, jnp.int32(1 << 30))
    cosine, sine = rope_tables(place, HEAD_DIM)

    x = tokens[0].astype(f32)
    unit_one, inverse_one, h1 = norm_forward(x, gain_attend)
    swap_in, swap_out = swap(2, arrange(attend_in, 3), arrange(attend_out.T, 1))
    w_in = over_rows(swap_in)
    w_out = over_rows(swap_out)
    h1_all, swap_gu = line_gather(3, after(h1, swap_in), swaps=[arrange(expand_in, 2)])
    w_gu = over_rows(swap_gu)

    mixed = jnp.dot(h1_all, w_in, preferred_element_type=f32).reshape(seq, 3, heads, HEAD_DIM)
    q = rotate(mixed[:, 0], cosine, sine).astype(bf16).transpose(1, 0, 2)
    k = rotate(mixed[:, 1], cosine, sine).astype(bf16).transpose(1, 0, 2)
    v = mixed[:, 2].astype(bf16).transpose(1, 0, 2)
    o, p, swap_red = attend(
        4, q, k, v, place, live_place, length, swaps=[arrange(reduce_out.T, 1)]
    )
    w_red = over_rows(swap_red)
    attended = o.transpose(1, 0, 2).reshape(seq, heads * HEAD_DIM)
    x1 = x + dot_scatter(5, attended, w_out)[0]
    unit_two, inverse_two, h2 = norm_forward(x1, gain_expand)
    h2_all, gate_up = line_gather(6, h2, w_gu)
    (g_all,) = line_gather(7, after(cotangent[0], gate_up))
    units = gate_up.shape[1] // 2
    gate, up = gate_up[:, :units].astype(f32), gate_up[:, units:].astype(f32)
    sigmoid = jax.nn.sigmoid(gate)
    silu = gate * sigmoid
    hidden = (silu * up).astype(bf16)
    part_reduce = over_tokens(g_all, hidden).astype(bf16)
    grad_hidden = jnp.dot(g_all, w_red, preferred_element_type=f32)
    grad_gate = grad_hidden * up * (sigmoid * (1.0 + gate * (1.0 - sigmoid)))
    grad_up = grad_hidden * silu
    grad_gu = jnp.concatenate([grad_gate, grad_up], axis=1).astype(bf16)
    part_expand = over_tokens(h2_all, grad_gu).astype(bf16)
    (grad_h2,) = dot_scatter(8, after(grad_gu, part_expand, part_reduce), w_gu)
    rows_reduce = sum_rows(part_reduce)
    rows_expand = sum_rows(part_expand)
    middle, gain_two = norm_backward(grad_h2, unit_two, inverse_two, gain_expand)
    grad_x1 = cotangent[0].astype(f32) + middle
    branch_all, grad_o = line_gather(9, grad_x1.astype(bf16), w_out)
    part_out = over_tokens(branch_all, attended).astype(bf16)
    rows_out = sum_rows(part_out)
    grad_o = jnp.where((place < length)[:, None], grad_o, jnp.zeros((), bf16))
    grad_o = grad_o.reshape(seq, heads, HEAD_DIM).transpose(1, 0, 2)
    grad_q, grad_k, grad_v, own_reduce = attend_back(
        10, q, k, v, o, after(grad_o, part_out), p, swaps=[rows_reduce]
    )

    def by_token(value):
        return value.astype(bf16).astype(f32).transpose(1, 0, 2)

    grad_mixed = jnp.stack(
        [
            rotate_back(by_token(grad_q), cosine, sine),
            rotate_back(by_token(grad_k), cosine, sine),
            by_token(grad_v),
        ],
        axis=1,
    ).reshape(seq, -1).astype(bf16)
    part_in = over_tokens(h1_all, grad_mixed).astype(bf16)
    grad_h1, own_expand = dot_scatter(11, after(grad_mixed, part_in), w_in, swaps=[rows_expand])
    rows_in = sum_rows(part_in)
    y, own_out, own_in = dot_scatter(
        12, after(hidden, grad_h1), w_red, swaps=[rows_out, rows_in]
    )
    y = x1 + y
    first, gain_one = norm_backward(grad_h1, unit_one, inverse_one, gain_attend)
    grad_input = grad_x1 + first
    gains = total_of(jnp.stack([gain_one, gain_two]), 13)
    set_three = step(own_expand, 2, (expand_in, expand_in_first, expand_in_second))
    set_four = step(own_reduce, 1, (reduce_out.T, reduce_out_first.T, reduce_out_second.T))
    set_two = step(own_out, 1, (attend_out_first.T, attend_out_second.T))
    set_one = step(own_in, 3, (attend_in, attend_in_first, attend_in_second))
    return (
        y.astype(bf16).reshape(tokens.shape),
        grad_input.reshape(tokens.shape),
        gains[0],
        gains[1],
        *set_one,
        *[value.T for value in set_two],
        *set_three,
        *[value.T for value in set_four],
    )


def solution(mesh):
    placed = (
        P("rows", "blk", None),
        P("rows", "blk", None),
        P("rows"),
        P("rows", None),
        P(),
        P(),
        P(("rows", "blk"), None),
        P(None, ("rows", "blk")),
        P(("rows", "blk"), None),
        P(None, ("rows", "blk")),
        P(("rows", "blk"), None),
        P(None, ("rows", "blk")),
        P(("rows", "blk"), None),
        P(None, ("rows", "blk")),
        P(("rows", "blk"), None),
        P(None, ("rows", "blk")),
        P(("rows", "blk"), None),
        P(None, ("rows", "blk")),
    )
    return jax.shard_map(
        shards,
        mesh=mesh,
        in_specs=placed,
        out_specs=(
            P("rows", "blk", None),
            P("rows", "blk", None),
            P(),
            P(),
            P(("rows", "blk"), None),
            P(("rows", "blk"), None),
            P(("rows", "blk"), None),
            P(None, ("rows", "blk")),
            P(None, ("rows", "blk")),
            P(("rows", "blk"), None),
            P(("rows", "blk"), None),
            P(("rows", "blk"), None),
            P(None, ("rows", "blk")),
            P(None, ("rows", "blk")),
            P(None, ("rows", "blk")),
        ),
        check_vma=False,
    )
```

```python
import functools
import math

import jax
import jax.numpy as jnp
from jax import lax
from jax.experimental import pallas as pl
from jax.experimental.pallas import tpu as pltpu
from jax.sharding import PartitionSpec as P

HEADS = 32
HEAD_DIM = 64
MESH = pl.DeviceIdType.MESH
MIB = 1 << 20

theta_base = 130000.0
norm_eps = 1e-05
neg_large = -1e30
beta_one = 0.9
beta_two = 0.95
learn_rate = 0.01
decay_rate = 0.1
adam_eps = 1e-08
step_count = 10


def line_place():
    b = lax.axis_index("blk")
    return lax.axis_index("rows"), b // 2, b % 2


def greet(chips, swaps):
    r, z, c = line_place()
    barrier = pltpu.get_barrier_semaphore()

    def signal(b):
        pl.semaphore_signal(barrier, inc=1, device_id=(r, b), device_id_type=MESH)

    if swaps:
        b, nb = 2 * z + c, 2 * chips
        for k in range(1, nb):
            signal(lax.rem(b + k, nb))
        pl.semaphore_wait(barrier, nb - 1)
        return
    signal(2 * z + 1 - c)
    pl.when(z < chips - 1)(lambda: signal(2 * (z + 1) + c))
    pl.when(z > 0)(lambda: signal(2 * (z - 1) + c))
    pl.semaphore_wait(barrier, 1 + (z < chips - 1).astype(jnp.int32) + (z > 0).astype(jnp.int32))


def swap_copies(src, dst, local, send, recv):
    r, b = lax.axis_index("rows"), lax.axis_index("blk")
    nb = src.shape[0]
    others = [lax.rem(b + k, nb) for k in range(1, nb)]

    def remote(other, slot):
        return pltpu.make_async_remote_copy(
            src_ref=src.at[other], dst_ref=dst.at[slot], send_sem=send.at[other],
            recv_sem=recv.at[slot], device_id=(r, other), device_id_type=MESH,
        )

    def start():
        for other in others:
            remote(other, b).start()
        pltpu.make_async_copy(src.at[b], dst.at[b], local).start()

    def wait():
        for other in others:
            remote(other, other).wait_recv()
        for other in others:
            remote(other, b).wait_send()
        pltpu.make_async_copy(src.at[b], dst.at[b], local).wait()

    return start, wait


def swap_sems(swaps):
    sems = []
    for pieces in swaps:
        sems += [pltpu.SemaphoreType.DMA] + [pltpu.SemaphoreType.DMA((pieces.shape[0],))] * 2
    return sems


def swap_list(srcs, dsts, sems):
    made = [swap_copies(s, d, *sems[3 * i : 3 * i + 3]) for i, (s, d) in enumerate(zip(srcs, dsts))]
    return [one[0] for one in made], [one[1] for one in made]


def like(value):
    return jax.ShapeDtypeStruct(value.shape, value.dtype)


ANY = pl.BlockSpec(memory_space=pl.ANY)
VMEM = pl.BlockSpec(memory_space=pltpu.VMEM)


def params(cid):
    return pltpu.CompilerParams(
        collective_id=cid, has_side_effects=True, vmem_limit_bytes=60 * MIB
    )


def cost(flops):
    return pl.CostEstimate(flops=flops, bytes_accessed=150_000_000, transcendentals=0)


def gather_task(chips, cuts, x_ref, o_ref, sems):
    copy_sem, send_up, send_down, send_side, recv = sems
    r, z, c = line_place()
    t = x_ref.shape[0]
    h = t // cuts
    up, down, side = (r, 2 * (z + 1) + c), (r, 2 * (z - 1) + c), (r, 2 * z + 1 - c)
    has_up, has_down = z < chips - 1, z > 0
    mine = 2 * z + c

    def piece(j, q):
        return o_ref.at[pl.ds(pl.multiple_of(j * t + q * h, h), h)]

    def remote(src, j, q, sem, dev):
        return pltpu.make_async_remote_copy(
            src_ref=src, dst_ref=piece(j, q), send_sem=sem.at[j, q], recv_sem=recv.at[j, q],
            device_id=dev, device_id_type=MESH,
        )

    def local():
        whole = o_ref.at[pl.ds(pl.multiple_of(mine * t, t), t)]
        return pltpu.make_async_copy(x_ref, whole, copy_sem)

    def start():
        for q in range(cuts):
            from_here = x_ref.at[pl.ds(q * h, h)]
            pl.when(has_up)(lambda: remote(from_here, mine, q, send_up, up).start())
            pl.when(has_down)(lambda: remote(from_here, mine, q, send_down, down).start())
            remote(from_here, mine, q, send_side, side).start()
        local().start()

    def hop(k):
        for q in range(cuts):
            @pl.when(z - k >= 0)
            def _():
                j = 2 * (z - k) + c
                remote(piece(j, q), j, q, send_up, up).wait_recv()
                pl.when(has_up)(lambda: remote(piece(j, q), j, q, send_up, up).start())
                remote(piece(j, q), j, q, send_side, side).start()

            @pl.when(z + k < chips)
            def _():
                j = 2 * (z + k) + c
                remote(piece(j, q), j, q, send_down, down).wait_recv()
                pl.when(has_down)(lambda: remote(piece(j, q), j, q, send_down, down).start())
                remote(piece(j, q), j, q, send_side, side).start()

    def from_side(y):
        for q in range(cuts):
            j = 2 * y + 1 - c
            remote(piece(j, q), j, q, send_side, side).wait_recv()

    def finish():
        for y in range(chips):
            j = 2 * y + c
            for q in range(cuts):
                pl.when(has_up & (z >= y))(
                    lambda: remote(piece(j, q), j, q, send_up, up).wait_send()
                )
                pl.when(has_down & (z <= y))(
                    lambda: remote(piece(j, q), j, q, send_down, down).wait_send()
                )
                remote(piece(j, q), j, q, send_side, side).wait_send()

    return start, hop, from_side, local, finish


def gather_sems(nb, cuts):
    return [pltpu.SemaphoreType.DMA] + [pltpu.SemaphoreType.DMA((nb, cuts))] * 4


def gather_kernel(chips, cuts, tile, n, ff, n_prod, *refs):
    refs = list(refs)
    x_ref = refs.pop(0)
    w_ref = refs.pop(0) if n_prod else None
    srcs = [refs.pop(0) for _ in range(n)]
    o_ref = refs.pop(0)
    prods = [refs.pop(0) for _ in range(n_prod)]
    dsts = [refs.pop(0) for _ in range(n)]
    begin, hop, from_side, local, finish = gather_task(chips, cuts, x_ref, o_ref, refs[:5])
    starts, waits = swap_list(srcs, dsts, refs[5:])
    r, z, c = line_place()
    t = x_ref.shape[0]
    f32 = jnp.float32
    greet(chips, n > 0)

    def dot(y):
        if not n_prod:
            return
        rows = pl.ds(pl.multiple_of(y * 2 * t, 2 * t), 2 * t)
        units = prods[0].shape[1]

        def product(at):
            cols = pl.ds(pl.multiple_of(at, tile), tile)
            return jnp.dot(o_ref[rows, :], w_ref[:, cols], preferred_element_type=f32)

        def one(i, _):
            cols = pl.ds(pl.multiple_of(i * tile, tile), tile)
            got = product(i * tile)
            if ff:
                up = product(units + i * tile)
                sigmoid = jax.nn.sigmoid(got)
                silu = got * sigmoid
                values = (silu * up, up * (sigmoid * (1.0 + got * (1.0 - sigmoid))), silu)
            else:
                values = (got,)
            for ref, value in zip(prods, values):
                ref[rows, cols] = value.astype(ref.dtype)
            return 0

        lax.fori_loop(0, units // tile, one, 0)

    begin()
    for start in starts:
        start()
    from_side(z)
    local().wait()
    dot(z)
    for k in range(1, chips):
        hop(k)

        @pl.when(z - k >= 0)
        def _():
            from_side(z - k)
            dot(z - k)

        @pl.when(z + k < chips)
        def _():
            from_side(z + k)
            dot(z + k)

    finish()
    for wait in waits:
        wait()


def line_gather(cid, x, w=None, swaps=(), ff=False, cuts=2, tile=512):
    nb = lax.axis_size("blk")
    all_rows = nb * x.shape[0]
    with_dot = w is not None
    place = VMEM if with_dot else ANY
    outs = [jax.ShapeDtypeStruct((all_rows, x.shape[1]), x.dtype)]
    flops, n_prod = 0, 0
    if with_dot:
        n_prod = 3 if ff else 1
        units = w.shape[1] // 2 if ff else w.shape[1]
        outs += [jax.ShapeDtypeStruct((all_rows, units), jnp.bfloat16)] * n_prod
        flops = 2 * all_rows * w.shape[0] * w.shape[1]
        tile = min(tile, units)
    return pl.pallas_call(
        functools.partial(gather_kernel, nb // 2, cuts, tile, len(swaps), ff, n_prod),
        out_shape=outs + [like(value) for value in swaps],
        in_specs=[place] * (1 + with_dot) + [ANY] * len(swaps),
        out_specs=[place] * (1 + n_prod) + [ANY] * len(swaps),
        scratch_shapes=gather_sems(nb, cuts) + swap_sems(swaps),
        compiler_params=params(cid),
        cost_estimate=cost(flops),
    )(*([x, w] if with_dot else [x]), *swaps)


def need_order(chips):
    table = []
    for z in range(chips):
        need = {
            y: (chips - 1 + z - y) if y > z else (chips - 1 - z + y)
            for y in range(chips) if y != z
        }
        table.append(sorted(need, key=lambda y: need[y]) + [z])
    return table


def pick(table, z, k):
    out = 0
    for at, row in enumerate(table):
        for step, block in enumerate(row):
            out = out + jnp.where((z == at) & (k == step), block, 0)
    return out


def scatter_task(chips, cuts, tile, o_ref, bufs, sems):
    mine, away, side_buf, line_buf = bufs
    send_side, recv_side, send_up, recv_up, send_down, recv_down = sems
    r, z, c = line_place()
    t, width = o_ref.shape
    low, f32 = away.dtype, jnp.float32
    up, down, side = (r, 2 * (z + 1) + c), (r, 2 * (z - 1) + c), (r, 2 * z + 1 - c)
    has_up, has_down = z < chips - 1, z > 0
    h = t // cuts
    table = need_order(chips)

    def remote(src, dst, y, q, send, recv, dev):
        return pltpu.make_async_remote_copy(
            src_ref=src.at[y, pl.ds(q * h, h)], dst_ref=dst.at[y, pl.ds(q * h, h)],
            send_sem=send.at[y, q], recv_sem=recv.at[y, q], device_id=dev, device_id_type=MESH,
        )

    def to_side(y, q):
        return remote(away, side_buf, y, q, send_side, recv_side, side)

    def along(y, slot, q, send, recv, dev):
        return pltpu.make_async_remote_copy(
            src_ref=mine.at[y, pl.ds(q * h, h)], dst_ref=line_buf.at[slot, pl.ds(q * h, h)],
            send_sem=send.at[y, q], recv_sem=recv.at[y, q], device_id=dev, device_id_type=MESH,
        )

    def to_up(y, q):
        return along(y, y, q, send_up, recv_up, up)

    def to_down(y, q):
        return along(y, jnp.where(y == z - 1, chips, y), q, send_down, recv_down, down)

    def from_up(y, q):
        return along(y, jnp.where(y == z, chips, y), q, send_down, recv_down, down)

    def rows(q):
        return pl.ds(q * h, h)

    def total(y, q):
        to_side(y, q).wait_recv()
        return mine[y, rows(q)].astype(f32) + side_buf[y, rows(q)].astype(f32)

    def put(s, rows_of, w_ref):
        y = pick(table, z, s)
        a = rows_of(pl.ds(pl.multiple_of(2 * y * t, 2 * t), 2 * t))

        def one(i, _):
            cols = pl.ds(pl.multiple_of(i * tile, tile), tile)
            got = lax.dot_general(
                a[...], w_ref[cols], (((1,), (1,)), ((), ())), preferred_element_type=f32
            ).astype(low)

            @pl.when(c == 0)
            def _():
                mine[y, :, cols] = got[:t]
                away[y, :, cols] = got[t:]

            @pl.when(c == 1)
            def _():
                mine[y, :, cols] = got[t:]
                away[y, :, cols] = got[:t]

            return 0

        lax.fori_loop(0, width // tile, one, 0)
        for q in range(cuts):
            to_side(y, q).start()

    def hop(s):
        y = chips - 1 + z - s
        w = s - (chips - 1) + z
        for q in range(cuts):
            @pl.when(y <= chips - 1)
            def _():
                now = total(y, q)

                @pl.when(has_down)
                def _():
                    to_up(y, q).wait_recv()
                    mine[y, rows(q)] = (now + line_buf[y, rows(q)].astype(f32)).astype(low)

                @pl.when(z == 0)
                def _():
                    mine[y, rows(q)] = now.astype(low)

                to_up(y, q).start()

            @pl.when(w >= 0)
            def _():
                now = total(w, q)

                @pl.when(has_up)
                def _():
                    from_up(w, q).wait_recv()
                    mine[w, rows(q)] = (now + line_buf[w, rows(q)].astype(f32)).astype(low)

                @pl.when(z == chips - 1)
                def _():
                    mine[w, rows(q)] = now.astype(low)

                to_down(w, q).start()

    def finish():
        for q in range(cuts):
            o_ref[rows(q)] = total(z, q)
        for q in range(cuts):
            @pl.when(has_down)
            def _():
                to_up(z, q).wait_recv()
                o_ref[rows(q)] += line_buf[z, rows(q)].astype(f32)

            @pl.when(has_up)
            def _():
                from_up(z, q).wait_recv()
                o_ref[rows(q)] += line_buf[chips, rows(q)].astype(f32)

        for y in range(chips):
            for q in range(cuts):
                to_side(y, q).wait_send()
                pl.when(y > z)(lambda: to_up(y, q).wait_send())
                pl.when(y < z)(lambda: to_down(y, q).wait_send())

    return put, hop, finish


def scatter_scratch(chips, cuts, t, width):
    return (
        [pltpu.VMEM((chips, t, width), jnp.bfloat16)] * 3
        + [pltpu.VMEM((chips + 1, t, width), jnp.bfloat16)]
        + [pltpu.SemaphoreType.DMA((chips, cuts))] * 6
    )


def scatter_kernel(chips, cuts, tile, n, *refs):
    a_ref, w_ref, srcs, o_ref = refs[0], refs[1], refs[2 : 2 + n], refs[2 + n]
    dsts, refs = refs[3 + n : 3 + 2 * n], refs[3 + 2 * n :]
    put, hop, finish = scatter_task(chips, cuts, tile, o_ref, refs[:4], refs[4:10])
    starts, waits = swap_list(srcs, dsts, refs[10:])
    greet(chips, n > 0)
    for s in range(chips):
        put(s, lambda rows: a_ref.at[rows], w_ref)
        if s < chips - 1:
            hop(s)
        if s == 0:
            for start in starts:
                start()
    finish()
    for wait in waits:
        wait()


def ff_back_kernel(
    chips, cuts, tile, g_ref, one_ref, two_ref, red_ref, w_ref, h2_ref, o_ref, dw_ref, grad_ref, *refs
):
    put, hop, finish = scatter_task(chips, cuts, tile, o_ref, refs[:4], refs[4:10])
    f32 = jnp.float32
    units = red_ref.shape[1]
    span = min(512, units)
    greet(chips, False)

    def rows_of(rows):
        def one(i, _):
            cols = pl.ds(pl.multiple_of(i * span, span), span)
            more = pl.ds(pl.multiple_of(units + i * span, span), span)
            grad = jnp.dot(g_ref[rows], red_ref[:, cols], preferred_element_type=f32)
            grad_ref[rows, cols] = (grad * one_ref[rows, cols].astype(f32)).astype(grad_ref.dtype)
            grad_ref[rows, more] = (grad * two_ref[rows, cols].astype(f32)).astype(grad_ref.dtype)
            return 0

        lax.fori_loop(0, units // span, one, 0)
        return grad_ref.at[rows]

    for s in range(chips):
        put(s, rows_of, w_ref)
        if s < chips - 1:
            hop(s)

    def one(i, _):
        cols = pl.ds(pl.multiple_of(i * 256, 256), 256)
        dw_ref[cols] = lax.dot_general(
            h2_ref[:, cols], grad_ref[...], (((0,), (0,)), ((), ())), preferred_element_type=f32
        ).astype(dw_ref.dtype)
        return 0

    lax.fori_loop(0, dw_ref.shape[0] // 256, one, 0)
    finish()


def ff_back(cid, g_all, slope_gate, slope_up, w_red, w_gu, h2_all, cuts=2, tile=1024):
    nb = lax.axis_size("blk")
    seq, width = g_all.shape
    both = w_gu.shape[1]
    t = seq // nb
    return pl.pallas_call(
        functools.partial(ff_back_kernel, nb // 2, cuts, tile),
        out_shape=[
            jax.ShapeDtypeStruct((t, width), jnp.float32),
            jax.ShapeDtypeStruct((width, both), jnp.bfloat16),
        ],
        in_specs=[VMEM] * 6,
        out_specs=[VMEM] * 2,
        scratch_shapes=[pltpu.VMEM((seq, both), jnp.bfloat16)]
        + scatter_scratch(nb // 2, cuts, t, width),
        compiler_params=params(cid),
        cost_estimate=cost(5 * seq * width * both),
    )(g_all, slope_gate, slope_up, w_red, w_gu, h2_all)


def dot_scatter(cid, a, w, swaps=(), cuts=2, tile=1024):
    nb = lax.axis_size("blk")
    t, width = a.shape[0] // nb, w.shape[0]
    n = len(swaps)
    return pl.pallas_call(
        functools.partial(scatter_kernel, nb // 2, cuts, tile, n),
        out_shape=[jax.ShapeDtypeStruct((t, width), jnp.float32)] + [like(s) for s in swaps],
        in_specs=[VMEM, VMEM] + [ANY] * n,
        out_specs=[VMEM] + [ANY] * n,
        scratch_shapes=scatter_scratch(nb // 2, cuts, t, width) + swap_sems(swaps),
        compiler_params=params(cid),
        cost_estimate=cost(2 * a.shape[0] * width * w.shape[1]),
    )(a, w, *swaps)


def pair_tables(positions):
    half = HEAD_DIM // 2
    frequency = jnp.exp(
        -jnp.arange(half, dtype=jnp.float32) * (2.0 / HEAD_DIM) * math.log(theta_base)
    )
    angles = positions.astype(jnp.float32)[:, None] * frequency[None, :]
    cosine, sine = jnp.cos(angles), jnp.sin(angles)
    return (
        jnp.concatenate([cosine] * 4, axis=1),
        jnp.concatenate([-sine, sine] * 2, axis=1),
    )


def norm_forward(values, gain_vector):
    inverse = lax.rsqrt(jnp.mean(values * values, axis=-1, keepdims=True) + norm_eps)
    unit_values = values * inverse
    return (unit_values, inverse, (unit_values * gain_vector).astype(jnp.bfloat16))


def norm_backward(grad_normed, unit_values, inverse, gain_vector):
    grad_unit = grad_normed * gain_vector
    grad_values = inverse * (
        grad_unit - unit_values * jnp.mean(grad_unit * unit_values, axis=-1, keepdims=True)
    )
    return (grad_values, jnp.sum(grad_normed * unit_values, axis=0))


def contract_last(left, right):
    return lax.dot_general(
        left, right, (((1,), (1,)), ((), ())), preferred_element_type=jnp.float32
    )


def adam_step(master, moment_one, moment_two, gradient):
    moment_one = beta_one * moment_one + (1.0 - beta_one) * gradient
    moment_two = beta_two * moment_two + (1.0 - beta_two) * gradient * gradient
    update = (
        moment_one
        / (1.0 - beta_one**step_count)
        / (jnp.sqrt(moment_two / (1.0 - beta_two**step_count)) + adam_eps)
    )
    return (master - learn_rate * (update + decay_rate * master), moment_one, moment_two)


def moment_step(moment_one, moment_two, gradient):
    moment_one = beta_one * moment_one + (1.0 - beta_one) * gradient
    moment_two = beta_two * moment_two + (1.0 - beta_two) * gradient * gradient
    return (moment_one, moment_two)


def once(*shape):
    return pl.BlockSpec(shape, lambda i: (0,) * len(shape), pipeline_mode=pl.Buffered(1))


def partner(values):
    width = values.shape[1]
    half = HEAD_DIM // 2
    feature = lax.broadcasted_iota(jnp.int32, values.shape, 1) % HEAD_DIM
    return jnp.where(
        feature < half, pltpu.roll(values, width - half, 1), pltpu.roll(values, half, 1)
    )


def spread_table(table, width):
    return jnp.concatenate([table] * (width // table.shape[1]), axis=1)


def head_lanes(shape):
    return lax.broadcasted_iota(jnp.int32, shape, 1) // HEAD_DIM


def attend_kernel(chips, cuts, n, h1_ref, w_ref, cos_ref, sin_ref, q_place, k_place, length_ref, g_ref, *refs):
    srcs, refs = refs[:n], refs[n:]
    o_ref, q_ref, k_ref, v_ref, p_ref, g_all = refs[:6]
    dsts, sems = refs[6 : 6 + n], refs[6 + n :]
    begin, hop, from_side, local, finish = gather_task(chips, cuts, g_ref, g_all, sems[:5])
    starts, waits = swap_list(srcs, dsts, sems[5:])
    step, steps = pl.program_id(0), pl.num_programs(0)
    tile, width = o_ref.shape
    f32, bf16 = jnp.float32, jnp.bfloat16

    @pl.when(step == 0)
    def _():
        greet(chips, True)
        for start in starts:
            start()
        begin()

        def one(i, _):
            rows = pl.ds(pl.multiple_of(i * tile, tile), tile)
            mixed = jnp.dot(h1_ref[rows], w_ref[...], preferred_element_type=f32)
            cosine, sine = spread_table(cos_ref[rows], width), spread_table(sin_ref[rows], width)
            for at, ref in enumerate((q_ref, k_ref)):
                got = mixed[:, at * width : (at + 1) * width]
                ref[rows] = (got * cosine + partner(got) * sine).astype(bf16)
            v_ref[rows] = mixed[:, 2 * width :].astype(bf16)
            return 0

        lax.fori_loop(0, steps, one, 0)

    @pl.when((step > 0) & (step < chips))
    def _():
        hop(step)

    rows = pl.ds(pl.multiple_of(step * tile, tile), tile)
    queries = q_ref[rows] * jnp.asarray(1.0 / math.sqrt(HEAD_DIM), bf16)
    lanes = head_lanes((tile, width))
    place = q_place[...]
    allowed = k_place[...] <= place
    out = jnp.zeros((tile, width), f32)
    for head in range(width // HEAD_DIM):
        here = lanes == head
        one_head = jnp.where(here, queries, jnp.zeros((), bf16))
        scores = lax.dot_general(
            one_head, k_ref[...], (((1,), (1,)), ((), ())), preferred_element_type=f32
        )
        scores = jnp.where(allowed, scores, neg_large)
        weights = jnp.exp(scores - jnp.max(scores, axis=-1, keepdims=True))
        weights = weights * (1.0 / jnp.sum(weights, axis=-1, keepdims=True))
        low = weights.astype(bf16)
        p_ref[head] = low
        out = jnp.where(here, jnp.dot(low, v_ref[...], preferred_element_type=f32), out)
    o_ref[...] = jnp.where(place < length_ref[0], out, 0.0).astype(bf16)

    @pl.when(step == steps - 1)
    def _():
        local().wait()
        for y in range(chips):
            from_side(y)
        finish()
        for wait in waits:
            wait()


def attend(cid, h1_all, w_in, cosine, sine, place, live_place, length, g, swaps=(), cuts=2):
    seq, wide = h1_all.shape
    width = w_in.shape[1] // 3
    heads = width // HEAD_DIM
    nb = lax.axis_size("blk")
    tile = seq // (nb // 2)
    n = len(swaps)
    part = pl.BlockSpec((tile, width), lambda i: (i, 0))

    full = jax.ShapeDtypeStruct((seq, width), jnp.bfloat16)
    return pl.pallas_call(
        functools.partial(attend_kernel, nb // 2, cuts, n),
        grid=(seq // tile,),
        in_specs=[
            once(seq, wide), once(wide, 3 * width), once(seq, 2 * HEAD_DIM), once(seq, 2 * HEAD_DIM),
            pl.BlockSpec((tile, 1), lambda i: (i, 0)),
            once(1, seq),
            pl.BlockSpec(memory_space=pltpu.SMEM),
            ANY,
        ]
        + [ANY] * n,
        out_specs=[part] + [once(seq, width)] * 3
        + [pl.BlockSpec((heads, tile, seq), lambda i: (0, i, 0)), ANY] + [ANY] * n,
        out_shape=[full] * 4
        + [
            jax.ShapeDtypeStruct((heads, seq, seq), jnp.bfloat16),
            jax.ShapeDtypeStruct((seq, g.shape[1]), g.dtype),
        ]
        + [like(value) for value in swaps],
        scratch_shapes=gather_sems(nb, cuts) + swap_sems(swaps),
        compiler_params=params(cid),
        cost_estimate=cost(4 * seq * seq * width + 6 * seq * wide * width),
    )(h1_all, w_in, cosine, sine, place[:, None], live_place[None, :], length.reshape(1), g, *swaps)


def attend_back_kernel(
    chips, cuts, tile_y, q_ref, k_ref, v_ref, o_ref, g_ref, p_ref, cos_ref, sin_ref, q_place, length_ref,
    hidden_ref, red_ref, mixed_ref, y_ref, ds_ref, qm_ref, gm_ref, dk_acc, dv_acc, *refs
):
    put, hop, finish = scatter_task(chips, cuts, tile_y, y_ref, refs[:4], refs[4:10])
    step, steps = pl.program_id(0), pl.num_programs(0)
    tile, width = o_ref.shape
    f32, bf16 = jnp.float32, jnp.bfloat16
    factor = 1.0 / math.sqrt(HEAD_DIM)

    @pl.when(step == 0)
    def _():
        greet(chips, False)
        dk_acc[...] = jnp.zeros_like(dk_acc)
        dv_acc[...] = jnp.zeros_like(dv_acc)

    put(step, lambda rows: hidden_ref.at[rows], red_ref)
    pl.when(step == 0)(lambda: hop(step))
    over_rows = (((0,), (0,)), ((), ()))
    rows = pl.ds(pl.multiple_of(step * tile, tile), tile)
    lanes = head_lanes((tile, width))
    nothing = jnp.zeros((), bf16)
    grad = jnp.where(q_place[...] < length_ref[0], g_ref[...], nothing)
    both = grad.astype(f32) * o_ref[...].astype(f32)
    queries = q_ref[rows]
    grad_q = jnp.zeros((tile, width), f32)
    for head in range(width // HEAD_DIM):
        here = lanes == head
        block = pl.ds(head * tile, tile)
        delta = jnp.sum(jnp.where(here, both, 0.0), axis=-1, keepdims=True)
        one_grad = jnp.where(here, grad, nothing)
        gm_ref[block] = one_grad
        qm_ref[block] = jnp.where(here, queries, nothing)
        grad_p = lax.dot_general(
            one_grad, v_ref[...], (((1,), (1,)), ((), ())), preferred_element_type=f32
        )
        grad_s = (p_ref[head].astype(f32) * (grad_p - delta)).astype(bf16)
        ds_ref[block] = grad_s
        grad_q = jnp.where(here, jnp.dot(grad_s, k_ref[...], preferred_element_type=f32), grad_q)
    heads = width // HEAD_DIM
    dv_acc[...] += lax.dot_general(
        p_ref[...].reshape(heads * tile, p_ref.shape[2]), gm_ref[...], over_rows,
        preferred_element_type=f32,
    )
    dk_acc[...] += lax.dot_general(ds_ref[...], qm_ref[...], over_rows, preferred_element_type=f32)

    def back(value, cosine, sine):
        value = (value * factor).astype(bf16).astype(f32)
        cosine, sine = spread_table(cosine, width), spread_table(sine, width)
        return (value * cosine - partner(value) * sine).astype(bf16)

    mixed_ref[rows, :width] = back(grad_q, cos_ref[rows], sin_ref[rows])
    pl.when((step > 0) & (step < steps - 1))(lambda: hop(step))

    @pl.when(step == steps - 1)
    def _():
        mixed_ref[:, width : 2 * width] = back(dk_acc[...], cos_ref[...], sin_ref[...])
        mixed_ref[:, 2 * width :] = dv_acc[...].astype(bf16)
        finish()


def attend_back(cid, q, k, v, o, g, p, cosine, sine, place, length, hidden, w_red, cuts=2):
    seq, width = q.shape
    heads = width // HEAD_DIM
    nb = lax.axis_size("blk")
    tile = seq // (nb // 2)
    wide, units = w_red.shape
    part = pl.BlockSpec((tile, width), lambda i: (i, 0))

    full = once(seq, width)
    return pl.pallas_call(
        functools.partial(attend_back_kernel, nb // 2, cuts, 1024),
        grid=(seq // tile,),
        in_specs=[
            full, full, full, part, part,
            pl.BlockSpec((heads, tile, seq), lambda i: (0, i, 0)),
            once(seq, 2 * HEAD_DIM), once(seq, 2 * HEAD_DIM),
            pl.BlockSpec((tile, 1), lambda i: (i, 0)),
            pl.BlockSpec(memory_space=pltpu.SMEM),
            once(seq, units),
            once(wide, units),
        ],
        out_specs=[once(seq, 3 * width), once(seq // nb, wide)],
        out_shape=[
            jax.ShapeDtypeStruct((seq, 3 * width), jnp.bfloat16),
            jax.ShapeDtypeStruct((seq // nb, wide), jnp.float32),
        ],
        scratch_shapes=[
            pltpu.VMEM((heads * tile, seq), jnp.bfloat16),
            pltpu.VMEM((heads * tile, width), jnp.bfloat16),
            pltpu.VMEM((heads * tile, width), jnp.bfloat16),
            pltpu.VMEM((seq, width), jnp.float32),
            pltpu.VMEM((seq, width), jnp.float32),
        ]
        + scatter_scratch(nb // 2, cuts, seq // nb, wide),
        compiler_params=params(cid),
        cost_estimate=cost(10 * seq * seq * width),
    )(q, k, v, o, g, p, cosine, sine, place[:, None], length.reshape(1), hidden, w_red)


def arrange(weight, out, parts):
    nb, _, wide = out.shape
    span = wide // parts
    for j in range(nb):
        for part in range(parts):
            at = (part * nb + j) * span
            out[j, :, part * span : (part + 1) * span] = weight[:, at : at + span].astype(out.dtype)


def first_swap_kernel(parts, *refs):
    n = len(parts)
    weights, dsts, later, held, sems = (
        refs[:n], refs[n : n + 2], refs[n + 2 : 2 * n], refs[2 * n : 2 * n + 2], refs[2 * n + 2 :],
    )
    starts, waits = swap_list(held, dsts, sems)
    greet(held[0].shape[0] // 2, True)
    for weight, out, part, start in zip(weights, held, parts, starts):
        arrange(weight, out, part)
        start()
    for weight, out, part in zip(weights[2:], later, parts[2:]):
        arrange(weight, out, part)
    for wait in waits:
        wait()


def first_swap(cid, weights, parts):
    nb = lax.axis_size("blk")
    shapes = [(nb, value.shape[0], value.shape[1] // nb) for value in weights]
    n = len(weights)
    return pl.pallas_call(
        functools.partial(first_swap_kernel, parts),
        out_shape=[jax.ShapeDtypeStruct(shape, jnp.bfloat16) for shape in shapes],
        in_specs=[VMEM] * n,
        out_specs=[ANY] * 2 + [VMEM] * (n - 2),
        scratch_shapes=[pltpu.VMEM(shape, jnp.bfloat16) for shape in shapes[:2]]
        + [pltpu.SemaphoreType.DMA, pltpu.SemaphoreType.DMA((nb,)), pltpu.SemaphoreType.DMA((nb,))] * 2,
        compiler_params=params(cid),
        cost_estimate=cost(0),
    )(*weights)


def over_rows(pieces):
    nb, rows, wide = pieces.shape
    return lax.all_gather(pieces.reshape(nb * rows, wide), "rows", axis=0, tiled=True)


def sum_rows(gradient):
    nb = lax.axis_size("blk")
    mine = lax.psum_scatter(
        gradient.astype(jnp.bfloat16), "rows", scatter_dimension=0, tiled=True
    )
    return mine.reshape(nb, mine.shape[0] // nb, mine.shape[1])


def total_task(nr, nb, x_ref, o_ref, held, rows_held, send_one, recv_one, send_two, recv_two):
    r, b = lax.axis_index("rows"), lax.axis_index("blk")
    across = [lax.rem(b + k, nb) for k in range(1, nb)]
    along = [lax.rem(r + k, nr) for k in range(1, nr)]

    def first(other, slot):
        return pltpu.make_async_remote_copy(
            src_ref=held.at[b], dst_ref=held.at[slot], send_sem=send_one.at[other],
            recv_sem=recv_one.at[slot], device_id=(r, other), device_id_type=MESH,
        )

    def second(other, slot):
        return pltpu.make_async_remote_copy(
            src_ref=rows_held.at[r], dst_ref=rows_held.at[slot], send_sem=send_two.at[other],
            recv_sem=recv_two.at[slot], device_id=(other, b), device_id_type=MESH,
        )

    def greet_all():
        barrier = pltpu.get_barrier_semaphore()
        for other in across:
            pl.semaphore_signal(barrier, inc=1, device_id=(r, other), device_id_type=MESH)
        for other in along:
            pl.semaphore_signal(barrier, inc=1, device_id=(other, b), device_id_type=MESH)
        pl.semaphore_wait(barrier, nb + nr - 2)

    def start():
        held[b] = x_ref[...]
        for other in across:
            first(other, b).start()

    def middle():
        for other in across:
            first(other, other).wait_recv()
        rows_held[r] = jnp.sum(held[...], axis=0)
        for other in along:
            second(other, r).start()

    def finish():
        for other in along:
            second(other, other).wait_recv()
        o_ref[...] = jnp.sum(rows_held[...], axis=0)
        for other in across:
            first(other, b).wait_send()
        for other in along:
            second(other, r).wait_send()

    return greet_all, start, middle, finish


def last_scatter_kernel(chips, nr, cuts, tile, n, a_ref, w_ref, x_ref, inverse_ref, gain_ref, resid_ref, gain_two_ref, *refs):
    srcs, refs = refs[:n], refs[n:]
    o_ref, total_ref, dsts, refs = refs[0], refs[1], refs[2 : 2 + n], refs[2 + n :]
    sum_ref, part_ref, refs = refs[0], refs[1], refs[2:]
    put, hop, finish = scatter_task(chips, cuts, tile, sum_ref, refs[:4], refs[4:10])
    greet_all, start_total, middle, finish_total = total_task(
        nr, 2 * chips, part_ref, total_ref, *refs[10:16]
    )
    starts, waits = swap_list(srcs, dsts, refs[16:])
    greet_all()
    for s in range(chips):
        put(s, lambda rows: a_ref.at[rows], w_ref)
        if s < chips - 1:
            hop(s)
        if s == 0:
            starts[0]()
    finish()
    inverse = inverse_ref[...]
    unit = x_ref[...].astype(jnp.float32) * inverse
    grad, gain = norm_backward(sum_ref[...], unit, inverse, gain_ref[...])
    part_ref[0:1] = gain[None]
    part_ref[1:2] = gain_two_ref[...]
    start_total()
    for start in starts[1:]:
        start()
    o_ref[...] = resid_ref[...] + grad
    middle()
    finish_total()
    for wait in waits:
        wait()


def last_scatter(cid, a, w, x, inverse, gain, resid, gain_two, swaps, cuts=2, tile=1024):
    nr, nb = lax.axis_size("rows"), lax.axis_size("blk")
    t, width = x.shape
    n = len(swaps)
    pair = (2, width)
    dma, f32 = pltpu.SemaphoreType.DMA, jnp.float32
    return pl.pallas_call(
        functools.partial(last_scatter_kernel, nb // 2, nr, cuts, tile, n),
        out_shape=[jax.ShapeDtypeStruct((t, width), f32), jax.ShapeDtypeStruct(pair, f32)]
        + [like(value) for value in swaps],
        in_specs=[VMEM] * 7 + [ANY] * n,
        out_specs=[VMEM] * 2 + [ANY] * n,
        scratch_shapes=[pltpu.VMEM((t, width), f32), pltpu.VMEM(pair, f32)]
        + scatter_scratch(nb // 2, cuts, t, width)
        + [pltpu.VMEM((nb,) + pair, f32), pltpu.VMEM((nr,) + pair, f32)]
        + [dma((nb,))] * 2 + [dma((nr,))] * 2
        + swap_sems(swaps),
        compiler_params=params(cid),
        cost_estimate=cost(2 * a.shape[0] * width * w.shape[1]),
    )(a, w, x, inverse, gain[None], resid, gain_two[None], *swaps)


def step_kernel(grad, *refs):
    outs = len(refs) // 2
    wide = grad.shape[2]
    for j in range(grad.shape[0]):
        cols = slice(j * wide, (j + 1) * wide)
        gradient = grad[j].astype(jnp.float32)
        rule = adam_step if outs == 3 else moment_step
        for ref, value in zip(refs[outs:], rule(*[ref[:, cols] for ref in refs[:outs]], gradient)):
            ref[:, cols] = value


def step(pieces, parts, states):
    nb = pieces.shape[0]
    rows, columns = states[0].shape
    span = columns // parts
    tile = max(16, min(rows, (1 << 17) // span))
    at = pl.BlockSpec((tile, span), lambda part, i: (i, part))
    outs = len(states)
    return pl.pallas_call(
        step_kernel,
        grid=(parts, rows // tile),
        in_specs=[pl.BlockSpec((nb, tile, span // nb), lambda part, i: (0, i, part))] + [at] * outs,
        out_specs=[at] * outs,
        out_shape=[jax.ShapeDtypeStruct((rows, columns), jnp.float32)] * outs,
        compiler_params=pltpu.CompilerParams(vmem_limit_bytes=60 * MIB),
        cost_estimate=pl.CostEstimate(
            flops=0, bytes_accessed=(8 * outs + 2) * rows * columns, transcendentals=0
        ),
    )(pieces, *states)


def after(value, *others):
    return lax.optimization_barrier((value,) + others)[0]


def over_tokens(left, right):
    return lax.dot_general(
        left, right, (((0,), (0,)), ((), ())), preferred_element_type=jnp.float32
    )


def shards(
    tokens, cotangent, lengths, block_map, gain_attend, gain_expand,
    attend_in, attend_out, expand_in, reduce_out,
    attend_in_first, attend_out_first, expand_in_first, reduce_out_first,
    attend_in_second, attend_out_second, expand_in_second, reduce_out_second,
):
    f32, bf16 = jnp.float32, jnp.bfloat16
    nb = lax.axis_size("blk")
    near = tokens.shape[1]
    seq = near * nb
    heads = HEADS // nb
    block_rows = near // 2
    length = lengths[0]
    offsets = jnp.arange(block_rows, dtype=jnp.int32)
    place = (block_map[0][:, None] * block_rows + offsets[None, :]).reshape(-1)
    live_place = jnp.where(place < length, place, jnp.int32(1 << 30))
    cosine, sine = pair_tables(place)

    x = tokens[0].astype(f32)
    unit_one, inverse_one, h1 = norm_forward(x, gain_attend)
    swap_in, swap_out, pieces_gu, pieces_red = first_swap(
        2, (attend_in, attend_out.T, expand_in, reduce_out.T), (3, 1, 2, 1)
    )
    w_in = over_rows(swap_in)
    w_out = over_rows(swap_out)
    h1_all, swap_gu = line_gather(3, after(h1, swap_in), swaps=[pieces_gu])
    w_gu = over_rows(swap_gu)

    attended, q, k, v, p, g_all, swap_red = attend(
        4, h1_all, w_in, cosine, sine, place, live_place, length, cotangent[0],
        swaps=[pieces_red],
    )
    w_red = over_rows(swap_red)
    x1 = x + dot_scatter(5, attended, w_out)[0]
    unit_two, inverse_two, h2 = norm_forward(x1, gain_expand)
    h2_all, hidden, slope_gate, slope_up = line_gather(6, h2, w_gu, ff=True)
    part_reduce = over_tokens(g_all, hidden).astype(bf16)
    grad_h2, part_expand = ff_back(
        8, after(g_all, part_reduce), slope_gate, slope_up, w_red, w_gu, h2_all
    )
    rows_reduce = sum_rows(part_reduce)
    rows_expand = sum_rows(part_expand)
    middle, gain_two = norm_backward(grad_h2, unit_two, inverse_two, gain_expand)
    grad_x1 = cotangent[0].astype(f32) + middle
    branch_all, grad_o = line_gather(9, grad_x1.astype(bf16), w_out)
    part_out = over_tokens(branch_all, attended).astype(bf16)
    rows_out = sum_rows(part_out)
    grad_mixed, y = attend_back(
        10, q, k, v, attended, after(grad_o, part_out), p, cosine, sine, place, length, hidden, w_red
    )
    y = x1 + y
    part_in = over_tokens(h1_all, grad_mixed).astype(bf16)
    grad_input, gains, own_expand, own_reduce = last_scatter(
        11, after(grad_mixed, part_in), w_in, tokens[0], inverse_one, gain_attend, grad_x1, gain_two,
        [rows_expand, rows_reduce],
    )
    rows_in = sum_rows(part_in)
    rows_in, rows_out = after((rows_in, rows_out), own_expand)
    both = lax.all_to_all(
        jnp.concatenate([rows_in, rows_out], axis=2), "blk", 0, 0, tiled=True
    )
    set_three = step(own_expand, 2, (expand_in, expand_in_first, expand_in_second))
    set_four = step(own_reduce, 1, (reduce_out.T, reduce_out_first.T, reduce_out_second.T))
    both = after(both, set_three[2], set_four[2])
    width_in = rows_in.shape[2]
    set_one = step(both[:, :, :width_in], 3, (attend_in, attend_in_first, attend_in_second))
    set_two = step(both[:, :, width_in:], 1, (attend_out_first.T, attend_out_second.T))
    return (
        y.astype(bf16).reshape(tokens.shape),
        grad_input.reshape(tokens.shape),
        gains[0],
        gains[1],
        *set_one,
        *[value.T for value in set_two],
        *set_three,
        *[value.T for value in set_four],
    )


def solution(mesh):
    placed = (
        P("rows", "blk", None),
        P("rows", "blk", None),
        P("rows"),
        P("rows", None),
        P(),
        P(),
        P(("rows", "blk"), None),
        P(None, ("rows", "blk")),
        P(("rows", "blk"), None),
        P(None, ("rows", "blk")),
        P(("rows", "blk"), None),
        P(None, ("rows", "blk")),
        P(("rows", "blk"), None),
        P(None, ("rows", "blk")),
        P(("rows", "blk"), None),
        P(None, ("rows", "blk")),
        P(("rows", "blk"), None),
        P(None, ("rows", "blk")),
    )
    return jax.shard_map(
        shards,
        mesh=mesh,
        in_specs=placed,
        out_specs=(
            P("rows", "blk", None),
            P("rows", "blk", None),
            P(),
            P(),
            P(("rows", "blk"), None),
            P(("rows", "blk"), None),
            P(("rows", "blk"), None),
            P(None, ("rows", "blk")),
            P(None, ("rows", "blk")),
            P(("rows", "blk"), None),
            P(("rows", "blk"), None),
            P(("rows", "blk"), None),
            P(None, ("rows", "blk")),
            P(None, ("rows", "blk")),
            P(None, ("rows", "blk")),
        ),
        check_vma=False,
    )
```

```python
import functools
import math

import jax
import jax.numpy as jnp
from jax import lax
from jax.experimental import pallas as pl
from jax.experimental.pallas import tpu as pltpu
from jax.sharding import PartitionSpec as P

HEADS = 32
HEAD_DIM = 64
MESH = pl.DeviceIdType.MESH
MIB = 1 << 20

theta_base = 130000.0
norm_eps = 1e-05
neg_large = -1e30
beta_one = 0.9
beta_two = 0.95
learn_rate = 0.01
decay_rate = 0.1
adam_eps = 1e-08
step_count = 10


def line_place():
    b = lax.axis_index("blk")
    return lax.axis_index("rows"), b // 2, b % 2


def greet(chips, swaps):
    r, z, c = line_place()
    barrier = pltpu.get_barrier_semaphore()

    def signal(b):
        pl.semaphore_signal(barrier, inc=1, device_id=(r, b), device_id_type=MESH)

    if swaps:
        b, nb = 2 * z + c, 2 * chips
        for k in range(1, nb):
            signal(lax.rem(b + k, nb))
        pl.semaphore_wait(barrier, nb - 1)
        return
    signal(2 * z + 1 - c)
    pl.when(z < chips - 1)(lambda: signal(2 * (z + 1) + c))
    pl.when(z > 0)(lambda: signal(2 * (z - 1) + c))
    pl.semaphore_wait(barrier, 1 + (z < chips - 1).astype(jnp.int32) + (z > 0).astype(jnp.int32))


def swap_copies(src, dst, local, send, recv):
    r, b = lax.axis_index("rows"), lax.axis_index("blk")
    nb = src.shape[0]
    others = [lax.rem(b + k, nb) for k in range(1, nb)]

    def remote(other, slot):
        return pltpu.make_async_remote_copy(
            src_ref=src.at[other], dst_ref=dst.at[slot], send_sem=send.at[other],
            recv_sem=recv.at[slot], device_id=(r, other), device_id_type=MESH,
        )

    def start():
        for other in others:
            remote(other, b).start()
        pltpu.make_async_copy(src.at[b], dst.at[b], local).start()

    def wait():
        for other in others:
            remote(other, other).wait_recv()
        for other in others:
            remote(other, b).wait_send()
        pltpu.make_async_copy(src.at[b], dst.at[b], local).wait()

    return start, wait


def swap_sems(swaps):
    sems = []
    for pieces in swaps:
        sems += [pltpu.SemaphoreType.DMA] + [pltpu.SemaphoreType.DMA((pieces.shape[0],))] * 2
    return sems


def swap_list(srcs, dsts, sems):
    made = [swap_copies(s, d, *sems[3 * i : 3 * i + 3]) for i, (s, d) in enumerate(zip(srcs, dsts))]
    return [one[0] for one in made], [one[1] for one in made]


def like(value):
    return jax.ShapeDtypeStruct(value.shape, value.dtype)


ANY = pl.BlockSpec(memory_space=pl.ANY)
VMEM = pl.BlockSpec(memory_space=pltpu.VMEM)


def params(cid):
    return pltpu.CompilerParams(
        collective_id=cid, has_side_effects=True, vmem_limit_bytes=60 * MIB
    )


def cost(flops):
    return pl.CostEstimate(flops=flops, bytes_accessed=150_000_000, transcendentals=0)


def mover(pairs, sem):
    copies = [pltpu.make_async_copy(a, b, sem.at[i]) for i, (a, b) in enumerate(pairs)]

    def start(*which):
        for i in which or range(len(copies)):
            copies[i].start()

    def wait(*which):
        for i in which or range(len(copies)):
            copies[i].wait()

    return start, wait


def gather_task(chips, cuts, x_ref, o_ref, sems):
    copy_sem, send_up, send_down, send_side, recv = sems
    r, z, c = line_place()
    t = x_ref.shape[0]
    h = t // cuts
    up, down, side = (r, 2 * (z + 1) + c), (r, 2 * (z - 1) + c), (r, 2 * z + 1 - c)
    has_up, has_down = z < chips - 1, z > 0
    mine = 2 * z + c

    def piece(j, q):
        return o_ref.at[pl.ds(pl.multiple_of(j * t + q * h, h), h)]

    def remote(src, j, q, sem, dev):
        return pltpu.make_async_remote_copy(
            src_ref=src, dst_ref=piece(j, q), send_sem=sem.at[j, q], recv_sem=recv.at[j, q],
            device_id=dev, device_id_type=MESH,
        )

    def local():
        whole = o_ref.at[pl.ds(pl.multiple_of(mine * t, t), t)]
        return pltpu.make_async_copy(x_ref, whole, copy_sem)

    def start():
        for q in range(cuts):
            from_here = x_ref.at[pl.ds(q * h, h)]
            pl.when(has_up)(lambda: remote(from_here, mine, q, send_up, up).start())
            pl.when(has_down)(lambda: remote(from_here, mine, q, send_down, down).start())
            remote(from_here, mine, q, send_side, side).start()
        local().start()

    def hop(k):
        for q in range(cuts):
            @pl.when(z - k >= 0)
            def _():
                j = 2 * (z - k) + c
                remote(piece(j, q), j, q, send_up, up).wait_recv()
                pl.when(has_up)(lambda: remote(piece(j, q), j, q, send_up, up).start())
                remote(piece(j, q), j, q, send_side, side).start()

            @pl.when(z + k < chips)
            def _():
                j = 2 * (z + k) + c
                remote(piece(j, q), j, q, send_down, down).wait_recv()
                pl.when(has_down)(lambda: remote(piece(j, q), j, q, send_down, down).start())
                remote(piece(j, q), j, q, send_side, side).start()

    def from_side(y):
        for q in range(cuts):
            j = 2 * y + 1 - c
            remote(piece(j, q), j, q, send_side, side).wait_recv()

    def finish():
        for y in range(chips):
            j = 2 * y + c
            for q in range(cuts):
                pl.when(has_up & (z >= y))(
                    lambda: remote(piece(j, q), j, q, send_up, up).wait_send()
                )
                pl.when(has_down & (z <= y))(
                    lambda: remote(piece(j, q), j, q, send_down, down).wait_send()
                )
                remote(piece(j, q), j, q, send_side, side).wait_send()

    return start, hop, from_side, local, finish


def gather_sems(nb, cuts):
    return [pltpu.SemaphoreType.DMA] + [pltpu.SemaphoreType.DMA((nb, cuts))] * 4


def gather_kernel(chips, cuts, n, x_ref, *refs):
    srcs, o_ref, dsts, refs = refs[:n], refs[n], refs[n + 1 : 2 * n + 1], refs[2 * n + 1 :]
    begin, hop, from_side, local, finish = gather_task(chips, cuts, x_ref, o_ref, refs[:5])
    starts, waits = swap_list(srcs, dsts, refs[5:])
    greet(chips, n > 0)
    begin()
    for k in range(1, chips):
        if k == min(3, chips - 1):
            for start in starts:
                start()
        hop(k)
    local().wait()
    for y in range(chips):
        from_side(y)
    finish()
    for wait in waits:
        wait()


def line_gather(cid, x, swaps=(), cuts=4):
    nb, n = lax.axis_size("blk"), len(swaps)
    return pl.pallas_call(
        functools.partial(gather_kernel, nb // 2, cuts, n),
        out_shape=[jax.ShapeDtypeStruct((nb * x.shape[0], x.shape[1]), x.dtype)]
        + [like(value) for value in swaps],
        in_specs=[ANY] * (1 + n),
        out_specs=[ANY] * (1 + n),
        scratch_shapes=gather_sems(nb, cuts) + swap_sems(swaps),
        compiler_params=params(cid),
        cost_estimate=cost(0),
    )(x, *swaps)


def gather_dot_kernel(chips, cuts, tile, ff, n_prod, x_ref, w_hbm, *refs):
    refs = list(refs)
    g_hbm = refs.pop(0) if ff else None
    outs = [refs.pop(0) for _ in range(1 + n_prod)]
    dw_out = refs.pop(0) if ff else None
    held = [refs.pop(0) for _ in range(1 + n_prod)]
    w_ref, load_sem, save_sem = [refs.pop(0) for _ in range(3)]
    if ff:
        g_ref, acc_ref, dw_ref, dw_sem = [refs.pop(0) for _ in range(4)]
    o_ref, prods = held[0], held[1:]
    begin, hop, from_side, local, finish = gather_task(chips, cuts, x_ref, o_ref, refs)
    load, loaded = mover([(w_hbm, w_ref)] + ([(g_hbm, g_ref)] if ff else []), load_sem)
    r, z, c = line_place()
    t = x_ref.shape[0]
    f32 = jnp.float32
    load()
    greet(chips, False)
    begin()

    def saves(y):
        rows = pl.ds(pl.multiple_of(y * 2 * t, 2 * t), 2 * t)
        return mover([(a.at[rows], b.at[rows]) for a, b in zip(held, outs)], save_sem.at[y])

    def dot(y):
        rows = pl.ds(pl.multiple_of(y * 2 * t, 2 * t), 2 * t)
        units = prods[0].shape[1]

        def product(at):
            cols = pl.ds(pl.multiple_of(at, tile), tile)
            return jnp.dot(o_ref[rows, :], w_ref[:, cols], preferred_element_type=f32)

        def one(i, _):
            cols = pl.ds(pl.multiple_of(i * tile, tile), tile)
            got = product(i * tile)
            if ff:
                up = product(units + i * tile)
                sigmoid = jax.nn.sigmoid(got)
                silu = got * sigmoid
                values = (silu * up, up * (sigmoid * (1.0 + got * (1.0 - sigmoid))), silu)
            else:
                values = (got,)
            for ref, value in zip(prods, values):
                ref[rows, cols] = value.astype(ref.dtype)
            return 0

        lax.fori_loop(0, units // tile, one, 0)
        saves(y)[0]()

    deep = 256

    def more(y, first=False, last=False):
        if not ff:
            return
        rows = pl.ds(pl.multiple_of(y * 2 * t, 2 * t), 2 * t)

        def one(i, _):
            at = pl.ds(pl.multiple_of(i * deep, deep), deep)
            got = lax.dot_general(
                g_ref[rows, at], prods[0][rows, :], (((0,), (0,)), ((), ())),
                preferred_element_type=f32,
            )
            if not first:
                got = got + acc_ref[at]
            if last:
                dw_ref[at] = got.astype(dw_ref.dtype)
                save_dw(i).start()
            else:
                acc_ref[at] = got
            return 0

        lax.fori_loop(0, g_ref.shape[1] // deep, one, 0)

    def save_dw(i):
        at = pl.ds(pl.multiple_of(i * deep, deep), deep)
        return pltpu.make_async_copy(dw_ref.at[at], dw_out.at[at], dw_sem.at[i])

    from_side(z)
    local().wait()
    loaded()
    dot(z)
    more(z, first=True)
    for k in range(1, chips):
        hop(k)

        @pl.when(z - k >= 0)
        def _():
            from_side(z - k)
            dot(z - k)

        @pl.when(z + k < chips)
        def _():
            from_side(z + k)
            dot(z + k)

        if k < chips - 1:
            more(pick(arrival_order(chips), z, k))
    more(pick(arrival_order(chips), z, chips - 1), last=True)
    finish()
    for y in range(chips):
        saves(y)[1]()
    if ff:
        for i in range(g_ref.shape[1] // deep):
            save_dw(i).wait()


def arrival_order(chips):
    table = []
    for z in range(chips):
        row = [z]
        for k in range(1, chips):
            row += [y for y in (z - k, z + k) if 0 <= y < chips]
        table.append(row)
    return table


def gather_dot(cid, x, w, g_all=None, cuts=2, tile=512):
    nb = lax.axis_size("blk")
    ff = g_all is not None
    all_rows = nb * x.shape[0]
    n_prod = 3 if ff else 1
    units = w.shape[1] // 2 if ff else w.shape[1]
    tile = min(tile, units)
    dma, bf16 = pltpu.SemaphoreType.DMA, jnp.bfloat16
    shapes = [(all_rows, x.shape[1])] + [(all_rows, units)] * n_prod
    weight = (x.shape[1], units)
    scratch = [pltpu.VMEM(shape, bf16) for shape in shapes]
    scratch += [pltpu.VMEM(w.shape, w.dtype), dma((2,)), dma((nb // 2, len(shapes)))]
    if ff:
        scratch += [
            pltpu.VMEM(g_all.shape, g_all.dtype), pltpu.VMEM(weight, jnp.float32),
            pltpu.VMEM(weight, bf16), dma((x.shape[1] // 256,)),
        ]
    outs = shapes + ([weight] if ff else [])
    return pl.pallas_call(
        functools.partial(gather_dot_kernel, nb // 2, cuts, tile, ff, n_prod),
        out_shape=[jax.ShapeDtypeStruct(shape, bf16) for shape in outs],
        in_specs=[VMEM, ANY] + [ANY] * ff,
        out_specs=[ANY] * len(outs),
        scratch_shapes=scratch + gather_sems(nb, cuts),
        compiler_params=params(cid),
        cost_estimate=cost(2 * all_rows * w.shape[0] * w.shape[1]),
    )(x, w, *([g_all] if ff else []))


def need_order(chips):
    table = []
    for z in range(chips):
        need = {
            y: (chips - 1 + z - y) if y > z else (chips - 1 - z + y)
            for y in range(chips) if y != z
        }
        table.append(sorted(need, key=lambda y: need[y]) + [z])
    return table


def pick(table, z, k):
    out = 0
    for at, row in enumerate(table):
        for step, block in enumerate(row):
            out = out + jnp.where((z == at) & (k == step), block, 0)
    return out


def scatter_task(chips, cuts, tile, o_ref, bufs, sems):
    mine, away, side_buf, line_buf = bufs
    send_side, recv_side, send_up, recv_up, send_down, recv_down = sems
    r, z, c = line_place()
    t, width = o_ref.shape
    low, f32 = away.dtype, jnp.float32
    up, down, side = (r, 2 * (z + 1) + c), (r, 2 * (z - 1) + c), (r, 2 * z + 1 - c)
    has_up, has_down = z < chips - 1, z > 0
    h = t // cuts
    table = need_order(chips)

    def remote(src, dst, y, q, send, recv, dev):
        return pltpu.make_async_remote_copy(
            src_ref=src.at[y, pl.ds(q * h, h)], dst_ref=dst.at[y, pl.ds(q * h, h)],
            send_sem=send.at[y, q], recv_sem=recv.at[y, q], device_id=dev, device_id_type=MESH,
        )

    def to_side(y, q):
        return remote(away, side_buf, y, q, send_side, recv_side, side)

    def along(y, slot, q, send, recv, dev):
        return pltpu.make_async_remote_copy(
            src_ref=mine.at[y, pl.ds(q * h, h)], dst_ref=line_buf.at[slot, pl.ds(q * h, h)],
            send_sem=send.at[y, q], recv_sem=recv.at[y, q], device_id=dev, device_id_type=MESH,
        )

    def to_up(y, q):
        return along(y, y, q, send_up, recv_up, up)

    def to_down(y, q):
        return along(y, jnp.where(y == z - 1, chips, y), q, send_down, recv_down, down)

    def from_up(y, q):
        return along(y, jnp.where(y == z, chips, y), q, send_down, recv_down, down)

    def rows(q):
        return pl.ds(q * h, h)

    def total(y, q):
        to_side(y, q).wait_recv()
        return mine[y, rows(q)].astype(f32) + side_buf[y, rows(q)].astype(f32)

    def put(s, rows_of, w_ref, seen=None):
        y = pick(table, z, s)
        block = pl.ds(pl.multiple_of(2 * y * t, 2 * t), 2 * t)
        a = rows_of(block)

        def one(i, _):
            cols = pl.ds(pl.multiple_of(i * tile, tile), tile)
            got = lax.dot_general(
                a[...], w_ref[cols], (((1,), (1,)), ((), ())), preferred_element_type=f32
            )
            if seen is not None:
                seen(block, cols, got)
            got = got.astype(low)

            @pl.when(c == 0)
            def _():
                mine[y, :, cols] = got[:t]
                away[y, :, cols] = got[t:]

            @pl.when(c == 1)
            def _():
                mine[y, :, cols] = got[t:]
                away[y, :, cols] = got[:t]

            return 0

        lax.fori_loop(0, width // tile, one, 0)
        for q in range(cuts):
            to_side(y, q).start()

    def hop(s):
        y = chips - 1 + z - s
        w = s - (chips - 1) + z
        for q in range(cuts):
            @pl.when(y <= chips - 1)
            def _():
                now = total(y, q)

                @pl.when(has_down)
                def _():
                    to_up(y, q).wait_recv()
                    mine[y, rows(q)] = (now + line_buf[y, rows(q)].astype(f32)).astype(low)

                @pl.when(z == 0)
                def _():
                    mine[y, rows(q)] = now.astype(low)

                to_up(y, q).start()

            @pl.when(w >= 0)
            def _():
                now = total(w, q)

                @pl.when(has_up)
                def _():
                    from_up(w, q).wait_recv()
                    mine[w, rows(q)] = (now + line_buf[w, rows(q)].astype(f32)).astype(low)

                @pl.when(z == chips - 1)
                def _():
                    mine[w, rows(q)] = now.astype(low)

                to_down(w, q).start()

    def finish():
        for q in range(cuts):
            o_ref[rows(q)] = total(z, q)
        for q in range(cuts):
            @pl.when(has_down)
            def _():
                to_up(z, q).wait_recv()
                o_ref[rows(q)] += line_buf[z, rows(q)].astype(f32)

            @pl.when(has_up)
            def _():
                from_up(z, q).wait_recv()
                o_ref[rows(q)] += line_buf[chips, rows(q)].astype(f32)

        for y in range(chips):
            for q in range(cuts):
                to_side(y, q).wait_send()
                pl.when(y > z)(lambda: to_up(y, q).wait_send())
                pl.when(y < z)(lambda: to_down(y, q).wait_send())

    return put, hop, finish


def scatter_scratch(chips, cuts, t, width):
    return (
        [pltpu.VMEM((chips, t, width), jnp.bfloat16)] * 3
        + [pltpu.VMEM((chips + 1, t, width), jnp.bfloat16)]
        + [pltpu.SemaphoreType.DMA((chips, cuts))] * 6
    )


def scatter_kernel(chips, cuts, tile, n, *refs):
    a_ref, w_ref, srcs, o_ref = refs[0], refs[1], refs[2 : 2 + n], refs[2 + n]
    dsts, refs = refs[3 + n : 3 + 2 * n], refs[3 + 2 * n :]
    put, hop, finish = scatter_task(chips, cuts, tile, o_ref, refs[:4], refs[4:10])
    starts, waits = swap_list(srcs, dsts, refs[10:])
    greet(chips, n > 0)
    for s in range(chips):
        put(s, lambda rows: a_ref.at[rows], w_ref)
        if s < chips - 1:
            hop(s)
        if s == 0:
            for start in starts:
                start()
    finish()
    for wait in waits:
        wait()


def ff_back_kernel(chips, cuts, tile, *refs):
    sources, (o_ref, dw_out), held, refs = refs[:6], refs[6:8], refs[8:14], refs[14:]
    grad_ref, dw_ref, load_sem, save_sem = refs[:4]
    g_ref, one_ref, two_ref, red_ref, w_ref, h2_ref = held
    put, hop, finish = scatter_task(chips, cuts, tile, o_ref, refs[4:8], refs[8:14])
    load, loaded = mover(list(zip(sources, held)), load_sem)
    f32 = jnp.float32
    units = red_ref.shape[1]
    span = min(512, units)
    load(3, 0, 1, 2, 4, 5)
    greet(chips, False)
    loaded(0, 1, 2, 3)

    def rows_of(rows):
        def one(i, _):
            cols = pl.ds(pl.multiple_of(i * span, span), span)
            more = pl.ds(pl.multiple_of(units + i * span, span), span)
            grad = jnp.dot(g_ref[rows], red_ref[:, cols], preferred_element_type=f32)
            grad_ref[rows, cols] = (grad * one_ref[rows, cols].astype(f32)).astype(grad_ref.dtype)
            grad_ref[rows, more] = (grad * two_ref[rows, cols].astype(f32)).astype(grad_ref.dtype)
            return 0

        lax.fori_loop(0, units // span, one, 0)
        return grad_ref.at[rows]

    for s in range(chips):
        if s == 0:
            put(s, lambda rows: (rows_of(rows), loaded(4))[0], w_ref)
        else:
            put(s, rows_of, w_ref)
        if s < chips - 1:
            hop(s)
    loaded(5)
    deep = 256
    turns = dw_ref.shape[0] // deep

    def save(i):
        cols = pl.ds(pl.multiple_of(i * deep, deep), deep)
        return pltpu.make_async_copy(dw_ref.at[cols], dw_out.at[cols], save_sem.at[i])

    def one(i, _):
        cols = pl.ds(pl.multiple_of(i * deep, deep), deep)
        dw_ref[cols] = lax.dot_general(
            h2_ref[:, cols], grad_ref[...], (((0,), (0,)), ((), ())), preferred_element_type=f32
        ).astype(dw_ref.dtype)
        save(i).start()
        return 0

    lax.fori_loop(0, turns, one, 0)
    finish()
    for i in range(turns):
        save(i).wait()


def ff_back(cid, *operands, cuts=2, tile=1024):
    nb = lax.axis_size("blk")
    g_all, w_gu = operands[0], operands[4]
    seq, width = g_all.shape
    both = w_gu.shape[1]
    t = seq // nb
    dma = pltpu.SemaphoreType.DMA
    return pl.pallas_call(
        functools.partial(ff_back_kernel, nb // 2, cuts, tile),
        out_shape=[
            jax.ShapeDtypeStruct((t, width), jnp.float32),
            jax.ShapeDtypeStruct((width, both), jnp.bfloat16),
        ],
        in_specs=[ANY] * 6,
        out_specs=[VMEM, ANY],
        scratch_shapes=[pltpu.VMEM(value.shape, value.dtype) for value in operands]
        + [pltpu.VMEM((seq, both), jnp.bfloat16), pltpu.VMEM((width, both), jnp.bfloat16)]
        + [dma((6,)), dma((width // 256,))]
        + scatter_scratch(nb // 2, cuts, t, width),
        compiler_params=params(cid),
        cost_estimate=cost(5 * seq * width * both),
    )(*operands)


def dot_scatter(cid, a, w, swaps=(), cuts=2, tile=1024):
    nb = lax.axis_size("blk")
    t, width = a.shape[0] // nb, w.shape[0]
    n = len(swaps)
    return pl.pallas_call(
        functools.partial(scatter_kernel, nb // 2, cuts, tile, n),
        out_shape=[jax.ShapeDtypeStruct((t, width), jnp.float32)] + [like(s) for s in swaps],
        in_specs=[VMEM, VMEM] + [ANY] * n,
        out_specs=[VMEM] + [ANY] * n,
        scratch_shapes=scatter_scratch(nb // 2, cuts, t, width) + swap_sems(swaps),
        compiler_params=params(cid),
        cost_estimate=cost(2 * a.shape[0] * width * w.shape[1]),
    )(a, w, *swaps)


def pair_tables(positions):
    half = HEAD_DIM // 2
    frequency = jnp.exp(
        -jnp.arange(half, dtype=jnp.float32) * (2.0 / HEAD_DIM) * math.log(theta_base)
    )
    angles = positions.astype(jnp.float32)[:, None] * frequency[None, :]
    cosine, sine = jnp.cos(angles), jnp.sin(angles)
    return (
        jnp.concatenate([cosine] * 4, axis=1),
        jnp.concatenate([-sine, sine] * 2, axis=1),
    )


def norm_forward(values, gain_vector):
    inverse = lax.rsqrt(jnp.mean(values * values, axis=-1, keepdims=True) + norm_eps)
    unit_values = values * inverse
    return (unit_values, inverse, (unit_values * gain_vector).astype(jnp.bfloat16))


def norm_backward(grad_normed, unit_values, inverse, gain_vector):
    grad_unit = grad_normed * gain_vector
    grad_values = inverse * (
        grad_unit - unit_values * jnp.mean(grad_unit * unit_values, axis=-1, keepdims=True)
    )
    return (grad_values, jnp.sum(grad_normed * unit_values, axis=0))


def contract_last(left, right):
    return lax.dot_general(
        left, right, (((1,), (1,)), ((), ())), preferred_element_type=jnp.float32
    )


def adam_step(master, moment_one, moment_two, gradient):
    moment_one = beta_one * moment_one + (1.0 - beta_one) * gradient
    moment_two = beta_two * moment_two + (1.0 - beta_two) * gradient * gradient
    update = (
        moment_one
        / (1.0 - beta_one**step_count)
        / (jnp.sqrt(moment_two / (1.0 - beta_two**step_count)) + adam_eps)
    )
    return (master - learn_rate * (update + decay_rate * master), moment_one, moment_two)


def moment_step(moment_one, moment_two, gradient):
    moment_one = beta_one * moment_one + (1.0 - beta_one) * gradient
    moment_two = beta_two * moment_two + (1.0 - beta_two) * gradient * gradient
    return (moment_one, moment_two)


def once(*shape):
    return pl.BlockSpec(shape, lambda i: (0,) * len(shape), pipeline_mode=pl.Buffered(1))


def partner(values):
    width = values.shape[1]
    half = HEAD_DIM // 2
    feature = lax.broadcasted_iota(jnp.int32, values.shape, 1) % HEAD_DIM
    return jnp.where(
        feature < half, pltpu.roll(values, width - half, 1), pltpu.roll(values, half, 1)
    )


def spread_table(table, width):
    return jnp.concatenate([table] * (width // table.shape[1]), axis=1)


def head_lanes(shape):
    return lax.broadcasted_iota(jnp.int32, shape, 1) // HEAD_DIM


def attend_kernel(chips, cuts, n, h1_hbm, w_hbm, cos_ref, sin_ref, q_place, k_place, length_ref, g_ref, *refs):
    srcs, refs = refs[:n], refs[n:]
    o_ref, q_ref, k_ref, v_ref, p_ref, g_all = refs[:6]
    dsts, (h1_ref, w_ref, load_sem), sems = refs[6 : 6 + n], refs[6 + n : 9 + n], refs[9 + n :]
    load, loaded = mover([(w_hbm, w_ref), (h1_hbm, h1_ref)], load_sem)
    begin, hop, from_side, local, finish = gather_task(chips, cuts, g_ref, g_all, sems[:5])
    starts, waits = swap_list(srcs, dsts, sems[5:])
    step, steps = pl.program_id(0), pl.num_programs(0)
    tile, width = o_ref.shape
    f32, bf16 = jnp.float32, jnp.bfloat16

    @pl.when(step == 0)
    def _():
        load()
        greet(chips, True)
        begin()
        for start in starts:
            start()
        loaded()

        def one(i, _):
            rows = pl.ds(pl.multiple_of(i * tile, tile), tile)
            mixed = jnp.dot(h1_ref[rows], w_ref[...], preferred_element_type=f32)
            cosine, sine = spread_table(cos_ref[rows], width), spread_table(sin_ref[rows], width)
            for at, ref in enumerate((q_ref, k_ref)):
                got = mixed[:, at * width : (at + 1) * width]
                ref[rows] = (got * cosine + partner(got) * sine).astype(bf16)
            v_ref[rows] = mixed[:, 2 * width :].astype(bf16)
            return 0

        lax.fori_loop(0, steps, one, 0)

    @pl.when((step > 0) & (step < chips))
    def _():
        hop(step)

    rows = pl.ds(pl.multiple_of(step * tile, tile), tile)
    queries = q_ref[rows] * jnp.asarray(1.0 / math.sqrt(HEAD_DIM), bf16)
    lanes = head_lanes((tile, width))
    place = q_place[...]
    allowed = k_place[...] <= place
    out = jnp.zeros((tile, width), f32)
    for head in range(width // HEAD_DIM):
        here = lanes == head
        one_head = jnp.where(here, queries, jnp.zeros((), bf16))
        scores = lax.dot_general(
            one_head, k_ref[...], (((1,), (1,)), ((), ())), preferred_element_type=f32
        )
        scores = jnp.where(allowed, scores, neg_large)
        weights = jnp.exp(scores - jnp.max(scores, axis=-1, keepdims=True))
        weights = weights * (1.0 / jnp.sum(weights, axis=-1, keepdims=True))
        low = weights.astype(bf16)
        p_ref[head] = low
        out = jnp.where(here, jnp.dot(low, v_ref[...], preferred_element_type=f32), out)
    o_ref[...] = jnp.where(place < length_ref[0], out, 0.0).astype(bf16)

    @pl.when(step == steps - 1)
    def _():
        local().wait()
        for y in range(chips):
            from_side(y)
        finish()
        for wait in waits:
            wait()


def attend(cid, h1_all, w_in, cosine, sine, place, live_place, length, g, swaps=(), cuts=2):
    seq, wide = h1_all.shape
    width = w_in.shape[1] // 3
    heads = width // HEAD_DIM
    nb = lax.axis_size("blk")
    tile = seq // (nb // 2)
    n = len(swaps)
    part = pl.BlockSpec((tile, width), lambda i: (i, 0))

    full = jax.ShapeDtypeStruct((seq, width), jnp.bfloat16)
    return pl.pallas_call(
        functools.partial(attend_kernel, nb // 2, cuts, n),
        grid=(seq // tile,),
        in_specs=[
            ANY, ANY, once(seq, 2 * HEAD_DIM), once(seq, 2 * HEAD_DIM),
            pl.BlockSpec((tile, 1), lambda i: (i, 0)),
            once(1, seq),
            pl.BlockSpec(memory_space=pltpu.SMEM),
            ANY,
        ]
        + [ANY] * n,
        out_specs=[part] + [once(seq, width)] * 3
        + [pl.BlockSpec((heads, tile, seq), lambda i: (0, i, 0)), ANY] + [ANY] * n,
        out_shape=[full] * 4
        + [
            jax.ShapeDtypeStruct((heads, seq, seq), jnp.bfloat16),
            jax.ShapeDtypeStruct((seq, g.shape[1]), g.dtype),
        ]
        + [like(value) for value in swaps],
        scratch_shapes=[
            pltpu.VMEM(h1_all.shape, h1_all.dtype),
            pltpu.VMEM(w_in.shape, w_in.dtype),
            pltpu.SemaphoreType.DMA((2,)),
        ]
        + gather_sems(nb, cuts)
        + swap_sems(swaps),
        compiler_params=params(cid),
        cost_estimate=cost(4 * seq * seq * width + 6 * seq * wide * width),
    )(h1_all, w_in, cosine, sine, place[:, None], live_place[None, :], length.reshape(1), g, *swaps)


def attend_back_kernel(
    chips, cuts, tile_y, n, q_ref, k_ref, v_ref, o_all, g_ref, p_ref, cos_ref, sin_ref, q_place, length_ref,
    hidden_hbm, red_hbm, branch_hbm, h1_hbm, *refs
):
    srcs, (mixed_ref, y_ref, dw_out, dw_in), dsts = refs[:n], refs[n : n + 4], refs[n + 4 : 2 * n + 4]
    refs = refs[2 * n + 4 :]
    (ds_ref, qm_ref, gm_ref, dk_acc, dv_acc, hidden_ref, red_ref, branch_ref, h1_ref, load_sem), refs = (
        refs[:10], refs[10:],
    )
    put, hop, finish = scatter_task(chips, cuts, tile_y, y_ref, refs[:4], refs[4:10])
    starts, waits = swap_list(srcs, dsts, refs[10:])
    load, loaded = mover(
        [(red_hbm, red_ref), (hidden_hbm, hidden_ref), (branch_hbm, branch_ref), (h1_hbm, h1_ref)], load_sem
    )
    step, steps = pl.program_id(0), pl.num_programs(0)
    tile, width = g_ref.shape
    f32, bf16 = jnp.float32, jnp.bfloat16
    factor = 1.0 / math.sqrt(HEAD_DIM)

    @pl.when(step == 0)
    def _():
        load()
        greet(chips, n > 0)
        for start in starts:
            start()
        dk_acc[...] = jnp.zeros_like(dk_acc)
        dv_acc[...] = jnp.zeros_like(dv_acc)

        loaded(0, 1)

    put(step, lambda rows: hidden_ref.at[rows], red_ref)

    pl.when(step == 0)(lambda: hop(step))
    over_rows = (((0,), (0,)), ((), ()))
    rows = pl.ds(pl.multiple_of(step * tile, tile), tile)
    lanes = head_lanes((tile, width))
    nothing = jnp.zeros((), bf16)
    grad = jnp.where(q_place[...] < length_ref[0], g_ref[...], nothing)
    both = grad.astype(f32) * o_all[rows].astype(f32)
    queries = q_ref[rows]
    grad_q = jnp.zeros((tile, width), f32)
    for head in range(width // HEAD_DIM):
        here = lanes == head
        block = pl.ds(head * tile, tile)
        delta = jnp.sum(jnp.where(here, both, 0.0), axis=-1, keepdims=True)
        one_grad = jnp.where(here, grad, nothing)
        gm_ref[block] = one_grad
        qm_ref[block] = jnp.where(here, queries, nothing)
        grad_p = lax.dot_general(
            one_grad, v_ref[...], (((1,), (1,)), ((), ())), preferred_element_type=f32
        )
        grad_s = (p_ref[head].astype(f32) * (grad_p - delta)).astype(bf16)
        ds_ref[block] = grad_s
        grad_q = jnp.where(here, jnp.dot(grad_s, k_ref[...], preferred_element_type=f32), grad_q)
    heads = width // HEAD_DIM
    dv_acc[...] += lax.dot_general(
        p_ref[...].reshape(heads * tile, p_ref.shape[2]), gm_ref[...], over_rows,
        preferred_element_type=f32,
    )
    dk_acc[...] += lax.dot_general(ds_ref[...], qm_ref[...], over_rows, preferred_element_type=f32)

    def back(value, cosine, sine):
        value = (value * factor).astype(bf16).astype(f32)
        cosine, sine = spread_table(cosine, width), spread_table(sine, width)
        return (value * cosine - partner(value) * sine).astype(bf16)

    mixed_ref[rows, :width] = back(grad_q, cos_ref[rows], sin_ref[rows])
    pl.when(step == 0)(lambda: loaded(2))
    share = dw_out.shape[0] // chips
    cols = pl.ds(pl.multiple_of(step * share, share), share)
    dw_out[cols] = lax.dot_general(
        branch_ref[:, cols], o_all[...], over_rows, preferred_element_type=f32
    ).astype(bf16)
    pl.when((step > 0) & (step < steps - 1))(lambda: hop(step))

    @pl.when(step == steps - 1)
    def _():
        mixed_ref[:, width : 2 * width] = back(dk_acc[...], cos_ref[...], sin_ref[...])
        mixed_ref[:, 2 * width :] = dv_acc[...].astype(bf16)
        loaded(3)
        deep = 256

        def one(i, _):
            at = pl.ds(pl.multiple_of(i * deep, deep), deep)
            dw_in[at] = lax.dot_general(
                h1_ref[:, at], mixed_ref[...], over_rows, preferred_element_type=f32
            ).astype(bf16)
            return 0

        lax.fori_loop(0, dw_in.shape[0] // deep, one, 0)
        finish()
        for wait in waits:
            wait()


def attend_back(
    cid, q, k, v, o, g, p, cosine, sine, place, length, hidden, w_red, branch_all, h1_all, swaps, cuts=2
):
    seq, width = q.shape
    heads = width // HEAD_DIM
    nb = lax.axis_size("blk")
    tile = seq // (nb // 2)
    wide, units = w_red.shape
    n = len(swaps)
    full = once(seq, width)
    f32, bf16 = jnp.float32, jnp.bfloat16
    loads = (hidden, w_red, branch_all, h1_all)
    return pl.pallas_call(
        functools.partial(attend_back_kernel, nb // 2, cuts, 1024, n),
        grid=(seq // tile,),
        in_specs=[
            full, full, full, full,
            pl.BlockSpec((tile, width), lambda i: (i, 0)),
            pl.BlockSpec((heads, tile, seq), lambda i: (0, i, 0)),
            once(seq, 2 * HEAD_DIM), once(seq, 2 * HEAD_DIM),
            pl.BlockSpec((tile, 1), lambda i: (i, 0)),
            pl.BlockSpec(memory_space=pltpu.SMEM),
        ]
        + [ANY] * (4 + n),
        out_specs=[
            once(seq, 3 * width), once(seq // nb, wide), once(wide, width), once(wide, 3 * width)
        ]
        + [ANY] * n,
        out_shape=[
            jax.ShapeDtypeStruct((seq, 3 * width), bf16),
            jax.ShapeDtypeStruct((seq // nb, wide), f32),
            jax.ShapeDtypeStruct((wide, width), bf16),
            jax.ShapeDtypeStruct((wide, 3 * width), bf16),
        ]
        + [like(value) for value in swaps],
        scratch_shapes=[
            pltpu.VMEM((heads * tile, seq), bf16),
            pltpu.VMEM((heads * tile, width), bf16),
            pltpu.VMEM((heads * tile, width), bf16),
            pltpu.VMEM((seq, width), f32),
            pltpu.VMEM((seq, width), f32),
        ]
        + [pltpu.VMEM(value.shape, value.dtype) for value in loads]
        + [pltpu.SemaphoreType.DMA((4,))]
        + scatter_scratch(nb // 2, cuts, seq // nb, wide)
        + swap_sems(swaps),
        compiler_params=params(cid),
        cost_estimate=cost(10 * seq * seq * width),
    )(q, k, v, o, g, p, cosine, sine, place[:, None], length.reshape(1), *loads, *swaps)


def arrange(weight, out, parts):
    nb, _, wide = out.shape
    span = wide // parts
    for j in range(nb):
        for part in range(parts):
            at = (part * nb + j) * span
            out[j, :, part * span : (part + 1) * span] = weight[:, at : at + span].astype(out.dtype)


def first_swap_kernel(parts, *refs):
    n = len(parts)
    sources, dsts, later, refs = refs[:n], refs[n : n + 2], refs[n + 2 : 2 * n], refs[2 * n :]
    weights, held, load_sem, sems = refs[:n], refs[n : n + 2], refs[n + 2], refs[n + 3 :]
    starts, waits = swap_list(held, dsts, sems)
    load, loaded = mover(list(zip(sources, weights)), load_sem)
    load()
    greet(held[0].shape[0] // 2, True)
    for i in range(n):
        loaded(i)
        arrange(weights[i], held[i] if i < 2 else later[i - 2], parts[i])
        if i < 2:
            starts[i]()
    for wait in waits:
        wait()


def first_swap(cid, weights, parts):
    nb = lax.axis_size("blk")
    shapes = [(nb, value.shape[0], value.shape[1] // nb) for value in weights]
    n = len(weights)
    dma = pltpu.SemaphoreType.DMA
    return pl.pallas_call(
        functools.partial(first_swap_kernel, parts),
        out_shape=[jax.ShapeDtypeStruct(shape, jnp.bfloat16) for shape in shapes],
        in_specs=[ANY] * n,
        out_specs=[ANY] * 2 + [VMEM] * (n - 2),
        scratch_shapes=[pltpu.VMEM(value.shape, value.dtype) for value in weights]
        + [pltpu.VMEM(shape, jnp.bfloat16) for shape in shapes[:2]]
        + [dma((n,))] + [dma, dma((nb,)), dma((nb,))] * 2,
        compiler_params=params(cid),
        cost_estimate=cost(0),
    )(*weights)


def over_rows(pieces):
    nb, rows, wide = pieces.shape
    return lax.all_gather(pieces.reshape(nb * rows, wide), "rows", axis=0, tiled=True)


def sum_rows(gradient):
    nb = lax.axis_size("blk")
    mine = lax.psum_scatter(
        gradient.astype(jnp.bfloat16), "rows", scatter_dimension=0, tiled=True
    )
    return mine.reshape(nb, mine.shape[0] // nb, mine.shape[1])


def total_task(nr, nb, x_ref, o_ref, held, rows_held, send_one, recv_one, send_two, recv_two):
    r, b = lax.axis_index("rows"), lax.axis_index("blk")
    across = [lax.rem(b + k, nb) for k in range(1, nb)]
    along = [lax.rem(r + k, nr) for k in range(1, nr)]

    def first(other, slot):
        return pltpu.make_async_remote_copy(
            src_ref=rows_held.at[r], dst_ref=rows_held.at[slot], send_sem=send_two.at[other],
            recv_sem=recv_two.at[slot], device_id=(other, b), device_id_type=MESH,
        )

    def second(other, slot):
        return pltpu.make_async_remote_copy(
            src_ref=held.at[b], dst_ref=held.at[slot], send_sem=send_one.at[other],
            recv_sem=recv_one.at[slot], device_id=(r, other), device_id_type=MESH,
        )

    def greet_all():
        barrier = pltpu.get_barrier_semaphore()
        for other in across:
            pl.semaphore_signal(barrier, inc=1, device_id=(r, other), device_id_type=MESH)
        for other in along:
            pl.semaphore_signal(barrier, inc=1, device_id=(other, b), device_id_type=MESH)
        pl.semaphore_wait(barrier, nb + nr - 2)

    def start():
        rows_held[r] = x_ref[...]
        for other in along:
            first(other, r).start()

    def middle():
        for other in along:
            first(other, other).wait_recv()
        held[b] = jnp.sum(rows_held[...], axis=0)
        for other in across:
            second(other, b).start()

    def finish():
        for other in across:
            second(other, other).wait_recv()
        o_ref[...] = jnp.sum(held[...], axis=0)
        for other in along:
            first(other, r).wait_send()
        for other in across:
            second(other, b).wait_send()

    return greet_all, start, middle, finish


def last_scatter_kernel(
    chips, nr, cuts, tile, n, a_ref, w_ref, x_ref, inverse_ref, gain_ref, resid_ref, gain_two_ref, h1_hbm, *refs
):
    srcs, refs = refs[:n], refs[n:]
    o_ref, total_ref, dsts, refs = refs[0], refs[1], refs[2 : 2 + n], refs[2 + n :]
    sum_ref, part_ref, h1_ref, load_sem, refs = refs[0], refs[1], refs[2], refs[3], refs[4:]
    put, hop, finish = scatter_task(chips, cuts, tile, sum_ref, refs[:4], refs[4:10])
    greet_all, start_total, middle, finish_total = total_task(
        nr, 2 * chips, part_ref, total_ref, *refs[10:16]
    )
    starts, waits = swap_list(srcs, dsts, refs[16:])
    load, loaded = mover([(h1_hbm, h1_ref)], load_sem)
    load()
    greet_all()
    for start in starts:
        start()
    part_ref[0:1] = jnp.zeros_like(part_ref[0:1])
    part_ref[1:2] = gain_two_ref[...]
    loaded()

    def seen(rows, cols, got):
        part_ref[0:1, cols] += jnp.sum(got * h1_ref[rows, cols].astype(jnp.float32), axis=0)[None]

    for s in range(chips):
        put(s, lambda rows: a_ref.at[rows], w_ref, seen)
        if s < chips - 1:
            hop(s)
    part_ref[0:1] = part_ref[0:1] / gain_ref[...]
    start_total()
    middle()
    finish()
    inverse = inverse_ref[...]
    unit = x_ref[...].astype(jnp.float32) * inverse
    o_ref[...] = resid_ref[...] + norm_backward(sum_ref[...], unit, inverse, gain_ref[...])[0]
    finish_total()
    for wait in waits:
        wait()


def last_scatter(cid, a, w, x, inverse, gain, resid, gain_two, h1_all, swaps, cuts=2, tile=1024):
    nr, nb = lax.axis_size("rows"), lax.axis_size("blk")
    t, width = x.shape
    n = len(swaps)
    pair = (2, width)
    dma, f32 = pltpu.SemaphoreType.DMA, jnp.float32
    return pl.pallas_call(
        functools.partial(last_scatter_kernel, nb // 2, nr, cuts, tile, n),
        out_shape=[jax.ShapeDtypeStruct((t, width), f32), jax.ShapeDtypeStruct(pair, f32)]
        + [like(value) for value in swaps],
        in_specs=[VMEM] * 7 + [ANY] * (1 + n),
        out_specs=[VMEM] * 2 + [ANY] * n,
        scratch_shapes=[
            pltpu.VMEM((t, width), f32),
            pltpu.VMEM(pair, f32),
            pltpu.VMEM(h1_all.shape, h1_all.dtype),
            dma((1,)),
        ]
        + scatter_scratch(nb // 2, cuts, t, width)
        + [pltpu.VMEM((nb,) + pair, f32), pltpu.VMEM((nr,) + pair, f32)]
        + [dma((nb,))] * 2 + [dma((nr,))] * 2
        + swap_sems(swaps),
        compiler_params=params(cid),
        cost_estimate=cost(2 * a.shape[0] * width * w.shape[1]),
    )(a, w, x, inverse, gain[None], resid, gain_two[None], h1_all, *swaps)


def step_kernel(grad, *refs):
    outs = len(refs) // 2
    wide = grad.shape[2]
    for j in range(grad.shape[0]):
        cols = slice(j * wide, (j + 1) * wide)
        gradient = grad[j].astype(jnp.float32)
        rule = adam_step if outs == 3 else moment_step
        for ref, value in zip(refs[outs:], rule(*[ref[:, cols] for ref in refs[:outs]], gradient)):
            ref[:, cols] = value


def step(pieces, parts, states):
    nb = pieces.shape[0]
    rows, columns = states[0].shape
    tile = min(rows, 64 if parts > 1 else 32)
    span = columns // parts
    at = pl.BlockSpec((tile, span), lambda part, i: (i, part))
    outs = len(states)
    return pl.pallas_call(
        step_kernel,
        grid=(parts, rows // tile),
        in_specs=[pl.BlockSpec((nb, tile, span // nb), lambda part, i: (0, i, part))] + [at] * outs,
        out_specs=[at] * outs,
        out_shape=[jax.ShapeDtypeStruct((rows, columns), jnp.float32)] * outs,
        compiler_params=pltpu.CompilerParams(vmem_limit_bytes=60 * MIB),
        cost_estimate=pl.CostEstimate(
            flops=0, bytes_accessed=(8 * outs + 2) * rows * columns, transcendentals=0
        ),
    )(pieces, *states)


def after(value, *others):
    return lax.optimization_barrier((value,) + others)[0]


def over_tokens(left, right):
    return lax.dot_general(
        left, right, (((0,), (0,)), ((), ())), preferred_element_type=jnp.float32
    )


def shards(
    tokens, cotangent, lengths, block_map, gain_attend, gain_expand,
    attend_in, attend_out, expand_in, reduce_out,
    attend_in_first, attend_out_first, expand_in_first, reduce_out_first,
    attend_in_second, attend_out_second, expand_in_second, reduce_out_second,
):
    f32, bf16 = jnp.float32, jnp.bfloat16
    nb = lax.axis_size("blk")
    near = tokens.shape[1]
    seq = near * nb
    heads = HEADS // nb
    block_rows = near // 2
    length = lengths[0]
    offsets = jnp.arange(block_rows, dtype=jnp.int32)
    place = (block_map[0][:, None] * block_rows + offsets[None, :]).reshape(-1)
    live_place = jnp.where(place < length, place, jnp.int32(1 << 30))
    cosine, sine = pair_tables(place)

    x = tokens[0].astype(f32)
    unit_one, inverse_one, h1 = norm_forward(x, gain_attend)
    swap_in, swap_out, pieces_gu, pieces_red = first_swap(
        2, (attend_in, attend_out.T, expand_in, reduce_out.T), (3, 1, 2, 1)
    )
    w_in = over_rows(swap_in)
    w_out = over_rows(swap_out)
    h1_all, swap_gu = line_gather(3, after(h1, swap_in), swaps=[pieces_gu])
    w_gu = over_rows(swap_gu)

    attended, q, k, v, p, g_all, swap_red = attend(
        4, h1_all, w_in, cosine, sine, place, live_place, length, cotangent[0],
        swaps=[pieces_red],
    )
    w_red = over_rows(swap_red)
    x1 = x + dot_scatter(5, attended, w_out)[0]
    unit_two, inverse_two, h2 = norm_forward(x1, gain_expand)
    h2_all, hidden, slope_gate, slope_up, part_reduce = gather_dot(6, h2, w_gu, g_all)
    grad_h2, part_expand = ff_back(8, g_all, slope_gate, slope_up, w_red, w_gu, h2_all)
    rows_reduce = sum_rows(part_reduce)
    rows_expand = sum_rows(part_expand)
    middle, gain_two = norm_backward(grad_h2, unit_two, inverse_two, gain_expand)
    grad_x1 = cotangent[0].astype(f32) + middle
    branch_all, grad_o = gather_dot(9, grad_x1.astype(bf16), w_out)
    grad_mixed, y, part_out, part_in, own_reduce = attend_back(
        10, q, k, v, attended, grad_o, p, cosine, sine, place, length,
        hidden, w_red, branch_all, h1_all, [rows_reduce],
    )
    rows_out = sum_rows(part_out)
    y = x1 + y
    grad_input, gain_one_two, own_expand = last_scatter(
        11, grad_mixed, w_in, tokens[0], inverse_one, gain_attend, grad_x1, gain_two,
        h1_all, [rows_expand],
    )
    gains = gain_one_two
    rows_in = sum_rows(part_in)
    rows_in, rows_out = after((rows_in, rows_out), own_expand)
    both = lax.all_to_all(
        jnp.concatenate([rows_in, rows_out], axis=2), "blk", 0, 0, tiled=True
    )
    set_three = step(own_expand, 2, (expand_in, expand_in_first, expand_in_second))
    set_four = step(own_reduce, 1, (reduce_out.T, reduce_out_first.T, reduce_out_second.T))
    both = after(both, set_three[2], set_four[2])
    width_in = rows_in.shape[2]
    set_one = step(both[:, :, :width_in], 3, (attend_in, attend_in_first, attend_in_second))
    set_two = step(both[:, :, width_in:], 1, (attend_out_first.T, attend_out_second.T))
    return (
        y.astype(bf16).reshape(tokens.shape),
        grad_input.reshape(tokens.shape),
        gains[0],
        gains[1],
        *set_one,
        *[value.T for value in set_two],
        *set_three,
        *[value.T for value in set_four],
    )


def solution(mesh):
    placed = (
        P("rows", "blk", None),
        P("rows", "blk", None),
        P("rows"),
        P("rows", None),
        P(),
        P(),
        P(("rows", "blk"), None),
        P(None, ("rows", "blk")),
        P(("rows", "blk"), None),
        P(None, ("rows", "blk")),
        P(("rows", "blk"), None),
        P(None, ("rows", "blk")),
        P(("rows", "blk"), None),
        P(None, ("rows", "blk")),
        P(("rows", "blk"), None),
        P(None, ("rows", "blk")),
        P(("rows", "blk"), None),
        P(None, ("rows", "blk")),
    )
    return jax.shard_map(
        shards,
        mesh=mesh,
        in_specs=placed,
        out_specs=(
            P("rows", "blk", None),
            P("rows", "blk", None),
            P(),
            P(),
            P(("rows", "blk"), None),
            P(("rows", "blk"), None),
            P(("rows", "blk"), None),
            P(None, ("rows", "blk")),
            P(None, ("rows", "blk")),
            P(("rows", "blk"), None),
            P(("rows", "blk"), None),
            P(("rows", "blk"), None),
            P(None, ("rows", "blk")),
            P(None, ("rows", "blk")),
            P(None, ("rows", "blk")),
        ),
        check_vma=False,
    )
```

```python
import functools
import math

import jax
import jax.numpy as jnp
from jax import lax
from jax.experimental import pallas as pl
from jax.experimental.pallas import tpu as pltpu
from jax.sharding import PartitionSpec as P

HEADS = 32
HEAD_DIM = 64
MESH = pl.DeviceIdType.MESH
MIB = 1 << 20

theta_base = 130000.0
norm_eps = 1e-05
neg_large = -1e30
beta_one = 0.9
beta_two = 0.95
learn_rate = 0.01
decay_rate = 0.1
adam_eps = 1e-08
step_count = 10


def line_place():
    b = lax.axis_index("blk")
    return lax.axis_index("rows"), b // 2, b % 2


def greet(chips, swaps=False, rows=False):
    r, z, c = line_place()
    barrier = pltpu.get_barrier_semaphore()
    count = 0

    def signal(row, b):
        pl.semaphore_signal(barrier, inc=1, device_id=(row, b), device_id_type=MESH)

    b, nb, nr = 2 * z + c, 2 * chips, lax.axis_size("rows")
    if rows:
        for k in range(1, nr):
            signal(lax.rem(r + k, nr), b)
        count = nr - 1
    if swaps:
        for k in range(1, nb):
            signal(r, lax.rem(b + k, nb))
        count = count + nb - 1
    else:
        signal(r, b + 1 - 2 * c)
        pl.when(z < chips - 1)(lambda: signal(r, b + 2))
        pl.when(z > 0)(lambda: signal(r, b - 2))
        count = count + 1 + (z < chips - 1).astype(jnp.int32) + (z > 0).astype(jnp.int32)
    pl.semaphore_wait(barrier, count)


def swap_task(src, dst, local, send, recv):
    r, b = lax.axis_index("rows"), lax.axis_index("blk")
    nb = src.shape[0]
    others = [lax.rem(b + k, nb) for k in range(1, nb)]

    def remote(other, slot):
        return pltpu.make_async_remote_copy(
            src_ref=src.at[other], dst_ref=dst.at[slot], send_sem=send.at[other],
            recv_sem=recv.at[slot], device_id=(r, other), device_id_type=MESH,
        )

    def start():
        for other in others:
            remote(other, b).start()
        pltpu.make_async_copy(src.at[b], dst.at[b], local).start()

    def wait():
        for other in others:
            remote(other, other).wait_recv()
        for other in others:
            remote(other, b).wait_send()
        pltpu.make_async_copy(src.at[b], dst.at[b], local).wait()

    return start, wait


def rows_copy(src, dst, send, recv, device):
    return pltpu.make_async_remote_copy(
        src_ref=src, dst_ref=dst, send_sem=send, recv_sem=recv,
        device_id=(device, lax.axis_index("blk")), device_id_type=MESH,
    )


def through(src, stage, dst, local):
    first = pltpu.make_async_copy(src, stage, local)
    second = pltpu.make_async_copy(stage, dst, local)

    def store():
        first.wait()
        second.start()

    return first.start, store, second.wait


def direct_gather(src, dst, stage, local, send, recv):
    r, nr = lax.axis_index("rows"), dst.shape[0]
    others = [lax.rem(r + k, nr) for k in range(1, nr)]
    load, store, stored = through(src, stage, dst.at[r], local)

    def start():
        for other in others:
            rows_copy(src, dst.at[r], send.at[other], recv.at[r], other).start()
        load()

    def wait():
        for other in others:
            rows_copy(src, dst.at[other], send.at[other], recv.at[other], other).wait()
        stored()

    return start, store, wait


def square_gather(src, dst, stage, local, send, recv):
    r = lax.axis_index("rows")
    half = src.shape[0] // 2
    load, store, stored = through(src, stage, dst.at[r], local)

    def near(sem, origin, device):
        return rows_copy(src, dst.at[origin], send.at[sem], recv.at[sem], device)

    def onward(sem, origin, device):
        part = dst.at[origin, pl.ds((sem - 2) * half, half)]
        return rows_copy(part, part, send.at[sem], recv.at[sem], device)

    def start():
        near(0, r, r ^ 1).start()
        near(1, r, r ^ 2).start()
        load()

    def middle():
        store()
        near(0, r ^ 1, r ^ 1).wait_recv()
        onward(2, r ^ 1, r ^ 2).start()
        near(1, r ^ 2, r ^ 2).wait_recv()
        onward(3, r ^ 2, r ^ 1).start()

    def wait():
        onward(2, r ^ 3, r ^ 2).wait_recv()
        onward(3, r ^ 3, r ^ 1).wait_recv()
        near(0, r, r ^ 1).wait_send()
        near(1, r, r ^ 2).wait_send()
        onward(2, r ^ 1, r ^ 2).wait_send()
        onward(3, r ^ 2, r ^ 1).wait_send()
        stored()

    return start, middle, wait


def direct_sum(src, dst, held, local, send, recv):
    r, nr = lax.axis_index("rows"), src.shape[0]
    others = [lax.rem(r + k, nr) for k in range(1, nr)]

    def start():
        for other in others:
            rows_copy(src.at[other], held.at[r], send.at[other], recv.at[r], other).start()
        pltpu.make_async_copy(src.at[r], held.at[r], local).start()

    def wait():
        for other in others:
            rows_copy(src.at[other], held.at[other], send.at[other], recv.at[other], other).wait()
        pltpu.make_async_copy(src.at[r], held.at[r], local).wait()

        def one(j, _):
            total = held[0, j].astype(jnp.float32)
            for slot in range(1, nr):
                total = total + held[slot, j].astype(jnp.float32)
            held[0, j] = total.astype(held.dtype)
            return 0

        lax.fori_loop(0, held.shape[1], one, 0)
        done = pltpu.make_async_copy(held.at[0], dst, local)
        done.start()
        done.wait()

    return start, lambda: None, wait


def square_sum(src, dst, held, local, send, recv):
    r = lax.axis_index("rows")
    half = src.shape[1] // 2
    parts = [(pl.ds(0, half), r ^ 1, r ^ 2), (pl.ds(half, half), r ^ 2, r ^ 1)]

    def out(i, k):
        at, one, two = parts[i]
        return rows_copy(
            src.at[one if k == 0 else r ^ 3, at], held.at[k, at], send.at[2 * i + k],
            recv.at[2 * i + k], one,
        )

    def own(i, k):
        at, one, two = parts[i]
        return pltpu.make_async_copy(
            src.at[r if k == 0 else two, at], held.at[2 + k, at], local.at[2 * i + k]
        )

    def onward(i):
        at, one, two = parts[i]
        return rows_copy(held.at[3, at], held.at[4, at], send.at[4 + i], recv.at[4 + i], two)

    def add(i, into, *slots):
        def one(j, _):
            j = i * half + j
            total = held[into, j].astype(jnp.float32)
            for slot in slots:
                total = total + held[slot, j].astype(jnp.float32)
            held[into, j] = total.astype(held.dtype)
            return 0

        lax.fori_loop(0, half, one, 0)

    def start():
        for i in range(2):
            for k in (1, 0):
                out(i, k).start()
                own(i, k).start()

    def start_as(make):
        for i, k in ((0, 1), (1, 1), (0, 0), (1, 0)):
            make((parts[i][1] if k == 0 else r ^ 3), i)
            out(i, k).start()
        for i, k in ((0, 1), (1, 1), (0, 0), (1, 0)):
            make((r if k == 0 else parts[i][2]), i)
            own(i, k).start()

    start.as_made = start_as

    def middle():
        for i in range(2):
            out(i, 1).wait_recv()
            own(i, 1).wait()
            add(i, 3, 1)
            onward(i).start()

    def wait():
        for i in range(2):
            out(i, 0).wait_recv()
            own(i, 0).wait()
            onward(i).wait_recv()
            add(i, 2, 0, 4)
        done = pltpu.make_async_copy(held.at[2], dst, local.at[0])
        done.start()
        done.wait()
        for i in range(2):
            out(i, 0).wait_send()
            out(i, 1).wait_send()
            onward(i).wait_send()

    return start, middle, wait


class Extras:
    def __init__(self, swaps=(), gathers=(), scatters=()):
        nr, nb = lax.axis_size("rows"), lax.axis_size("blk")
        dma = pltpu.SemaphoreType.DMA
        self.swaps, self.gathers, self.scatters = len(swaps), [g[1:] for g in gathers], len(scatters)
        self.operands = [*swaps, *[g[0] for g in gathers], *scatters]
        self.n = len(self.operands)
        self.rows = bool(gathers) or bool(scatters)
        self.specs = [ANY] * self.n
        self.shapes = [like(value) for value in swaps]
        self.scratch = [dma, dma((nb,)), dma((nb,))] * len(swaps)
        self.square = nr == 4
        sems = 6 if self.square else nr
        for value, _, count in gathers:
            self.shapes.append(jax.ShapeDtypeStruct((nr, count, value.shape[1]), value.dtype))
            self.scratch += [pltpu.VMEM((count, value.shape[1]), value.dtype)]
            self.scratch += [dma, dma((sems,)), dma((sems,))]
        for value in scatters:
            self.shapes.append(jax.ShapeDtypeStruct(value.shape[1:], value.dtype))
            slots = 5 if self.square else nr
            local = dma((4,)) if self.square else dma
            self.scratch += [pltpu.VMEM((slots,) + value.shape[1:], value.dtype)]
            self.scratch += [local, dma((sems,)), dma((sems,))]

    def tasks(self, srcs, dsts, scratch):
        scratch = list(scratch)
        swaps, rows = [], []
        for i, (src, dst) in enumerate(zip(srcs, dsts)):
            if i < self.swaps:
                swaps.append(swap_task(src, dst, *scratch[:3]))
                scratch = scratch[3:]
            elif i < self.swaps + len(self.gathers):
                first, count = self.gathers[i - self.swaps]
                task = square_gather if self.square else direct_gather
                rows.append(task(src.at[pl.ds(first, count)], dst, *scratch[:4]))
                scratch = scratch[4:]
            else:
                task = square_sum if self.square else direct_sum
                rows.append(task(src, dst, *scratch[:4]))
                scratch = scratch[4:]

        def start_swaps():
            for start, _ in swaps:
                start()

        def start_rows():
            for start, _, _ in rows:
                start()

        def middle():
            for _, one, _ in rows:
                one()

        def wait_rows():
            for _, _, one in rows:
                one()

        def wait_swaps():
            for _, one in swaps:
                one()

        return start_swaps, start_rows, middle, wait_rows, wait_swaps


def like(value):
    return jax.ShapeDtypeStruct(value.shape, value.dtype)


ANY = pl.BlockSpec(memory_space=pl.ANY)
VMEM = pl.BlockSpec(memory_space=pltpu.VMEM)


def params(cid):
    return pltpu.CompilerParams(
        collective_id=cid, has_side_effects=True, vmem_limit_bytes=60 * MIB
    )


def cost(flops):
    return pl.CostEstimate(flops=flops, bytes_accessed=150_000_000, transcendentals=0)


def mover(pairs, sem):
    copies = [pltpu.make_async_copy(a, b, sem.at[i]) for i, (a, b) in enumerate(pairs)]

    def start(*which):
        for i in which or range(len(copies)):
            copies[i].start()

    def wait(*which):
        for i in which or range(len(copies)):
            copies[i].wait()

    return start, wait


def gather_task(chips, cuts, x_ref, o_ref, sems):
    copy_sem, send_up, send_down, send_side, recv = sems
    r, z, c = line_place()
    t = x_ref.shape[0]
    h = t // cuts
    up, down, side = (r, 2 * (z + 1) + c), (r, 2 * (z - 1) + c), (r, 2 * z + 1 - c)
    has_up, has_down = z < chips - 1, z > 0
    mine = 2 * z + c

    def piece(j, q):
        return o_ref.at[pl.ds(pl.multiple_of(j * t + q * h, h), h)]

    def remote(src, j, q, sem, dev):
        return pltpu.make_async_remote_copy(
            src_ref=src, dst_ref=piece(j, q), send_sem=sem.at[j, q], recv_sem=recv.at[j, q],
            device_id=dev, device_id_type=MESH,
        )

    def local():
        whole = o_ref.at[pl.ds(pl.multiple_of(mine * t, t), t)]
        return pltpu.make_async_copy(x_ref, whole, copy_sem)

    def start():
        for q in range(cuts):
            from_here = x_ref.at[pl.ds(q * h, h)]
            pl.when(has_up)(lambda: remote(from_here, mine, q, send_up, up).start())
            pl.when(has_down)(lambda: remote(from_here, mine, q, send_down, down).start())
            remote(from_here, mine, q, send_side, side).start()
        local().start()

    def hop(k):
        for q in range(cuts):
            @pl.when(z - k >= 0)
            def _():
                j = 2 * (z - k) + c
                remote(piece(j, q), j, q, send_up, up).wait_recv()
                pl.when(has_up)(lambda: remote(piece(j, q), j, q, send_up, up).start())
                remote(piece(j, q), j, q, send_side, side).start()

            @pl.when(z + k < chips)
            def _():
                j = 2 * (z + k) + c
                remote(piece(j, q), j, q, send_down, down).wait_recv()
                pl.when(has_down)(lambda: remote(piece(j, q), j, q, send_down, down).start())
                remote(piece(j, q), j, q, send_side, side).start()

    def from_side(y):
        for q in range(cuts):
            j = 2 * y + 1 - c
            remote(piece(j, q), j, q, send_side, side).wait_recv()

    def finish():
        for y in range(chips):
            j = 2 * y + c
            for q in range(cuts):
                pl.when(has_up & (z >= y))(
                    lambda: remote(piece(j, q), j, q, send_up, up).wait_send()
                )
                pl.when(has_down & (z <= y))(
                    lambda: remote(piece(j, q), j, q, send_down, down).wait_send()
                )
                remote(piece(j, q), j, q, send_side, side).wait_send()

    return start, hop, from_side, local, finish


def gather_sems(nb, cuts):
    return [pltpu.SemaphoreType.DMA] + [pltpu.SemaphoreType.DMA((nb, cuts))] * 4


def gather_kernel(chips, cuts, extras, x_ref, *refs):
    n = extras.n
    srcs, o_ref, dsts, refs = refs[:n], refs[n], refs[n + 1 : 2 * n + 1], refs[2 * n + 1 :]
    begin, hop, from_side, local, finish = gather_task(chips, cuts, x_ref, o_ref, refs[:5])
    start_swaps, start_rows, middle, wait_rows, wait_swaps = extras.tasks(srcs, dsts, refs[5:])
    greet(chips, True, extras.rows)
    begin()
    start_rows()
    for k in range(1, chips):
        if k == min(3, chips - 1):
            start_swaps()
        hop(k)
    middle()
    local().wait()
    for y in range(chips):
        from_side(y)
    finish()
    wait_rows()
    wait_swaps()


def line_gather(cid, x, extras, cuts=4):
    nb = lax.axis_size("blk")
    return pl.pallas_call(
        functools.partial(gather_kernel, nb // 2, cuts, extras),
        out_shape=[jax.ShapeDtypeStruct((nb * x.shape[0], x.shape[1]), x.dtype)] + extras.shapes,
        in_specs=[VMEM] + extras.specs,
        out_specs=[ANY] + extras.specs,
        scratch_shapes=gather_sems(nb, cuts) + extras.scratch,
        compiler_params=params(cid),
        cost_estimate=cost(0),
    )(x, *extras.operands)


def gather_dot_kernel(chips, cuts, extras, x_ref, w_ref, *refs):
    n = extras.n
    srcs, outs, dsts, refs = refs[:n], refs[n : n + 2], refs[n + 2 : 2 * n + 2], refs[2 * n + 2 :]
    held, save_sem, refs = refs[:2], refs[2], refs[3:]
    o_ref, prod_ref = held
    begin, hop, from_side, local, finish = gather_task(chips, cuts, x_ref, o_ref, refs[:5])
    start_swaps, start_rows, middle, wait_rows, wait_swaps = extras.tasks(srcs, dsts, refs[5:])
    r, z, c = line_place()
    t = x_ref.shape[0]
    greet(chips, False, extras.rows)
    begin()
    start_rows()

    def rows_of(y):
        return pl.ds(pl.multiple_of(y * 2 * t, 2 * t), 2 * t)

    def saves(y):
        return mover([(a.at[rows_of(y)], b.at[rows_of(y)]) for a, b in zip(held, outs)], save_sem.at[y])

    def dot(y):
        rows = rows_of(y)
        prod_ref[rows] = jnp.dot(
            o_ref[rows], w_ref[...], preferred_element_type=jnp.float32
        ).astype(prod_ref.dtype)
        saves(y)[0]()

    from_side(z)
    local().wait()
    dot(z)
    for k in range(1, chips):
        hop(k)

        @pl.when(z - k >= 0)
        def _():
            from_side(z - k)
            dot(z - k)

        @pl.when(z + k < chips)
        def _():
            from_side(z + k)
            dot(z + k)

        if k == max(1, chips - 2):
            middle()
    finish()
    for y in range(chips):
        saves(y)[1]()
    wait_rows()


def gather_dot(cid, x, w, extras, cuts=2):
    nb = lax.axis_size("blk")
    all_rows = nb * x.shape[0]
    dma, bf16 = pltpu.SemaphoreType.DMA, jnp.bfloat16
    shapes = [(all_rows, x.shape[1]), (all_rows, w.shape[1])]
    return pl.pallas_call(
        functools.partial(gather_dot_kernel, nb // 2, cuts, extras),
        out_shape=[jax.ShapeDtypeStruct(shape, bf16) for shape in shapes] + extras.shapes,
        in_specs=[VMEM, VMEM] + extras.specs,
        out_specs=[ANY] * 2 + extras.specs,
        scratch_shapes=[pltpu.VMEM(shape, bf16) for shape in shapes]
        + [dma((nb // 2, 2))]
        + gather_sems(nb, cuts)
        + extras.scratch,
        compiler_params=params(cid),
        cost_estimate=cost(2 * all_rows * w.shape[0] * w.shape[1]),
    )(x, w, *extras.operands)


def need_order(chips):
    table = []
    for z in range(chips):
        need = {
            y: (chips - 1 + z - y) if y > z else (chips - 1 - z + y)
            for y in range(chips) if y != z
        }
        table.append(sorted(need, key=lambda y: need[y]) + [z])
    return table


def pick(table, z, k):
    out = 0
    for at, row in enumerate(table):
        for step, block in enumerate(row):
            out = out + jnp.where((z == at) & (k == step), block, 0)
    return out


def scatter_task(chips, cuts, tile, o_ref, bufs, sems):
    mine, away, side_buf, line_buf = bufs
    send_side, recv_side, send_up, recv_up, send_down, recv_down = sems
    r, z, c = line_place()
    t, width = o_ref.shape
    low, f32 = away.dtype, jnp.float32
    up, down, side = (r, 2 * (z + 1) + c), (r, 2 * (z - 1) + c), (r, 2 * z + 1 - c)
    has_up, has_down = z < chips - 1, z > 0
    h = t // cuts
    table = need_order(chips)

    def remote(src, dst, y, q, send, recv, dev):
        return pltpu.make_async_remote_copy(
            src_ref=src.at[y, pl.ds(q * h, h)], dst_ref=dst.at[y, pl.ds(q * h, h)],
            send_sem=send.at[y, q], recv_sem=recv.at[y, q], device_id=dev, device_id_type=MESH,
        )

    def to_side(y, q):
        return remote(away, side_buf, y, q, send_side, recv_side, side)

    def along(y, slot, q, send, recv, dev):
        return pltpu.make_async_remote_copy(
            src_ref=mine.at[y, pl.ds(q * h, h)], dst_ref=line_buf.at[slot, pl.ds(q * h, h)],
            send_sem=send.at[y, q], recv_sem=recv.at[y, q], device_id=dev, device_id_type=MESH,
        )

    def to_up(y, q):
        return along(y, y, q, send_up, recv_up, up)

    def to_down(y, q):
        return along(y, jnp.where(y == z - 1, chips, y), q, send_down, recv_down, down)

    def from_up(y, q):
        return along(y, jnp.where(y == z, chips, y), q, send_down, recv_down, down)

    def rows(q):
        return pl.ds(q * h, h)

    def total(y, q):
        to_side(y, q).wait_recv()
        return mine[y, rows(q)].astype(f32) + side_buf[y, rows(q)].astype(f32)

    def put(s, rows_of, w_ref, seen=None):
        put_at(pick(table, z, s), rows_of, w_ref, seen)

    def put_at(y, rows_of, w_ref, seen=None):
        block = pl.ds(pl.multiple_of(2 * y * t, 2 * t), 2 * t)
        a = rows_of(block)

        def one(i, _):
            cols = pl.ds(pl.multiple_of(i * tile, tile), tile)
            got = lax.dot_general(
                a[...], w_ref[cols], (((1,), (1,)), ((), ())), preferred_element_type=f32
            )
            if seen is not None:
                seen(block, cols, got)
            got = got.astype(low)

            @pl.when(c == 0)
            def _():
                mine[y, :, cols] = got[:t]
                away[y, :, cols] = got[t:]

            @pl.when(c == 1)
            def _():
                mine[y, :, cols] = got[t:]
                away[y, :, cols] = got[:t]

            return 0

        lax.fori_loop(0, width // tile, one, 0)
        for q in range(cuts):
            to_side(y, q).start()

    def hop(s):
        hop_up(chips - 1 + z - s)
        hop_down(s - (chips - 1) + z)

    def hop_up(y):
        for q in range(cuts):
            @pl.when((y > z) & (y <= chips - 1))
            def _():
                now = total(y, q)

                @pl.when(has_down)
                def _():
                    to_up(y, q).wait_recv()
                    mine[y, rows(q)] = (now + line_buf[y, rows(q)].astype(f32)).astype(low)

                @pl.when(z == 0)
                def _():
                    mine[y, rows(q)] = now.astype(low)

                to_up(y, q).start()

    def hop_down(w):
        for q in range(cuts):
            @pl.when((w >= 0) & (w < z))
            def _():
                now = total(w, q)

                @pl.when(has_up)
                def _():
                    from_up(w, q).wait_recv()
                    mine[w, rows(q)] = (now + line_buf[w, rows(q)].astype(f32)).astype(low)

                @pl.when(z == chips - 1)
                def _():
                    mine[w, rows(q)] = now.astype(low)

                to_down(w, q).start()

    def finish():
        for q in range(cuts):
            o_ref[rows(q)] = total(z, q)
        for q in range(cuts):
            @pl.when(has_down)
            def _():
                to_up(z, q).wait_recv()
                o_ref[rows(q)] += line_buf[z, rows(q)].astype(f32)

            @pl.when(has_up)
            def _():
                from_up(z, q).wait_recv()
                o_ref[rows(q)] += line_buf[chips, rows(q)].astype(f32)

        for y in range(chips):
            for q in range(cuts):
                to_side(y, q).wait_send()
                pl.when(y > z)(lambda: to_up(y, q).wait_send())
                pl.when(y < z)(lambda: to_down(y, q).wait_send())

    return put, (put_at, hop_up, hop_down), hop, finish


def scatter_scratch(chips, cuts, t, width):
    return (
        [pltpu.VMEM((chips, t, width), jnp.bfloat16)] * 3
        + [pltpu.VMEM((chips + 1, t, width), jnp.bfloat16)]
        + [pltpu.SemaphoreType.DMA((chips, cuts))] * 6
    )


def attend_out_kernel(chips, cuts, tile, extras, a_ref, w_ref, x_ref, gain_ref, *refs):
    n = extras.n
    srcs, (x1_ref, inverse_ref, h2_ref), dsts, refs = (
        refs[:n], refs[n : n + 3], refs[3 + n : 3 + 2 * n], refs[3 + 2 * n :],
    )
    put, _, hop, finish = scatter_task(chips, cuts, tile, x1_ref, refs[:4], refs[4:10])
    start_swaps, start_rows, middle, wait_rows, wait_swaps = extras.tasks(srcs, dsts, refs[10:])
    greet(chips, False, extras.rows)
    start_rows()
    for s in range(chips):
        put(s, lambda rows: a_ref.at[rows], w_ref)
        if s < chips - 1:
            hop(s)
    middle()
    finish()
    x1 = x_ref[...].astype(jnp.float32) + x1_ref[...]
    x1_ref[...] = x1
    _, inverse_ref[...], h2_ref[...] = norm_forward(x1, gain_ref[...])
    wait_rows()


def feed_forward_kernel(
    chips, cuts, tile, h2_here, x1_ref, inverse_ref, gain_ref, cotangent_ref, early_hbm, late_hbm, red_hbm, g_hbm,
    grad_out, low_out, gain_out, hidden_out, gate_out, up_out, reduce_out,
    h2_ref, hidden_ref, grad_ref, w_ref, red_ref, g_ref, dw_red, dw_ref, red_held,
    load_sem, save_sem, dw_sem, red_local, red_send, red_recv, *refs
):
    begin, pass_on, from_side, local, sent = gather_task(chips, cuts, h2_here, h2_ref, refs[:5])
    _, (put_at, hop_up, hop_down), _, finish = scatter_task(chips, cuts, tile, grad_out, refs[5:9], refs[9:])
    task = square_sum if dw_red.shape[0] == 4 else direct_sum
    start_red, middle_red, wait_red = task(
        dw_red, reduce_out, red_held, red_local, red_send, red_recv
    )
    nr, early, late = early_hbm.shape[0], early_hbm.shape[1], late_hbm.shape[1]
    pairs = [(g_hbm, g_ref), (red_hbm, red_ref)]
    for q in range(nr):
        first = q * (early + late)
        pairs += [
            (early_hbm.at[q], w_ref.at[pl.ds(first, early)]),
            (late_hbm.at[q], w_ref.at[pl.ds(first + early, late)]),
        ]
    load, loaded = mover(pairs, load_sem)
    w_loads = range(2, len(pairs))
    r, z, c = line_place()
    t, width = h2_here.shape
    units = hidden_ref.shape[1]
    span = min(512, units)
    f32, low = jnp.float32, jnp.bfloat16
    over_rows = (((0,), (0,)), ((), ()))
    load(*w_loads, 0, 1)
    greet(chips, False, True)
    begin()

    def rows_of(y):
        return pl.ds(pl.multiple_of(y * 2 * t, 2 * t), 2 * t)

    def save(y):
        return pltpu.make_async_copy(
            hidden_ref.at[rows_of(y)], hidden_out.at[rows_of(y)], save_sem.at[y]
        )

    def columns(i):
        at, more = i * span, units + i * span
        return pl.ds(pl.multiple_of(at, span), span), pl.ds(pl.multiple_of(more, span), span)

    def forward(y):
        rows = rows_of(y)

        def one(i, _):
            cols, more = columns(i)
            gate = jnp.dot(h2_ref[rows], w_ref[:, cols], preferred_element_type=f32)
            up = jnp.dot(h2_ref[rows], w_ref[:, more], preferred_element_type=f32)
            sigmoid = jax.nn.sigmoid(gate)
            silu = gate * sigmoid
            hidden_ref[rows, cols] = (silu * up).astype(low)
            grad_ref[rows, cols] = (up * (sigmoid * (1.0 + gate * (1.0 - sigmoid)))).astype(low)
            grad_ref[rows, more] = silu.astype(low)
            return 0

        lax.fori_loop(0, units // span, one, 0)
        save(y).start()

    def backward(rows):
        def one(i, _):
            cols, more = columns(i)
            grad = jnp.dot(g_ref[rows], red_ref[:, cols], preferred_element_type=f32)
            grad_ref[rows, cols] = (grad * grad_ref[rows, cols].astype(f32)).astype(low)
            grad_ref[rows, more] = (grad * grad_ref[rows, more].astype(f32)).astype(low)
            return 0

        lax.fori_loop(0, units // span, one, 0)
        return grad_ref.at[rows]

    from_side(z)
    local().wait()
    loaded(*w_loads)
    forward(z)
    loaded(0, 1)
    put_at(z, backward, w_ref)
    deep = 256
    turns = width // deep
    piece = dw_red.shape[2]
    run = dw_red.shape[1] * piece

    def reduce_grad(i, _):
        at = pl.ds(pl.multiple_of(i * deep, deep), deep)
        got = lax.dot_general(g_ref[:, at], hidden_ref[...], over_rows, preferred_element_type=f32)
        first = i * deep
        dw_red[first // run, pl.ds(lax.rem(first, run) // piece, deep // piece)] = (
            got.astype(low).reshape(deep // piece, piece, units)
        )
        return 0

    def make_reduce_grad():
        if dw_red.shape[0] == 4:
            tiles = turns // 8

            def make(slot, half):
                first = (slot * 2 + half) * tiles
                lax.fori_loop(first, first + tiles, reduce_grad, 0)

            start_red.as_made(make)
        else:
            lax.fori_loop(0, turns, reduce_grad, 0)
            start_red()

    def save_dw(i, half):
        at = pl.ds(pl.multiple_of(i * deep, deep), deep)
        return pltpu.make_async_copy(
            dw_ref.at[lax.rem(i, 2), half], (gate_out, up_out)[half].at[at], dw_sem.at[lax.rem(i, 2), half]
        )

    def expand_grad(i, _):
        at = pl.ds(pl.multiple_of(i * deep, deep), deep)
        for half in range(2):
            pl.when(i >= 2)(lambda: save_dw(i - 2, half).wait())
            dw_ref[lax.rem(i, 2), half] = lax.dot_general(
                h2_ref[:, at], grad_ref[:, half * units : (half + 1) * units], over_rows,
                preferred_element_type=f32,
            ).astype(low)
            save_dw(i, half).start()
        return 0

    last = 2 * chips - 3
    done = 0
    for turn in range(1, last + 1):
        if turn < chips:
            pass_on(turn)

            @pl.when(z - turn >= 0)
            def _():
                from_side(z - turn)
                forward(z - turn)
                put_at(z - turn, backward, w_ref)

            @pl.when(z + turn < chips)
            def _():
                from_side(z + turn)
                forward(z + turn)
                put_at(z + turn, backward, w_ref)

        hop_up(turn - z)
        hop_down(2 * (chips - 1) - z - turn)
        if turn == chips - 1:
            make_reduce_grad()
        elif turn >= chips:
            until = turns * (turn - chips + 1) // (last - chips + 1)
            lax.fori_loop(done, until, expand_grad, 0)
            done = until
    middle_red()
    finish()
    inverse = inverse_ref[...]
    middle_grad, gain = norm_backward(grad_out[...], x1_ref[...] * inverse, inverse, gain_ref[...])
    grad_x1 = cotangent_ref[...].astype(f32) + middle_grad
    grad_out[...] = grad_x1
    low_out[...] = grad_x1.astype(low)
    gain_out[...] = gain[None]
    wait_red()
    sent()
    for y in range(chips):
        save(y).wait()
    for i in range(max(0, turns - 2), turns):
        for half in range(2):
            save_dw(i, half).wait()


def feed_forward(
    cid, h2, x1, inverse, gain, cotangent, gu_early, gu_late, w_red, g_all, cuts=2, tile=1024
):
    nr, nb = lax.axis_size("rows"), lax.axis_size("blk")
    seq, width = g_all.shape
    both = gu_early.shape[2]
    units = both // 2
    t = seq // nb
    piece = width // (nr * nb)
    dma, f32, bf16 = pltpu.SemaphoreType.DMA, jnp.float32, jnp.bfloat16
    half = jax.ShapeDtypeStruct((width, units), bf16)
    slots, sems = (5, 6) if nr == 4 else (nr, nr)
    return pl.pallas_call(
        functools.partial(feed_forward_kernel, nb // 2, cuts, tile),
        out_shape=[
            jax.ShapeDtypeStruct((t, width), f32),
            jax.ShapeDtypeStruct((t, width), bf16),
            jax.ShapeDtypeStruct((1, width), f32),
            jax.ShapeDtypeStruct((seq, units), bf16),
            half,
            half,
            jax.ShapeDtypeStruct((nb, piece, units), bf16),
        ],
        in_specs=[VMEM] * 5 + [ANY] * 4,
        out_specs=[VMEM] * 3 + [ANY] * 4,
        scratch_shapes=[
            pltpu.VMEM((seq, width), bf16),
            pltpu.VMEM((seq, units), bf16),
            pltpu.VMEM((seq, both), bf16),
            pltpu.VMEM((width, both), bf16),
            pltpu.VMEM((width, units), bf16),
            pltpu.VMEM((seq, width), bf16),
            pltpu.VMEM((nr, nb, piece, units), bf16),
            pltpu.VMEM((2, 2, 256, units), bf16),
            pltpu.VMEM((slots, nb, piece, units), bf16),
            dma((2 + 2 * nr,)),
            dma((nb // 2,)),
            dma((2, 2)),
            dma((4,)) if nr == 4 else dma,
            dma((sems,)),
            dma((sems,)),
        ]
        + gather_sems(nb, cuts)
        + scatter_scratch(nb // 2, cuts, t, width),
        compiler_params=params(cid),
        cost_estimate=cost(9 * seq * width * both),
    )(h2, x1, inverse, gain[None], cotangent, gu_early, gu_late, w_red, g_all)


def attend_out_kernel(chips, cuts, tile, extras, a_ref, w_ref, x_ref, gain_ref, *refs):
    n = extras.n
    srcs, (x1_ref, inverse_ref, h2_ref), dsts, refs = (
        refs[:n], refs[n : n + 3], refs[3 + n : 3 + 2 * n], refs[3 + 2 * n :],
    )
    put, _, hop, finish = scatter_task(chips, cuts, tile, x1_ref, refs[:4], refs[4:10])
    start_swaps, start_rows, middle, wait_rows, wait_swaps = extras.tasks(srcs, dsts, refs[10:])
    greet(chips, False, extras.rows)
    start_rows()
    for s in range(chips):
        put(s, lambda rows: a_ref.at[rows], w_ref)
        if s < chips - 1:
            hop(s)
    middle()
    finish()
    x1 = x_ref[...].astype(jnp.float32) + x1_ref[...]
    x1_ref[...] = x1
    _, inverse_ref[...], h2_ref[...] = norm_forward(x1, gain_ref[...])
    wait_rows()


def attend_out_sum(cid, a, w, x, gain, extras, cuts=2, tile=1024):
    nb = lax.axis_size("blk")
    t, width = x.shape
    f32 = jnp.float32
    return pl.pallas_call(
        functools.partial(attend_out_kernel, nb // 2, cuts, tile, extras),
        out_shape=[
            jax.ShapeDtypeStruct((t, width), f32),
            jax.ShapeDtypeStruct((t, 1), f32),
            jax.ShapeDtypeStruct((t, width), jnp.bfloat16),
        ]
        + extras.shapes,
        in_specs=[VMEM] * 4 + extras.specs,
        out_specs=[VMEM] * 3 + extras.specs,
        scratch_shapes=scatter_scratch(nb // 2, cuts, t, width) + extras.scratch,
        compiler_params=params(cid),
        cost_estimate=cost(2 * a.shape[0] * width * w.shape[1]),
    )(a, w, x, gain[None], *extras.operands)


def norm_forward(values, gain_vector):
    inverse = lax.rsqrt(jnp.mean(values * values, axis=-1, keepdims=True) + norm_eps)
    unit_values = values * inverse
    return (unit_values, inverse, (unit_values * gain_vector).astype(jnp.bfloat16))


def norm_backward(grad_normed, unit_values, inverse, gain_vector):
    grad_unit = grad_normed * gain_vector
    grad_values = inverse * (
        grad_unit - unit_values * jnp.mean(grad_unit * unit_values, axis=-1, keepdims=True)
    )
    return (grad_values, jnp.sum(grad_normed * unit_values, axis=0))


def contract_last(left, right):
    return lax.dot_general(
        left, right, (((1,), (1,)), ((), ())), preferred_element_type=jnp.float32
    )


def adam_step(master, moment_one, moment_two, gradient):
    moment_one = beta_one * moment_one + (1.0 - beta_one) * gradient
    moment_two = beta_two * moment_two + (1.0 - beta_two) * gradient * gradient
    update = (
        moment_one
        / (1.0 - beta_one**step_count)
        / (jnp.sqrt(moment_two / (1.0 - beta_two**step_count)) + adam_eps)
    )
    return (master - learn_rate * (update + decay_rate * master), moment_one, moment_two)


def moment_step(moment_one, moment_two, gradient):
    moment_one = beta_one * moment_one + (1.0 - beta_one) * gradient
    moment_two = beta_two * moment_two + (1.0 - beta_two) * gradient * gradient
    return (moment_one, moment_two)


def once(*shape):
    return pl.BlockSpec(shape, lambda i: (0,) * len(shape), pipeline_mode=pl.Buffered(1))


def partner(values):
    width = values.shape[1]
    half = HEAD_DIM // 2
    feature = lax.broadcasted_iota(jnp.int32, values.shape, 1) % HEAD_DIM
    return jnp.where(
        feature < half, pltpu.roll(values, width - half, 1), pltpu.roll(values, half, 1)
    )


def spread_table(table, width):
    return jnp.concatenate([table] * (width // table.shape[1]), axis=1)


def head_lanes(shape):
    return lax.broadcasted_iota(jnp.int32, shape, 1) // HEAD_DIM


def attend_kernel(
    chips, cuts, extras, h1_hbm, w_hbm, cos_ref, sin_ref, q_place, k_place, length_ref, g_ref, *refs
):
    n = extras.n
    srcs, refs = refs[:n], refs[n:]
    o_ref, q_ref, k_ref, v_ref, p_ref, g_all = refs[:6]
    dsts, (h1_ref, w_ref, load_sem), sems = refs[6 : 6 + n], refs[6 + n : 9 + n], refs[9 + n :]
    load, loaded = mover([(w_hbm, w_ref), (h1_hbm, h1_ref)], load_sem)
    begin, hop, from_side, local, finish = gather_task(chips, cuts, g_ref, g_all, sems[:5])
    start_swaps, start_rows, middle, wait_rows, wait_swaps = extras.tasks(srcs, dsts, sems[5:])
    step, steps = pl.program_id(0), pl.num_programs(0)
    tile, width = o_ref.shape
    f32, bf16 = jnp.float32, jnp.bfloat16

    @pl.when(step == 0)
    def _():
        load()
        greet(chips, extras.swaps > 0, extras.rows)
        begin()
        start_rows()
        start_swaps()
        loaded()

        def one(i, _):
            rows = pl.ds(pl.multiple_of(i * tile, tile), tile)
            mixed = jnp.dot(h1_ref[rows], w_ref[...], preferred_element_type=f32)
            cosine, sine = spread_table(cos_ref[rows], width), spread_table(sin_ref[rows], width)
            for at, ref in enumerate((q_ref, k_ref)):
                got = mixed[:, at * width : (at + 1) * width]
                ref[rows] = (got * cosine + partner(got) * sine).astype(bf16)
            v_ref[rows] = mixed[:, 2 * width :].astype(bf16)
            return 0

        lax.fori_loop(0, steps, one, 0)

    @pl.when((step > 0) & (step < chips))
    def _():
        hop(step)


    rows = pl.ds(pl.multiple_of(step * tile, tile), tile)
    queries = q_ref[rows] * jnp.asarray(1.0 / math.sqrt(HEAD_DIM), bf16)
    lanes = head_lanes((tile, width))
    place = q_place[...]
    allowed = k_place[...] <= place
    out = jnp.zeros((tile, width), f32)
    for head in range(width // HEAD_DIM):
        here = lanes == head
        one_head = jnp.where(here, queries, jnp.zeros((), bf16))
        scores = lax.dot_general(
            one_head, k_ref[...], (((1,), (1,)), ((), ())), preferred_element_type=f32
        )
        scores = jnp.where(allowed, scores, neg_large)
        weights = jnp.exp(scores - jnp.max(scores, axis=-1, keepdims=True))
        weights = weights * (1.0 / jnp.sum(weights, axis=-1, keepdims=True))
        low = weights.astype(bf16)
        p_ref[head] = low
        out = jnp.where(here, jnp.dot(low, v_ref[...], preferred_element_type=f32), out)
    o_ref[...] = jnp.where(place < length_ref[0], out, 0.0).astype(bf16)
    pl.when(step == max(0, chips - 2))(middle)

    @pl.when(step == steps - 1)
    def _():
        local().wait()
        for y in range(chips):
            from_side(y)
        finish()
        wait_rows()
        wait_swaps()


def attend(cid, h1_all, w_in, cosine, sine, place, live_place, length, g, extras, cuts=2):
    seq, wide = h1_all.shape
    width = w_in.shape[1] // 3
    heads = width // HEAD_DIM
    nb = lax.axis_size("blk")
    tile = seq // (nb // 2)
    part = pl.BlockSpec((tile, width), lambda i: (i, 0))

    full = jax.ShapeDtypeStruct((seq, width), jnp.bfloat16)
    return pl.pallas_call(
        functools.partial(attend_kernel, nb // 2, cuts, extras),
        grid=(seq // tile,),
        in_specs=[
            ANY, ANY, once(seq, 2 * HEAD_DIM), once(seq, 2 * HEAD_DIM),
            pl.BlockSpec((tile, 1), lambda i: (i, 0)),
            once(1, seq),
            pl.BlockSpec(memory_space=pltpu.SMEM),
            once(*g.shape),
        ]
        + extras.specs,
        out_specs=[part] + [once(seq, width)] * 3
        + [pl.BlockSpec((heads, tile, seq), lambda i: (0, i, 0)), ANY]
        + extras.specs,
        out_shape=[full] * 4
        + [
            jax.ShapeDtypeStruct((heads, seq, seq), jnp.bfloat16),
            jax.ShapeDtypeStruct((seq, g.shape[1]), g.dtype),
        ]
        + extras.shapes,
        scratch_shapes=[
            pltpu.VMEM(h1_all.shape, h1_all.dtype),
            pltpu.VMEM(w_in.shape, w_in.dtype),
            pltpu.SemaphoreType.DMA((2,)),
        ]
        + gather_sems(nb, cuts)
        + extras.scratch,
        compiler_params=params(cid),
        cost_estimate=cost(4 * seq * seq * width + 6 * seq * wide * width),
    )(h1_all, w_in, cosine, sine, place, live_place, length.reshape(1), g, *extras.operands)


def attend_back_kernel(
    chips, cuts, tile_y, extras, q_ref, k_ref, v_ref, o_all, g_ref, p_ref, cos_ref, sin_ref, q_place, length_ref,
    hidden_hbm, red_hbm, branch_hbm, h1_hbm, *refs
):
    n = extras.n
    srcs, (mixed_ref, y_ref, dw_ref), dsts = refs[:n], refs[n : n + 3], refs[n + 3 : 2 * n + 3]
    refs = refs[2 * n + 3 :]
    (ds_ref, qm_ref, gm_ref, dk_acc, dv_acc, hidden_ref, red_ref, branch_ref, h1_ref, load_sem), refs = (
        refs[:10], refs[10:],
    )
    put, _, hop, finish = scatter_task(chips, cuts, tile_y, y_ref, refs[:4], refs[4:10])
    start_swaps, start_rows, middle, wait_rows, wait_swaps = extras.tasks(srcs, dsts, refs[10:])
    load, loaded = mover(
        [(red_hbm, red_ref), (hidden_hbm, hidden_ref), (branch_hbm, branch_ref), (h1_hbm, h1_ref)], load_sem
    )
    step, steps = pl.program_id(0), pl.num_programs(0)
    tile, width = g_ref.shape
    f32, bf16 = jnp.float32, jnp.bfloat16
    factor = 1.0 / math.sqrt(HEAD_DIM)

    @pl.when(step == 0)
    def _():
        load()
        greet(chips, True, extras.rows)
        start_swaps()
        start_rows()
        dk_acc[...] = jnp.zeros_like(dk_acc)
        dv_acc[...] = jnp.zeros_like(dv_acc)

        loaded(0, 1)

    pl.when(step == steps // 2)(middle)
    put(step, lambda rows: hidden_ref.at[rows], red_ref)

    pl.when(step == 0)(lambda: hop(step))
    over_rows = (((0,), (0,)), ((), ()))
    rows = pl.ds(pl.multiple_of(step * tile, tile), tile)
    lanes = head_lanes((tile, width))
    nothing = jnp.zeros((), bf16)
    grad = jnp.where(q_place[...] < length_ref[0], g_ref[...], nothing)
    both = grad.astype(f32) * o_all[rows].astype(f32)
    queries = q_ref[rows]
    grad_q = jnp.zeros((tile, width), f32)
    for head in range(width // HEAD_DIM):
        here = lanes == head
        block = pl.ds(head * tile, tile)
        delta = jnp.sum(jnp.where(here, both, 0.0), axis=-1, keepdims=True)
        one_grad = jnp.where(here, grad, nothing)
        gm_ref[block] = one_grad
        qm_ref[block] = jnp.where(here, queries, nothing)
        grad_p = lax.dot_general(
            one_grad, v_ref[...], (((1,), (1,)), ((), ())), preferred_element_type=f32
        )
        grad_s = (p_ref[head].astype(f32) * (grad_p - delta)).astype(bf16)
        ds_ref[block] = grad_s
        grad_q = jnp.where(here, jnp.dot(grad_s, k_ref[...], preferred_element_type=f32), grad_q)
    heads = width // HEAD_DIM
    dv_acc[...] += lax.dot_general(
        p_ref[...].reshape(heads * tile, p_ref.shape[2]), gm_ref[...], over_rows,
        preferred_element_type=f32,
    )
    dk_acc[...] += lax.dot_general(ds_ref[...], qm_ref[...], over_rows, preferred_element_type=f32)

    def back(value, cosine, sine):
        value = (value * factor).astype(bf16).astype(f32)
        cosine, sine = spread_table(cosine, width), spread_table(sine, width)
        return (value * cosine - partner(value) * sine).astype(bf16)

    mixed_ref[rows, :width] = back(grad_q, cos_ref[rows], sin_ref[rows])
    pl.when(step == 0)(lambda: loaded(2))
    share = dw_ref.shape[0] // chips
    cols = pl.ds(pl.multiple_of(step * share, share), share)
    dw_ref[cols, 3 * width :] = lax.dot_general(
        branch_ref[:, cols], o_all[...], over_rows, preferred_element_type=f32
    ).astype(bf16)
    pl.when((step > 0) & (step < steps - 1))(lambda: hop(step))

    @pl.when(step == steps - 1)
    def _():
        mixed_ref[:, width : 2 * width] = back(dk_acc[...], cos_ref[...], sin_ref[...])
        mixed_ref[:, 2 * width :] = dv_acc[...].astype(bf16)
        loaded(3)
        deep = 256

        def one(i, _):
            at = pl.ds(pl.multiple_of(i * deep, deep), deep)
            dw_ref[at, : 3 * width] = lax.dot_general(
                h1_ref[:, at], mixed_ref[...], over_rows, preferred_element_type=f32
            ).astype(bf16)
            return 0

        lax.fori_loop(0, dw_ref.shape[0] // deep, one, 0)
        wait_rows()
        finish()
        wait_swaps()


def attend_back(
    cid, q, k, v, o, g, p, cosine, sine, place, length, hidden, w_red, branch_all, h1_all, extras, cuts=2
):
    seq, width = q.shape
    heads = width // HEAD_DIM
    nb = lax.axis_size("blk")
    tile = seq // (nb // 2)
    wide, units = w_red.shape
    full = once(seq, width)
    f32, bf16 = jnp.float32, jnp.bfloat16
    loads = (hidden, w_red, branch_all, h1_all)
    return pl.pallas_call(
        functools.partial(attend_back_kernel, nb // 2, cuts, 1024, extras),
        grid=(seq // tile,),
        in_specs=[
            full, full, full, full,
            pl.BlockSpec((tile, width), lambda i: (i, 0)),
            pl.BlockSpec((heads, tile, seq), lambda i: (0, i, 0)),
            once(seq, 2 * HEAD_DIM), once(seq, 2 * HEAD_DIM),
            pl.BlockSpec((tile, 1), lambda i: (i, 0)),
            pl.BlockSpec(memory_space=pltpu.SMEM),
        ]
        + [ANY] * 4
        + extras.specs,
        out_specs=[
            once(seq, 3 * width), once(seq // nb, wide), once(wide, 4 * width)
        ]
        + extras.specs,
        out_shape=[
            jax.ShapeDtypeStruct((seq, 3 * width), bf16),
            jax.ShapeDtypeStruct((seq // nb, wide), f32),
            jax.ShapeDtypeStruct((wide, 4 * width), bf16),
        ]
        + extras.shapes,
        scratch_shapes=[
            pltpu.VMEM((heads * tile, seq), bf16),
            pltpu.VMEM((heads * tile, width), bf16),
            pltpu.VMEM((heads * tile, width), bf16),
            pltpu.VMEM((seq, width), f32),
            pltpu.VMEM((seq, width), f32),
        ]
        + [pltpu.VMEM(value.shape, value.dtype) for value in loads]
        + [pltpu.SemaphoreType.DMA((4,))]
        + scatter_scratch(nb // 2, cuts, seq // nb, wide)
        + extras.scratch,
        compiler_params=params(cid),
        cost_estimate=cost(10 * seq * seq * width),
    )(q, k, v, o, g, p, cosine, sine, place, length.reshape(1), *loads, *extras.operands)


def arrange(weight, out, parts):
    nb, _, wide = out.shape
    span = wide // parts
    for j in range(nb):
        for part in range(parts):
            at = (part * nb + j) * span
            out[j, :, part * span : (part + 1) * span] = weight[:, at : at + span].astype(out.dtype)


def first_kernel(parts, m, map_ref, tokens_ref, gain_ref, frequency_ref, *refs):
    n = len(parts)
    sources, dsts, later, refs = refs[:n], refs[n : n + m], refs[n + m : 2 * n], refs[2 * n :]
    (h1_ref, inverse_ref, place_ref, cos_ref, sin_ref), refs = refs[:5], refs[5:]
    weights, held, load_sem, sems = refs[:n], refs[n : n + m], refs[n + m], refs[n + m + 1 :]
    swaps = [swap_task(a, b, *sems[3 * i : 3 * i + 3]) for i, (a, b) in enumerate(zip(held, dsts))]
    load, loaded = mover(list(zip(sources, weights)), load_sem)
    load()
    greet(held[0].shape[0] // 2, True)
    for i in range(m):
        loaded(i)
        arrange(weights[i], held[i], parts[i])
        swaps[i][0]()
    _, inverse_ref[...], h1_ref[...] = norm_forward(
        tokens_ref[...].astype(jnp.float32), gain_ref[...]
    )
    for i in range(m, n):
        loaded(i)
        arrange(weights[i], later[i - m], parts[i])
    blocks = map_ref.shape[1]
    block = place_ref.shape[0] // blocks
    lanes = cos_ref.shape[1]
    front = lax.broadcasted_iota(jnp.int32, (block, lanes), 1) % HEAD_DIM < HEAD_DIM // 2
    for j in range(blocks):
        rows = slice(j * block, (j + 1) * block)
        place = map_ref[0, j] * block + lax.broadcasted_iota(jnp.int32, (block, lanes), 0)
        place_ref[rows] = place[:, :1]
        angle = place.astype(jnp.float32) * frequency_ref[...]
        cos_ref[rows] = jnp.cos(angle)
        sine = jnp.sin(angle)
        sin_ref[rows] = jnp.where(front, -sine, sine)
    for _, wait in swaps:
        wait()


def first(cid, block_map, tokens, gain, weights, parts, m):
    nb = lax.axis_size("blk")
    shapes = [(nb, value.shape[0], value.shape[1] // nb) for value in weights]
    n = len(weights)
    t, width = tokens.shape
    half = HEAD_DIM // 2
    frequency = jnp.exp(
        -jnp.arange(half, dtype=jnp.float32) * (2.0 / HEAD_DIM) * math.log(theta_base)
    )
    dma, f32 = pltpu.SemaphoreType.DMA, jnp.float32
    table = jax.ShapeDtypeStruct((nb * t, 2 * HEAD_DIM), f32)
    return pl.pallas_call(
        functools.partial(first_kernel, parts, m),
        out_shape=[jax.ShapeDtypeStruct(shape, jnp.bfloat16) for shape in shapes]
        + [
            jax.ShapeDtypeStruct((t, width), jnp.bfloat16),
            jax.ShapeDtypeStruct((t, 1), f32),
            jax.ShapeDtypeStruct((nb * t, 1), jnp.int32),
            table,
            table,
        ],
        in_specs=[pl.BlockSpec(memory_space=pltpu.SMEM)] + [VMEM] * 3 + [ANY] * n,
        out_specs=[ANY] * m + [VMEM] * (n - m + 5),
        scratch_shapes=[pltpu.VMEM(value.shape, value.dtype) for value in weights]
        + [pltpu.VMEM(shape, jnp.bfloat16) for shape in shapes[:m]]
        + [dma((n,))] + [dma, dma((nb,)), dma((nb,))] * m,
        compiler_params=params(cid),
        cost_estimate=cost(0),
    )(block_map, tokens, gain[None], jnp.tile(frequency, 4)[None], *weights)


def total_task(nr, nb, x_ref, o_ref, held, rows_held, send_one, recv_one, send_two, recv_two):
    r, b = lax.axis_index("rows"), lax.axis_index("blk")
    across = [lax.rem(b + k, nb) for k in range(1, nb)]
    along = [lax.rem(r + k, nr) for k in range(1, nr)]

    def first(other, slot):
        return pltpu.make_async_remote_copy(
            src_ref=rows_held.at[r], dst_ref=rows_held.at[slot], send_sem=send_two.at[other],
            recv_sem=recv_two.at[slot], device_id=(other, b), device_id_type=MESH,
        )

    def second(other, slot):
        return pltpu.make_async_remote_copy(
            src_ref=held.at[b], dst_ref=held.at[slot], send_sem=send_one.at[other],
            recv_sem=recv_one.at[slot], device_id=(r, other), device_id_type=MESH,
        )

    def start():
        rows_held[r] = x_ref[...]
        for other in along:
            first(other, r).start()

    def middle():
        for other in along:
            first(other, other).wait_recv()
        held[b] = jnp.sum(rows_held[...], axis=0)
        for other in across:
            second(other, b).start()

    def finish():
        for other in across:
            second(other, other).wait_recv()
        o_ref[...] = jnp.sum(held[...], axis=0)
        for other in along:
            first(other, r).wait_send()
        for other in across:
            second(other, b).wait_send()

    return start, middle, finish


def last_scatter_kernel(
    chips, nr, cuts, tile, extras, a_ref, w_ref, x_ref, inverse_ref, gain_ref, resid_ref, gain_two_ref, h1_hbm, *refs
):
    n = extras.n
    srcs, refs = refs[:n], refs[n:]
    o_ref, total_ref, dsts, refs = refs[0], refs[1], refs[2 : 2 + n], refs[2 + n :]
    sum_ref, part_ref, h1_ref, load_sem, refs = refs[0], refs[1], refs[2], refs[3], refs[4:]
    put, _, hop, finish = scatter_task(chips, cuts, tile, sum_ref, refs[:4], refs[4:10])
    start_total, middle_total, finish_total = total_task(
        nr, 2 * chips, part_ref, total_ref, *refs[10:16]
    )
    start_swaps, start_rows, middle, wait_rows, wait_swaps = extras.tasks(srcs, dsts, refs[16:])
    load, loaded = mover([(h1_hbm, h1_ref)], load_sem)
    load()
    greet(chips, True, True)
    start_swaps()
    start_rows()
    part_ref[0:1] = jnp.zeros_like(part_ref[0:1])
    part_ref[1:2] = gain_two_ref[...]
    loaded()

    def seen(rows, cols, got):
        part_ref[0:1, cols] += jnp.sum(got * h1_ref[rows, cols].astype(jnp.float32), axis=0)[None]

    for s in range(chips):
        put(s, lambda rows: a_ref.at[rows], w_ref, seen)
        if s < chips - 1:
            hop(s)
    part_ref[0:1] = part_ref[0:1] / gain_ref[...]
    start_total()
    middle()
    middle_total()
    wait_rows()
    finish()
    inverse = inverse_ref[...]
    unit = x_ref[...].astype(jnp.float32) * inverse
    o_ref[...] = resid_ref[...] + norm_backward(sum_ref[...], unit, inverse, gain_ref[...])[0]
    finish_total()
    wait_swaps()


def last_scatter(cid, a, w, x, inverse, gain, resid, gain_two, h1_all, extras, cuts=2, tile=1024):
    nr, nb = lax.axis_size("rows"), lax.axis_size("blk")
    t, width = x.shape
    pair = (2, width)
    dma, f32 = pltpu.SemaphoreType.DMA, jnp.float32
    return pl.pallas_call(
        functools.partial(last_scatter_kernel, nb // 2, nr, cuts, tile, extras),
        out_shape=[jax.ShapeDtypeStruct((t, width), f32), jax.ShapeDtypeStruct(pair, f32)]
        + extras.shapes,
        in_specs=[VMEM] * 7 + [ANY] + extras.specs,
        out_specs=[VMEM] * 2 + extras.specs,
        scratch_shapes=[
            pltpu.VMEM((t, width), f32),
            pltpu.VMEM(pair, f32),
            pltpu.VMEM(h1_all.shape, h1_all.dtype),
            dma((1,)),
        ]
        + scatter_scratch(nb // 2, cuts, t, width)
        + [pltpu.VMEM((nb,) + pair, f32), pltpu.VMEM((nr,) + pair, f32)]
        + [dma((nb,))] * 2 + [dma((nr,))] * 2
        + extras.scratch,
        compiler_params=params(cid),
        cost_estimate=cost(2 * a.shape[0] * width * w.shape[1]),
    )(a, w, x, inverse, gain[None], resid, gain_two, h1_all, *extras.operands)


def step_kernel(parts, one_array, *refs):
    count = 1 if one_array else parts
    grads, refs = refs[:count], refs[count:]
    outs = len(refs) // 2
    rule = adam_step if outs == 3 else moment_step

    def go(grad):
        wide = grad.shape[2]
        for j in range(grad.shape[0]):
            cols = slice(j * wide, (j + 1) * wide)
            gradient = grad[j].astype(jnp.float32)
            for ref, value in zip(
                refs[outs:], rule(*[ref[:, cols] for ref in refs[:outs]], gradient)
            ):
                ref[:, cols] = value

    if one_array:
        go(grads[0])
        return
    for part, grad in enumerate(grads):
        pl.when(pl.program_id(0) == part)(functools.partial(go, grad))


def step(pieces, parts, states, first=0):
    one_array = not isinstance(pieces, list)
    pieces = [pieces] if one_array else pieces
    nb = pieces[0].shape[0]
    rows, columns = states[0].shape
    tile = min(rows, 64 if parts > 1 else 32)
    span = columns // parts
    at = pl.BlockSpec((tile, span), lambda part, i: (i, part))
    block = (nb, tile, span // nb)
    if one_array:
        grads = [pl.BlockSpec(block, lambda part, i: (0, i, first + part))]
    else:
        grads = [pl.BlockSpec(block, lambda part, i: (0, i, 0))] * parts
    outs = len(states)
    return pl.pallas_call(
        functools.partial(step_kernel, parts, one_array),
        grid=(parts, rows // tile),
        in_specs=grads + [at] * outs,
        out_specs=[at] * outs,
        out_shape=[jax.ShapeDtypeStruct((rows, columns), jnp.float32)] * outs,
        compiler_params=pltpu.CompilerParams(vmem_limit_bytes=60 * MIB),
        cost_estimate=pl.CostEstimate(
            flops=0, bytes_accessed=(8 * outs + 2) * rows * columns, transcendentals=0
        ),
    )(*pieces, *states)


def after(value, *others):
    return lax.optimization_barrier((value,) + others)[0]


def over_tokens(left, right):
    return lax.dot_general(
        left, right, (((0,), (0,)), ((), ())), preferred_element_type=jnp.float32
    )


def shards(
    tokens, cotangent, lengths, block_map, gain_attend, gain_expand,
    attend_in, attend_out, expand_in, reduce_out,
    attend_in_first, attend_out_first, expand_in_first, reduce_out_first,
    attend_in_second, attend_out_second, expand_in_second, reduce_out_second,
):
    nb = lax.axis_size("blk")
    length = lengths[0]
    swap_in, swap_out, swap_red, pieces_gu, h1, inverse_one, place, cosine, sine = first(
        2, block_map, tokens[0], gain_attend,
        (attend_in, attend_out.T, reduce_out.T, expand_in), (3, 1, 1, 2), 3,
    )
    block_rows = tokens.shape[1] // 2
    row_place = (block_map[0][:, None] * block_rows + jnp.arange(block_rows)[None, :]).reshape(1, -1)
    live_place = jnp.where(row_place < length, row_place, jnp.int32(1 << 30))
    nr = lax.axis_size("rows")
    deep = nb * attend_in.shape[0]
    wide = tokens.shape[2]

    def flat(pieces):
        return pieces.reshape(deep, pieces.shape[2])

    h1_all, swap_gu, w_in, w_out, w_red = line_gather(
        3, h1,
        Extras([pieces_gu], [(flat(value), 0, deep) for value in (swap_in, swap_out, swap_red)]),
    )
    w_in, w_out, w_red = [value.reshape(wide, -1) for value in (w_in, w_out, w_red)]
    early = deep * 5 // 8
    attended, q, k, v, p, g_all, gu_early = attend(
        4, h1_all, w_in, cosine, sine, place, live_place, length, cotangent[0],
        Extras([], [(flat(swap_gu), 0, early)]),
    )
    x1, inverse_two, h2, gu_late = attend_out_sum(
        5, attended, w_out, tokens[0], gain_expand,
        Extras([], [(flat(swap_gu), early, deep - early)]),
    )

    def by_rows(gradient):
        return gradient.reshape(nr, nb, deep // nb, gradient.shape[1])

    grad_x1, branch, gain_two, hidden, part_gate, part_up, rows_reduce = feed_forward(
        6, h2, x1, inverse_two, gain_expand, cotangent[0], gu_early, gu_late, w_red, g_all
    )
    branch_all, grad_o, rows_gate = gather_dot(
        9, branch, w_out, Extras([], [], [by_rows(part_gate)])
    )
    grad_mixed, y, part_both, own_reduce, rows_up = attend_back(
        10, q, k, v, attended, grad_o, p, cosine, sine, place, length,
        hidden, w_red, branch_all, h1_all, Extras([rows_reduce], [], [by_rows(part_up)]),
    )
    y = x1 + y
    grad_input, gains, own_gate, own_up, rows_both = last_scatter(
        11, grad_mixed, w_in, tokens[0], inverse_one, gain_attend, grad_x1, gain_two, h1_all,
        Extras([rows_gate, rows_up], [], [by_rows(part_both)]),
    )
    both = lax.all_to_all(rows_both, "blk", 0, 0, tiled=True)
    set_four = step(own_reduce, 1, (reduce_out.T, reduce_out_first.T, reduce_out_second.T))
    set_three = step([own_gate, own_up], 2, (expand_in, expand_in_first, expand_in_second))
    both = after(both, set_three[2], set_four[2])
    set_one = step(both, 3, (attend_in, attend_in_first, attend_in_second))
    set_two = step(both, 1, (attend_out_first.T, attend_out_second.T), 3)
    return (
        y.astype(jnp.bfloat16).reshape(tokens.shape),
        grad_input.reshape(tokens.shape),
        gains[0],
        gains[1],
        *set_one,
        *[value.T for value in set_two],
        *set_three,
        *[value.T for value in set_four],
    )


def solution(mesh):
    placed = (
        P("rows", "blk", None),
        P("rows", "blk", None),
        P("rows"),
        P("rows", None),
        P(),
        P(),
        P(("rows", "blk"), None),
        P(None, ("rows", "blk")),
        P(("rows", "blk"), None),
        P(None, ("rows", "blk")),
        P(("rows", "blk"), None),
        P(None, ("rows", "blk")),
        P(("rows", "blk"), None),
        P(None, ("rows", "blk")),
        P(("rows", "blk"), None),
        P(None, ("rows", "blk")),
        P(("rows", "blk"), None),
        P(None, ("rows", "blk")),
    )
    return jax.shard_map(
        shards,
        mesh=mesh,
        in_specs=placed,
        out_specs=(
            P("rows", "blk", None),
            P("rows", "blk", None),
            P(),
            P(),
            P(("rows", "blk"), None),
            P(("rows", "blk"), None),
            P(("rows", "blk"), None),
            P(None, ("rows", "blk")),
            P(None, ("rows", "blk")),
            P(("rows", "blk"), None),
            P(("rows", "blk"), None),
            P(("rows", "blk"), None),
            P(None, ("rows", "blk")),
            P(None, ("rows", "blk")),
            P(None, ("rows", "blk")),
        ),
        check_vma=False,
    )
```

```python
import functools
import math

import jax
import jax.numpy as jnp
from jax import lax
from jax.experimental import pallas as pl
from jax.experimental.pallas import tpu as pltpu
from jax.sharding import PartitionSpec as P

HEADS = 32
HEAD_DIM = 64
MESH = pl.DeviceIdType.MESH
MIB = 1 << 20

theta_base = 130000.0
norm_eps = 1e-05
neg_large = -1e30
beta_one = 0.9
beta_two = 0.95
learn_rate = 0.01
decay_rate = 0.1
adam_eps = 1e-08
step_count = 10


def line_place():
    b = lax.axis_index("blk")
    return lax.axis_index("rows"), b // 2, b % 2


def greet(chips, swaps=False, rows=False):
    r, z, c = line_place()
    barrier = pltpu.get_barrier_semaphore()
    count = 0

    def signal(row, b):
        pl.semaphore_signal(barrier, inc=1, device_id=(row, b), device_id_type=MESH)

    b, nb, nr = 2 * z + c, 2 * chips, lax.axis_size("rows")
    if rows:
        for k in range(1, nr):
            signal(lax.rem(r + k, nr), b)
        count = nr - 1
    if swaps:
        for k in range(1, nb):
            signal(r, lax.rem(b + k, nb))
        count = count + nb - 1
    else:
        signal(r, b + 1 - 2 * c)
        pl.when(z < chips - 1)(lambda: signal(r, b + 2))
        pl.when(z > 0)(lambda: signal(r, b - 2))
        count = count + 1 + (z < chips - 1).astype(jnp.int32) + (z > 0).astype(jnp.int32)
    pl.semaphore_wait(barrier, count)


def swap_task(src, dst, local, send, recv):
    r, b = lax.axis_index("rows"), lax.axis_index("blk")
    nb = src.shape[0]
    others = [lax.rem(b + k, nb) for k in range(1, nb)]

    def remote(other, slot):
        return pltpu.make_async_remote_copy(
            src_ref=src.at[other], dst_ref=dst.at[slot], send_sem=send.at[other],
            recv_sem=recv.at[slot], device_id=(r, other), device_id_type=MESH,
        )

    def start():
        for other in others:
            remote(other, b).start()
        pltpu.make_async_copy(src.at[b], dst.at[b], local).start()

    def wait():
        for other in others:
            remote(other, other).wait_recv()
        for other in others:
            remote(other, b).wait_send()
        pltpu.make_async_copy(src.at[b], dst.at[b], local).wait()

    return start, wait


def rows_copy(src, dst, send, recv, device):
    return pltpu.make_async_remote_copy(
        src_ref=src, dst_ref=dst, send_sem=send, recv_sem=recv,
        device_id=(device, lax.axis_index("blk")), device_id_type=MESH,
    )


def through(src, stage, dst, local):
    first = pltpu.make_async_copy(src, stage, local)
    second = pltpu.make_async_copy(stage, dst, local)

    def store():
        first.wait()
        second.start()

    return first.start, store, second.wait


def direct_gather(src, dst, stage, local, send, recv):
    r, nr = lax.axis_index("rows"), dst.shape[0]
    others = [lax.rem(r + k, nr) for k in range(1, nr)]
    load, store, stored = through(src, stage, dst.at[r], local)

    def start():
        for other in others:
            rows_copy(src, dst.at[r], send.at[other], recv.at[r], other).start()
        load()

    def wait():
        for other in others:
            rows_copy(src, dst.at[other], send.at[other], recv.at[other], other).wait()
        stored()

    return start, store, wait


def square_gather(src, dst, stage, local, send, recv):
    r = lax.axis_index("rows")
    half = src.shape[0] // 2
    load, store, stored = through(src, stage, dst.at[r], local)

    def near(sem, origin, device):
        return rows_copy(src, dst.at[origin], send.at[sem], recv.at[sem], device)

    def onward(sem, origin, device):
        part = dst.at[origin, pl.ds((sem - 2) * half, half)]
        return rows_copy(part, part, send.at[sem], recv.at[sem], device)

    def start():
        near(0, r, r ^ 1).start()
        near(1, r, r ^ 2).start()
        load()

    def middle():
        store()
        near(0, r ^ 1, r ^ 1).wait_recv()
        onward(2, r ^ 1, r ^ 2).start()
        near(1, r ^ 2, r ^ 2).wait_recv()
        onward(3, r ^ 2, r ^ 1).start()

    def wait():
        onward(2, r ^ 3, r ^ 2).wait_recv()
        onward(3, r ^ 3, r ^ 1).wait_recv()
        near(0, r, r ^ 1).wait_send()
        near(1, r, r ^ 2).wait_send()
        onward(2, r ^ 1, r ^ 2).wait_send()
        onward(3, r ^ 2, r ^ 1).wait_send()
        stored()

    return start, middle, wait


def direct_sum(src, dst, held, local, send, recv):
    r, nr = lax.axis_index("rows"), src.shape[0]
    others = [lax.rem(r + k, nr) for k in range(1, nr)]

    def start():
        for other in others:
            rows_copy(src.at[other], held.at[r], send.at[other], recv.at[r], other).start()
        pltpu.make_async_copy(src.at[r], held.at[r], local).start()

    def wait():
        for other in others:
            rows_copy(src.at[other], held.at[other], send.at[other], recv.at[other], other).wait()
        pltpu.make_async_copy(src.at[r], held.at[r], local).wait()

        def one(j, _):
            total = held[0, j].astype(jnp.float32)
            for slot in range(1, nr):
                total = total + held[slot, j].astype(jnp.float32)
            held[0, j] = total.astype(held.dtype)
            return 0

        lax.fori_loop(0, held.shape[1], one, 0)
        done = pltpu.make_async_copy(held.at[0], dst, local)
        done.start()
        done.wait()

    return start, lambda: None, wait


def square_sum(src, dst, held, local, send, recv):
    r = lax.axis_index("rows")
    half = src.shape[1] // 2
    parts = [(pl.ds(0, half), r ^ 1, r ^ 2), (pl.ds(half, half), r ^ 2, r ^ 1)]

    def out(i, k):
        at, one, two = parts[i]
        return rows_copy(
            src.at[one if k == 0 else r ^ 3, at], held.at[k, at], send.at[2 * i + k],
            recv.at[2 * i + k], one,
        )

    def own(i, k):
        at, one, two = parts[i]
        return pltpu.make_async_copy(
            src.at[r if k == 0 else two, at], held.at[2 + k, at], local.at[2 * i + k]
        )

    def onward(i):
        at, one, two = parts[i]
        return rows_copy(held.at[3, at], held.at[4, at], send.at[4 + i], recv.at[4 + i], two)

    def add(i, into, *slots):
        def one(j, _):
            j = i * half + j
            total = held[into, j].astype(jnp.float32)
            for slot in slots:
                total = total + held[slot, j].astype(jnp.float32)
            held[into, j] = total.astype(held.dtype)
            return 0

        lax.fori_loop(0, half, one, 0)

    def start():
        for i in range(2):
            for k in (1, 0):
                out(i, k).start()
                own(i, k).start()

    def start_as(make):
        for i, k in ((0, 1), (1, 1), (0, 0), (1, 0)):
            make((parts[i][1] if k == 0 else r ^ 3), i)
            out(i, k).start()
        for i, k in ((0, 1), (1, 1), (0, 0), (1, 0)):
            make((r if k == 0 else parts[i][2]), i)
            own(i, k).start()

    start.as_made = start_as

    def middle():
        for i in range(2):
            out(i, 1).wait_recv()
            own(i, 1).wait()
            add(i, 3, 1)
            onward(i).start()

    def wait():
        for i in range(2):
            out(i, 0).wait_recv()
            own(i, 0).wait()
            onward(i).wait_recv()
            add(i, 2, 0, 4)
        done = pltpu.make_async_copy(held.at[2], dst, local.at[0])
        done.start()
        done.wait()
        for i in range(2):
            out(i, 0).wait_send()
            out(i, 1).wait_send()
            onward(i).wait_send()

    return start, middle, wait


class Extras:
    def __init__(self, swaps=(), gathers=(), scatters=()):
        nr, nb = lax.axis_size("rows"), lax.axis_size("blk")
        dma = pltpu.SemaphoreType.DMA
        self.swaps, self.gathers, self.scatters = len(swaps), [g[1:] for g in gathers], len(scatters)
        self.operands = [*swaps, *[g[0] for g in gathers], *scatters]
        self.n = len(self.operands)
        self.rows = bool(gathers) or bool(scatters)
        self.specs = [ANY] * self.n
        self.shapes = [like(value) for value in swaps]
        self.scratch = [dma, dma((nb,)), dma((nb,))] * len(swaps)
        self.square = nr == 4
        sems = 6 if self.square else nr
        for value, _, count in gathers:
            self.shapes.append(jax.ShapeDtypeStruct((nr, count, value.shape[1]), value.dtype))
            self.scratch += [pltpu.VMEM((count, value.shape[1]), value.dtype)]
            self.scratch += [dma, dma((sems,)), dma((sems,))]
        for value in scatters:
            self.shapes.append(jax.ShapeDtypeStruct(value.shape[1:], value.dtype))
            slots = 5 if self.square else nr
            local = dma((4,)) if self.square else dma
            self.scratch += [pltpu.VMEM((slots,) + value.shape[1:], value.dtype)]
            self.scratch += [local, dma((sems,)), dma((sems,))]

    def tasks(self, srcs, dsts, scratch):
        scratch = list(scratch)
        swaps, rows = [], []
        for i, (src, dst) in enumerate(zip(srcs, dsts)):
            if i < self.swaps:
                swaps.append(swap_task(src, dst, *scratch[:3]))
                scratch = scratch[3:]
            elif i < self.swaps + len(self.gathers):
                first, count = self.gathers[i - self.swaps]
                task = square_gather if self.square else direct_gather
                rows.append(task(src.at[pl.ds(first, count)], dst, *scratch[:4]))
                scratch = scratch[4:]
            else:
                task = square_sum if self.square else direct_sum
                rows.append(task(src, dst, *scratch[:4]))
                scratch = scratch[4:]

        def start_swaps():
            for start, _ in swaps:
                start()

        def start_rows():
            for start, _, _ in rows:
                start()

        def middle():
            for _, one, _ in rows:
                one()

        def wait_rows():
            for _, _, one in rows:
                one()

        def wait_swaps():
            for _, one in swaps:
                one()

        return start_swaps, start_rows, middle, wait_rows, wait_swaps


def like(value):
    return jax.ShapeDtypeStruct(value.shape, value.dtype)


ANY = pl.BlockSpec(memory_space=pl.ANY)
VMEM = pl.BlockSpec(memory_space=pltpu.VMEM)


def params(cid):
    return pltpu.CompilerParams(
        collective_id=cid, has_side_effects=True, vmem_limit_bytes=60 * MIB
    )


def cost(flops):
    return pl.CostEstimate(flops=flops, bytes_accessed=150_000_000, transcendentals=0)


def mover(pairs, sem):
    copies = [pltpu.make_async_copy(a, b, sem.at[i]) for i, (a, b) in enumerate(pairs)]

    def start(*which):
        for i in which or range(len(copies)):
            copies[i].start()

    def wait(*which):
        for i in which or range(len(copies)):
            copies[i].wait()

    return start, wait


def gather_task(chips, cuts, x_ref, o_ref, sems):
    copy_sem, send_up, send_down, send_side, recv = sems
    r, z, c = line_place()
    t = x_ref.shape[0]
    h = t // cuts
    up, down, side = (r, 2 * (z + 1) + c), (r, 2 * (z - 1) + c), (r, 2 * z + 1 - c)
    has_up, has_down = z < chips - 1, z > 0
    mine = 2 * z + c

    def piece(j, q):
        return o_ref.at[pl.ds(pl.multiple_of(j * t + q * h, h), h)]

    def remote(src, j, q, sem, dev):
        return pltpu.make_async_remote_copy(
            src_ref=src, dst_ref=piece(j, q), send_sem=sem.at[j, q], recv_sem=recv.at[j, q],
            device_id=dev, device_id_type=MESH,
        )

    def local():
        whole = o_ref.at[pl.ds(pl.multiple_of(mine * t, t), t)]
        return pltpu.make_async_copy(x_ref, whole, copy_sem)

    def start():
        for q in range(cuts):
            from_here = x_ref.at[pl.ds(q * h, h)]
            pl.when(has_up)(lambda: remote(from_here, mine, q, send_up, up).start())
            pl.when(has_down)(lambda: remote(from_here, mine, q, send_down, down).start())
            remote(from_here, mine, q, send_side, side).start()
        local().start()

    def hop(k):
        for q in range(cuts):
            @pl.when(z - k >= 0)
            def _():
                j = 2 * (z - k) + c
                remote(piece(j, q), j, q, send_up, up).wait_recv()
                pl.when(has_up)(lambda: remote(piece(j, q), j, q, send_up, up).start())
                remote(piece(j, q), j, q, send_side, side).start()

            @pl.when(z + k < chips)
            def _():
                j = 2 * (z + k) + c
                remote(piece(j, q), j, q, send_down, down).wait_recv()
                pl.when(has_down)(lambda: remote(piece(j, q), j, q, send_down, down).start())
                remote(piece(j, q), j, q, send_side, side).start()

    def from_side(y):
        for q in range(cuts):
            j = 2 * y + 1 - c
            remote(piece(j, q), j, q, send_side, side).wait_recv()

    def finish():
        for y in range(chips):
            j = 2 * y + c
            for q in range(cuts):
                pl.when(has_up & (z >= y))(
                    lambda: remote(piece(j, q), j, q, send_up, up).wait_send()
                )
                pl.when(has_down & (z <= y))(
                    lambda: remote(piece(j, q), j, q, send_down, down).wait_send()
                )
                remote(piece(j, q), j, q, send_side, side).wait_send()

    return start, hop, from_side, local, finish


def gather_sems(nb, cuts):
    return [pltpu.SemaphoreType.DMA] + [pltpu.SemaphoreType.DMA((nb, cuts))] * 4


def gather_kernel(chips, cuts, extras, x_ref, *refs):
    n = extras.n
    srcs, o_ref, dsts, refs = refs[:n], refs[n], refs[n + 1 : 2 * n + 1], refs[2 * n + 1 :]
    begin, hop, from_side, local, finish = gather_task(chips, cuts, x_ref, o_ref, refs[:5])
    start_swaps, start_rows, middle, wait_rows, wait_swaps = extras.tasks(srcs, dsts, refs[5:])
    greet(chips, True, extras.rows)
    begin()
    start_rows()
    for k in range(1, chips):
        if k == min(3, chips - 1):
            start_swaps()
        hop(k)
    middle()
    local().wait()
    for y in range(chips):
        from_side(y)
    finish()
    wait_rows()
    wait_swaps()


def line_gather(cid, x, extras, cuts=4):
    nb = lax.axis_size("blk")
    return pl.pallas_call(
        functools.partial(gather_kernel, nb // 2, cuts, extras),
        out_shape=[jax.ShapeDtypeStruct((nb * x.shape[0], x.shape[1]), x.dtype)] + extras.shapes,
        in_specs=[VMEM] + extras.specs,
        out_specs=[ANY] + extras.specs,
        scratch_shapes=gather_sems(nb, cuts) + extras.scratch,
        compiler_params=params(cid),
        cost_estimate=cost(0),
    )(x, *extras.operands)


def arrival_order(chips):
    table = []
    for z in range(chips):
        row = [z]
        for k in range(1, chips):
            row += [y for y in (z - k, z + k) if 0 <= y < chips]
        table.append(row)
    return table


def need_order(chips):
    table = []
    for z in range(chips):
        need = {
            y: (chips - 1 + z - y) if y > z else (chips - 1 - z + y)
            for y in range(chips) if y != z
        }
        table.append(sorted(need, key=lambda y: need[y]) + [z])
    return table


def pick(table, z, k):
    out = 0
    for at, row in enumerate(table):
        for step, block in enumerate(row):
            out = out + jnp.where((z == at) & (k == step), block, 0)
    return out


def scatter_task(chips, cuts, tile, o_ref, bufs, sems):
    mine, away, side_buf, line_buf = bufs
    send_side, recv_side, send_up, recv_up, send_down, recv_down = sems
    r, z, c = line_place()
    t, width = o_ref.shape
    low, f32 = away.dtype, jnp.float32
    up, down, side = (r, 2 * (z + 1) + c), (r, 2 * (z - 1) + c), (r, 2 * z + 1 - c)
    has_up, has_down = z < chips - 1, z > 0
    h = t // cuts
    table = need_order(chips)

    def remote(src, dst, y, q, send, recv, dev):
        return pltpu.make_async_remote_copy(
            src_ref=src.at[y, pl.ds(q * h, h)], dst_ref=dst.at[y, pl.ds(q * h, h)],
            send_sem=send.at[y, q], recv_sem=recv.at[y, q], device_id=dev, device_id_type=MESH,
        )

    def to_side(y, q):
        return remote(away, side_buf, y, q, send_side, recv_side, side)

    def along(y, slot, q, send, recv, dev):
        return pltpu.make_async_remote_copy(
            src_ref=mine.at[y, pl.ds(q * h, h)], dst_ref=line_buf.at[slot, pl.ds(q * h, h)],
            send_sem=send.at[y, q], recv_sem=recv.at[y, q], device_id=dev, device_id_type=MESH,
        )

    def to_up(y, q):
        return along(y, y, q, send_up, recv_up, up)

    def to_down(y, q):
        return along(y, jnp.where(y == z - 1, chips, y), q, send_down, recv_down, down)

    def from_up(y, q):
        return along(y, jnp.where(y == z, chips, y), q, send_down, recv_down, down)

    def rows(q):
        return pl.ds(q * h, h)

    def total(y, q):
        to_side(y, q).wait_recv()
        return mine[y, rows(q)].astype(f32) + side_buf[y, rows(q)].astype(f32)

    def put(s, rows_of, w_ref, seen=None):
        put_at(pick(table, z, s), rows_of, w_ref, seen)

    def put_at(y, rows_of, w_ref, seen=None):
        block = pl.ds(pl.multiple_of(2 * y * t, 2 * t), 2 * t)
        a = rows_of(block)

        def one(i, _):
            cols = pl.ds(pl.multiple_of(i * tile, tile), tile)
            got = lax.dot_general(
                a[...], w_ref[cols], (((1,), (1,)), ((), ())), preferred_element_type=f32
            )
            if seen is not None:
                seen(block, cols, got)
            got = got.astype(low)

            @pl.when(c == 0)
            def _():
                mine[y, :, cols] = got[:t]
                away[y, :, cols] = got[t:]

            @pl.when(c == 1)
            def _():
                mine[y, :, cols] = got[t:]
                away[y, :, cols] = got[:t]

            return 0

        lax.fori_loop(0, width // tile, one, 0)
        for q in range(cuts):
            to_side(y, q).start()

    def hop(s):
        hop_up(chips - 1 + z - s)
        hop_down(s - (chips - 1) + z)

    def hop_up(y):
        for q in range(cuts):
            @pl.when((y > z) & (y <= chips - 1))
            def _():
                now = total(y, q)

                @pl.when(has_down)
                def _():
                    to_up(y, q).wait_recv()
                    mine[y, rows(q)] = (now + line_buf[y, rows(q)].astype(f32)).astype(low)

                @pl.when(z == 0)
                def _():
                    mine[y, rows(q)] = now.astype(low)

                to_up(y, q).start()

    def hop_down(w):
        for q in range(cuts):
            @pl.when((w >= 0) & (w < z))
            def _():
                now = total(w, q)

                @pl.when(has_up)
                def _():
                    from_up(w, q).wait_recv()
                    mine[w, rows(q)] = (now + line_buf[w, rows(q)].astype(f32)).astype(low)

                @pl.when(z == chips - 1)
                def _():
                    mine[w, rows(q)] = now.astype(low)

                to_down(w, q).start()

    def finish():
        for q in range(cuts):
            o_ref[rows(q)] = total(z, q)
        for q in range(cuts):
            @pl.when(has_down)
            def _():
                to_up(z, q).wait_recv()
                o_ref[rows(q)] += line_buf[z, rows(q)].astype(f32)

            @pl.when(has_up)
            def _():
                from_up(z, q).wait_recv()
                o_ref[rows(q)] += line_buf[chips, rows(q)].astype(f32)

        for y in range(chips):
            for q in range(cuts):
                to_side(y, q).wait_send()
                pl.when(y > z)(lambda: to_up(y, q).wait_send())
                pl.when(y < z)(lambda: to_down(y, q).wait_send())

    return put, (put_at, hop_up, hop_down), hop, finish


def scatter_scratch(chips, cuts, t, width):
    return (
        [pltpu.VMEM((chips, t, width), jnp.bfloat16)] * 3
        + [pltpu.VMEM((chips + 1, t, width), jnp.bfloat16)]
        + [pltpu.SemaphoreType.DMA((chips, cuts))] * 6
    )


def feed_forward_kernel(
    chips, cuts, tile, h2_here, x1_ref, inverse_ref, gain_ref, cotangent_ref, w_hbm, red_hbm, g_hbm,
    grad_out, low_out, gain_out, hidden_out, gate_out, up_out, reduce_out,
    h2_ref, hidden_ref, grad_ref, w_ref, red_ref, g_ref, dw_red, dw_ref, red_held,
    load_sem, save_sem, dw_sem, red_local, red_send, red_recv, *refs
):
    begin, pass_on, from_side, local, sent = gather_task(chips, cuts, h2_here, h2_ref, refs[:5])
    _, (put_at, hop_up, hop_down), _, finish = scatter_task(chips, cuts, tile, grad_out, refs[5:9], refs[9:])
    task = square_sum if dw_red.shape[0] == 4 else direct_sum
    start_red, middle_red, wait_red = task(
        dw_red, reduce_out, red_held, red_local, red_send, red_recv
    )
    load, loaded = mover([(w_hbm, w_ref), (g_hbm, g_ref), (red_hbm, red_ref)], load_sem)
    r, z, c = line_place()
    t, width = h2_here.shape
    units = hidden_ref.shape[1]
    span = min(512, units)
    f32, low = jnp.float32, jnp.bfloat16
    over_rows = (((0,), (0,)), ((), ()))
    load()
    greet(chips, False, True)
    begin()

    def rows_of(y):
        return pl.ds(pl.multiple_of(y * 2 * t, 2 * t), 2 * t)

    def save(y):
        return pltpu.make_async_copy(
            hidden_ref.at[rows_of(y)], hidden_out.at[rows_of(y)], save_sem.at[y]
        )

    def columns(i):
        at, more = i * span, units + i * span
        return pl.ds(pl.multiple_of(at, span), span), pl.ds(pl.multiple_of(more, span), span)

    def forward(y):
        rows = rows_of(y)

        def one(i, _):
            cols, more = columns(i)
            gate = jnp.dot(h2_ref[rows], w_ref[:, cols], preferred_element_type=f32)
            up = jnp.dot(h2_ref[rows], w_ref[:, more], preferred_element_type=f32)
            sigmoid = jax.nn.sigmoid(gate)
            silu = gate * sigmoid
            hidden_ref[rows, cols] = (silu * up).astype(low)
            grad_ref[rows, cols] = (up * (sigmoid * (1.0 + gate * (1.0 - sigmoid)))).astype(low)
            grad_ref[rows, more] = silu.astype(low)
            return 0

        lax.fori_loop(0, units // span, one, 0)
        save(y).start()

    def backward(rows):
        def one(i, _):
            cols, more = columns(i)
            grad = jnp.dot(g_ref[rows], red_ref[:, cols], preferred_element_type=f32)
            grad_ref[rows, cols] = (grad * grad_ref[rows, cols].astype(f32)).astype(low)
            grad_ref[rows, more] = (grad * grad_ref[rows, more].astype(f32)).astype(low)
            return 0

        lax.fori_loop(0, units // span, one, 0)
        return grad_ref.at[rows]

    from_side(z)
    local().wait()
    loaded(0)
    forward(z)
    loaded(1, 2)
    put_at(z, backward, w_ref)
    deep = 256
    turns = width // deep
    piece = dw_red.shape[2]
    run = dw_red.shape[1] * piece

    def reduce_grad(i, _):
        at = pl.ds(pl.multiple_of(i * deep, deep), deep)
        got = lax.dot_general(g_ref[:, at], hidden_ref[...], over_rows, preferred_element_type=f32)
        first = i * deep
        dw_red[first // run, pl.ds(lax.rem(first, run) // piece, deep // piece)] = (
            got.astype(low).reshape(deep // piece, piece, units)
        )
        return 0

    def make_reduce_grad():
        if dw_red.shape[0] == 4:
            tiles = turns // 8

            def make(slot, half):
                first = (slot * 2 + half) * tiles
                lax.fori_loop(first, first + tiles, reduce_grad, 0)

            start_red.as_made(make)
        else:
            lax.fori_loop(0, turns, reduce_grad, 0)
            start_red()

    def save_dw(i, half):
        at = pl.ds(pl.multiple_of(i * deep, deep), deep)
        return pltpu.make_async_copy(
            dw_ref.at[lax.rem(i, 2), half], (gate_out, up_out)[half].at[at], dw_sem.at[lax.rem(i, 2), half]
        )

    def expand_grad(i, _):
        at = pl.ds(pl.multiple_of(i * deep, deep), deep)
        for half in range(2):
            pl.when(i >= 2)(lambda: save_dw(i - 2, half).wait())
            dw_ref[lax.rem(i, 2), half] = lax.dot_general(
                h2_ref[:, at], grad_ref[:, half * units : (half + 1) * units], over_rows,
                preferred_element_type=f32,
            ).astype(low)
            save_dw(i, half).start()
        return 0

    last = 2 * chips - 3
    done = 0
    for turn in range(1, last + 1):
        if turn < chips:
            pass_on(turn)

            @pl.when(z - turn >= 0)
            def _():
                from_side(z - turn)
                forward(z - turn)
                put_at(z - turn, backward, w_ref)

            @pl.when(z + turn < chips)
            def _():
                from_side(z + turn)
                forward(z + turn)
                put_at(z + turn, backward, w_ref)

        hop_up(turn - z)
        hop_down(2 * (chips - 1) - z - turn)
        if turn == chips - 1:
            make_reduce_grad()
        elif turn >= chips:
            until = turns * (turn - chips + 1) // (last - chips + 1)
            lax.fori_loop(done, until, expand_grad, 0)
            done = until
    middle_red()
    finish()
    inverse = inverse_ref[...]
    middle_grad, gain = norm_backward(grad_out[...], x1_ref[...] * inverse, inverse, gain_ref[...])
    grad_x1 = cotangent_ref[...].astype(f32) + middle_grad
    grad_out[...] = grad_x1
    low_out[...] = grad_x1.astype(low)
    gain_out[...] = gain[None]
    wait_red()
    sent()
    for y in range(chips):
        save(y).wait()
    for i in range(max(0, turns - 2), turns):
        for half in range(2):
            save_dw(i, half).wait()


def feed_forward(
    cid, h2, x1, inverse, gain, cotangent, w_gu, w_red, g_all, cuts=2, tile=1024
):
    nr, nb = lax.axis_size("rows"), lax.axis_size("blk")
    seq, width = g_all.shape
    both = w_gu.shape[1]
    units = both // 2
    t = seq // nb
    piece = width // (nr * nb)
    dma, f32, bf16 = pltpu.SemaphoreType.DMA, jnp.float32, jnp.bfloat16
    half = jax.ShapeDtypeStruct((width, units), bf16)
    slots, sems = (5, 6) if nr == 4 else (nr, nr)
    return pl.pallas_call(
        functools.partial(feed_forward_kernel, nb // 2, cuts, tile),
        out_shape=[
            jax.ShapeDtypeStruct((t, width), f32),
            jax.ShapeDtypeStruct((t, width), bf16),
            jax.ShapeDtypeStruct((1, width), f32),
            jax.ShapeDtypeStruct((seq, units), bf16),
            half,
            half,
            jax.ShapeDtypeStruct((nb, piece, units), bf16),
        ],
        in_specs=[VMEM] * 5 + [ANY] * 3,
        out_specs=[VMEM] * 3 + [ANY] * 4,
        scratch_shapes=[
            pltpu.VMEM((seq, width), bf16),
            pltpu.VMEM((seq, units), bf16),
            pltpu.VMEM((seq, both), bf16),
            pltpu.VMEM((width, both), bf16),
            pltpu.VMEM((width, units), bf16),
            pltpu.VMEM((seq, width), bf16),
            pltpu.VMEM((nr, nb, piece, units), bf16),
            pltpu.VMEM((2, 2, 256, units), bf16),
            pltpu.VMEM((slots, nb, piece, units), bf16),
            dma((3,)),
            dma((nb // 2,)),
            dma((2, 2)),
            dma((4,)) if nr == 4 else dma,
            dma((sems,)),
            dma((sems,)),
        ]
        + gather_sems(nb, cuts)
        + scatter_scratch(nb // 2, cuts, t, width),
        compiler_params=params(cid),
        cost_estimate=cost(9 * seq * width * both),
    )(h2, x1, inverse, gain[None], cotangent, w_gu, w_red, g_all)


def attend_out_kernel(chips, cuts, tile, extras, a_ref, w_ref, x_ref, gain_ref, *refs):
    n = extras.n
    srcs, (x1_ref, inverse_ref, h2_ref), dsts, refs = (
        refs[:n], refs[n : n + 3], refs[3 + n : 3 + 2 * n], refs[3 + 2 * n :],
    )
    put, _, hop, finish = scatter_task(chips, cuts, tile, x1_ref, refs[:4], refs[4:10])
    start_swaps, start_rows, middle, wait_rows, wait_swaps = extras.tasks(srcs, dsts, refs[10:])
    greet(chips, False, extras.rows)
    start_rows()
    for s in range(chips):
        put(s, lambda rows: a_ref.at[rows], w_ref)
        if s < chips - 1:
            hop(s)
    middle()
    finish()
    x1 = x_ref[...].astype(jnp.float32) + x1_ref[...]
    x1_ref[...] = x1
    _, inverse_ref[...], h2_ref[...] = norm_forward(x1, gain_ref[...])
    wait_rows()


def norm_forward(values, gain_vector):
    inverse = lax.rsqrt(jnp.mean(values * values, axis=-1, keepdims=True) + norm_eps)
    unit_values = values * inverse
    return (unit_values, inverse, (unit_values * gain_vector).astype(jnp.bfloat16))


def norm_backward(grad_normed, unit_values, inverse, gain_vector):
    grad_unit = grad_normed * gain_vector
    grad_values = inverse * (
        grad_unit - unit_values * jnp.mean(grad_unit * unit_values, axis=-1, keepdims=True)
    )
    return (grad_values, jnp.sum(grad_normed * unit_values, axis=0))


def contract_last(left, right):
    return lax.dot_general(
        left, right, (((1,), (1,)), ((), ())), preferred_element_type=jnp.float32
    )


def adam_step(master, moment_one, moment_two, gradient):
    moment_one = beta_one * moment_one + (1.0 - beta_one) * gradient
    moment_two = beta_two * moment_two + (1.0 - beta_two) * gradient * gradient
    update = (
        moment_one
        / (1.0 - beta_one**step_count)
        / (jnp.sqrt(moment_two / (1.0 - beta_two**step_count)) + adam_eps)
    )
    return (master - learn_rate * (update + decay_rate * master), moment_one, moment_two)


def moment_step(moment_one, moment_two, gradient):
    moment_one = beta_one * moment_one + (1.0 - beta_one) * gradient
    moment_two = beta_two * moment_two + (1.0 - beta_two) * gradient * gradient
    return (moment_one, moment_two)


def once(*shape):
    return pl.BlockSpec(shape, lambda i: (0,) * len(shape), pipeline_mode=pl.Buffered(1))


def partner(values):
    width = values.shape[1]
    half = HEAD_DIM // 2
    feature = lax.broadcasted_iota(jnp.int32, values.shape, 1) % HEAD_DIM
    return jnp.where(
        feature < half, pltpu.roll(values, width - half, 1), pltpu.roll(values, half, 1)
    )


def spread_table(table, width):
    return jnp.concatenate([table] * (width // table.shape[1]), axis=1)


def head_lanes(shape):
    return lax.broadcasted_iota(jnp.int32, shape, 1) // HEAD_DIM


def attend_kernel(
    chips, cuts, tile_o, extras, h1_hbm, w_hbm, cos_ref, sin_ref, q_place, k_place, length_ref, g_ref,
    x_ref, gain_ref, w_out_ref, *refs
):
    n = extras.n
    srcs, refs = refs[:n], refs[n:]
    (o_ref, q_ref, k_ref, v_ref, p_out, g_all, x1_ref, inverse_ref, h2_ref), refs = refs[:9], refs[9:]
    dsts, (h1_ref, w_ref, p_ref, load_sem, p_sem), refs = refs[:n], refs[n : n + 5], refs[n + 5 :]
    load, loaded = mover([(w_hbm, w_ref), (h1_hbm, h1_ref)], load_sem)
    begin, pass_on, from_side, local, sent = gather_task(chips, cuts, g_ref, g_all, refs[:5])
    put, _, hop, finish = scatter_task(chips, cuts, tile_o, x1_ref, refs[5:9], refs[9:15])
    start_swaps, start_rows, middle, wait_rows, wait_swaps = extras.tasks(srcs, dsts, refs[15:])
    step, steps = pl.program_id(0), pl.num_programs(0)
    seq, width = o_ref.shape
    tile = seq // chips
    f32, bf16 = jnp.float32, jnp.bfloat16
    table = need_order(chips)
    _, z, _ = line_place()

    @pl.when(step == 0)
    def _():
        load()
        greet(chips, False, extras.rows)
        begin()
        start_rows()
        loaded()

        def one(i, _):
            rows = pl.ds(pl.multiple_of(i * tile, tile), tile)
            mixed = jnp.dot(h1_ref[rows], w_ref[...], preferred_element_type=f32)
            cosine, sine = spread_table(cos_ref[rows], width), spread_table(sin_ref[rows], width)
            for at, ref in enumerate((q_ref, k_ref)):
                got = mixed[:, at * width : (at + 1) * width]
                ref[rows] = (got * cosine + partner(got) * sine).astype(bf16)
            v_ref[rows] = mixed[:, 2 * width :].astype(bf16)
            return 0

        lax.fori_loop(0, steps, one, 0)

    pl.when(step == steps - 1)(middle)

    @pl.when(step > 0)
    def _():
        pass_on(step)

    def rows_at(s):
        return pl.ds(pl.multiple_of(pick(table, z, s) * tile, tile), tile)

    def save(s):
        slot = lax.rem(s, 2)
        return pltpu.make_async_copy(p_ref.at[slot], p_out.at[:, rows_at(s)], p_sem.at[slot])

    pl.when(step >= 2)(lambda: save(step - 2).wait())
    rows = rows_at(step)
    queries = q_ref[rows] * jnp.asarray(1.0 / math.sqrt(HEAD_DIM), bf16)
    lanes = head_lanes((tile, width))
    place = q_place[rows]
    allowed = k_place[...] <= place
    out = jnp.zeros((tile, width), f32)
    for head in range(width // HEAD_DIM):
        here = lanes == head
        one_head = jnp.where(here, queries, jnp.zeros((), bf16))
        scores = lax.dot_general(
            one_head, k_ref[...], (((1,), (1,)), ((), ())), preferred_element_type=f32
        )
        scores = jnp.where(allowed, scores, neg_large)
        weights = jnp.exp(scores - jnp.max(scores, axis=-1, keepdims=True))
        weights = weights * (1.0 / jnp.sum(weights, axis=-1, keepdims=True))
        low = weights.astype(bf16)
        p_ref[lax.rem(step, 2), head] = low
        out = jnp.where(here, jnp.dot(low, v_ref[...], preferred_element_type=f32), out)
    save(step).start()
    o_ref[rows] = jnp.where(place < length_ref[0], out, 0.0).astype(bf16)
    put(step, lambda rows: o_ref.at[rows], w_out_ref)
    pl.when(step < steps - 1)(lambda: hop(step))

    @pl.when(step == steps - 1)
    def _():
        finish()
        x1 = x_ref[...].astype(f32) + x1_ref[...]
        x1_ref[...] = x1
        _, inverse_ref[...], h2_ref[...] = norm_forward(x1, gain_ref[...])
        for s in range(max(0, chips - 2), chips):
            save(s).wait()
        local().wait()
        for y in range(chips):
            from_side(y)
        sent()
        wait_rows()


def attend(
    cid, h1_all, w_in, cosine, sine, place, live_place, length, g, x, gain, w_out, extras, cuts=2, tile_o=1024
):
    seq, wide = h1_all.shape
    width = w_in.shape[1] // 3
    heads = width // HEAD_DIM
    nb = lax.axis_size("blk")
    chips = nb // 2
    tile = seq // chips
    t = x.shape[0]
    full = jax.ShapeDtypeStruct((seq, width), jnp.bfloat16)
    return pl.pallas_call(
        functools.partial(attend_kernel, chips, cuts, tile_o, extras),
        grid=(chips,),
        in_specs=[
            ANY, ANY, once(seq, 2 * HEAD_DIM), once(seq, 2 * HEAD_DIM), once(seq, 1), once(1, seq),
            pl.BlockSpec(memory_space=pltpu.SMEM),
            once(*g.shape), once(t, wide), once(1, wide), once(wide, width),
        ]
        + extras.specs,
        out_specs=[once(seq, width)] * 4
        + [ANY, ANY, once(t, wide), once(t, 1), once(t, wide)]
        + extras.specs,
        out_shape=[full] * 4
        + [
            jax.ShapeDtypeStruct((heads, seq, seq), jnp.bfloat16),
            jax.ShapeDtypeStruct((seq, g.shape[1]), g.dtype),
            jax.ShapeDtypeStruct((t, wide), jnp.float32),
            jax.ShapeDtypeStruct((t, 1), jnp.float32),
            jax.ShapeDtypeStruct((t, wide), jnp.bfloat16),
        ]
        + extras.shapes,
        scratch_shapes=[
            pltpu.VMEM(h1_all.shape, h1_all.dtype),
            pltpu.VMEM(w_in.shape, w_in.dtype),
            pltpu.VMEM((2, heads, tile, seq), jnp.bfloat16),
            pltpu.SemaphoreType.DMA((2,)),
            pltpu.SemaphoreType.DMA((2,)),
        ]
        + gather_sems(nb, cuts)
        + scatter_scratch(chips, cuts, t, wide)
        + extras.scratch,
        compiler_params=params(cid),
        cost_estimate=cost(4 * seq * seq * width + 6 * seq * wide * width),
    )(
        h1_all, w_in, cosine, sine, place, live_place, length.reshape(1), g, x, gain[None], w_out,
        *extras.operands,
    )


def attend_back_kernel(
    chips, cuts, tile_y, extras, q_ref, k_ref, v_ref, o_all, cos_ref, sin_ref, q_place, length_ref, x_ref,
    w_out_ref, p_hbm, hidden_hbm, red_hbm, h1_hbm, *refs
):
    n = extras.n
    srcs, (mixed_ref, y_ref, dw_ref), dsts = refs[:n], refs[n : n + 3], refs[n + 3 : 2 * n + 3]
    refs = refs[2 * n + 3 :]
    (
        branch_ref, p_ref, ds_ref, qm_ref, gm_ref, dk_acc, dv_acc, hidden_ref, red_ref, h1_ref, load_sem, p_sem,
    ), refs = refs[:12], refs[12:]
    begin, pass_on, from_side, local, sent = gather_task(chips, cuts, x_ref, branch_ref, refs[:5])
    put, _, hop, finish = scatter_task(chips, cuts, tile_y, y_ref, refs[5:9], refs[9:15])
    start_swaps, start_rows, middle, wait_rows, wait_swaps = extras.tasks(srcs, dsts, refs[15:])
    one_buffer = h1_ref.shape != branch_ref.shape
    h1_ref = branch_ref if one_buffer else h1_ref
    load, loaded = mover([(red_hbm, red_ref), (hidden_hbm, hidden_ref), (h1_hbm, h1_ref)], load_sem)
    step, steps = pl.program_id(0), pl.num_programs(0)
    seq, width = q_ref.shape
    tile = seq // chips
    f32, bf16 = jnp.float32, jnp.bfloat16
    factor = 1.0 / math.sqrt(HEAD_DIM)
    over_rows = (((0,), (0,)), ((), ()))
    table = arrival_order(chips)
    _, z, _ = line_place()

    def rows_at(s):
        return pl.ds(pl.multiple_of(pick(table, z, s) * tile, tile), tile)

    def p_load(s):
        slot = lax.rem(s, 2)
        return pltpu.make_async_copy(p_hbm.at[:, rows_at(s)], p_ref.at[slot], p_sem.at[slot])

    @pl.when(step == 0)
    def _():
        p_load(step).start()
        load(0, 1)
        if not one_buffer:
            load(2)
        greet(chips, True, extras.rows)
        begin()
        start_rows()
        start_swaps()
        dk_acc[...] = jnp.zeros_like(dk_acc)
        dv_acc[...] = jnp.zeros_like(dv_acc)
        loaded(0, 1)
        local().wait()

    pl.when(step < steps - 1)(lambda: p_load(step + 1).start())
    put(step, lambda rows: hidden_ref.at[rows], red_ref)
    pl.when(step == 0)(lambda: hop(step))

    @pl.when(step > 0)
    def _():
        pass_on(step)

    pl.when(step == steps - 1)(middle)
    from_side(pick(table, z, step))
    rows = rows_at(step)
    lanes = head_lanes((tile, width))
    nothing = jnp.zeros((), bf16)
    grad = jnp.dot(branch_ref[rows], w_out_ref[...], preferred_element_type=f32).astype(bf16)
    grad = jnp.where(q_place[rows] < length_ref[0], grad, nothing)
    both = grad.astype(f32) * o_all[rows].astype(f32)
    queries = q_ref[rows]
    grad_q = jnp.zeros((tile, width), f32)
    p_load(step).wait()
    low = p_ref.at[lax.rem(step, 2)]
    heads = width // HEAD_DIM
    for head in range(heads):
        here = lanes == head
        block = pl.ds(head * tile, tile)
        delta = jnp.sum(jnp.where(here, both, 0.0), axis=-1, keepdims=True)
        one_grad = jnp.where(here, grad, nothing)
        gm_ref[block] = one_grad
        qm_ref[block] = jnp.where(here, queries, nothing)
        grad_p = lax.dot_general(
            one_grad, v_ref[...], (((1,), (1,)), ((), ())), preferred_element_type=f32
        )
        grad_s = (low[head].astype(f32) * (grad_p - delta)).astype(bf16)
        ds_ref[block] = grad_s
        grad_q = jnp.where(here, jnp.dot(grad_s, k_ref[...], preferred_element_type=f32), grad_q)
    dv_acc[...] += lax.dot_general(
        low[...].reshape(heads * tile, seq), gm_ref[...], over_rows, preferred_element_type=f32
    )
    dk_acc[...] += lax.dot_general(ds_ref[...], qm_ref[...], over_rows, preferred_element_type=f32)

    def back(value, cosine, sine):
        value = (value * factor).astype(bf16).astype(f32)
        cosine, sine = spread_table(cosine, width), spread_table(sine, width)
        return (value * cosine - partner(value) * sine).astype(bf16)

    mixed_ref[rows, :width] = back(grad_q, cos_ref[rows], sin_ref[rows])
    pl.when((step > 0) & (step < steps - 1))(lambda: hop(step))

    @pl.when(step == steps - 1)
    def _():
        mixed_ref[:, width : 2 * width] = back(dk_acc[...], cos_ref[...], sin_ref[...])
        mixed_ref[:, 2 * width :] = dv_acc[...].astype(bf16)
        deep = 256

        def out_grad(i, _):
            at = pl.ds(pl.multiple_of(i * deep, deep), deep)
            dw_ref[at, 3 * width :] = lax.dot_general(
                branch_ref[:, at], o_all[...], over_rows, preferred_element_type=f32
            ).astype(bf16)
            return 0

        def in_grad(i, _):
            at = pl.ds(pl.multiple_of(i * deep, deep), deep)
            dw_ref[at, : 3 * width] = lax.dot_general(
                h1_ref[:, at], mixed_ref[...], over_rows, preferred_element_type=f32
            ).astype(bf16)
            return 0

        turns = dw_ref.shape[0] // deep
        lax.fori_loop(0, turns, out_grad, 0)
        if one_buffer:
            sent()
            load(2)
        loaded(2)
        lax.fori_loop(0, turns, in_grad, 0)
        wait_rows()
        finish()
        if not one_buffer:
            sent()
        wait_swaps()


def attend_back(
    cid, q, k, v, o, p, cosine, sine, place, length, branch, w_out, hidden, w_red, h1_all, extras, cuts=2
):
    seq, width = q.shape
    heads = width // HEAD_DIM
    nb = lax.axis_size("blk")
    chips = nb // 2
    tile = seq // chips
    wide, units = w_red.shape
    t = seq // nb
    full = once(seq, width)
    f32, bf16 = jnp.float32, jnp.bfloat16
    loads = (hidden, w_red, h1_all)
    dma = pltpu.SemaphoreType.DMA
    return pl.pallas_call(
        functools.partial(attend_back_kernel, chips, cuts, 1024, extras),
        grid=(chips,),
        in_specs=[
            full, full, full, full, once(seq, 2 * HEAD_DIM), once(seq, 2 * HEAD_DIM), once(seq, 1),
            pl.BlockSpec(memory_space=pltpu.SMEM), once(t, wide), once(wide, width),
        ]
        + [ANY] * 4
        + extras.specs,
        out_specs=[once(seq, 3 * width), once(t, wide), once(wide, 4 * width)] + extras.specs,
        out_shape=[
            jax.ShapeDtypeStruct((seq, 3 * width), bf16),
            jax.ShapeDtypeStruct((t, wide), f32),
            jax.ShapeDtypeStruct((wide, 4 * width), bf16),
        ]
        + extras.shapes,
        scratch_shapes=[
            pltpu.VMEM((seq, wide), bf16),
            pltpu.VMEM((2, heads, tile, seq), bf16),
            pltpu.VMEM((heads * tile, seq), bf16),
            pltpu.VMEM((heads * tile, width), bf16),
            pltpu.VMEM((heads * tile, width), bf16),
            pltpu.VMEM((seq, width), f32),
            pltpu.VMEM((seq, width), f32),
        ]
        + [pltpu.VMEM(value.shape, value.dtype) for value in loads[:2]]
        + [pltpu.VMEM(h1_all.shape if seq <= 1024 else (16, 128), bf16)]
        + [dma((3,)), dma((2,))]
        + gather_sems(nb, cuts)
        + scatter_scratch(chips, cuts, t, wide)
        + extras.scratch,
        compiler_params=params(cid),
        cost_estimate=cost(10 * seq * seq * width),
    )(q, k, v, o, cosine, sine, place, length.reshape(1), branch, w_out, p, *loads, *extras.operands)


def arrange(weight, out, parts):
    nb, _, wide = out.shape
    span = wide // parts
    for j in range(nb):
        for part in range(parts):
            at = (part * nb + j) * span
            out[j, :, part * span : (part + 1) * span] = weight[:, at : at + span].astype(out.dtype)


def first_kernel(parts, m, map_ref, tokens_ref, gain_ref, frequency_ref, *refs):
    n = len(parts)
    sources, dsts, later, refs = refs[:n], refs[n : n + m], refs[n + m : 2 * n], refs[2 * n :]
    (h1_ref, inverse_ref, place_ref, cos_ref, sin_ref), refs = refs[:5], refs[5:]
    weights, held, load_sem, sems = refs[:n], refs[n : n + m], refs[n + m], refs[n + m + 1 :]
    swaps = [swap_task(a, b, *sems[3 * i : 3 * i + 3]) for i, (a, b) in enumerate(zip(held, dsts))]
    load, loaded = mover(list(zip(sources, weights)), load_sem)
    load()
    greet(held[0].shape[0] // 2, True)
    for i in range(m):
        loaded(i)
        arrange(weights[i], held[i], parts[i])
        swaps[i][0]()
    _, inverse_ref[...], h1_ref[...] = norm_forward(
        tokens_ref[...].astype(jnp.float32), gain_ref[...]
    )
    for i in range(m, n):
        loaded(i)
        arrange(weights[i], later[i - m], parts[i])
    blocks = map_ref.shape[1]
    block = place_ref.shape[0] // blocks
    lanes = cos_ref.shape[1]
    front = lax.broadcasted_iota(jnp.int32, (block, lanes), 1) % HEAD_DIM < HEAD_DIM // 2
    for j in range(blocks):
        rows = slice(j * block, (j + 1) * block)
        place = map_ref[0, j] * block + lax.broadcasted_iota(jnp.int32, (block, lanes), 0)
        place_ref[rows] = place[:, :1]
        angle = place.astype(jnp.float32) * frequency_ref[...]
        cos_ref[rows] = jnp.cos(angle)
        sine = jnp.sin(angle)
        sin_ref[rows] = jnp.where(front, -sine, sine)
    for _, wait in swaps:
        wait()


def first(cid, block_map, tokens, gain, weights, parts, m):
    nb = lax.axis_size("blk")
    shapes = [(nb, value.shape[0], value.shape[1] // nb) for value in weights]
    n = len(weights)
    t, width = tokens.shape
    half = HEAD_DIM // 2
    frequency = jnp.exp(
        -jnp.arange(half, dtype=jnp.float32) * (2.0 / HEAD_DIM) * math.log(theta_base)
    )
    dma, f32 = pltpu.SemaphoreType.DMA, jnp.float32
    table = jax.ShapeDtypeStruct((nb * t, 2 * HEAD_DIM), f32)
    return pl.pallas_call(
        functools.partial(first_kernel, parts, m),
        out_shape=[jax.ShapeDtypeStruct(shape, jnp.bfloat16) for shape in shapes]
        + [
            jax.ShapeDtypeStruct((t, width), jnp.bfloat16),
            jax.ShapeDtypeStruct((t, 1), f32),
            jax.ShapeDtypeStruct((nb * t, 1), jnp.int32),
            table,
            table,
        ],
        in_specs=[pl.BlockSpec(memory_space=pltpu.SMEM)] + [VMEM] * 3 + [ANY] * n,
        out_specs=[ANY] * m + [VMEM] * (n - m + 5),
        scratch_shapes=[pltpu.VMEM(value.shape, value.dtype) for value in weights]
        + [pltpu.VMEM(shape, jnp.bfloat16) for shape in shapes[:m]]
        + [dma((n,))] + [dma, dma((nb,)), dma((nb,))] * m,
        compiler_params=params(cid),
        cost_estimate=cost(0),
    )(block_map, tokens, gain[None], jnp.tile(frequency, 4)[None], *weights)


def total_task(nr, nb, x_ref, o_ref, held, rows_held, send_one, recv_one, send_two, recv_two):
    r, b = lax.axis_index("rows"), lax.axis_index("blk")
    across = [lax.rem(b + k, nb) for k in range(1, nb)]
    along = [lax.rem(r + k, nr) for k in range(1, nr)]

    def first(other, slot):
        return pltpu.make_async_remote_copy(
            src_ref=rows_held.at[r], dst_ref=rows_held.at[slot], send_sem=send_two.at[other],
            recv_sem=recv_two.at[slot], device_id=(other, b), device_id_type=MESH,
        )

    def second(other, slot):
        return pltpu.make_async_remote_copy(
            src_ref=held.at[b], dst_ref=held.at[slot], send_sem=send_one.at[other],
            recv_sem=recv_one.at[slot], device_id=(r, other), device_id_type=MESH,
        )

    def start():
        rows_held[r] = x_ref[...]
        for other in along:
            first(other, r).start()

    def middle():
        for other in along:
            first(other, other).wait_recv()
        held[b] = jnp.sum(rows_held[...], axis=0)
        for other in across:
            second(other, b).start()

    def finish():
        for other in across:
            second(other, other).wait_recv()
        o_ref[...] = jnp.sum(held[...], axis=0)
        for other in along:
            first(other, r).wait_send()
        for other in across:
            second(other, b).wait_send()

    return start, middle, finish


def last_scatter_kernel(
    chips, nr, cuts, tile, extras, a_ref, w_ref, x_ref, inverse_ref, gain_ref, resid_ref, gain_two_ref, h1_hbm, *refs
):
    n = extras.n
    srcs, refs = refs[:n], refs[n:]
    o_ref, total_ref, dsts, refs = refs[0], refs[1], refs[2 : 2 + n], refs[2 + n :]
    sum_ref, part_ref, h1_ref, load_sem, refs = refs[0], refs[1], refs[2], refs[3], refs[4:]
    put, _, hop, finish = scatter_task(chips, cuts, tile, sum_ref, refs[:4], refs[4:10])
    start_total, middle_total, finish_total = total_task(
        nr, 2 * chips, part_ref, total_ref, *refs[10:16]
    )
    start_swaps, start_rows, middle, wait_rows, wait_swaps = extras.tasks(srcs, dsts, refs[16:])
    load, loaded = mover([(h1_hbm, h1_ref)], load_sem)
    load()
    greet(chips, True, True)
    start_swaps()
    start_rows()
    part_ref[0:1] = jnp.zeros_like(part_ref[0:1])
    part_ref[1:2] = gain_two_ref[...]
    loaded()

    def seen(rows, cols, got):
        part_ref[0:1, cols] += jnp.sum(got * h1_ref[rows, cols].astype(jnp.float32), axis=0)[None]

    for s in range(chips):
        put(s, lambda rows: a_ref.at[rows], w_ref, seen)
        if s < chips - 1:
            hop(s)
    part_ref[0:1] = part_ref[0:1] / gain_ref[...]
    start_total()
    middle()
    middle_total()
    wait_rows()
    finish()
    inverse = inverse_ref[...]
    unit = x_ref[...].astype(jnp.float32) * inverse
    o_ref[...] = resid_ref[...] + norm_backward(sum_ref[...], unit, inverse, gain_ref[...])[0]
    finish_total()
    wait_swaps()


def last_scatter(cid, a, w, x, inverse, gain, resid, gain_two, h1_all, extras, cuts=2, tile=1024):
    nr, nb = lax.axis_size("rows"), lax.axis_size("blk")
    t, width = x.shape
    pair = (2, width)
    dma, f32 = pltpu.SemaphoreType.DMA, jnp.float32
    return pl.pallas_call(
        functools.partial(last_scatter_kernel, nb // 2, nr, cuts, tile, extras),
        out_shape=[jax.ShapeDtypeStruct((t, width), f32), jax.ShapeDtypeStruct(pair, f32)]
        + extras.shapes,
        in_specs=[VMEM] * 7 + [ANY] + extras.specs,
        out_specs=[VMEM] * 2 + extras.specs,
        scratch_shapes=[
            pltpu.VMEM((t, width), f32),
            pltpu.VMEM(pair, f32),
            pltpu.VMEM(h1_all.shape, h1_all.dtype),
            dma((1,)),
        ]
        + scatter_scratch(nb // 2, cuts, t, width)
        + [pltpu.VMEM((nb,) + pair, f32), pltpu.VMEM((nr,) + pair, f32)]
        + [dma((nb,))] * 2 + [dma((nr,))] * 2
        + extras.scratch,
        compiler_params=params(cid),
        cost_estimate=cost(2 * a.shape[0] * width * w.shape[1]),
    )(a, w, x, inverse, gain[None], resid, gain_two, h1_all, *extras.operands)


def step_kernel(parts, one_array, *refs):
    count = 1 if one_array else parts
    grads, refs = refs[:count], refs[count:]
    outs = len(refs) // 2
    rule = adam_step if outs == 3 else moment_step

    def go(grad):
        wide = grad.shape[2]
        for j in range(grad.shape[0]):
            cols = slice(j * wide, (j + 1) * wide)
            gradient = grad[j].astype(jnp.float32)
            for ref, value in zip(
                refs[outs:], rule(*[ref[:, cols] for ref in refs[:outs]], gradient)
            ):
                ref[:, cols] = value

    if one_array:
        go(grads[0])
        return
    for part, grad in enumerate(grads):
        pl.when(pl.program_id(0) == part)(functools.partial(go, grad))


def step(pieces, parts, states, first=0):
    one_array = not isinstance(pieces, list)
    pieces = [pieces] if one_array else pieces
    nb = pieces[0].shape[0]
    rows, columns = states[0].shape
    tile = min(rows, 64 if parts > 1 else 32)
    span = columns // parts
    at = pl.BlockSpec((tile, span), lambda part, i: (i, part))
    block = (nb, tile, span // nb)
    if one_array:
        grads = [pl.BlockSpec(block, lambda part, i: (0, i, first + part))]
    else:
        grads = [pl.BlockSpec(block, lambda part, i: (0, i, 0))] * parts
    outs = len(states)
    return pl.pallas_call(
        functools.partial(step_kernel, parts, one_array),
        grid=(parts, rows // tile),
        in_specs=grads + [at] * outs,
        out_specs=[at] * outs,
        out_shape=[jax.ShapeDtypeStruct((rows, columns), jnp.float32)] * outs,
        compiler_params=pltpu.CompilerParams(vmem_limit_bytes=60 * MIB),
        cost_estimate=pl.CostEstimate(
            flops=0, bytes_accessed=(8 * outs + 2) * rows * columns, transcendentals=0
        ),
    )(*pieces, *states)


def after(value, *others):
    return lax.optimization_barrier((value,) + others)[0]


def over_tokens(left, right):
    return lax.dot_general(
        left, right, (((0,), (0,)), ((), ())), preferred_element_type=jnp.float32
    )


def shards(
    tokens, cotangent, lengths, block_map, gain_attend, gain_expand,
    attend_in, attend_out, expand_in, reduce_out,
    attend_in_first, attend_out_first, expand_in_first, reduce_out_first,
    attend_in_second, attend_out_second, expand_in_second, reduce_out_second,
):
    nb = lax.axis_size("blk")
    length = lengths[0]
    swap_in, swap_out, swap_red, pieces_gu, h1, inverse_one, place, cosine, sine = first(
        2, block_map, tokens[0], gain_attend,
        (attend_in, attend_out.T, reduce_out.T, expand_in), (3, 1, 1, 2), 3,
    )
    block_rows = tokens.shape[1] // 2
    row_place = (block_map[0][:, None] * block_rows + jnp.arange(block_rows)[None, :]).reshape(1, -1)
    live_place = jnp.where(row_place < length, row_place, jnp.int32(1 << 30))
    nr = lax.axis_size("rows")
    deep = nb * attend_in.shape[0]
    wide = tokens.shape[2]

    def flat(pieces):
        return pieces.reshape(deep, pieces.shape[2])

    h1_all, swap_gu, w_in, w_out, w_red = line_gather(
        3, h1,
        Extras([pieces_gu], [(flat(value), 0, deep) for value in (swap_in, swap_out, swap_red)]),
    )
    w_in, w_out, w_red = [value.reshape(wide, -1) for value in (w_in, w_out, w_red)]
    attended, q, k, v, p, g_all, x1, inverse_two, h2, w_gu = attend(
        4, h1_all, w_in, cosine, sine, place, live_place, length, cotangent[0],
        tokens[0], gain_expand, w_out, Extras([], [(flat(swap_gu), 0, deep)]),
    )
    w_gu = w_gu.reshape(wide, -1)

    def by_rows(gradient):
        return gradient.reshape(nr, nb, deep // nb, gradient.shape[1])

    grad_x1, branch, gain_two, hidden, part_gate, part_up, rows_reduce = feed_forward(
        6, h2, x1, inverse_two, gain_expand, cotangent[0], w_gu, w_red, g_all
    )
    grad_mixed, y, part_both, own_reduce, rows_gate, rows_up = attend_back(
        10, q, k, v, attended, p, cosine, sine, place, length, branch, w_out, hidden, w_red, h1_all,
        Extras([rows_reduce], [], [by_rows(part_gate), by_rows(part_up)]),
    )
    y = x1 + y
    grad_input, gains, own_gate, own_up, rows_both = last_scatter(
        11, grad_mixed, w_in, tokens[0], inverse_one, gain_attend, grad_x1, gain_two, h1_all,
        Extras([rows_gate, rows_up], [], [by_rows(part_both)]),
    )
    both = lax.all_to_all(rows_both, "blk", 0, 0, tiled=True)
    set_four = step(own_reduce, 1, (reduce_out.T, reduce_out_first.T, reduce_out_second.T))
    set_three = step([own_gate, own_up], 2, (expand_in, expand_in_first, expand_in_second))
    both = after(both, set_three[2], set_four[2])
    set_one = step(both, 3, (attend_in, attend_in_first, attend_in_second))
    set_two = step(both, 1, (attend_out_first.T, attend_out_second.T), 3)
    return (
        y.astype(jnp.bfloat16).reshape(tokens.shape),
        grad_input.reshape(tokens.shape),
        gains[0],
        gains[1],
        *set_one,
        *[value.T for value in set_two],
        *set_three,
        *[value.T for value in set_four],
    )


def solution(mesh):
    placed = (
        P("rows", "blk", None),
        P("rows", "blk", None),
        P("rows"),
        P("rows", None),
        P(),
        P(),
        P(("rows", "blk"), None),
        P(None, ("rows", "blk")),
        P(("rows", "blk"), None),
        P(None, ("rows", "blk")),
        P(("rows", "blk"), None),
        P(None, ("rows", "blk")),
        P(("rows", "blk"), None),
        P(None, ("rows", "blk")),
        P(("rows", "blk"), None),
        P(None, ("rows", "blk")),
        P(("rows", "blk"), None),
        P(None, ("rows", "blk")),
    )
    return jax.shard_map(
        shards,
        mesh=mesh,
        in_specs=placed,
        out_specs=(
            P("rows", "blk", None),
            P("rows", "blk", None),
            P(),
            P(),
            P(("rows", "blk"), None),
            P(("rows", "blk"), None),
            P(("rows", "blk"), None),
            P(None, ("rows", "blk")),
            P(None, ("rows", "blk")),
            P(("rows", "blk"), None),
            P(("rows", "blk"), None),
            P(("rows", "blk"), None),
            P(None, ("rows", "blk")),
            P(None, ("rows", "blk")),
            P(None, ("rows", "blk")),
        ),
        check_vma=False,
    )
```

```python
import functools
import math

import jax
import jax.numpy as jnp
from jax import lax
from jax.experimental import pallas as pl
from jax.experimental.pallas import tpu as pltpu
from jax.sharding import PartitionSpec as P

HEADS = 32
HEAD_DIM = 64
MESH = pl.DeviceIdType.MESH
MIB = 1 << 20

theta_base = 130000.0
norm_eps = 1e-05
neg_large = -1e30
beta_one = 0.9
beta_two = 0.95
learn_rate = 0.01
decay_rate = 0.1
adam_eps = 1e-08
step_count = 10


def line_place():
    b = lax.axis_index("blk")
    return lax.axis_index("rows"), b // 2, b % 2


def greet(chips, swaps=False, rows=False):
    r, z, c = line_place()
    barrier = pltpu.get_barrier_semaphore()
    count = 0

    def signal(row, b):
        pl.semaphore_signal(barrier, inc=1, device_id=(row, b), device_id_type=MESH)

    b, nb, nr = 2 * z + c, 2 * chips, lax.axis_size("rows")
    if rows:
        for k in range(1, nr):
            signal(lax.rem(r + k, nr), b)
        count = nr - 1
    if swaps:
        for k in range(1, nb):
            signal(r, lax.rem(b + k, nb))
        count = count + nb - 1
    else:
        signal(r, b + 1 - 2 * c)
        pl.when(z < chips - 1)(lambda: signal(r, b + 2))
        pl.when(z > 0)(lambda: signal(r, b - 2))
        count = count + 1 + (z < chips - 1).astype(jnp.int32) + (z > 0).astype(jnp.int32)
    pl.semaphore_wait(barrier, count)


def swap_task(src, dst, local, send, recv):
    r, b = lax.axis_index("rows"), lax.axis_index("blk")
    nb = src.shape[0]
    others = [lax.rem(b + k, nb) for k in range(1, nb)]

    def remote(other, slot):
        return pltpu.make_async_remote_copy(
            src_ref=src.at[other], dst_ref=dst.at[slot], send_sem=send.at[other],
            recv_sem=recv.at[slot], device_id=(r, other), device_id_type=MESH,
        )

    def start():
        for other in others:
            remote(other, b).start()
        pltpu.make_async_copy(src.at[b], dst.at[b], local).start()

    def wait():
        for other in others:
            remote(other, other).wait_recv()
        for other in others:
            remote(other, b).wait_send()
        pltpu.make_async_copy(src.at[b], dst.at[b], local).wait()

    return start, wait


def rows_copy(src, dst, send, recv, device):
    return pltpu.make_async_remote_copy(
        src_ref=src, dst_ref=dst, send_sem=send, recv_sem=recv,
        device_id=(device, lax.axis_index("blk")), device_id_type=MESH,
    )


def through(src, stage, dst, local):
    first = pltpu.make_async_copy(src, stage, local)
    second = pltpu.make_async_copy(stage, dst, local)

    def store():
        first.wait()
        second.start()

    return first.start, store, second.wait


def direct_gather(src, dst, stage, local, send, recv):
    r, nr = lax.axis_index("rows"), dst.shape[0]
    others = [lax.rem(r + k, nr) for k in range(1, nr)]
    load, store, stored = through(src, stage, dst.at[r], local)

    def start():
        for other in others:
            rows_copy(src, dst.at[r], send.at[other], recv.at[r], other).start()
        load()

    def wait():
        for other in others:
            rows_copy(src, dst.at[other], send.at[other], recv.at[other], other).wait()
        stored()

    return start, store, wait


def square_gather(src, dst, stage, local, send, recv):
    r = lax.axis_index("rows")
    half = src.shape[0] // 2
    load, store, stored = through(src, stage, dst.at[r], local)

    def near(sem, origin, device):
        return rows_copy(src, dst.at[origin], send.at[sem], recv.at[sem], device)

    def onward(sem, origin, device):
        part = dst.at[origin, pl.ds((sem - 2) * half, half)]
        return rows_copy(part, part, send.at[sem], recv.at[sem], device)

    def start():
        near(0, r, r ^ 1).start()
        near(1, r, r ^ 2).start()
        load()

    def middle():
        store()
        near(0, r ^ 1, r ^ 1).wait_recv()
        onward(2, r ^ 1, r ^ 2).start()
        near(1, r ^ 2, r ^ 2).wait_recv()
        onward(3, r ^ 2, r ^ 1).start()

    def wait():
        onward(2, r ^ 3, r ^ 2).wait_recv()
        onward(3, r ^ 3, r ^ 1).wait_recv()
        near(0, r, r ^ 1).wait_send()
        near(1, r, r ^ 2).wait_send()
        onward(2, r ^ 1, r ^ 2).wait_send()
        onward(3, r ^ 2, r ^ 1).wait_send()
        stored()

    return start, middle, wait


def direct_sum(src, dst, held, local, send, recv):
    r, nr = lax.axis_index("rows"), src.shape[0]
    others = [lax.rem(r + k, nr) for k in range(1, nr)]

    def start():
        for other in others:
            rows_copy(src.at[other], held.at[r], send.at[other], recv.at[r], other).start()
        pltpu.make_async_copy(src.at[r], held.at[r], local).start()

    def wait():
        for other in others:
            rows_copy(src.at[other], held.at[other], send.at[other], recv.at[other], other).wait()
        pltpu.make_async_copy(src.at[r], held.at[r], local).wait()

        def one(j, _):
            total = held[0, j].astype(jnp.float32)
            for slot in range(1, nr):
                total = total + held[slot, j].astype(jnp.float32)
            held[0, j] = total.astype(held.dtype)
            return 0

        lax.fori_loop(0, held.shape[1], one, 0)
        done = pltpu.make_async_copy(held.at[0], dst, local)
        done.start()
        done.wait()

    return start, lambda: None, wait


def square_sum(src, dst, held, local, send, recv):
    r = lax.axis_index("rows")
    half = src.shape[1] // 2
    parts = [(pl.ds(0, half), r ^ 1, r ^ 2), (pl.ds(half, half), r ^ 2, r ^ 1)]

    def out(i, k):
        at, one, two = parts[i]
        return rows_copy(
            src.at[one if k == 0 else r ^ 3, at], held.at[k, at], send.at[2 * i + k],
            recv.at[2 * i + k], one,
        )

    def own(i, k):
        at, one, two = parts[i]
        return pltpu.make_async_copy(
            src.at[r if k == 0 else two, at], held.at[2 + k, at], local.at[2 * i + k]
        )

    def onward(i):
        at, one, two = parts[i]
        return rows_copy(held.at[3, at], held.at[4, at], send.at[4 + i], recv.at[4 + i], two)

    def add(i, into, *slots):
        def one(j, _):
            j = i * half + j
            total = held[into, j].astype(jnp.float32)
            for slot in slots:
                total = total + held[slot, j].astype(jnp.float32)
            held[into, j] = total.astype(held.dtype)
            return 0

        lax.fori_loop(0, half, one, 0)

    def start():
        for i in range(2):
            for k in (1, 0):
                out(i, k).start()
                own(i, k).start()

    def start_as(make):
        for i, k in ((0, 1), (1, 1), (0, 0), (1, 0)):
            make((parts[i][1] if k == 0 else r ^ 3), i)
            out(i, k).start()
        for i, k in ((0, 1), (1, 1), (0, 0), (1, 0)):
            make((r if k == 0 else parts[i][2]), i)
            own(i, k).start()

    start.as_made = start_as

    def middle():
        for i in range(2):
            out(i, 1).wait_recv()
            own(i, 1).wait()
            add(i, 3, 1)
            onward(i).start()

    def wait():
        for i in range(2):
            out(i, 0).wait_recv()
            own(i, 0).wait()
            onward(i).wait_recv()
            add(i, 2, 0, 4)
        done = pltpu.make_async_copy(held.at[2], dst, local.at[0])
        done.start()
        done.wait()
        for i in range(2):
            out(i, 0).wait_send()
            out(i, 1).wait_send()
            onward(i).wait_send()

    return start, middle, wait


class Extras:
    def __init__(self, swaps=(), gathers=(), scatters=()):
        nr, nb = lax.axis_size("rows"), lax.axis_size("blk")
        dma = pltpu.SemaphoreType.DMA
        self.swaps, self.gathers, self.scatters = len(swaps), [g[1:] for g in gathers], len(scatters)
        self.operands = [*swaps, *[g[0] for g in gathers], *scatters]
        self.n = len(self.operands)
        self.rows = bool(gathers) or bool(scatters)
        self.specs = [ANY] * self.n
        self.shapes = [like(value) for value in swaps]
        self.scratch = [dma, dma((nb,)), dma((nb,))] * len(swaps)
        self.square = nr == 4
        sems = 6 if self.square else nr
        for value, _, count in gathers:
            self.shapes.append(jax.ShapeDtypeStruct((nr, count, value.shape[1]), value.dtype))
            self.scratch += [pltpu.VMEM((count, value.shape[1]), value.dtype)]
            self.scratch += [dma, dma((sems,)), dma((sems,))]
        for value in scatters:
            self.shapes.append(jax.ShapeDtypeStruct(value.shape[1:], value.dtype))
            slots = 5 if self.square else nr
            local = dma((4,)) if self.square else dma
            self.scratch += [pltpu.VMEM((slots,) + value.shape[1:], value.dtype)]
            self.scratch += [local, dma((sems,)), dma((sems,))]

    def tasks(self, srcs, dsts, scratch):
        scratch = list(scratch)
        swaps, rows = [], []
        for i, (src, dst) in enumerate(zip(srcs, dsts)):
            if i < self.swaps:
                swaps.append(swap_task(src, dst, *scratch[:3]))
                scratch = scratch[3:]
            elif i < self.swaps + len(self.gathers):
                first, count = self.gathers[i - self.swaps]
                task = square_gather if self.square else direct_gather
                rows.append(task(src.at[pl.ds(first, count)], dst, *scratch[:4]))
                scratch = scratch[4:]
            else:
                task = square_sum if self.square else direct_sum
                rows.append(task(src, dst, *scratch[:4]))
                scratch = scratch[4:]

        def start_swaps():
            for start, _ in swaps:
                start()

        def start_rows():
            for start, _, _ in rows:
                start()

        def middle():
            for _, one, _ in rows:
                one()

        def wait_rows():
            for _, _, one in rows:
                one()

        def wait_swaps():
            for _, one in swaps:
                one()

        return start_swaps, start_rows, middle, wait_rows, wait_swaps


def like(value):
    return jax.ShapeDtypeStruct(value.shape, value.dtype)


ANY = pl.BlockSpec(memory_space=pl.ANY)
VMEM = pl.BlockSpec(memory_space=pltpu.VMEM)


def params(cid):
    return pltpu.CompilerParams(
        collective_id=cid, has_side_effects=True, vmem_limit_bytes=60 * MIB
    )


def cost(flops):
    return pl.CostEstimate(flops=flops, bytes_accessed=150_000_000, transcendentals=0)


def mover(pairs, sem):
    copies = [pltpu.make_async_copy(a, b, sem.at[i]) for i, (a, b) in enumerate(pairs)]

    def start(*which):
        for i in which or range(len(copies)):
            copies[i].start()

    def wait(*which):
        for i in which or range(len(copies)):
            copies[i].wait()

    return start, wait


def gather_task(chips, cuts, x_ref, o_ref, sems):
    copy_sem, send_up, send_down, send_side, recv = sems
    r, z, c = line_place()
    t = x_ref.shape[0]
    h = t // cuts
    up, down, side = (r, 2 * (z + 1) + c), (r, 2 * (z - 1) + c), (r, 2 * z + 1 - c)
    has_up, has_down = z < chips - 1, z > 0
    mine = 2 * z + c

    def piece(j, q):
        return o_ref.at[pl.ds(pl.multiple_of(j * t + q * h, h), h)]

    def remote(src, j, q, sem, dev):
        return pltpu.make_async_remote_copy(
            src_ref=src, dst_ref=piece(j, q), send_sem=sem.at[j, q], recv_sem=recv.at[j, q],
            device_id=dev, device_id_type=MESH,
        )

    def local():
        whole = o_ref.at[pl.ds(pl.multiple_of(mine * t, t), t)]
        return pltpu.make_async_copy(x_ref, whole, copy_sem)

    def start():
        for q in range(cuts):
            from_here = x_ref.at[pl.ds(q * h, h)]
            pl.when(has_up)(lambda: remote(from_here, mine, q, send_up, up).start())
            pl.when(has_down)(lambda: remote(from_here, mine, q, send_down, down).start())
            remote(from_here, mine, q, send_side, side).start()
        local().start()

    def hop(k):
        for q in range(cuts):
            @pl.when(z - k >= 0)
            def _():
                j = 2 * (z - k) + c
                remote(piece(j, q), j, q, send_up, up).wait_recv()
                pl.when(has_up)(lambda: remote(piece(j, q), j, q, send_up, up).start())
                remote(piece(j, q), j, q, send_side, side).start()

            @pl.when(z + k < chips)
            def _():
                j = 2 * (z + k) + c
                remote(piece(j, q), j, q, send_down, down).wait_recv()
                pl.when(has_down)(lambda: remote(piece(j, q), j, q, send_down, down).start())
                remote(piece(j, q), j, q, send_side, side).start()

    def from_side(y):
        for q in range(cuts):
            j = 2 * y + 1 - c
            remote(piece(j, q), j, q, send_side, side).wait_recv()

    def finish():
        for y in range(chips):
            j = 2 * y + c
            for q in range(cuts):
                pl.when(has_up & (z >= y))(
                    lambda: remote(piece(j, q), j, q, send_up, up).wait_send()
                )
                pl.when(has_down & (z <= y))(
                    lambda: remote(piece(j, q), j, q, send_down, down).wait_send()
                )
                remote(piece(j, q), j, q, send_side, side).wait_send()

    return start, hop, from_side, local, finish


def gather_sems(nb, cuts):
    return [pltpu.SemaphoreType.DMA] + [pltpu.SemaphoreType.DMA((nb, cuts))] * 4


def arrival_order(chips):
    table = []
    for z in range(chips):
        row = [z]
        for k in range(1, chips):
            row += [y for y in (z - k, z + k) if 0 <= y < chips]
        table.append(row)
    return table


def need_order(chips):
    table = []
    for z in range(chips):
        need = {
            y: (chips - 1 + z - y) if y > z else (chips - 1 - z + y)
            for y in range(chips) if y != z
        }
        table.append(sorted(need, key=lambda y: need[y]) + [z])
    return table


def pick(table, z, k):
    out = 0
    for at, row in enumerate(table):
        for step, block in enumerate(row):
            out = out + jnp.where((z == at) & (k == step), block, 0)
    return out


def scatter_task(chips, cuts, tile, o_ref, bufs, sems):
    mine, away, side_buf, line_buf = bufs
    send_side, recv_side, send_up, recv_up, send_down, recv_down = sems
    r, z, c = line_place()
    t, width = o_ref.shape
    low, f32 = away.dtype, jnp.float32
    up, down, side = (r, 2 * (z + 1) + c), (r, 2 * (z - 1) + c), (r, 2 * z + 1 - c)
    has_up, has_down = z < chips - 1, z > 0
    h = t // cuts
    table = need_order(chips)

    def remote(src, dst, y, q, send, recv, dev):
        return pltpu.make_async_remote_copy(
            src_ref=src.at[y, pl.ds(q * h, h)], dst_ref=dst.at[y, pl.ds(q * h, h)],
            send_sem=send.at[y, q], recv_sem=recv.at[y, q], device_id=dev, device_id_type=MESH,
        )

    def to_side(y, q):
        return remote(away, side_buf, y, q, send_side, recv_side, side)

    def along(y, slot, q, send, recv, dev):
        return pltpu.make_async_remote_copy(
            src_ref=mine.at[y, pl.ds(q * h, h)], dst_ref=line_buf.at[slot, pl.ds(q * h, h)],
            send_sem=send.at[y, q], recv_sem=recv.at[y, q], device_id=dev, device_id_type=MESH,
        )

    def to_up(y, q):
        return along(y, y, q, send_up, recv_up, up)

    def to_down(y, q):
        return along(y, jnp.where(y == z - 1, chips, y), q, send_down, recv_down, down)

    def from_up(y, q):
        return along(y, jnp.where(y == z, chips, y), q, send_down, recv_down, down)

    def rows(q):
        return pl.ds(q * h, h)

    def total(y, q):
        to_side(y, q).wait_recv()
        return mine[y, rows(q)].astype(f32) + side_buf[y, rows(q)].astype(f32)

    def put(s, rows_of, w_ref, seen=None):
        put_at(pick(table, z, s), rows_of, w_ref, seen)

    def put_at(y, rows_of, w_ref, seen=None):
        block = pl.ds(pl.multiple_of(2 * y * t, 2 * t), 2 * t)
        a = rows_of(block)

        def one(i, _):
            cols = pl.ds(pl.multiple_of(i * tile, tile), tile)
            got = lax.dot_general(
                a[...], w_ref[cols], (((1,), (1,)), ((), ())), preferred_element_type=f32
            )
            if seen is not None:
                seen(block, cols, got)
            got = got.astype(low)

            @pl.when(c == 0)
            def _():
                mine[y, :, cols] = got[:t]
                away[y, :, cols] = got[t:]

            @pl.when(c == 1)
            def _():
                mine[y, :, cols] = got[t:]
                away[y, :, cols] = got[:t]

            return 0

        lax.fori_loop(0, width // tile, one, 0)
        for q in range(cuts):
            to_side(y, q).start()

    def hop(s):
        hop_up(chips - 1 + z - s)
        hop_down(s - (chips - 1) + z)

    def hop_up(y):
        for q in range(cuts):
            @pl.when((y > z) & (y <= chips - 1))
            def _():
                now = total(y, q)

                @pl.when(has_down)
                def _():
                    to_up(y, q).wait_recv()
                    mine[y, rows(q)] = (now + line_buf[y, rows(q)].astype(f32)).astype(low)

                @pl.when(z == 0)
                def _():
                    mine[y, rows(q)] = now.astype(low)

                to_up(y, q).start()

    def hop_down(w):
        for q in range(cuts):
            @pl.when((w >= 0) & (w < z))
            def _():
                now = total(w, q)

                @pl.when(has_up)
                def _():
                    from_up(w, q).wait_recv()
                    mine[w, rows(q)] = (now + line_buf[w, rows(q)].astype(f32)).astype(low)

                @pl.when(z == chips - 1)
                def _():
                    mine[w, rows(q)] = now.astype(low)

                to_down(w, q).start()

    def finish():
        for q in range(cuts):
            o_ref[rows(q)] = total(z, q)
        for q in range(cuts):
            @pl.when(has_down)
            def _():
                to_up(z, q).wait_recv()
                o_ref[rows(q)] += line_buf[z, rows(q)].astype(f32)

            @pl.when(has_up)
            def _():
                from_up(z, q).wait_recv()
                o_ref[rows(q)] += line_buf[chips, rows(q)].astype(f32)

        for y in range(chips):
            for q in range(cuts):
                to_side(y, q).wait_send()
                pl.when(y > z)(lambda: to_up(y, q).wait_send())
                pl.when(y < z)(lambda: to_down(y, q).wait_send())

    return put, (put_at, hop_up, hop_down), hop, finish


def scatter_scratch(chips, cuts, t, width):
    return (
        [pltpu.VMEM((chips, t, width), jnp.bfloat16)] * 3
        + [pltpu.VMEM((chips + 1, t, width), jnp.bfloat16)]
        + [pltpu.SemaphoreType.DMA((chips, cuts))] * 6
    )


def feed_forward_kernel(
    chips, cuts, tile, h2_here, x1_ref, inverse_ref, gain_ref, cotangent_ref, w_hbm, red_hbm, g_hbm,
    grad_out, low_out, gain_out, hidden_out, gate_out, up_out, reduce_out,
    h2_ref, hidden_ref, grad_ref, w_ref, red_ref, g_ref, dw_red, dw_ref, red_held,
    load_sem, save_sem, dw_sem, red_local, red_send, red_recv, *refs
):
    begin, pass_on, from_side, local, sent = gather_task(chips, cuts, h2_here, h2_ref, refs[:5])
    _, (put_at, hop_up, hop_down), _, finish = scatter_task(chips, cuts, tile, grad_out, refs[5:9], refs[9:])
    task = square_sum if dw_red.shape[0] == 4 else direct_sum
    start_red, middle_red, wait_red = task(
        dw_red, reduce_out, red_held, red_local, red_send, red_recv
    )
    load, loaded = mover([(w_hbm, w_ref), (g_hbm, g_ref), (red_hbm, red_ref)], load_sem)
    r, z, c = line_place()
    t, width = h2_here.shape
    units = hidden_ref.shape[1]
    span = min(512, units)
    f32, low = jnp.float32, jnp.bfloat16
    over_rows = (((0,), (0,)), ((), ()))
    load()
    greet(chips, False, True)
    begin()

    def rows_of(y):
        return pl.ds(pl.multiple_of(y * 2 * t, 2 * t), 2 * t)

    def save(y):
        return pltpu.make_async_copy(
            hidden_ref.at[rows_of(y)], hidden_out.at[rows_of(y)], save_sem.at[y]
        )

    def columns(i):
        at, more = i * span, units + i * span
        return pl.ds(pl.multiple_of(at, span), span), pl.ds(pl.multiple_of(more, span), span)

    def forward(y):
        rows = rows_of(y)

        def one(i, _):
            cols, more = columns(i)
            gate = jnp.dot(h2_ref[rows], w_ref[:, cols], preferred_element_type=f32)
            up = jnp.dot(h2_ref[rows], w_ref[:, more], preferred_element_type=f32)
            sigmoid = jax.nn.sigmoid(gate)
            silu = gate * sigmoid
            hidden_ref[rows, cols] = (silu * up).astype(low)
            grad_ref[rows, cols] = (up * (sigmoid * (1.0 + gate * (1.0 - sigmoid)))).astype(low)
            grad_ref[rows, more] = silu.astype(low)
            return 0

        lax.fori_loop(0, units // span, one, 0)
        save(y).start()

    def backward(rows):
        def one(i, _):
            cols, more = columns(i)
            grad = jnp.dot(g_ref[rows], red_ref[:, cols], preferred_element_type=f32)
            grad_ref[rows, cols] = (grad * grad_ref[rows, cols].astype(f32)).astype(low)
            grad_ref[rows, more] = (grad * grad_ref[rows, more].astype(f32)).astype(low)
            return 0

        lax.fori_loop(0, units // span, one, 0)
        return grad_ref.at[rows]

    from_side(z)
    local().wait()
    loaded(0)
    forward(z)
    loaded(1, 2)
    put_at(z, backward, w_ref)
    deep = 256
    turns = width // deep
    piece = dw_red.shape[2]
    run = dw_red.shape[1] * piece

    def reduce_grad(i, _):
        at = pl.ds(pl.multiple_of(i * deep, deep), deep)
        got = lax.dot_general(g_ref[:, at], hidden_ref[...], over_rows, preferred_element_type=f32)
        first = i * deep
        dw_red[first // run, pl.ds(lax.rem(first, run) // piece, deep // piece)] = (
            got.astype(low).reshape(deep // piece, piece, units)
        )
        return 0

    def make_reduce_grad():
        if dw_red.shape[0] == 4:
            tiles = turns // 8

            def make(slot, half):
                first = (slot * 2 + half) * tiles
                lax.fori_loop(first, first + tiles, reduce_grad, 0)

            start_red.as_made(make)
        else:
            lax.fori_loop(0, turns, reduce_grad, 0)
            start_red()

    def save_dw(i, half):
        at = pl.ds(pl.multiple_of(i * deep, deep), deep)
        return pltpu.make_async_copy(
            dw_ref.at[lax.rem(i, 2), half], (gate_out, up_out)[half].at[at], dw_sem.at[lax.rem(i, 2), half]
        )

    def expand_grad(i, _):
        at = pl.ds(pl.multiple_of(i * deep, deep), deep)
        for half in range(2):
            pl.when(i >= 2)(lambda: save_dw(i - 2, half).wait())
            dw_ref[lax.rem(i, 2), half] = lax.dot_general(
                h2_ref[:, at], grad_ref[:, half * units : (half + 1) * units], over_rows,
                preferred_element_type=f32,
            ).astype(low)
            save_dw(i, half).start()
        return 0

    last = 2 * chips - 3
    done = 0
    for turn in range(1, last + 1):
        if turn < chips:
            pass_on(turn)

            @pl.when(z - turn >= 0)
            def _():
                from_side(z - turn)
                forward(z - turn)
                put_at(z - turn, backward, w_ref)

            @pl.when(z + turn < chips)
            def _():
                from_side(z + turn)
                forward(z + turn)
                put_at(z + turn, backward, w_ref)

        hop_up(turn - z)
        hop_down(2 * (chips - 1) - z - turn)
        if turn == chips - 1:
            make_reduce_grad()
        elif turn >= chips:
            until = turns * (turn - chips + 1) // (last - chips + 1)
            lax.fori_loop(done, until, expand_grad, 0)
            done = until
    middle_red()
    finish()
    inverse = inverse_ref[...]
    middle_grad, gain = norm_backward(grad_out[...], x1_ref[...] * inverse, inverse, gain_ref[...])
    grad_x1 = cotangent_ref[...].astype(f32) + middle_grad
    grad_out[...] = grad_x1
    low_out[...] = grad_x1.astype(low)
    gain_out[...] = gain[None]
    wait_red()
    sent()
    for y in range(chips):
        save(y).wait()
    for i in range(max(0, turns - 2), turns):
        for half in range(2):
            save_dw(i, half).wait()


def feed_forward(
    cid, h2, x1, inverse, gain, cotangent, w_gu, w_red, g_all, cuts=2, tile=1024
):
    nr, nb = lax.axis_size("rows"), lax.axis_size("blk")
    seq, width = g_all.shape
    both = w_gu.shape[1]
    units = both // 2
    t = seq // nb
    piece = width // (nr * nb)
    dma, f32, bf16 = pltpu.SemaphoreType.DMA, jnp.float32, jnp.bfloat16
    half = jax.ShapeDtypeStruct((width, units), bf16)
    slots, sems = (5, 6) if nr == 4 else (nr, nr)
    return pl.pallas_call(
        functools.partial(feed_forward_kernel, nb // 2, cuts, tile),
        out_shape=[
            jax.ShapeDtypeStruct((t, width), f32),
            jax.ShapeDtypeStruct((t, width), bf16),
            jax.ShapeDtypeStruct((1, width), f32),
            jax.ShapeDtypeStruct((seq, units), bf16),
            half,
            half,
            jax.ShapeDtypeStruct((nb, piece, units), bf16),
        ],
        in_specs=[VMEM] * 5 + [ANY] * 3,
        out_specs=[VMEM] * 3 + [ANY] * 4,
        scratch_shapes=[
            pltpu.VMEM((seq, width), bf16),
            pltpu.VMEM((seq, units), bf16),
            pltpu.VMEM((seq, both), bf16),
            pltpu.VMEM((width, both), bf16),
            pltpu.VMEM((width, units), bf16),
            pltpu.VMEM((seq, width), bf16),
            pltpu.VMEM((nr, nb, piece, units), bf16),
            pltpu.VMEM((2, 2, 256, units), bf16),
            pltpu.VMEM((slots, nb, piece, units), bf16),
            dma((3,)),
            dma((nb // 2,)),
            dma((2, 2)),
            dma((4,)) if nr == 4 else dma,
            dma((sems,)),
            dma((sems,)),
        ]
        + gather_sems(nb, cuts)
        + scatter_scratch(nb // 2, cuts, t, width),
        compiler_params=params(cid),
        cost_estimate=cost(9 * seq * width * both),
    )(h2, x1, inverse, gain[None], cotangent, w_gu, w_red, g_all)


def attend_out_kernel(chips, cuts, tile, extras, a_ref, w_ref, x_ref, gain_ref, *refs):
    n = extras.n
    srcs, (x1_ref, inverse_ref, h2_ref), dsts, refs = (
        refs[:n], refs[n : n + 3], refs[3 + n : 3 + 2 * n], refs[3 + 2 * n :],
    )
    put, _, hop, finish = scatter_task(chips, cuts, tile, x1_ref, refs[:4], refs[4:10])
    start_swaps, start_rows, middle, wait_rows, wait_swaps = extras.tasks(srcs, dsts, refs[10:])
    greet(chips, False, extras.rows)
    start_rows()
    for s in range(chips):
        put(s, lambda rows: a_ref.at[rows], w_ref)
        if s < chips - 1:
            hop(s)
    middle()
    finish()
    x1 = x_ref[...].astype(jnp.float32) + x1_ref[...]
    x1_ref[...] = x1
    _, inverse_ref[...], h2_ref[...] = norm_forward(x1, gain_ref[...])
    wait_rows()


def norm_forward(values, gain_vector):
    inverse = lax.rsqrt(jnp.mean(values * values, axis=-1, keepdims=True) + norm_eps)
    unit_values = values * inverse
    return (unit_values, inverse, (unit_values * gain_vector).astype(jnp.bfloat16))


def norm_backward(grad_normed, unit_values, inverse, gain_vector):
    grad_unit = grad_normed * gain_vector
    grad_values = inverse * (
        grad_unit - unit_values * jnp.mean(grad_unit * unit_values, axis=-1, keepdims=True)
    )
    return (grad_values, jnp.sum(grad_normed * unit_values, axis=0))


def contract_last(left, right):
    return lax.dot_general(
        left, right, (((1,), (1,)), ((), ())), preferred_element_type=jnp.float32
    )


def adam_step(master, moment_one, moment_two, gradient):
    moment_one = beta_one * moment_one + (1.0 - beta_one) * gradient
    moment_two = beta_two * moment_two + (1.0 - beta_two) * gradient * gradient
    update = (
        moment_one
        / (1.0 - beta_one**step_count)
        / (jnp.sqrt(moment_two / (1.0 - beta_two**step_count)) + adam_eps)
    )
    return (master - learn_rate * (update + decay_rate * master), moment_one, moment_two)


def moment_step(moment_one, moment_two, gradient):
    moment_one = beta_one * moment_one + (1.0 - beta_one) * gradient
    moment_two = beta_two * moment_two + (1.0 - beta_two) * gradient * gradient
    return (moment_one, moment_two)


def once(*shape):
    return pl.BlockSpec(shape, lambda i: (0,) * len(shape), pipeline_mode=pl.Buffered(1))


def partner(values):
    width = values.shape[1]
    half = HEAD_DIM // 2
    feature = lax.broadcasted_iota(jnp.int32, values.shape, 1) % HEAD_DIM
    return jnp.where(
        feature < half, pltpu.roll(values, width - half, 1), pltpu.roll(values, half, 1)
    )


def spread_table(table, width):
    return jnp.concatenate([table] * (width // table.shape[1]), axis=1)


def head_lanes(shape):
    return lax.broadcasted_iota(jnp.int32, shape, 1) // HEAD_DIM


def attend_kernel(
    chips, cuts, tile_o, extras, h1_hbm, w_hbm, cos_ref, sin_ref, q_place, k_place, length_ref, g_ref,
    x_ref, gain_ref, w_out_ref, *refs
):
    n = extras.n
    srcs, refs = refs[:n], refs[n:]
    (o_ref, q_ref, k_ref, v_ref, p_out, g_all, x1_ref, inverse_ref, h2_ref), refs = refs[:9], refs[9:]
    dsts, (h1_ref, w_ref, p_ref, load_sem, p_sem), refs = refs[:n], refs[n : n + 5], refs[n + 5 :]
    load, loaded = mover([(w_hbm, w_ref), (h1_hbm, h1_ref)], load_sem)
    begin, pass_on, from_side, local, sent = gather_task(chips, cuts, g_ref, g_all, refs[:5])
    put, _, hop, finish = scatter_task(chips, cuts, tile_o, x1_ref, refs[5:9], refs[9:15])
    start_swaps, start_rows, middle, wait_rows, wait_swaps = extras.tasks(srcs, dsts, refs[15:])
    step, steps = pl.program_id(0), pl.num_programs(0)
    seq, width = o_ref.shape
    tile = seq // chips
    f32, bf16 = jnp.float32, jnp.bfloat16
    table = need_order(chips)
    _, z, _ = line_place()

    @pl.when(step == 0)
    def _():
        load()
        greet(chips, False, extras.rows)
        begin()
        start_rows()
        loaded()

        def one(i, _):
            rows = pl.ds(pl.multiple_of(i * tile, tile), tile)
            mixed = jnp.dot(h1_ref[rows], w_ref[...], preferred_element_type=f32)
            cosine, sine = spread_table(cos_ref[rows], width), spread_table(sin_ref[rows], width)
            for at, ref in enumerate((q_ref, k_ref)):
                got = mixed[:, at * width : (at + 1) * width]
                ref[rows] = (got * cosine + partner(got) * sine).astype(bf16)
            v_ref[rows] = mixed[:, 2 * width :].astype(bf16)
            return 0

        lax.fori_loop(0, steps, one, 0)

    pl.when(step == steps - 1)(middle)

    @pl.when(step > 0)
    def _():
        pass_on(step)

    def rows_at(s):
        return pl.ds(pl.multiple_of(pick(table, z, s) * tile, tile), tile)

    def save(s):
        slot = lax.rem(s, 2)
        return pltpu.make_async_copy(p_ref.at[slot], p_out.at[:, rows_at(s)], p_sem.at[slot])

    pl.when(step >= 2)(lambda: save(step - 2).wait())
    rows = rows_at(step)
    queries = q_ref[rows] * jnp.asarray(1.0 / math.sqrt(HEAD_DIM), bf16)
    lanes = head_lanes((tile, width))
    place = q_place[rows]
    allowed = k_place[...] <= place
    out = jnp.zeros((tile, width), f32)
    for head in range(width // HEAD_DIM):
        here = lanes == head
        one_head = jnp.where(here, queries, jnp.zeros((), bf16))
        scores = lax.dot_general(
            one_head, k_ref[...], (((1,), (1,)), ((), ())), preferred_element_type=f32
        )
        scores = jnp.where(allowed, scores, neg_large)
        weights = jnp.exp(scores - jnp.max(scores, axis=-1, keepdims=True))
        weights = weights * (1.0 / jnp.sum(weights, axis=-1, keepdims=True))
        low = weights.astype(bf16)
        p_ref[lax.rem(step, 2), head] = low
        out = jnp.where(here, jnp.dot(low, v_ref[...], preferred_element_type=f32), out)
    save(step).start()
    o_ref[rows] = jnp.where(place < length_ref[0], out, 0.0).astype(bf16)
    put(step, lambda rows: o_ref.at[rows], w_out_ref)
    pl.when(step < steps - 1)(lambda: hop(step))

    @pl.when(step == steps - 1)
    def _():
        finish()
        x1 = x_ref[...].astype(f32) + x1_ref[...]
        x1_ref[...] = x1
        _, inverse_ref[...], h2_ref[...] = norm_forward(x1, gain_ref[...])
        for s in range(max(0, chips - 2), chips):
            save(s).wait()
        local().wait()
        for y in range(chips):
            from_side(y)
        sent()
        wait_rows()


def attend(
    cid, h1_all, w_in, cosine, sine, place, live_place, length, g, x, gain, w_out, extras, cuts=2, tile_o=1024
):
    seq, wide = h1_all.shape
    width = w_in.shape[1] // 3
    heads = width // HEAD_DIM
    nb = lax.axis_size("blk")
    chips = nb // 2
    tile = seq // chips
    t = x.shape[0]
    full = jax.ShapeDtypeStruct((seq, width), jnp.bfloat16)
    return pl.pallas_call(
        functools.partial(attend_kernel, chips, cuts, tile_o, extras),
        grid=(chips,),
        in_specs=[
            ANY, ANY, once(seq, 2 * HEAD_DIM), once(seq, 2 * HEAD_DIM), once(seq, 1), once(1, seq),
            pl.BlockSpec(memory_space=pltpu.SMEM),
            once(*g.shape), once(t, wide), once(1, wide), once(wide, width),
        ]
        + extras.specs,
        out_specs=[once(seq, width)] * 4
        + [ANY, ANY, once(t, wide), once(t, 1), once(t, wide)]
        + extras.specs,
        out_shape=[full] * 4
        + [
            jax.ShapeDtypeStruct((heads, seq, seq), jnp.bfloat16),
            jax.ShapeDtypeStruct((seq, g.shape[1]), g.dtype),
            jax.ShapeDtypeStruct((t, wide), jnp.float32),
            jax.ShapeDtypeStruct((t, 1), jnp.float32),
            jax.ShapeDtypeStruct((t, wide), jnp.bfloat16),
        ]
        + extras.shapes,
        scratch_shapes=[
            pltpu.VMEM(h1_all.shape, h1_all.dtype),
            pltpu.VMEM(w_in.shape, w_in.dtype),
            pltpu.VMEM((2, heads, tile, seq), jnp.bfloat16),
            pltpu.SemaphoreType.DMA((2,)),
            pltpu.SemaphoreType.DMA((2,)),
        ]
        + gather_sems(nb, cuts)
        + scatter_scratch(chips, cuts, t, wide)
        + extras.scratch,
        compiler_params=params(cid),
        cost_estimate=cost(4 * seq * seq * width + 6 * seq * wide * width),
    )(
        h1_all, w_in, cosine, sine, place, live_place, length.reshape(1), g, x, gain[None], w_out,
        *extras.operands,
    )


def attend_back_kernel(
    chips, cuts, tile_y, extras, q_ref, k_ref, v_ref, o_all, cos_ref, sin_ref, q_place, length_ref, x_ref,
    w_out_ref, p_hbm, hidden_hbm, red_hbm, h1_hbm, *refs
):
    n = extras.n
    srcs, (mixed_ref, y_ref, dw_ref), dsts = refs[:n], refs[n : n + 3], refs[n + 3 : 2 * n + 3]
    refs = refs[2 * n + 3 :]
    (
        branch_ref, p_ref, ds_ref, qm_ref, gm_ref, dk_acc, dv_acc, hidden_ref, red_ref, h1_ref, load_sem, p_sem,
    ), refs = refs[:12], refs[12:]
    begin, pass_on, from_side, local, sent = gather_task(chips, cuts, x_ref, branch_ref, refs[:5])
    put, _, hop, finish = scatter_task(chips, cuts, tile_y, y_ref, refs[5:9], refs[9:15])
    start_swaps, start_rows, middle, wait_rows, wait_swaps = extras.tasks(srcs, dsts, refs[15:])
    one_buffer = h1_ref.shape != branch_ref.shape
    h1_ref = branch_ref if one_buffer else h1_ref
    load, loaded = mover([(red_hbm, red_ref), (hidden_hbm, hidden_ref), (h1_hbm, h1_ref)], load_sem)
    step, steps = pl.program_id(0), pl.num_programs(0)
    seq, width = q_ref.shape
    tile = seq // chips
    f32, bf16 = jnp.float32, jnp.bfloat16
    factor = 1.0 / math.sqrt(HEAD_DIM)
    over_rows = (((0,), (0,)), ((), ()))
    table = arrival_order(chips)
    _, z, _ = line_place()

    def rows_at(s):
        return pl.ds(pl.multiple_of(pick(table, z, s) * tile, tile), tile)

    def p_load(s):
        slot = lax.rem(s, 2)
        return pltpu.make_async_copy(p_hbm.at[:, rows_at(s)], p_ref.at[slot], p_sem.at[slot])

    @pl.when(step == 0)
    def _():
        p_load(step).start()
        load(0, 1)
        if not one_buffer:
            load(2)
        greet(chips, True, extras.rows)
        begin()
        start_rows()
        start_swaps()
        dk_acc[...] = jnp.zeros_like(dk_acc)
        dv_acc[...] = jnp.zeros_like(dv_acc)
        loaded(0, 1)
        local().wait()

    pl.when(step < steps - 1)(lambda: p_load(step + 1).start())
    put(step, lambda rows: hidden_ref.at[rows], red_ref)
    pl.when(step == 0)(lambda: hop(step))

    @pl.when(step > 0)
    def _():
        pass_on(step)

    pl.when(step == steps - 1)(middle)
    from_side(pick(table, z, step))
    rows = rows_at(step)
    lanes = head_lanes((tile, width))
    nothing = jnp.zeros((), bf16)
    grad = jnp.dot(branch_ref[rows], w_out_ref[...], preferred_element_type=f32).astype(bf16)
    grad = jnp.where(q_place[rows] < length_ref[0], grad, nothing)
    both = grad.astype(f32) * o_all[rows].astype(f32)
    queries = q_ref[rows]
    grad_q = jnp.zeros((tile, width), f32)
    p_load(step).wait()
    low = p_ref.at[lax.rem(step, 2)]
    heads = width // HEAD_DIM
    for head in range(heads):
        here = lanes == head
        block = pl.ds(head * tile, tile)
        delta = jnp.sum(jnp.where(here, both, 0.0), axis=-1, keepdims=True)
        one_grad = jnp.where(here, grad, nothing)
        gm_ref[block] = one_grad
        qm_ref[block] = jnp.where(here, queries, nothing)
        grad_p = lax.dot_general(
            one_grad, v_ref[...], (((1,), (1,)), ((), ())), preferred_element_type=f32
        )
        grad_s = (low[head].astype(f32) * (grad_p - delta)).astype(bf16)
        ds_ref[block] = grad_s
        grad_q = jnp.where(here, jnp.dot(grad_s, k_ref[...], preferred_element_type=f32), grad_q)
    dv_acc[...] += lax.dot_general(
        low[...].reshape(heads * tile, seq), gm_ref[...], over_rows, preferred_element_type=f32
    )
    dk_acc[...] += lax.dot_general(ds_ref[...], qm_ref[...], over_rows, preferred_element_type=f32)

    def back(value, cosine, sine):
        value = (value * factor).astype(bf16).astype(f32)
        cosine, sine = spread_table(cosine, width), spread_table(sine, width)
        return (value * cosine - partner(value) * sine).astype(bf16)

    mixed_ref[rows, :width] = back(grad_q, cos_ref[rows], sin_ref[rows])
    pl.when((step > 0) & (step < steps - 1))(lambda: hop(step))

    @pl.when(step == steps - 1)
    def _():
        mixed_ref[:, width : 2 * width] = back(dk_acc[...], cos_ref[...], sin_ref[...])
        mixed_ref[:, 2 * width :] = dv_acc[...].astype(bf16)
        deep = 256

        def out_grad(i, _):
            at = pl.ds(pl.multiple_of(i * deep, deep), deep)
            dw_ref[at, 3 * width :] = lax.dot_general(
                branch_ref[:, at], o_all[...], over_rows, preferred_element_type=f32
            ).astype(bf16)
            return 0

        def in_grad(i, _):
            at = pl.ds(pl.multiple_of(i * deep, deep), deep)
            dw_ref[at, : 3 * width] = lax.dot_general(
                h1_ref[:, at], mixed_ref[...], over_rows, preferred_element_type=f32
            ).astype(bf16)
            return 0

        turns = dw_ref.shape[0] // deep
        lax.fori_loop(0, turns, out_grad, 0)
        if one_buffer:
            sent()
            load(2)
        loaded(2)
        lax.fori_loop(0, turns, in_grad, 0)
        wait_rows()
        finish()
        if not one_buffer:
            sent()
        wait_swaps()


def attend_back(
    cid, q, k, v, o, p, cosine, sine, place, length, branch, w_out, hidden, w_red, h1_all, extras, cuts=2
):
    seq, width = q.shape
    heads = width // HEAD_DIM
    nb = lax.axis_size("blk")
    chips = nb // 2
    tile = seq // chips
    wide, units = w_red.shape
    t = seq // nb
    full = once(seq, width)
    f32, bf16 = jnp.float32, jnp.bfloat16
    loads = (hidden, w_red, h1_all)
    dma = pltpu.SemaphoreType.DMA
    return pl.pallas_call(
        functools.partial(attend_back_kernel, chips, cuts, 1024, extras),
        grid=(chips,),
        in_specs=[
            full, full, full, full, once(seq, 2 * HEAD_DIM), once(seq, 2 * HEAD_DIM), once(seq, 1),
            pl.BlockSpec(memory_space=pltpu.SMEM), once(t, wide), once(wide, width),
        ]
        + [ANY] * 4
        + extras.specs,
        out_specs=[once(seq, 3 * width), once(t, wide), once(wide, 4 * width)] + extras.specs,
        out_shape=[
            jax.ShapeDtypeStruct((seq, 3 * width), bf16),
            jax.ShapeDtypeStruct((t, wide), f32),
            jax.ShapeDtypeStruct((wide, 4 * width), bf16),
        ]
        + extras.shapes,
        scratch_shapes=[
            pltpu.VMEM((seq, wide), bf16),
            pltpu.VMEM((2, heads, tile, seq), bf16),
            pltpu.VMEM((heads * tile, seq), bf16),
            pltpu.VMEM((heads * tile, width), bf16),
            pltpu.VMEM((heads * tile, width), bf16),
            pltpu.VMEM((seq, width), f32),
            pltpu.VMEM((seq, width), f32),
        ]
        + [pltpu.VMEM(value.shape, value.dtype) for value in loads[:2]]
        + [pltpu.VMEM(h1_all.shape if seq <= 1024 else (16, 128), bf16)]
        + [dma((3,)), dma((2,))]
        + gather_sems(nb, cuts)
        + scatter_scratch(chips, cuts, t, wide)
        + extras.scratch,
        compiler_params=params(cid),
        cost_estimate=cost(10 * seq * seq * width),
    )(q, k, v, o, cosine, sine, place, length.reshape(1), branch, w_out, p, *loads, *extras.operands)


def arrange(weight, out, parts):
    nb, _, wide = out.shape
    span = wide // parts
    for j in range(nb):
        for part in range(parts):
            at = (part * nb + j) * span
            out[j, :, part * span : (part + 1) * span] = weight[:, at : at + span].astype(out.dtype)


def first_kernel(chips, cuts, parts, map_ref, tokens_ref, gain_ref, frequency_ref, *refs):
    n = len(parts)
    refs = list(refs)

    def take(count):
        return [refs.pop(0) for _ in range(count)]

    sources, h1_all, swapped, gathered = take(n), take(1)[0], take(n), take(n - 1)
    inverse_ref, place_ref, cos_ref, sin_ref = take(4)
    weights, held, (h1_ref, load_sem) = take(n), take(n), take(2)
    swaps = [swap_task(a, b, *take(3)) for a, b in zip(held, swapped)]
    task = square_gather if gathered[0].shape[0] == 4 else direct_gather
    rows = [task(a, b, *take(4)) for a, b in zip(swapped, gathered)]
    begin, pass_on, from_side, local, sent = gather_task(chips, cuts, h1_ref, h1_all, refs)
    load, loaded = mover(list(zip(sources, weights)), load_sem)
    load()
    greet(chips, True, True)
    for i in range(n - 1):
        loaded(i)
        arrange(weights[i], held[i], parts[i])
        swaps[i][0]()
    _, inverse_ref[...], h1_ref[...] = norm_forward(
        tokens_ref[...].astype(jnp.float32), gain_ref[...]
    )
    loaded(n - 1)
    arrange(weights[n - 1], held[n - 1], parts[n - 1])
    blocks = map_ref.shape[1]
    block = place_ref.shape[0] // blocks
    lanes = cos_ref.shape[1]
    front = lax.broadcasted_iota(jnp.int32, (block, lanes), 1) % HEAD_DIM < HEAD_DIM // 2
    for j in range(blocks):
        at = slice(j * block, (j + 1) * block)
        place = map_ref[0, j] * block + lax.broadcasted_iota(jnp.int32, (block, lanes), 0)
        place_ref[at] = place[:, :1]
        angle = place.astype(jnp.float32) * frequency_ref[...]
        cos_ref[at] = jnp.cos(angle)
        sine = jnp.sin(angle)
        sin_ref[at] = jnp.where(front, -sine, sine)
    for i in range(n - 2):
        swaps[i][1]()
        rows[i][0]()
    swaps[n - 2][1]()
    rows[n - 2][0]()
    begin()
    for k in range(1, chips):
        if k == min(3, chips - 1):
            swaps[n - 1][0]()
        pass_on(k)
    for _, middle, _ in rows:
        middle()
    local().wait()
    for y in range(chips):
        from_side(y)
    sent()
    for _, _, wait in rows:
        wait()
    swaps[n - 1][1]()


def first(cid, block_map, tokens, gain, weights, parts, cuts=4):
    nr, nb = lax.axis_size("rows"), lax.axis_size("blk")
    shapes = [(nb, value.shape[0], value.shape[1] // nb) for value in weights]
    n = len(weights)
    t, width = tokens.shape
    half = HEAD_DIM // 2
    frequency = jnp.exp(
        -jnp.arange(half, dtype=jnp.float32) * (2.0 / HEAD_DIM) * math.log(theta_base)
    )
    dma, f32, bf16 = pltpu.SemaphoreType.DMA, jnp.float32, jnp.bfloat16
    table = jax.ShapeDtypeStruct((nb * t, 2 * HEAD_DIM), f32)
    sems = 6 if nr == 4 else nr
    scratch = [pltpu.VMEM(value.shape, value.dtype) for value in weights]
    scratch += [pltpu.VMEM(shape, bf16) for shape in shapes]
    scratch += [pltpu.VMEM((t, width), bf16), dma((n,))]
    scratch += [dma, dma((nb,)), dma((nb,))] * n
    for shape in shapes[:-1]:
        scratch += [pltpu.VMEM(shape, bf16), dma, dma((sems,)), dma((sems,))]
    return pl.pallas_call(
        functools.partial(first_kernel, nb // 2, cuts, parts),
        out_shape=[jax.ShapeDtypeStruct((nb * t, width), bf16)]
        + [jax.ShapeDtypeStruct(shape, bf16) for shape in shapes]
        + [jax.ShapeDtypeStruct((nr,) + shape, bf16) for shape in shapes[:-1]]
        + [
            jax.ShapeDtypeStruct((t, 1), f32),
            jax.ShapeDtypeStruct((nb * t, 1), jnp.int32),
            table,
            table,
        ],
        in_specs=[pl.BlockSpec(memory_space=pltpu.SMEM)] + [VMEM] * 3 + [ANY] * n,
        out_specs=[ANY] * (2 * n) + [VMEM] * 4,
        scratch_shapes=scratch + gather_sems(nb, cuts),
        compiler_params=params(cid),
        cost_estimate=cost(0),
    )(block_map, tokens, gain[None], jnp.tile(frequency, 4)[None], *weights)


def total_task(nr, nb, x_ref, o_ref, held, rows_held, send_one, recv_one, send_two, recv_two):
    r, b = lax.axis_index("rows"), lax.axis_index("blk")
    across = [lax.rem(b + k, nb) for k in range(1, nb)]
    along = [lax.rem(r + k, nr) for k in range(1, nr)]

    def first(other, slot):
        return pltpu.make_async_remote_copy(
            src_ref=rows_held.at[r], dst_ref=rows_held.at[slot], send_sem=send_two.at[other],
            recv_sem=recv_two.at[slot], device_id=(other, b), device_id_type=MESH,
        )

    def second(other, slot):
        return pltpu.make_async_remote_copy(
            src_ref=held.at[b], dst_ref=held.at[slot], send_sem=send_one.at[other],
            recv_sem=recv_one.at[slot], device_id=(r, other), device_id_type=MESH,
        )

    def start():
        rows_held[r] = x_ref[...]
        for other in along:
            first(other, r).start()

    def middle():
        for other in along:
            first(other, other).wait_recv()
        held[b] = jnp.sum(rows_held[...], axis=0)
        for other in across:
            second(other, b).start()

    def finish():
        for other in across:
            second(other, other).wait_recv()
        o_ref[...] = jnp.sum(held[...], axis=0)
        for other in along:
            first(other, r).wait_send()
        for other in across:
            second(other, b).wait_send()

    return start, middle, finish


def last_scatter_kernel(
    chips, nr, cuts, tile, extras, a_ref, w_ref, x_ref, inverse_ref, gain_ref, resid_ref, gain_two_ref, h1_hbm, *refs
):
    n = extras.n
    srcs, refs = refs[:n], refs[n:]
    o_ref, total_ref, dsts, refs = refs[0], refs[1], refs[2 : 2 + n], refs[2 + n :]
    sum_ref, part_ref, h1_ref, load_sem, refs = refs[0], refs[1], refs[2], refs[3], refs[4:]
    put, _, hop, finish = scatter_task(chips, cuts, tile, sum_ref, refs[:4], refs[4:10])
    start_total, middle_total, finish_total = total_task(
        nr, 2 * chips, part_ref, total_ref, *refs[10:16]
    )
    start_swaps, start_rows, middle, wait_rows, wait_swaps = extras.tasks(srcs, dsts, refs[16:])
    load, loaded = mover([(h1_hbm, h1_ref)], load_sem)
    load()
    greet(chips, True, True)
    start_swaps()
    start_rows()
    part_ref[0:1] = jnp.zeros_like(part_ref[0:1])
    part_ref[1:2] = gain_two_ref[...]
    loaded()

    def seen(rows, cols, got):
        part_ref[0:1, cols] += jnp.sum(got * h1_ref[rows, cols].astype(jnp.float32), axis=0)[None]

    for s in range(chips):
        put(s, lambda rows: a_ref.at[rows], w_ref, seen)
        if s < chips - 1:
            hop(s)
    part_ref[0:1] = part_ref[0:1] / gain_ref[...]
    start_total()
    middle()
    middle_total()
    wait_rows()
    finish()
    inverse = inverse_ref[...]
    unit = x_ref[...].astype(jnp.float32) * inverse
    o_ref[...] = resid_ref[...] + norm_backward(sum_ref[...], unit, inverse, gain_ref[...])[0]
    finish_total()
    wait_swaps()


def last_scatter(cid, a, w, x, inverse, gain, resid, gain_two, h1_all, extras, cuts=2, tile=1024):
    nr, nb = lax.axis_size("rows"), lax.axis_size("blk")
    t, width = x.shape
    pair = (2, width)
    dma, f32 = pltpu.SemaphoreType.DMA, jnp.float32
    return pl.pallas_call(
        functools.partial(last_scatter_kernel, nb // 2, nr, cuts, tile, extras),
        out_shape=[jax.ShapeDtypeStruct((t, width), f32), jax.ShapeDtypeStruct(pair, f32)]
        + extras.shapes,
        in_specs=[VMEM] * 7 + [ANY] + extras.specs,
        out_specs=[VMEM] * 2 + extras.specs,
        scratch_shapes=[
            pltpu.VMEM((t, width), f32),
            pltpu.VMEM(pair, f32),
            pltpu.VMEM(h1_all.shape, h1_all.dtype),
            dma((1,)),
        ]
        + scatter_scratch(nb // 2, cuts, t, width)
        + [pltpu.VMEM((nb,) + pair, f32), pltpu.VMEM((nr,) + pair, f32)]
        + [dma((nb,))] * 2 + [dma((nr,))] * 2
        + extras.scratch,
        compiler_params=params(cid),
        cost_estimate=cost(2 * a.shape[0] * width * w.shape[1]),
    )(a, w, x, inverse, gain[None], resid, gain_two, h1_all, *extras.operands)


def step_kernel(parts, one_array, *refs):
    count = 1 if one_array else parts
    grads, refs = refs[:count], refs[count:]
    outs = len(refs) // 2
    rule = adam_step if outs == 3 else moment_step

    def go(grad):
        wide = grad.shape[2]
        for j in range(grad.shape[0]):
            cols = slice(j * wide, (j + 1) * wide)
            gradient = grad[j].astype(jnp.float32)
            for ref, value in zip(
                refs[outs:], rule(*[ref[:, cols] for ref in refs[:outs]], gradient)
            ):
                ref[:, cols] = value

    if one_array:
        go(grads[0])
        return
    for part, grad in enumerate(grads):
        pl.when(pl.program_id(0) == part)(functools.partial(go, grad))


def step(pieces, parts, states, first=0):
    one_array = not isinstance(pieces, list)
    pieces = [pieces] if one_array else pieces
    nb = pieces[0].shape[0]
    rows, columns = states[0].shape
    tile = min(rows, 64 if parts > 1 else 32)
    span = columns // parts
    at = pl.BlockSpec((tile, span), lambda part, i: (i, part))
    block = (nb, tile, span // nb)
    if one_array:
        grads = [pl.BlockSpec(block, lambda part, i: (0, i, first + part))]
    else:
        grads = [pl.BlockSpec(block, lambda part, i: (0, i, 0))] * parts
    outs = len(states)
    return pl.pallas_call(
        functools.partial(step_kernel, parts, one_array),
        grid=(parts, rows // tile),
        in_specs=grads + [at] * outs,
        out_specs=[at] * outs,
        out_shape=[jax.ShapeDtypeStruct((rows, columns), jnp.float32)] * outs,
        compiler_params=pltpu.CompilerParams(vmem_limit_bytes=60 * MIB),
        cost_estimate=pl.CostEstimate(
            flops=0, bytes_accessed=(8 * outs + 2) * rows * columns, transcendentals=0
        ),
    )(*pieces, *states)


def after(value, *others):
    return lax.optimization_barrier((value,) + others)[0]


def over_tokens(left, right):
    return lax.dot_general(
        left, right, (((0,), (0,)), ((), ())), preferred_element_type=jnp.float32
    )


def shards(
    tokens, cotangent, lengths, block_map, gain_attend, gain_expand,
    attend_in, attend_out, expand_in, reduce_out,
    attend_in_first, attend_out_first, expand_in_first, reduce_out_first,
    attend_in_second, attend_out_second, expand_in_second, reduce_out_second,
):
    nb = lax.axis_size("blk")
    length = lengths[0]
    h1_all, _, _, _, swap_gu, w_in, w_out, w_red, inverse_one, place, cosine, sine = first(
        2, block_map, tokens[0], gain_attend,
        (attend_in, attend_out.T, reduce_out.T, expand_in), (3, 1, 1, 2),
    )
    block_rows = tokens.shape[1] // 2
    row_place = (block_map[0][:, None] * block_rows + jnp.arange(block_rows)[None, :]).reshape(1, -1)
    live_place = jnp.where(row_place < length, row_place, jnp.int32(1 << 30))
    nr = lax.axis_size("rows")
    deep = nb * attend_in.shape[0]
    wide = tokens.shape[2]

    def flat(pieces):
        return pieces.reshape(deep, pieces.shape[2])

    w_in, w_out, w_red = [value.reshape(wide, value.shape[3]) for value in (w_in, w_out, w_red)]
    attended, q, k, v, p, g_all, x1, inverse_two, h2, w_gu = attend(
        4, h1_all, w_in, cosine, sine, place, live_place, length, cotangent[0],
        tokens[0], gain_expand, w_out, Extras([], [(flat(swap_gu), 0, deep)]),
    )
    w_gu = w_gu.reshape(wide, -1)

    def by_rows(gradient):
        return gradient.reshape(nr, nb, deep // nb, gradient.shape[1])

    grad_x1, branch, gain_two, hidden, part_gate, part_up, rows_reduce = feed_forward(
        6, h2, x1, inverse_two, gain_expand, cotangent[0], w_gu, w_red, g_all
    )
    grad_mixed, y, part_both, own_reduce, rows_gate, rows_up = attend_back(
        10, q, k, v, attended, p, cosine, sine, place, length, branch, w_out, hidden, w_red, h1_all,
        Extras([rows_reduce], [], [by_rows(part_gate), by_rows(part_up)]),
    )
    y = x1 + y
    grad_input, gains, own_gate, own_up, rows_both = last_scatter(
        11, grad_mixed, w_in, tokens[0], inverse_one, gain_attend, grad_x1, gain_two, h1_all,
        Extras([rows_gate, rows_up], [], [by_rows(part_both)]),
    )
    both = lax.all_to_all(rows_both, "blk", 0, 0, tiled=True)
    set_four = step(own_reduce, 1, (reduce_out.T, reduce_out_first.T, reduce_out_second.T))
    set_three = step([own_gate, own_up], 2, (expand_in, expand_in_first, expand_in_second))
    both = after(both, set_three[2], set_four[2])
    set_one = step(both, 3, (attend_in, attend_in_first, attend_in_second))
    set_two = step(both, 1, (attend_out_first.T, attend_out_second.T), 3)
    return (
        y.astype(jnp.bfloat16).reshape(tokens.shape),
        grad_input.reshape(tokens.shape),
        gains[0],
        gains[1],
        *set_one,
        *[value.T for value in set_two],
        *set_three,
        *[value.T for value in set_four],
    )


def solution(mesh):
    placed = (
        P("rows", "blk", None),
        P("rows", "blk", None),
        P("rows"),
        P("rows", None),
        P(),
        P(),
        P(("rows", "blk"), None),
        P(None, ("rows", "blk")),
        P(("rows", "blk"), None),
        P(None, ("rows", "blk")),
        P(("rows", "blk"), None),
        P(None, ("rows", "blk")),
        P(("rows", "blk"), None),
        P(None, ("rows", "blk")),
        P(("rows", "blk"), None),
        P(None, ("rows", "blk")),
        P(("rows", "blk"), None),
        P(None, ("rows", "blk")),
    )
    return jax.shard_map(
        shards,
        mesh=mesh,
        in_specs=placed,
        out_specs=(
            P("rows", "blk", None),
            P("rows", "blk", None),
            P(),
            P(),
            P(("rows", "blk"), None),
            P(("rows", "blk"), None),
            P(("rows", "blk"), None),
            P(None, ("rows", "blk")),
            P(None, ("rows", "blk")),
            P(("rows", "blk"), None),
            P(("rows", "blk"), None),
            P(("rows", "blk"), None),
            P(None, ("rows", "blk")),
            P(None, ("rows", "blk")),
            P(None, ("rows", "blk")),
        ),
        check_vma=False,
    )
```

```python
import functools
import math

import jax
import jax.numpy as jnp
from jax import lax
from jax.experimental import pallas as pl
from jax.experimental.pallas import tpu as pltpu
from jax.sharding import PartitionSpec as P

HEADS = 32
HEAD_DIM = 64
MESH = pl.DeviceIdType.MESH
MIB = 1 << 20

theta_base = 130000.0
norm_eps = 1e-05
neg_large = -1e30
beta_one = 0.9
beta_two = 0.95
learn_rate = 0.01
decay_rate = 0.1
adam_eps = 1e-08
step_count = 10


def line_place():
    b = lax.axis_index("blk")
    return lax.axis_index("rows"), b // 2, b % 2


def greet(chips, swaps=False, rows=False):
    r, z, c = line_place()
    barrier = pltpu.get_barrier_semaphore()
    count = 0

    def signal(row, b):
        pl.semaphore_signal(barrier, inc=1, device_id=(row, b), device_id_type=MESH)

    b, nb, nr = 2 * z + c, 2 * chips, lax.axis_size("rows")
    if rows:
        for k in range(1, nr):
            signal(lax.rem(r + k, nr), b)
        count = nr - 1
    if swaps:
        for k in range(1, nb):
            signal(r, lax.rem(b + k, nb))
        count = count + nb - 1
    else:
        signal(r, b + 1 - 2 * c)
        pl.when(z < chips - 1)(lambda: signal(r, b + 2))
        pl.when(z > 0)(lambda: signal(r, b - 2))
        count = count + 1 + (z < chips - 1).astype(jnp.int32) + (z > 0).astype(jnp.int32)
    pl.semaphore_wait(barrier, count)


def swap_task(src, dst, local, send, recv):
    r, b = lax.axis_index("rows"), lax.axis_index("blk")
    nb = src.shape[0]
    others = [lax.rem(b + k, nb) for k in range(1, nb)]

    def remote(other, slot):
        return pltpu.make_async_remote_copy(
            src_ref=src.at[other], dst_ref=dst.at[slot], send_sem=send.at[other],
            recv_sem=recv.at[slot], device_id=(r, other), device_id_type=MESH,
        )

    def start():
        for other in others:
            remote(other, b).start()
        pltpu.make_async_copy(src.at[b], dst.at[b], local).start()

    def wait():
        for other in others:
            remote(other, other).wait_recv()
        for other in others:
            remote(other, b).wait_send()
        pltpu.make_async_copy(src.at[b], dst.at[b], local).wait()

    return start, wait


def rows_copy(src, dst, send, recv, device):
    return pltpu.make_async_remote_copy(
        src_ref=src, dst_ref=dst, send_sem=send, recv_sem=recv,
        device_id=(device, lax.axis_index("blk")), device_id_type=MESH,
    )


def through(src, stage, dst, local):
    first = pltpu.make_async_copy(src, stage, local)
    second = pltpu.make_async_copy(stage, dst, local)

    def store():
        first.wait()
        second.start()

    return first.start, store, second.wait


def direct_gather(src, dst, stage, local, send, recv):
    r, nr = lax.axis_index("rows"), dst.shape[0]
    others = [lax.rem(r + k, nr) for k in range(1, nr)]
    load, store, stored = through(src, stage, dst.at[r], local)

    def start():
        for other in others:
            rows_copy(src, dst.at[r], send.at[other], recv.at[r], other).start()
        load()

    def wait():
        for other in others:
            rows_copy(src, dst.at[other], send.at[other], recv.at[other], other).wait()
        stored()

    return start, store, wait


def square_gather(src, dst, stage, local, send, recv):
    r = lax.axis_index("rows")
    half = src.shape[0] // 2
    load, store, stored = through(src, stage, dst.at[r], local)

    def near(sem, origin, device):
        return rows_copy(src, dst.at[origin], send.at[sem], recv.at[sem], device)

    def onward(sem, origin, device):
        part = dst.at[origin, pl.ds((sem - 2) * half, half)]
        return rows_copy(part, part, send.at[sem], recv.at[sem], device)

    def start():
        near(0, r, r ^ 1).start()
        near(1, r, r ^ 2).start()
        load()

    def middle():
        store()
        near(0, r ^ 1, r ^ 1).wait_recv()
        onward(2, r ^ 1, r ^ 2).start()
        near(1, r ^ 2, r ^ 2).wait_recv()
        onward(3, r ^ 2, r ^ 1).start()

    def wait():
        onward(2, r ^ 3, r ^ 2).wait_recv()
        onward(3, r ^ 3, r ^ 1).wait_recv()
        near(0, r, r ^ 1).wait_send()
        near(1, r, r ^ 2).wait_send()
        onward(2, r ^ 1, r ^ 2).wait_send()
        onward(3, r ^ 2, r ^ 1).wait_send()
        stored()

    return start, middle, wait


def direct_sum(src, dst, held, local, send, recv):
    r, nr = lax.axis_index("rows"), src.shape[0]
    others = [lax.rem(r + k, nr) for k in range(1, nr)]

    def start():
        for other in others:
            rows_copy(src.at[other], held.at[r], send.at[other], recv.at[r], other).start()
        pltpu.make_async_copy(src.at[r], held.at[r], local).start()

    def wait():
        for other in others:
            rows_copy(src.at[other], held.at[other], send.at[other], recv.at[other], other).wait()
        pltpu.make_async_copy(src.at[r], held.at[r], local).wait()

        def one(j, _):
            total = held[0, j].astype(jnp.float32)
            for slot in range(1, nr):
                total = total + held[slot, j].astype(jnp.float32)
            held[0, j] = total.astype(held.dtype)
            return 0

        lax.fori_loop(0, held.shape[1], one, 0)
        done = pltpu.make_async_copy(held.at[0], dst, local)
        done.start()
        done.wait()

    return start, lambda: None, wait


def square_sum(src, dst, held, local, send, recv):
    r = lax.axis_index("rows")
    half = src.shape[1] // 2
    parts = [(pl.ds(0, half), r ^ 1, r ^ 2), (pl.ds(half, half), r ^ 2, r ^ 1)]

    def out(i, k):
        at, one, two = parts[i]
        return rows_copy(
            src.at[one if k == 0 else r ^ 3, at], held.at[k, at], send.at[2 * i + k],
            recv.at[2 * i + k], one,
        )

    def own(i, k):
        at, one, two = parts[i]
        return pltpu.make_async_copy(
            src.at[r if k == 0 else two, at], held.at[2 + k, at], local.at[2 * i + k]
        )

    def onward(i):
        at, one, two = parts[i]
        return rows_copy(held.at[3, at], held.at[4, at], send.at[4 + i], recv.at[4 + i], two)

    def add(i, into, *slots):
        def one(j, _):
            j = i * half + j
            total = held[into, j].astype(jnp.float32)
            for slot in slots:
                total = total + held[slot, j].astype(jnp.float32)
            held[into, j] = total.astype(held.dtype)
            return 0

        lax.fori_loop(0, half, one, 0)

    def start():
        for i in range(2):
            for k in (1, 0):
                out(i, k).start()
                own(i, k).start()

    def start_as(make):
        for i, k in ((0, 1), (1, 1), (0, 0), (1, 0)):
            make((parts[i][1] if k == 0 else r ^ 3), i)
            out(i, k).start()
        for i, k in ((0, 1), (1, 1), (0, 0), (1, 0)):
            make((r if k == 0 else parts[i][2]), i)
            own(i, k).start()

    start.as_made = start_as

    def middle():
        for i in range(2):
            out(i, 1).wait_recv()
            own(i, 1).wait()
            add(i, 3, 1)
            onward(i).start()

    def wait():
        for i in range(2):
            out(i, 0).wait_recv()
            own(i, 0).wait()
            onward(i).wait_recv()
            add(i, 2, 0, 4)
        done = pltpu.make_async_copy(held.at[2], dst, local.at[0])
        done.start()
        done.wait()
        for i in range(2):
            out(i, 0).wait_send()
            out(i, 1).wait_send()
            onward(i).wait_send()

    return start, middle, wait


class Extras:
    def __init__(self, swaps=(), gathers=(), scatters=()):
        nr, nb = lax.axis_size("rows"), lax.axis_size("blk")
        dma = pltpu.SemaphoreType.DMA
        self.swaps, self.gathers, self.scatters = len(swaps), [g[1:] for g in gathers], len(scatters)
        self.operands = [*swaps, *[g[0] for g in gathers], *scatters]
        self.n = len(self.operands)
        self.rows = bool(gathers) or bool(scatters)
        self.specs = [ANY] * self.n
        self.shapes = [like(value) for value in swaps]
        self.scratch = [dma, dma((nb,)), dma((nb,))] * len(swaps)
        self.square = nr == 4
        sems = 6 if self.square else nr
        for value, _, count in gathers:
            self.shapes.append(jax.ShapeDtypeStruct((nr, count, value.shape[1]), value.dtype))
            self.scratch += [pltpu.VMEM((count, value.shape[1]), value.dtype)]
            self.scratch += [dma, dma((sems,)), dma((sems,))]
        for value in scatters:
            self.shapes.append(jax.ShapeDtypeStruct(value.shape[1:], value.dtype))
            slots = 5 if self.square else nr
            local = dma((4,)) if self.square else dma
            self.scratch += [pltpu.VMEM((slots,) + value.shape[1:], value.dtype)]
            self.scratch += [local, dma((sems,)), dma((sems,))]

    def tasks(self, srcs, dsts, scratch):
        scratch = list(scratch)
        swaps, rows = [], []
        for i, (src, dst) in enumerate(zip(srcs, dsts)):
            if i < self.swaps:
                swaps.append(swap_task(src, dst, *scratch[:3]))
                scratch = scratch[3:]
            elif i < self.swaps + len(self.gathers):
                first, count = self.gathers[i - self.swaps]
                task = square_gather if self.square else direct_gather
                rows.append(task(src.at[pl.ds(first, count)], dst, *scratch[:4]))
                scratch = scratch[4:]
            else:
                task = square_sum if self.square else direct_sum
                rows.append(task(src, dst, *scratch[:4]))
                scratch = scratch[4:]

        def start_swaps():
            for start, _ in swaps:
                start()

        def start_rows():
            for start, _, _ in rows:
                start()

        def middle():
            for _, one, _ in rows:
                one()

        def wait_rows():
            for _, _, one in rows:
                one()

        def wait_swaps():
            for _, one in swaps:
                one()

        return start_swaps, start_rows, middle, wait_rows, wait_swaps


def like(value):
    return jax.ShapeDtypeStruct(value.shape, value.dtype)


ANY = pl.BlockSpec(memory_space=pl.ANY)
VMEM = pl.BlockSpec(memory_space=pltpu.VMEM)


def params(cid):
    return pltpu.CompilerParams(
        collective_id=cid, has_side_effects=True, vmem_limit_bytes=60 * MIB
    )


def cost(flops):
    return pl.CostEstimate(flops=flops, bytes_accessed=150_000_000, transcendentals=0)


def mover(pairs, sem):
    copies = [pltpu.make_async_copy(a, b, sem.at[i]) for i, (a, b) in enumerate(pairs)]

    def start(*which):
        for i in which or range(len(copies)):
            copies[i].start()

    def wait(*which):
        for i in which or range(len(copies)):
            copies[i].wait()

    return start, wait


def gather_task(chips, cuts, x_ref, o_ref, sems):
    copy_sem, send_up, send_down, send_side, recv = sems
    r, z, c = line_place()
    t = x_ref.shape[0]
    h = t // cuts
    up, down, side = (r, 2 * (z + 1) + c), (r, 2 * (z - 1) + c), (r, 2 * z + 1 - c)
    has_up, has_down = z < chips - 1, z > 0
    mine = 2 * z + c

    def piece(j, q):
        return o_ref.at[pl.ds(pl.multiple_of(j * t + q * h, h), h)]

    def remote(src, j, q, sem, dev):
        return pltpu.make_async_remote_copy(
            src_ref=src, dst_ref=piece(j, q), send_sem=sem.at[j, q], recv_sem=recv.at[j, q],
            device_id=dev, device_id_type=MESH,
        )

    def local():
        whole = o_ref.at[pl.ds(pl.multiple_of(mine * t, t), t)]
        return pltpu.make_async_copy(x_ref, whole, copy_sem)

    def start():
        for q in range(cuts):
            from_here = x_ref.at[pl.ds(q * h, h)]
            pl.when(has_up)(lambda: remote(from_here, mine, q, send_up, up).start())
            pl.when(has_down)(lambda: remote(from_here, mine, q, send_down, down).start())
            remote(from_here, mine, q, send_side, side).start()
        local().start()

    def hop(k):
        for q in range(cuts):
            @pl.when(z - k >= 0)
            def _():
                j = 2 * (z - k) + c
                remote(piece(j, q), j, q, send_up, up).wait_recv()
                pl.when(has_up)(lambda: remote(piece(j, q), j, q, send_up, up).start())
                remote(piece(j, q), j, q, send_side, side).start()

            @pl.when(z + k < chips)
            def _():
                j = 2 * (z + k) + c
                remote(piece(j, q), j, q, send_down, down).wait_recv()
                pl.when(has_down)(lambda: remote(piece(j, q), j, q, send_down, down).start())
                remote(piece(j, q), j, q, send_side, side).start()

    def from_side(y):
        for q in range(cuts):
            j = 2 * y + 1 - c
            remote(piece(j, q), j, q, send_side, side).wait_recv()

    def finish():
        for y in range(chips):
            j = 2 * y + c
            for q in range(cuts):
                pl.when(has_up & (z >= y))(
                    lambda: remote(piece(j, q), j, q, send_up, up).wait_send()
                )
                pl.when(has_down & (z <= y))(
                    lambda: remote(piece(j, q), j, q, send_down, down).wait_send()
                )
                remote(piece(j, q), j, q, send_side, side).wait_send()

    return start, hop, from_side, local, finish


def gather_sems(nb, cuts):
    return [pltpu.SemaphoreType.DMA] + [pltpu.SemaphoreType.DMA((nb, cuts))] * 4


def arrival_order(chips):
    table = []
    for z in range(chips):
        row = [z]
        for k in range(1, chips):
            row += [y for y in (z - k, z + k) if 0 <= y < chips]
        table.append(row)
    return table


def need_order(chips):
    table = []
    for z in range(chips):
        need = {
            y: (chips - 1 + z - y) if y > z else (chips - 1 - z + y)
            for y in range(chips) if y != z
        }
        table.append(sorted(need, key=lambda y: need[y]) + [z])
    return table


def pick(table, z, k):
    out = 0
    for at, row in enumerate(table):
        for step, block in enumerate(row):
            out = out + jnp.where((z == at) & (k == step), block, 0)
    return out


def scatter_task(chips, cuts, tile, o_ref, bufs, sems):
    mine, away, side_buf, line_buf = bufs
    send_side, recv_side, send_up, recv_up, send_down, recv_down = sems
    r, z, c = line_place()
    t, width = o_ref.shape
    low, f32 = away.dtype, jnp.float32
    up, down, side = (r, 2 * (z + 1) + c), (r, 2 * (z - 1) + c), (r, 2 * z + 1 - c)
    has_up, has_down = z < chips - 1, z > 0
    h = t // cuts
    table = need_order(chips)

    def remote(src, dst, y, q, send, recv, dev):
        return pltpu.make_async_remote_copy(
            src_ref=src.at[y, pl.ds(q * h, h)], dst_ref=dst.at[y, pl.ds(q * h, h)],
            send_sem=send.at[y, q], recv_sem=recv.at[y, q], device_id=dev, device_id_type=MESH,
        )

    def to_side(y, q):
        return remote(away, side_buf, y, q, send_side, recv_side, side)

    def along(y, slot, q, send, recv, dev):
        return pltpu.make_async_remote_copy(
            src_ref=mine.at[y, pl.ds(q * h, h)], dst_ref=line_buf.at[slot, pl.ds(q * h, h)],
            send_sem=send.at[y, q], recv_sem=recv.at[y, q], device_id=dev, device_id_type=MESH,
        )

    def to_up(y, q):
        return along(y, y, q, send_up, recv_up, up)

    def to_down(y, q):
        return along(y, jnp.where(y == z - 1, chips, y), q, send_down, recv_down, down)

    def from_up(y, q):
        return along(y, jnp.where(y == z, chips, y), q, send_down, recv_down, down)

    def rows(q):
        return pl.ds(q * h, h)

    def total(y, q):
        to_side(y, q).wait_recv()
        return mine[y, rows(q)].astype(f32) + side_buf[y, rows(q)].astype(f32)

    def put(s, rows_of, w_ref, seen=None):
        put_at(pick(table, z, s), rows_of, w_ref, seen)

    def put_at(y, rows_of, w_ref, seen=None):
        block = pl.ds(pl.multiple_of(2 * y * t, 2 * t), 2 * t)
        a = rows_of(block)

        def one(i, _):
            cols = pl.ds(pl.multiple_of(i * tile, tile), tile)
            got = lax.dot_general(
                a[...], w_ref[cols], (((1,), (1,)), ((), ())), preferred_element_type=f32
            )
            if seen is not None:
                seen(block, cols, got)
            got = got.astype(low)

            @pl.when(c == 0)
            def _():
                mine[y, :, cols] = got[:t]
                away[y, :, cols] = got[t:]

            @pl.when(c == 1)
            def _():
                mine[y, :, cols] = got[t:]
                away[y, :, cols] = got[:t]

            return 0

        lax.fori_loop(0, width // tile, one, 0)
        for q in range(cuts):
            to_side(y, q).start()

    def hop(s):
        hop_up(chips - 1 + z - s)
        hop_down(s - (chips - 1) + z)

    def hop_up(y):
        for q in range(cuts):
            @pl.when((y > z) & (y <= chips - 1))
            def _():
                now = total(y, q)

                @pl.when(has_down)
                def _():
                    to_up(y, q).wait_recv()
                    mine[y, rows(q)] = (now + line_buf[y, rows(q)].astype(f32)).astype(low)

                @pl.when(z == 0)
                def _():
                    mine[y, rows(q)] = now.astype(low)

                to_up(y, q).start()

    def hop_down(w):
        for q in range(cuts):
            @pl.when((w >= 0) & (w < z))
            def _():
                now = total(w, q)

                @pl.when(has_up)
                def _():
                    from_up(w, q).wait_recv()
                    mine[w, rows(q)] = (now + line_buf[w, rows(q)].astype(f32)).astype(low)

                @pl.when(z == chips - 1)
                def _():
                    mine[w, rows(q)] = now.astype(low)

                to_down(w, q).start()

    def finish():
        for q in range(cuts):
            o_ref[rows(q)] = total(z, q)
        for q in range(cuts):
            @pl.when(has_down)
            def _():
                to_up(z, q).wait_recv()
                o_ref[rows(q)] += line_buf[z, rows(q)].astype(f32)

            @pl.when(has_up)
            def _():
                from_up(z, q).wait_recv()
                o_ref[rows(q)] += line_buf[chips, rows(q)].astype(f32)

        for y in range(chips):
            for q in range(cuts):
                to_side(y, q).wait_send()
                pl.when(y > z)(lambda: to_up(y, q).wait_send())
                pl.when(y < z)(lambda: to_down(y, q).wait_send())

    return put, (put_at, hop_up, hop_down), hop, finish


def scatter_scratch(chips, cuts, t, width):
    return (
        [pltpu.VMEM((chips, t, width), jnp.bfloat16)] * 3
        + [pltpu.VMEM((chips + 1, t, width), jnp.bfloat16)]
        + [pltpu.SemaphoreType.DMA((chips, cuts))] * 6
    )


def feed_forward_kernel(
    chips, cuts, tile, h2_here, x1_ref, inverse_ref, gain_ref, cotangent_ref, w_hbm, red_hbm, g_hbm,
    grad_out, low_out, gain_out, hidden_out, gate_out, up_out, reduce_out,
    h2_ref, hidden_ref, grad_ref, w_ref, red_ref, g_ref, dw_red, dw_ref, red_held,
    load_sem, save_sem, dw_sem, red_local, red_send, red_recv, *refs
):
    begin, pass_on, from_side, local, sent = gather_task(chips, cuts, h2_here, h2_ref, refs[:5])
    _, (put_at, hop_up, hop_down), _, finish = scatter_task(chips, cuts, tile, grad_out, refs[5:9], refs[9:])
    task = square_sum if dw_red.shape[0] == 4 else direct_sum
    start_red, middle_red, wait_red = task(
        dw_red, reduce_out, red_held, red_local, red_send, red_recv
    )
    load, loaded = mover([(w_hbm, w_ref), (g_hbm, g_ref), (red_hbm, red_ref)], load_sem)
    r, z, c = line_place()
    t, width = h2_here.shape
    units = hidden_ref.shape[1]
    span = min(512, units)
    f32, low = jnp.float32, jnp.bfloat16
    over_rows = (((0,), (0,)), ((), ()))
    load()
    greet(chips, False, True)
    begin()

    def rows_of(y):
        return pl.ds(pl.multiple_of(y * 2 * t, 2 * t), 2 * t)

    def save(y):
        return pltpu.make_async_copy(
            hidden_ref.at[rows_of(y)], hidden_out.at[rows_of(y)], save_sem.at[y]
        )

    def columns(i):
        at, more = i * span, units + i * span
        return pl.ds(pl.multiple_of(at, span), span), pl.ds(pl.multiple_of(more, span), span)

    def forward(y):
        rows = rows_of(y)

        def one(i, _):
            cols, more = columns(i)
            gate = jnp.dot(h2_ref[rows], w_ref[:, cols], preferred_element_type=f32)
            up = jnp.dot(h2_ref[rows], w_ref[:, more], preferred_element_type=f32)
            sigmoid = jax.nn.sigmoid(gate)
            silu = gate * sigmoid
            hidden_ref[rows, cols] = (silu * up).astype(low)
            grad_ref[rows, cols] = (up * (sigmoid * (1.0 + gate * (1.0 - sigmoid)))).astype(low)
            grad_ref[rows, more] = silu.astype(low)
            return 0

        lax.fori_loop(0, units // span, one, 0)
        save(y).start()

    def backward(rows):
        def one(i, _):
            cols, more = columns(i)
            grad = jnp.dot(g_ref[rows], red_ref[:, cols], preferred_element_type=f32)
            grad_ref[rows, cols] = (grad * grad_ref[rows, cols].astype(f32)).astype(low)
            grad_ref[rows, more] = (grad * grad_ref[rows, more].astype(f32)).astype(low)
            return 0

        lax.fori_loop(0, units // span, one, 0)
        return grad_ref.at[rows]

    from_side(z)
    local().wait()
    loaded(0)
    forward(z)
    loaded(1, 2)
    put_at(z, backward, w_ref)
    deep = 256
    turns = width // deep
    piece = dw_red.shape[2]
    run = dw_red.shape[1] * piece

    def reduce_grad(i, _):
        at = pl.ds(pl.multiple_of(i * deep, deep), deep)
        got = lax.dot_general(g_ref[:, at], hidden_ref[...], over_rows, preferred_element_type=f32)
        first = i * deep
        dw_red[first // run, pl.ds(lax.rem(first, run) // piece, deep // piece)] = (
            got.astype(low).reshape(deep // piece, piece, units)
        )
        return 0

    def make_reduce_grad():
        if dw_red.shape[0] == 4:
            tiles = turns // 8

            def make(slot, half):
                first = (slot * 2 + half) * tiles
                lax.fori_loop(first, first + tiles, reduce_grad, 0)

            start_red.as_made(make)
        else:
            lax.fori_loop(0, turns, reduce_grad, 0)
            start_red()

    def save_dw(i, half):
        at = pl.ds(pl.multiple_of(i * deep, deep), deep)
        return pltpu.make_async_copy(
            dw_ref.at[lax.rem(i, 2), half], (gate_out, up_out)[half].at[at], dw_sem.at[lax.rem(i, 2), half]
        )

    def expand_grad(i, _):
        at = pl.ds(pl.multiple_of(i * deep, deep), deep)
        for half in range(2):
            pl.when(i >= 2)(lambda: save_dw(i - 2, half).wait())
            dw_ref[lax.rem(i, 2), half] = lax.dot_general(
                h2_ref[:, at], grad_ref[:, half * units : (half + 1) * units], over_rows,
                preferred_element_type=f32,
            ).astype(low)
            save_dw(i, half).start()
        return 0

    last = 2 * chips - 3
    done = 0
    for turn in range(1, last + 1):
        if turn < chips:
            pass_on(turn)

            @pl.when(z - turn >= 0)
            def _():
                from_side(z - turn)
                forward(z - turn)
                put_at(z - turn, backward, w_ref)

            @pl.when(z + turn < chips)
            def _():
                from_side(z + turn)
                forward(z + turn)
                put_at(z + turn, backward, w_ref)

        hop_up(turn - z)
        hop_down(2 * (chips - 1) - z - turn)
        if turn == chips - 1:
            make_reduce_grad()
        elif turn >= chips:
            until = turns * (turn - chips + 1) // (last - chips + 1)
            lax.fori_loop(done, until, expand_grad, 0)
            done = until
    middle_red()
    finish()
    inverse = inverse_ref[...]
    middle_grad, gain = norm_backward(grad_out[...], x1_ref[...] * inverse, inverse, gain_ref[...])
    grad_x1 = cotangent_ref[...].astype(f32) + middle_grad
    grad_out[...] = grad_x1
    low_out[...] = grad_x1.astype(low)
    gain_out[...] = gain[None]
    wait_red()
    sent()
    for y in range(chips):
        save(y).wait()
    for i in range(max(0, turns - 2), turns):
        for half in range(2):
            save_dw(i, half).wait()


def feed_forward(
    cid, h2, x1, inverse, gain, cotangent, w_gu, w_red, g_all, cuts=2, tile=1024
):
    nr, nb = lax.axis_size("rows"), lax.axis_size("blk")
    seq, width = g_all.shape
    both = w_gu.shape[1]
    units = both // 2
    t = seq // nb
    piece = width // (nr * nb)
    dma, f32, bf16 = pltpu.SemaphoreType.DMA, jnp.float32, jnp.bfloat16
    half = jax.ShapeDtypeStruct((width, units), bf16)
    slots, sems = (5, 6) if nr == 4 else (nr, nr)
    return pl.pallas_call(
        functools.partial(feed_forward_kernel, nb // 2, cuts, tile),
        out_shape=[
            jax.ShapeDtypeStruct((t, width), f32),
            jax.ShapeDtypeStruct((t, width), bf16),
            jax.ShapeDtypeStruct((1, width), f32),
            jax.ShapeDtypeStruct((seq, units), bf16),
            half,
            half,
            jax.ShapeDtypeStruct((nb, piece, units), bf16),
        ],
        in_specs=[VMEM] * 5 + [ANY] * 3,
        out_specs=[VMEM] * 3 + [ANY] * 4,
        scratch_shapes=[
            pltpu.VMEM((seq, width), bf16),
            pltpu.VMEM((seq, units), bf16),
            pltpu.VMEM((seq, both), bf16),
            pltpu.VMEM((width, both), bf16),
            pltpu.VMEM((width, units), bf16),
            pltpu.VMEM((seq, width), bf16),
            pltpu.VMEM((nr, nb, piece, units), bf16),
            pltpu.VMEM((2, 2, 256, units), bf16),
            pltpu.VMEM((slots, nb, piece, units), bf16),
            dma((3,)),
            dma((nb // 2,)),
            dma((2, 2)),
            dma((4,)) if nr == 4 else dma,
            dma((sems,)),
            dma((sems,)),
        ]
        + gather_sems(nb, cuts)
        + scatter_scratch(nb // 2, cuts, t, width),
        compiler_params=params(cid),
        cost_estimate=cost(9 * seq * width * both),
    )(h2, x1, inverse, gain[None], cotangent, w_gu, w_red, g_all)


def attend_out_kernel(chips, cuts, tile, extras, a_ref, w_ref, x_ref, gain_ref, *refs):
    n = extras.n
    srcs, (x1_ref, inverse_ref, h2_ref), dsts, refs = (
        refs[:n], refs[n : n + 3], refs[3 + n : 3 + 2 * n], refs[3 + 2 * n :],
    )
    put, _, hop, finish = scatter_task(chips, cuts, tile, x1_ref, refs[:4], refs[4:10])
    start_swaps, start_rows, middle, wait_rows, wait_swaps = extras.tasks(srcs, dsts, refs[10:])
    greet(chips, False, extras.rows)
    start_rows()
    for s in range(chips):
        put(s, lambda rows: a_ref.at[rows], w_ref)
        if s < chips - 1:
            hop(s)
    middle()
    finish()
    x1 = x_ref[...].astype(jnp.float32) + x1_ref[...]
    x1_ref[...] = x1
    _, inverse_ref[...], h2_ref[...] = norm_forward(x1, gain_ref[...])
    wait_rows()


def norm_forward(values, gain_vector):
    inverse = lax.rsqrt(jnp.mean(values * values, axis=-1, keepdims=True) + norm_eps)
    unit_values = values * inverse
    return (unit_values, inverse, (unit_values * gain_vector).astype(jnp.bfloat16))


def norm_backward(grad_normed, unit_values, inverse, gain_vector):
    grad_unit = grad_normed * gain_vector
    grad_values = inverse * (
        grad_unit - unit_values * jnp.mean(grad_unit * unit_values, axis=-1, keepdims=True)
    )
    return (grad_values, jnp.sum(grad_normed * unit_values, axis=0))


def contract_last(left, right):
    return lax.dot_general(
        left, right, (((1,), (1,)), ((), ())), preferred_element_type=jnp.float32
    )


def adam_step(master, moment_one, moment_two, gradient):
    moment_one = beta_one * moment_one + (1.0 - beta_one) * gradient
    moment_two = beta_two * moment_two + (1.0 - beta_two) * gradient * gradient
    update = (
        moment_one
        / (1.0 - beta_one**step_count)
        / (jnp.sqrt(moment_two / (1.0 - beta_two**step_count)) + adam_eps)
    )
    return (master - learn_rate * (update + decay_rate * master), moment_one, moment_two)


def moment_step(moment_one, moment_two, gradient):
    moment_one = beta_one * moment_one + (1.0 - beta_one) * gradient
    moment_two = beta_two * moment_two + (1.0 - beta_two) * gradient * gradient
    return (moment_one, moment_two)


def once(*shape):
    return pl.BlockSpec(shape, lambda i: (0,) * len(shape), pipeline_mode=pl.Buffered(1))


def partner(values):
    width = values.shape[1]
    half = HEAD_DIM // 2
    feature = lax.broadcasted_iota(jnp.int32, values.shape, 1) % HEAD_DIM
    return jnp.where(
        feature < half, pltpu.roll(values, width - half, 1), pltpu.roll(values, half, 1)
    )


def spread_table(table, width):
    return jnp.concatenate([table] * (width // table.shape[1]), axis=1)


def head_lanes(shape):
    return lax.broadcasted_iota(jnp.int32, shape, 1) // HEAD_DIM


def attend_kernel(
    chips, cuts, tile_o, extras, h1_hbm, w_hbm, cos_ref, sin_ref, q_place, k_place, length_ref, g_ref,
    x_ref, gain_ref, w_out_ref, *refs
):
    n = extras.n
    srcs, refs = refs[:n], refs[n:]
    (o_ref, q_ref, k_ref, v_ref, p_out, g_all, x1_ref, inverse_ref, h2_ref), refs = refs[:9], refs[9:]
    dsts, (h1_ref, w_ref, p_ref, load_sem, p_sem), refs = refs[:n], refs[n : n + 5], refs[n + 5 :]
    load, loaded = mover([(w_hbm, w_ref), (h1_hbm, h1_ref)], load_sem)
    begin, pass_on, from_side, local, sent = gather_task(chips, cuts, g_ref, g_all, refs[:5])
    put, _, hop, finish = scatter_task(chips, cuts, tile_o, x1_ref, refs[5:9], refs[9:15])
    start_swaps, start_rows, middle, wait_rows, wait_swaps = extras.tasks(srcs, dsts, refs[15:])
    step, steps = pl.program_id(0), pl.num_programs(0)
    seq, width = o_ref.shape
    tile = seq // chips
    f32, bf16 = jnp.float32, jnp.bfloat16
    table = need_order(chips)
    _, z, _ = line_place()

    @pl.when(step == 0)
    def _():
        load()
        greet(chips, False, extras.rows)
        begin()
        start_rows()
        loaded()

        def one(i, _):
            rows = pl.ds(pl.multiple_of(i * tile, tile), tile)
            mixed = jnp.dot(h1_ref[rows], w_ref[...], preferred_element_type=f32)
            cosine, sine = spread_table(cos_ref[rows], width), spread_table(sin_ref[rows], width)
            for at, ref in enumerate((q_ref, k_ref)):
                got = mixed[:, at * width : (at + 1) * width]
                ref[rows] = (got * cosine + partner(got) * sine).astype(bf16)
            v_ref[rows] = mixed[:, 2 * width :].astype(bf16)
            return 0

        lax.fori_loop(0, steps, one, 0)

    pl.when(step == steps - 1)(middle)

    @pl.when(step > 0)
    def _():
        pass_on(step)

    def rows_at(s):
        return pl.ds(pl.multiple_of(pick(table, z, s) * tile, tile), tile)

    def save(s):
        slot = lax.rem(s, 2)
        return pltpu.make_async_copy(p_ref.at[slot], p_out.at[:, rows_at(s)], p_sem.at[slot])

    pl.when(step >= 2)(lambda: save(step - 2).wait())
    rows = rows_at(step)
    queries = q_ref[rows] * jnp.asarray(1.0 / math.sqrt(HEAD_DIM), bf16)
    lanes = head_lanes((tile, width))
    place = q_place[rows]
    allowed = k_place[...] <= place
    out = jnp.zeros((tile, width), f32)
    for head in range(width // HEAD_DIM):
        here = lanes == head
        one_head = jnp.where(here, queries, jnp.zeros((), bf16))
        scores = lax.dot_general(
            one_head, k_ref[...], (((1,), (1,)), ((), ())), preferred_element_type=f32
        )
        scores = jnp.where(allowed, scores, neg_large)
        weights = jnp.exp(scores - jnp.max(scores, axis=-1, keepdims=True))
        weights = weights * (1.0 / jnp.sum(weights, axis=-1, keepdims=True))
        low = weights.astype(bf16)
        p_ref[lax.rem(step, 2), head] = low
        out = jnp.where(here, jnp.dot(low, v_ref[...], preferred_element_type=f32), out)
    save(step).start()
    o_ref[rows] = jnp.where(place < length_ref[0], out, 0.0).astype(bf16)
    put(step, lambda rows: o_ref.at[rows], w_out_ref)
    pl.when(step < steps - 1)(lambda: hop(step))

    @pl.when(step == steps - 1)
    def _():
        finish()
        x1 = x_ref[...].astype(f32) + x1_ref[...]
        x1_ref[...] = x1
        _, inverse_ref[...], h2_ref[...] = norm_forward(x1, gain_ref[...])
        for s in range(max(0, chips - 2), chips):
            save(s).wait()
        local().wait()
        for y in range(chips):
            from_side(y)
        sent()
        wait_rows()


def attend(
    cid, h1_all, w_in, cosine, sine, place, live_place, length, g, x, gain, w_out, extras, cuts=2, tile_o=1024
):
    seq, wide = h1_all.shape
    width = w_in.shape[1] // 3
    heads = width // HEAD_DIM
    nb = lax.axis_size("blk")
    chips = nb // 2
    tile = seq // chips
    t = x.shape[0]
    full = jax.ShapeDtypeStruct((seq, width), jnp.bfloat16)
    return pl.pallas_call(
        functools.partial(attend_kernel, chips, cuts, tile_o, extras),
        grid=(chips,),
        in_specs=[
            ANY, ANY, once(seq, 2 * HEAD_DIM), once(seq, 2 * HEAD_DIM), once(seq, 1), once(1, seq),
            pl.BlockSpec(memory_space=pltpu.SMEM),
            once(*g.shape), once(t, wide), once(1, wide), once(wide, width),
        ]
        + extras.specs,
        out_specs=[once(seq, width)] * 4
        + [ANY, ANY, once(t, wide), once(t, 1), once(t, wide)]
        + extras.specs,
        out_shape=[full] * 4
        + [
            jax.ShapeDtypeStruct((heads, seq, seq), jnp.bfloat16),
            jax.ShapeDtypeStruct((seq, g.shape[1]), g.dtype),
            jax.ShapeDtypeStruct((t, wide), jnp.float32),
            jax.ShapeDtypeStruct((t, 1), jnp.float32),
            jax.ShapeDtypeStruct((t, wide), jnp.bfloat16),
        ]
        + extras.shapes,
        scratch_shapes=[
            pltpu.VMEM(h1_all.shape, h1_all.dtype),
            pltpu.VMEM(w_in.shape, w_in.dtype),
            pltpu.VMEM((2, heads, tile, seq), jnp.bfloat16),
            pltpu.SemaphoreType.DMA((2,)),
            pltpu.SemaphoreType.DMA((2,)),
        ]
        + gather_sems(nb, cuts)
        + scatter_scratch(chips, cuts, t, wide)
        + extras.scratch,
        compiler_params=params(cid),
        cost_estimate=cost(4 * seq * seq * width + 6 * seq * wide * width),
    )(
        h1_all, w_in, cosine, sine, place, live_place, length.reshape(1), g, x, gain[None], w_out,
        *extras.operands,
    )


def attend_back_kernel(
    chips, cuts, tile_y, extras, q_ref, k_ref, v_ref, o_all, cos_ref, sin_ref, q_place, length_ref, x_ref,
    w_out_ref, p_hbm, hidden_hbm, red_hbm, h1_hbm, *refs
):
    n = extras.n
    srcs, (mixed_ref, y_ref, dw_ref), dsts = refs[:n], refs[n : n + 3], refs[n + 3 : 2 * n + 3]
    refs = refs[2 * n + 3 :]
    (
        branch_ref, p_ref, ds_ref, qm_ref, gm_ref, dk_acc, dv_acc, hidden_ref, red_ref, h1_ref, load_sem, p_sem,
    ), refs = refs[:12], refs[12:]
    begin, pass_on, from_side, local, sent = gather_task(chips, cuts, x_ref, branch_ref, refs[:5])
    put, _, hop, finish = scatter_task(chips, cuts, tile_y, y_ref, refs[5:9], refs[9:15])
    start_swaps, start_rows, middle, wait_rows, wait_swaps = extras.tasks(srcs, dsts, refs[15:])
    one_buffer = h1_ref.shape != branch_ref.shape
    h1_ref = branch_ref if one_buffer else h1_ref
    load, loaded = mover([(red_hbm, red_ref), (hidden_hbm, hidden_ref), (h1_hbm, h1_ref)], load_sem)
    step, steps = pl.program_id(0), pl.num_programs(0)
    seq, width = q_ref.shape
    tile = seq // chips
    f32, bf16 = jnp.float32, jnp.bfloat16
    factor = 1.0 / math.sqrt(HEAD_DIM)
    over_rows = (((0,), (0,)), ((), ()))
    table = arrival_order(chips)
    _, z, _ = line_place()

    def rows_at(s):
        return pl.ds(pl.multiple_of(pick(table, z, s) * tile, tile), tile)

    def p_load(s):
        slot = lax.rem(s, 2)
        return pltpu.make_async_copy(p_hbm.at[:, rows_at(s)], p_ref.at[slot], p_sem.at[slot])

    @pl.when(step == 0)
    def _():
        p_load(step).start()
        load(0, 1)
        if not one_buffer:
            load(2)
        greet(chips, True, extras.rows)
        begin()
        start_rows()
        dk_acc[...] = jnp.zeros_like(dk_acc)
        dv_acc[...] = jnp.zeros_like(dv_acc)
        loaded(0, 1)
        local().wait()

    pl.when(step < steps - 1)(lambda: p_load(step + 1).start())
    put(step, lambda rows: hidden_ref.at[rows], red_ref)
    pl.when(step == 0)(lambda: hop(step))

    @pl.when(step > 0)
    def _():
        pass_on(step)

    pl.when(step == steps // 2)(start_swaps)
    pl.when(step == steps - 1)(middle)
    from_side(pick(table, z, step))
    rows = rows_at(step)
    lanes = head_lanes((tile, width))
    nothing = jnp.zeros((), bf16)
    grad = jnp.dot(branch_ref[rows], w_out_ref[...], preferred_element_type=f32).astype(bf16)
    grad = jnp.where(q_place[rows] < length_ref[0], grad, nothing)
    both = grad.astype(f32) * o_all[rows].astype(f32)
    queries = q_ref[rows]
    grad_q = jnp.zeros((tile, width), f32)
    p_load(step).wait()
    low = p_ref.at[lax.rem(step, 2)]
    heads = width // HEAD_DIM
    for head in range(heads):
        here = lanes == head
        block = pl.ds(head * tile, tile)
        delta = jnp.sum(jnp.where(here, both, 0.0), axis=-1, keepdims=True)
        one_grad = jnp.where(here, grad, nothing)
        gm_ref[block] = one_grad
        qm_ref[block] = jnp.where(here, queries, nothing)
        grad_p = lax.dot_general(
            one_grad, v_ref[...], (((1,), (1,)), ((), ())), preferred_element_type=f32
        )
        grad_s = (low[head].astype(f32) * (grad_p - delta)).astype(bf16)
        ds_ref[block] = grad_s
        grad_q = jnp.where(here, jnp.dot(grad_s, k_ref[...], preferred_element_type=f32), grad_q)
    dv_acc[...] += lax.dot_general(
        low[...].reshape(heads * tile, seq), gm_ref[...], over_rows, preferred_element_type=f32
    )
    dk_acc[...] += lax.dot_general(ds_ref[...], qm_ref[...], over_rows, preferred_element_type=f32)

    def back(value, cosine, sine):
        value = (value * factor).astype(bf16).astype(f32)
        cosine, sine = spread_table(cosine, width), spread_table(sine, width)
        return (value * cosine - partner(value) * sine).astype(bf16)

    mixed_ref[rows, :width] = back(grad_q, cos_ref[rows], sin_ref[rows])
    pl.when((step > 0) & (step < steps - 1))(lambda: hop(step))

    @pl.when(step == steps - 1)
    def _():
        mixed_ref[:, width : 2 * width] = back(dk_acc[...], cos_ref[...], sin_ref[...])
        mixed_ref[:, 2 * width :] = dv_acc[...].astype(bf16)
        deep = 256

        def out_grad(i, _):
            at = pl.ds(pl.multiple_of(i * deep, deep), deep)
            dw_ref[at, 3 * width :] = lax.dot_general(
                branch_ref[:, at], o_all[...], over_rows, preferred_element_type=f32
            ).astype(bf16)
            return 0

        def in_grad(i, _):
            at = pl.ds(pl.multiple_of(i * deep, deep), deep)
            dw_ref[at, : 3 * width] = lax.dot_general(
                h1_ref[:, at], mixed_ref[...], over_rows, preferred_element_type=f32
            ).astype(bf16)
            return 0

        turns = dw_ref.shape[0] // deep
        lax.fori_loop(0, turns, out_grad, 0)
        if one_buffer:
            sent()
            load(2)
        loaded(2)
        lax.fori_loop(0, turns, in_grad, 0)
        wait_rows()
        finish()
        if not one_buffer:
            sent()
        wait_swaps()


def attend_back(
    cid, q, k, v, o, p, cosine, sine, place, length, branch, w_out, hidden, w_red, h1_all, extras, cuts=2
):
    seq, width = q.shape
    heads = width // HEAD_DIM
    nb = lax.axis_size("blk")
    chips = nb // 2
    tile = seq // chips
    wide, units = w_red.shape
    t = seq // nb
    full = once(seq, width)
    f32, bf16 = jnp.float32, jnp.bfloat16
    loads = (hidden, w_red, h1_all)
    dma = pltpu.SemaphoreType.DMA
    return pl.pallas_call(
        functools.partial(attend_back_kernel, chips, cuts, 1024, extras),
        grid=(chips,),
        in_specs=[
            full, full, full, full, once(seq, 2 * HEAD_DIM), once(seq, 2 * HEAD_DIM), once(seq, 1),
            pl.BlockSpec(memory_space=pltpu.SMEM), once(t, wide), once(wide, width),
        ]
        + [ANY] * 4
        + extras.specs,
        out_specs=[once(seq, 3 * width), once(t, wide), once(wide, 4 * width)] + extras.specs,
        out_shape=[
            jax.ShapeDtypeStruct((seq, 3 * width), bf16),
            jax.ShapeDtypeStruct((t, wide), f32),
            jax.ShapeDtypeStruct((wide, 4 * width), bf16),
        ]
        + extras.shapes,
        scratch_shapes=[
            pltpu.VMEM((seq, wide), bf16),
            pltpu.VMEM((2, heads, tile, seq), bf16),
            pltpu.VMEM((heads * tile, seq), bf16),
            pltpu.VMEM((heads * tile, width), bf16),
            pltpu.VMEM((heads * tile, width), bf16),
            pltpu.VMEM((seq, width), f32),
            pltpu.VMEM((seq, width), f32),
        ]
        + [pltpu.VMEM(value.shape, value.dtype) for value in loads[:2]]
        + [pltpu.VMEM(h1_all.shape if seq <= 1024 else (16, 128), bf16)]
        + [dma((3,)), dma((2,))]
        + gather_sems(nb, cuts)
        + scatter_scratch(chips, cuts, t, wide)
        + extras.scratch,
        compiler_params=params(cid),
        cost_estimate=cost(10 * seq * seq * width),
    )(q, k, v, o, cosine, sine, place, length.reshape(1), branch, w_out, p, *loads, *extras.operands)


def arrange(weight, out, parts):
    nb, _, wide = out.shape
    span = wide // parts
    for j in range(nb):
        for part in range(parts):
            at = (part * nb + j) * span
            out[j, :, part * span : (part + 1) * span] = weight[:, at : at + span].astype(out.dtype)


def first_kernel(chips, cuts, parts, map_ref, tokens_ref, gain_ref, frequency_ref, *refs):
    n = len(parts)
    refs = list(refs)

    def take(count):
        return [refs.pop(0) for _ in range(count)]

    sources, h1_all, swapped, gathered = take(n), take(1)[0], take(n), take(n - 1)
    inverse_ref, place_ref, cos_ref, sin_ref = take(4)
    weights, held, (h1_ref, load_sem) = take(n), take(n), take(2)
    swaps = [swap_task(a, b, *take(3)) for a, b in zip(held, swapped)]
    task = square_gather if gathered[0].shape[0] == 4 else direct_gather
    rows = [task(a, b, *take(4)) for a, b in zip(swapped, gathered)]
    begin, pass_on, from_side, local, sent = gather_task(chips, cuts, h1_ref, h1_all, refs)
    load, loaded = mover(list(zip(sources, weights)), load_sem)
    load()
    greet(chips, True, True)
    for i in range(n - 1):
        loaded(i)
        arrange(weights[i], held[i], parts[i])
        swaps[i][0]()
    _, inverse_ref[...], h1_ref[...] = norm_forward(
        tokens_ref[...].astype(jnp.float32), gain_ref[...]
    )
    loaded(n - 1)
    arrange(weights[n - 1], held[n - 1], parts[n - 1])
    blocks = map_ref.shape[1]
    block = place_ref.shape[0] // blocks
    lanes = cos_ref.shape[1]
    front = lax.broadcasted_iota(jnp.int32, (block, lanes), 1) % HEAD_DIM < HEAD_DIM // 2
    for j in range(blocks):
        at = slice(j * block, (j + 1) * block)
        place = map_ref[0, j] * block + lax.broadcasted_iota(jnp.int32, (block, lanes), 0)
        place_ref[at] = place[:, :1]
        angle = place.astype(jnp.float32) * frequency_ref[...]
        cos_ref[at] = jnp.cos(angle)
        sine = jnp.sin(angle)
        sin_ref[at] = jnp.where(front, -sine, sine)
    for i in range(n - 2):
        swaps[i][1]()
        rows[i][0]()
    swaps[n - 2][1]()
    rows[n - 2][0]()
    begin()
    for k in range(1, chips):
        if k == min(3, chips - 1):
            swaps[n - 1][0]()
        pass_on(k)
    for _, middle, _ in rows:
        middle()
    local().wait()
    for y in range(chips):
        from_side(y)
    sent()
    for _, _, wait in rows:
        wait()
    swaps[n - 1][1]()


def first(cid, block_map, tokens, gain, weights, parts, cuts=4):
    nr, nb = lax.axis_size("rows"), lax.axis_size("blk")
    shapes = [(nb, value.shape[0], value.shape[1] // nb) for value in weights]
    n = len(weights)
    t, width = tokens.shape
    half = HEAD_DIM // 2
    frequency = jnp.exp(
        -jnp.arange(half, dtype=jnp.float32) * (2.0 / HEAD_DIM) * math.log(theta_base)
    )
    dma, f32, bf16 = pltpu.SemaphoreType.DMA, jnp.float32, jnp.bfloat16
    table = jax.ShapeDtypeStruct((nb * t, 2 * HEAD_DIM), f32)
    sems = 6 if nr == 4 else nr
    scratch = [pltpu.VMEM(value.shape, value.dtype) for value in weights]
    scratch += [pltpu.VMEM(shape, bf16) for shape in shapes]
    scratch += [pltpu.VMEM((t, width), bf16), dma((n,))]
    scratch += [dma, dma((nb,)), dma((nb,))] * n
    for shape in shapes[:-1]:
        scratch += [pltpu.VMEM(shape, bf16), dma, dma((sems,)), dma((sems,))]
    return pl.pallas_call(
        functools.partial(first_kernel, nb // 2, cuts, parts),
        out_shape=[jax.ShapeDtypeStruct((nb * t, width), bf16)]
        + [jax.ShapeDtypeStruct(shape, bf16) for shape in shapes]
        + [jax.ShapeDtypeStruct((nr,) + shape, bf16) for shape in shapes[:-1]]
        + [
            jax.ShapeDtypeStruct((t, 1), f32),
            jax.ShapeDtypeStruct((nb * t, 1), jnp.int32),
            table,
            table,
        ],
        in_specs=[pl.BlockSpec(memory_space=pltpu.SMEM)] + [VMEM] * 3 + [ANY] * n,
        out_specs=[ANY] * (2 * n) + [VMEM] * 4,
        scratch_shapes=scratch + gather_sems(nb, cuts),
        compiler_params=params(cid),
        cost_estimate=cost(0),
    )(block_map, tokens, gain[None], jnp.tile(frequency, 4)[None], *weights)


def total_task(nr, nb, x_ref, o_ref, held, rows_held, send_one, recv_one, send_two, recv_two):
    r, b = lax.axis_index("rows"), lax.axis_index("blk")
    across = [lax.rem(b + k, nb) for k in range(1, nb)]
    along = [lax.rem(r + k, nr) for k in range(1, nr)]

    def first(other, slot):
        return pltpu.make_async_remote_copy(
            src_ref=rows_held.at[r], dst_ref=rows_held.at[slot], send_sem=send_two.at[other],
            recv_sem=recv_two.at[slot], device_id=(other, b), device_id_type=MESH,
        )

    def second(other, slot):
        return pltpu.make_async_remote_copy(
            src_ref=held.at[b], dst_ref=held.at[slot], send_sem=send_one.at[other],
            recv_sem=recv_one.at[slot], device_id=(r, other), device_id_type=MESH,
        )

    def start():
        rows_held[r] = x_ref[...]
        for other in along:
            first(other, r).start()

    def middle():
        for other in along:
            first(other, other).wait_recv()
        held[b] = jnp.sum(rows_held[...], axis=0)
        for other in across:
            second(other, b).start()

    def finish():
        for other in across:
            second(other, other).wait_recv()
        o_ref[...] = jnp.sum(held[...], axis=0)
        for other in along:
            first(other, r).wait_send()
        for other in across:
            second(other, b).wait_send()

    return start, middle, finish


def last_scatter_kernel(
    chips, nr, cuts, tile, extras, a_ref, w_ref, x_ref, inverse_ref, gain_ref, resid_ref, gain_two_ref, h1_hbm, *refs
):
    n = extras.n
    srcs, refs = refs[:n], refs[n:]
    o_ref, total_ref, dsts, refs = refs[0], refs[1], refs[2 : 2 + n], refs[2 + n :]
    sum_ref, part_ref, h1_ref, load_sem, refs = refs[0], refs[1], refs[2], refs[3], refs[4:]
    put, _, hop, finish = scatter_task(chips, cuts, tile, sum_ref, refs[:4], refs[4:10])
    start_total, middle_total, finish_total = total_task(
        nr, 2 * chips, part_ref, total_ref, *refs[10:16]
    )
    start_swaps, start_rows, middle, wait_rows, wait_swaps = extras.tasks(srcs, dsts, refs[16:])
    load, loaded = mover([(h1_hbm, h1_ref)], load_sem)
    load()
    greet(chips, True, True)
    start_swaps()
    start_rows()
    part_ref[0:1] = jnp.zeros_like(part_ref[0:1])
    part_ref[1:2] = gain_two_ref[...]
    loaded()

    def seen(rows, cols, got):
        part_ref[0:1, cols] += jnp.sum(got * h1_ref[rows, cols].astype(jnp.float32), axis=0)[None]

    for s in range(chips):
        put(s, lambda rows: a_ref.at[rows], w_ref, seen)
        if s < chips - 1:
            hop(s)
    part_ref[0:1] = part_ref[0:1] / gain_ref[...]
    start_total()
    middle()
    middle_total()
    wait_rows()
    finish()
    inverse = inverse_ref[...]
    unit = x_ref[...].astype(jnp.float32) * inverse
    o_ref[...] = resid_ref[...] + norm_backward(sum_ref[...], unit, inverse, gain_ref[...])[0]
    finish_total()
    wait_swaps()


def last_scatter(cid, a, w, x, inverse, gain, resid, gain_two, h1_all, extras, cuts=2, tile=1024):
    nr, nb = lax.axis_size("rows"), lax.axis_size("blk")
    t, width = x.shape
    pair = (2, width)
    dma, f32 = pltpu.SemaphoreType.DMA, jnp.float32
    return pl.pallas_call(
        functools.partial(last_scatter_kernel, nb // 2, nr, cuts, tile, extras),
        out_shape=[jax.ShapeDtypeStruct((t, width), f32), jax.ShapeDtypeStruct(pair, f32)]
        + extras.shapes,
        in_specs=[VMEM] * 7 + [ANY] + extras.specs,
        out_specs=[VMEM] * 2 + extras.specs,
        scratch_shapes=[
            pltpu.VMEM((t, width), f32),
            pltpu.VMEM(pair, f32),
            pltpu.VMEM(h1_all.shape, h1_all.dtype),
            dma((1,)),
        ]
        + scatter_scratch(nb // 2, cuts, t, width)
        + [pltpu.VMEM((nb,) + pair, f32), pltpu.VMEM((nr,) + pair, f32)]
        + [dma((nb,))] * 2 + [dma((nr,))] * 2
        + extras.scratch,
        compiler_params=params(cid),
        cost_estimate=cost(2 * a.shape[0] * width * w.shape[1]),
    )(a, w, x, inverse, gain[None], resid, gain_two, h1_all, *extras.operands)


def step_kernel(parts, one_array, *refs):
    count = 1 if one_array else parts
    grads, refs = refs[:count], refs[count:]
    outs = len(refs) // 2
    rule = adam_step if outs == 3 else moment_step

    def go(grad):
        wide = grad.shape[2]
        for j in range(grad.shape[0]):
            cols = slice(j * wide, (j + 1) * wide)
            gradient = grad[j].astype(jnp.float32)
            for ref, value in zip(
                refs[outs:], rule(*[ref[:, cols] for ref in refs[:outs]], gradient)
            ):
                ref[:, cols] = value

    if one_array:
        go(grads[0])
        return
    for part, grad in enumerate(grads):
        pl.when(pl.program_id(0) == part)(functools.partial(go, grad))


def step(pieces, parts, states, first=0):
    one_array = not isinstance(pieces, list)
    pieces = [pieces] if one_array else pieces
    nb = pieces[0].shape[0]
    rows, columns = states[0].shape
    tile = min(rows, 64 if parts > 1 else 32)
    span = columns // parts
    at = pl.BlockSpec((tile, span), lambda part, i: (i, part))
    block = (nb, tile, span // nb)
    if one_array:
        grads = [pl.BlockSpec(block, lambda part, i: (0, i, first + part))]
    else:
        grads = [pl.BlockSpec(block, lambda part, i: (0, i, 0))] * parts
    outs = len(states)
    return pl.pallas_call(
        functools.partial(step_kernel, parts, one_array),
        grid=(parts, rows // tile),
        in_specs=grads + [at] * outs,
        out_specs=[at] * outs,
        out_shape=[jax.ShapeDtypeStruct((rows, columns), jnp.float32)] * outs,
        compiler_params=pltpu.CompilerParams(vmem_limit_bytes=60 * MIB),
        cost_estimate=pl.CostEstimate(
            flops=0, bytes_accessed=(8 * outs + 2) * rows * columns, transcendentals=0
        ),
    )(*pieces, *states)


def after(value, *others):
    return lax.optimization_barrier((value,) + others)[0]


def over_tokens(left, right):
    return lax.dot_general(
        left, right, (((0,), (0,)), ((), ())), preferred_element_type=jnp.float32
    )


def shards(
    tokens, cotangent, lengths, block_map, gain_attend, gain_expand,
    attend_in, attend_out, expand_in, reduce_out,
    attend_in_first, attend_out_first, expand_in_first, reduce_out_first,
    attend_in_second, attend_out_second, expand_in_second, reduce_out_second,
):
    nb = lax.axis_size("blk")
    length = lengths[0]
    h1_all, _, _, _, swap_gu, w_in, w_out, w_red, inverse_one, place, cosine, sine = first(
        2, block_map, tokens[0], gain_attend,
        (attend_in, attend_out.T, reduce_out.T, expand_in), (3, 1, 1, 2),
    )
    block_rows = tokens.shape[1] // 2
    row_place = (block_map[0][:, None] * block_rows + jnp.arange(block_rows)[None, :]).reshape(1, -1)
    live_place = jnp.where(row_place < length, row_place, jnp.int32(1 << 30))
    nr = lax.axis_size("rows")
    deep = nb * attend_in.shape[0]
    wide = tokens.shape[2]

    def flat(pieces):
        return pieces.reshape(deep, pieces.shape[2])

    w_in, w_out, w_red = [value.reshape(wide, value.shape[3]) for value in (w_in, w_out, w_red)]
    attended, q, k, v, p, g_all, x1, inverse_two, h2, w_gu = attend(
        4, h1_all, w_in, cosine, sine, place, live_place, length, cotangent[0],
        tokens[0], gain_expand, w_out, Extras([], [(flat(swap_gu), 0, deep)]),
    )
    w_gu = w_gu.reshape(wide, -1)

    def by_rows(gradient):
        return gradient.reshape(nr, nb, deep // nb, gradient.shape[1])

    grad_x1, branch, gain_two, hidden, part_gate, part_up, rows_reduce = feed_forward(
        6, h2, x1, inverse_two, gain_expand, cotangent[0], w_gu, w_red, g_all
    )
    grad_mixed, y, part_both, own_reduce, rows_gate, rows_up = attend_back(
        10, q, k, v, attended, p, cosine, sine, place, length, branch, w_out, hidden, w_red, h1_all,
        Extras([rows_reduce], [], [by_rows(part_gate), by_rows(part_up)]),
    )
    y = x1 + y
    grad_input, gains, own_gate, own_up, rows_both = last_scatter(
        11, grad_mixed, w_in, tokens[0], inverse_one, gain_attend, grad_x1, gain_two, h1_all,
        Extras([rows_gate, rows_up], [], [by_rows(part_both)]),
    )
    both = lax.all_to_all(rows_both, "blk", 0, 0, tiled=True)
    set_four = step(own_reduce, 1, (reduce_out.T, reduce_out_first.T, reduce_out_second.T))
    set_three = step([own_gate, own_up], 2, (expand_in, expand_in_first, expand_in_second))
    both = after(both, set_three[2], set_four[2])
    set_one = step(both, 3, (attend_in, attend_in_first, attend_in_second))
    set_two = step(both, 1, (attend_out_first.T, attend_out_second.T), 3)
    return (
        y.astype(jnp.bfloat16).reshape(tokens.shape),
        grad_input.reshape(tokens.shape),
        gains[0],
        gains[1],
        *set_one,
        *[value.T for value in set_two],
        *set_three,
        *[value.T for value in set_four],
    )


def solution(mesh):
    placed = (
        P("rows", "blk", None),
        P("rows", "blk", None),
        P("rows"),
        P("rows", None),
        P(),
        P(),
        P(("rows", "blk"), None),
        P(None, ("rows", "blk")),
        P(("rows", "blk"), None),
        P(None, ("rows", "blk")),
        P(("rows", "blk"), None),
        P(None, ("rows", "blk")),
        P(("rows", "blk"), None),
        P(None, ("rows", "blk")),
        P(("rows", "blk"), None),
        P(None, ("rows", "blk")),
        P(("rows", "blk"), None),
        P(None, ("rows", "blk")),
    )
    return jax.shard_map(
        shards,
        mesh=mesh,
        in_specs=placed,
        out_specs=(
            P("rows", "blk", None),
            P("rows", "blk", None),
            P(),
            P(),
            P(("rows", "blk"), None),
            P(("rows", "blk"), None),
            P(("rows", "blk"), None),
            P(None, ("rows", "blk")),
            P(None, ("rows", "blk")),
            P(("rows", "blk"), None),
            P(("rows", "blk"), None),
            P(("rows", "blk"), None),
            P(None, ("rows", "blk")),
            P(None, ("rows", "blk")),
            P(None, ("rows", "blk")),
        ),
        check_vma=False,
    )
```

```python
import functools
import math

import jax
import jax.numpy as jnp
from jax import lax
from jax.experimental import pallas as pl
from jax.experimental.pallas import tpu as pltpu
from jax.sharding import PartitionSpec as P

HEADS = 32
HEAD_DIM = 64
MESH = pl.DeviceIdType.MESH
MIB = 1 << 20

theta_base = 130000.0
norm_eps = 1e-05
neg_large = -1e30
beta_one = 0.9
beta_two = 0.95
learn_rate = 0.01
decay_rate = 0.1
adam_eps = 1e-08
step_count = 10


def line_place():
    b = lax.axis_index("blk")
    return lax.axis_index("rows"), b // 2, b % 2


def greet(chips, swaps=False, rows=False):
    r, z, c = line_place()
    barrier = pltpu.get_barrier_semaphore()
    count = 0

    def signal(row, b):
        pl.semaphore_signal(barrier, inc=1, device_id=(row, b), device_id_type=MESH)

    b, nb, nr = 2 * z + c, 2 * chips, lax.axis_size("rows")
    if rows:
        for k in range(1, nr):
            signal(lax.rem(r + k, nr), b)
        count = nr - 1
    if swaps:
        for k in range(1, nb):
            signal(r, lax.rem(b + k, nb))
        count = count + nb - 1
    else:
        signal(r, b + 1 - 2 * c)
        pl.when(z < chips - 1)(lambda: signal(r, b + 2))
        pl.when(z > 0)(lambda: signal(r, b - 2))
        count = count + 1 + (z < chips - 1).astype(jnp.int32) + (z > 0).astype(jnp.int32)
    pl.semaphore_wait(barrier, count)


def swap_task(src, dst, local, send, recv):
    r, b = lax.axis_index("rows"), lax.axis_index("blk")
    nb = src.shape[0]
    others = [lax.rem(b + k, nb) for k in range(1, nb)]

    def remote(other, slot):
        return pltpu.make_async_remote_copy(
            src_ref=src.at[other], dst_ref=dst.at[slot], send_sem=send.at[other],
            recv_sem=recv.at[slot], device_id=(r, other), device_id_type=MESH,
        )

    def start():
        for other in others:
            remote(other, b).start()
        pltpu.make_async_copy(src.at[b], dst.at[b], local).start()

    def wait():
        for other in others:
            remote(other, other).wait_recv()
        for other in others:
            remote(other, b).wait_send()
        pltpu.make_async_copy(src.at[b], dst.at[b], local).wait()

    return start, wait


def rows_copy(src, dst, send, recv, device):
    return pltpu.make_async_remote_copy(
        src_ref=src, dst_ref=dst, send_sem=send, recv_sem=recv,
        device_id=(device, lax.axis_index("blk")), device_id_type=MESH,
    )


def through(src, stage, dst, local):
    first = pltpu.make_async_copy(src, stage, local)
    second = pltpu.make_async_copy(stage, dst, local)

    def store():
        first.wait()
        second.start()

    return first.start, store, second.wait


def direct_gather(src, dst, stage, local, send, recv):
    r, nr = lax.axis_index("rows"), dst.shape[0]
    others = [lax.rem(r + k, nr) for k in range(1, nr)]
    load, store, stored = through(src, stage, dst.at[r], local)

    def start():
        for other in others:
            rows_copy(src, dst.at[r], send.at[other], recv.at[r], other).start()
        load()

    def wait():
        for other in others:
            rows_copy(src, dst.at[other], send.at[other], recv.at[other], other).wait()
        stored()

    return start, store, wait


def square_gather(src, dst, stage, local, send, recv):
    r = lax.axis_index("rows")
    half = src.shape[0] // 2
    load, store, stored = through(src, stage, dst.at[r], local)

    def near(sem, origin, device):
        return rows_copy(src, dst.at[origin], send.at[sem], recv.at[sem], device)

    def onward(sem, origin, device):
        part = dst.at[origin, pl.ds((sem - 2) * half, half)]
        return rows_copy(part, part, send.at[sem], recv.at[sem], device)

    def start():
        near(0, r, r ^ 1).start()
        near(1, r, r ^ 2).start()
        load()

    def middle():
        store()
        near(0, r ^ 1, r ^ 1).wait_recv()
        onward(2, r ^ 1, r ^ 2).start()
        near(1, r ^ 2, r ^ 2).wait_recv()
        onward(3, r ^ 2, r ^ 1).start()

    def wait():
        onward(2, r ^ 3, r ^ 2).wait_recv()
        onward(3, r ^ 3, r ^ 1).wait_recv()
        near(0, r, r ^ 1).wait_send()
        near(1, r, r ^ 2).wait_send()
        onward(2, r ^ 1, r ^ 2).wait_send()
        onward(3, r ^ 2, r ^ 1).wait_send()
        stored()

    return start, middle, wait


def direct_sum(src, dst, held, local, send, recv):
    r, nr = lax.axis_index("rows"), src.shape[0]
    others = [lax.rem(r + k, nr) for k in range(1, nr)]

    def start():
        for other in others:
            rows_copy(src.at[other], held.at[r], send.at[other], recv.at[r], other).start()
        pltpu.make_async_copy(src.at[r], held.at[r], local).start()

    def wait():
        for other in others:
            rows_copy(src.at[other], held.at[other], send.at[other], recv.at[other], other).wait()
        pltpu.make_async_copy(src.at[r], held.at[r], local).wait()

        def one(j, _):
            total = held[0, j].astype(jnp.float32)
            for slot in range(1, nr):
                total = total + held[slot, j].astype(jnp.float32)
            held[0, j] = total.astype(held.dtype)
            return 0

        lax.fori_loop(0, held.shape[1], one, 0)
        done = pltpu.make_async_copy(held.at[0], dst, local)
        done.start()
        done.wait()

    return start, lambda: None, wait


def square_sum(src, dst, held, local, send, recv):
    r = lax.axis_index("rows")
    half = src.shape[1] // 2
    parts = [(pl.ds(0, half), r ^ 1, r ^ 2), (pl.ds(half, half), r ^ 2, r ^ 1)]

    def out(i, k):
        at, one, two = parts[i]
        return rows_copy(
            src.at[one if k == 0 else r ^ 3, at], held.at[k, at], send.at[2 * i + k],
            recv.at[2 * i + k], one,
        )

    def own(i, k):
        at, one, two = parts[i]
        return pltpu.make_async_copy(
            src.at[r if k == 0 else two, at], held.at[2 + k, at], local.at[2 * i + k]
        )

    def onward(i):
        at, one, two = parts[i]
        return rows_copy(held.at[3, at], held.at[4, at], send.at[4 + i], recv.at[4 + i], two)

    def add(i, into, *slots):
        def one(j, _):
            j = i * half + j
            total = held[into, j].astype(jnp.float32)
            for slot in slots:
                total = total + held[slot, j].astype(jnp.float32)
            held[into, j] = total.astype(held.dtype)
            return 0

        lax.fori_loop(0, half, one, 0)

    def start():
        for i in range(2):
            for k in (1, 0):
                out(i, k).start()
                own(i, k).start()

    def start_as(make):
        for i, k in ((0, 1), (1, 1), (0, 0), (1, 0)):
            make((parts[i][1] if k == 0 else r ^ 3), i)
            out(i, k).start()
        for i, k in ((0, 1), (1, 1), (0, 0), (1, 0)):
            make((r if k == 0 else parts[i][2]), i)
            own(i, k).start()

    start.as_made = start_as

    def middle():
        for i in range(2):
            out(i, 1).wait_recv()
            own(i, 1).wait()
            add(i, 3, 1)
            onward(i).start()

    def wait():
        for i in range(2):
            out(i, 0).wait_recv()
            own(i, 0).wait()
            onward(i).wait_recv()
            add(i, 2, 0, 4)
        done = pltpu.make_async_copy(held.at[2], dst, local.at[0])
        done.start()
        done.wait()
        for i in range(2):
            out(i, 0).wait_send()
            out(i, 1).wait_send()
            onward(i).wait_send()

    return start, middle, wait


class Extras:
    def __init__(self, swaps=(), gathers=(), scatters=()):
        nr, nb = lax.axis_size("rows"), lax.axis_size("blk")
        dma = pltpu.SemaphoreType.DMA
        self.swaps, self.gathers, self.scatters = len(swaps), [g[1:] for g in gathers], len(scatters)
        self.operands = [*swaps, *[g[0] for g in gathers], *scatters]
        self.n = len(self.operands)
        self.rows = bool(gathers) or bool(scatters)
        self.specs = [ANY] * self.n
        self.shapes = [like(value) for value in swaps]
        self.scratch = [dma, dma((nb,)), dma((nb,))] * len(swaps)
        self.square = nr == 4
        sems = 6 if self.square else nr
        for value, _, count in gathers:
            self.shapes.append(jax.ShapeDtypeStruct((nr, count, value.shape[1]), value.dtype))
            self.scratch += [pltpu.VMEM((count, value.shape[1]), value.dtype)]
            self.scratch += [dma, dma((sems,)), dma((sems,))]
        for value in scatters:
            self.shapes.append(jax.ShapeDtypeStruct(value.shape[1:], value.dtype))
            slots = 5 if self.square else nr
            local = dma((4,)) if self.square else dma
            self.scratch += [pltpu.VMEM((slots,) + value.shape[1:], value.dtype)]
            self.scratch += [local, dma((sems,)), dma((sems,))]

    def tasks(self, srcs, dsts, scratch):
        scratch = list(scratch)
        swaps, rows = [], []
        for i, (src, dst) in enumerate(zip(srcs, dsts)):
            if i < self.swaps:
                swaps.append(swap_task(src, dst, *scratch[:3]))
                scratch = scratch[3:]
            elif i < self.swaps + len(self.gathers):
                first, count = self.gathers[i - self.swaps]
                task = square_gather if self.square else direct_gather
                rows.append(task(src.at[pl.ds(first, count)], dst, *scratch[:4]))
                scratch = scratch[4:]
            else:
                task = square_sum if self.square else direct_sum
                rows.append(task(src, dst, *scratch[:4]))
                scratch = scratch[4:]

        def start_swaps():
            for start, _ in swaps:
                start()

        def start_rows():
            for start, _, _ in rows:
                start()

        def middle():
            for _, one, _ in rows:
                one()

        def wait_rows():
            for _, _, one in rows:
                one()

        def wait_swaps():
            for _, one in swaps:
                one()

        return start_swaps, start_rows, middle, wait_rows, wait_swaps


def like(value):
    return jax.ShapeDtypeStruct(value.shape, value.dtype)


ANY = pl.BlockSpec(memory_space=pl.ANY)
VMEM = pl.BlockSpec(memory_space=pltpu.VMEM)


def params(cid):
    return pltpu.CompilerParams(
        collective_id=cid, has_side_effects=True, vmem_limit_bytes=60 * MIB
    )


def cost(flops):
    return pl.CostEstimate(flops=flops, bytes_accessed=150_000_000, transcendentals=0)


def mover(pairs, sem):
    copies = [pltpu.make_async_copy(a, b, sem.at[i]) for i, (a, b) in enumerate(pairs)]

    def start(*which):
        for i in which or range(len(copies)):
            copies[i].start()

    def wait(*which):
        for i in which or range(len(copies)):
            copies[i].wait()

    return start, wait


def gather_task(chips, cuts, x_ref, o_ref, sems):
    copy_sem, send_up, send_down, send_side, recv = sems
    r, z, c = line_place()
    t = x_ref.shape[0]
    h = t // cuts
    up, down, side = (r, 2 * (z + 1) + c), (r, 2 * (z - 1) + c), (r, 2 * z + 1 - c)
    has_up, has_down = z < chips - 1, z > 0
    mine = 2 * z + c

    def piece(j, q):
        return o_ref.at[pl.ds(pl.multiple_of(j * t + q * h, h), h)]

    def remote(src, j, q, sem, dev):
        return pltpu.make_async_remote_copy(
            src_ref=src, dst_ref=piece(j, q), send_sem=sem.at[j, q], recv_sem=recv.at[j, q],
            device_id=dev, device_id_type=MESH,
        )

    def local():
        whole = o_ref.at[pl.ds(pl.multiple_of(mine * t, t), t)]
        return pltpu.make_async_copy(x_ref, whole, copy_sem)

    def start():
        for q in range(cuts):
            from_here = x_ref.at[pl.ds(q * h, h)]
            pl.when(has_up)(lambda: remote(from_here, mine, q, send_up, up).start())
            pl.when(has_down)(lambda: remote(from_here, mine, q, send_down, down).start())
            remote(from_here, mine, q, send_side, side).start()
        local().start()

    def hop(k):
        for q in range(cuts):
            @pl.when(z - k >= 0)
            def _():
                j = 2 * (z - k) + c
                remote(piece(j, q), j, q, send_up, up).wait_recv()
                pl.when(has_up)(lambda: remote(piece(j, q), j, q, send_up, up).start())
                remote(piece(j, q), j, q, send_side, side).start()

            @pl.when(z + k < chips)
            def _():
                j = 2 * (z + k) + c
                remote(piece(j, q), j, q, send_down, down).wait_recv()
                pl.when(has_down)(lambda: remote(piece(j, q), j, q, send_down, down).start())
                remote(piece(j, q), j, q, send_side, side).start()

    def from_side(y):
        for q in range(cuts):
            j = 2 * y + 1 - c
            remote(piece(j, q), j, q, send_side, side).wait_recv()

    def finish():
        for y in range(chips):
            j = 2 * y + c
            for q in range(cuts):
                pl.when(has_up & (z >= y))(
                    lambda: remote(piece(j, q), j, q, send_up, up).wait_send()
                )
                pl.when(has_down & (z <= y))(
                    lambda: remote(piece(j, q), j, q, send_down, down).wait_send()
                )
                remote(piece(j, q), j, q, send_side, side).wait_send()

    return start, hop, from_side, local, finish


def gather_sems(nb, cuts):
    return [pltpu.SemaphoreType.DMA] + [pltpu.SemaphoreType.DMA((nb, cuts))] * 4


def arrival_order(chips):
    table = []
    for z in range(chips):
        row = [z]
        for k in range(1, chips):
            row += [y for y in (z - k, z + k) if 0 <= y < chips]
        table.append(row)
    return table


def need_order(chips):
    table = []
    for z in range(chips):
        need = {
            y: (chips - 1 + z - y) if y > z else (chips - 1 - z + y)
            for y in range(chips) if y != z
        }
        table.append(sorted(need, key=lambda y: need[y]) + [z])
    return table


def pick(table, z, k):
    out = 0
    for at, row in enumerate(table):
        for step, block in enumerate(row):
            out = out + jnp.where((z == at) & (k == step), block, 0)
    return out


def scatter_task(chips, cuts, tile, o_ref, bufs, sems):
    mine, away, side_buf, line_buf = bufs
    send_side, recv_side, send_up, recv_up, send_down, recv_down = sems
    r, z, c = line_place()
    t, width = o_ref.shape
    low, f32 = away.dtype, jnp.float32
    up, down, side = (r, 2 * (z + 1) + c), (r, 2 * (z - 1) + c), (r, 2 * z + 1 - c)
    has_up, has_down = z < chips - 1, z > 0
    h = t // cuts
    table = need_order(chips)

    def remote(src, dst, y, q, send, recv, dev):
        return pltpu.make_async_remote_copy(
            src_ref=src.at[y, pl.ds(q * h, h)], dst_ref=dst.at[y, pl.ds(q * h, h)],
            send_sem=send.at[y, q], recv_sem=recv.at[y, q], device_id=dev, device_id_type=MESH,
        )

    def to_side(y, q):
        return remote(away, side_buf, y, q, send_side, recv_side, side)

    def along(y, slot, q, send, recv, dev):
        return pltpu.make_async_remote_copy(
            src_ref=mine.at[y, pl.ds(q * h, h)], dst_ref=line_buf.at[slot, pl.ds(q * h, h)],
            send_sem=send.at[y, q], recv_sem=recv.at[y, q], device_id=dev, device_id_type=MESH,
        )

    def to_up(y, q):
        return along(y, y, q, send_up, recv_up, up)

    def to_down(y, q):
        return along(y, jnp.where(y == z - 1, chips, y), q, send_down, recv_down, down)

    def from_up(y, q):
        return along(y, jnp.where(y == z, chips, y), q, send_down, recv_down, down)

    def rows(q):
        return pl.ds(q * h, h)

    def total(y, q):
        to_side(y, q).wait_recv()
        return mine[y, rows(q)].astype(f32) + side_buf[y, rows(q)].astype(f32)

    def put(s, rows_of, w_ref, seen=None):
        put_at(pick(table, z, s), rows_of, w_ref, seen)

    def put_at(y, rows_of, w_ref, seen=None):
        block = pl.ds(pl.multiple_of(2 * y * t, 2 * t), 2 * t)
        a = rows_of(block)

        def one(i, _):
            cols = pl.ds(pl.multiple_of(i * tile, tile), tile)
            got = lax.dot_general(
                a[...], w_ref[cols], (((1,), (1,)), ((), ())), preferred_element_type=f32
            )
            if seen is not None:
                seen(block, cols, got)
            got = got.astype(low)

            @pl.when(c == 0)
            def _():
                mine[y, :, cols] = got[:t]
                away[y, :, cols] = got[t:]

            @pl.when(c == 1)
            def _():
                mine[y, :, cols] = got[t:]
                away[y, :, cols] = got[:t]

            return 0

        lax.fori_loop(0, width // tile, one, 0)
        for q in range(cuts):
            to_side(y, q).start()

    def hop(s):
        hop_up(chips - 1 + z - s)
        hop_down(s - (chips - 1) + z)

    def hop_up(y):
        for q in range(cuts):
            @pl.when((y > z) & (y <= chips - 1))
            def _():
                now = total(y, q)

                @pl.when(has_down)
                def _():
                    to_up(y, q).wait_recv()
                    mine[y, rows(q)] = (now + line_buf[y, rows(q)].astype(f32)).astype(low)

                @pl.when(z == 0)
                def _():
                    mine[y, rows(q)] = now.astype(low)

                to_up(y, q).start()

    def hop_down(w):
        for q in range(cuts):
            @pl.when((w >= 0) & (w < z))
            def _():
                now = total(w, q)

                @pl.when(has_up)
                def _():
                    from_up(w, q).wait_recv()
                    mine[w, rows(q)] = (now + line_buf[w, rows(q)].astype(f32)).astype(low)

                @pl.when(z == chips - 1)
                def _():
                    mine[w, rows(q)] = now.astype(low)

                to_down(w, q).start()

    def finish():
        for q in range(cuts):
            o_ref[rows(q)] = total(z, q)
        for q in range(cuts):
            @pl.when(has_down)
            def _():
                to_up(z, q).wait_recv()
                o_ref[rows(q)] += line_buf[z, rows(q)].astype(f32)

            @pl.when(has_up)
            def _():
                from_up(z, q).wait_recv()
                o_ref[rows(q)] += line_buf[chips, rows(q)].astype(f32)

        for y in range(chips):
            for q in range(cuts):
                to_side(y, q).wait_send()
                pl.when(y > z)(lambda: to_up(y, q).wait_send())
                pl.when(y < z)(lambda: to_down(y, q).wait_send())

    return put, (put_at, hop_up, hop_down), hop, finish


def scatter_scratch(chips, cuts, t, width):
    return (
        [pltpu.VMEM((chips, t, width), jnp.bfloat16)] * 3
        + [pltpu.VMEM((chips + 1, t, width), jnp.bfloat16)]
        + [pltpu.SemaphoreType.DMA((chips, cuts))] * 6
    )


def feed_forward_kernel(
    chips, cuts, tile, h2_here, x1_ref, inverse_ref, gain_ref, cotangent_ref, w_hbm, red_hbm, g_hbm,
    grad_out, low_out, gain_out, hidden_out, gate_out, up_out, reduce_out,
    h2_ref, hidden_ref, grad_ref, w_ref, red_ref, g_ref, dw_red, dw_ref, red_held,
    load_sem, save_sem, dw_sem, red_local, red_send, red_recv, *refs
):
    begin, pass_on, from_side, local, sent = gather_task(chips, cuts, h2_here, h2_ref, refs[:5])
    _, (put_at, hop_up, hop_down), _, finish = scatter_task(chips, cuts, tile, grad_out, refs[5:9], refs[9:])
    task = square_sum if dw_red.shape[0] == 4 else direct_sum
    start_red, middle_red, wait_red = task(
        dw_red, reduce_out, red_held, red_local, red_send, red_recv
    )
    load, loaded = mover([(w_hbm, w_ref), (g_hbm, g_ref), (red_hbm, red_ref)], load_sem)
    r, z, c = line_place()
    t, width = h2_here.shape
    units = hidden_ref.shape[1]
    span = min(512, units)
    f32, low = jnp.float32, jnp.bfloat16
    over_rows = (((0,), (0,)), ((), ()))
    load()
    greet(chips, False, True)
    begin()

    def rows_of(y):
        return pl.ds(pl.multiple_of(y * 2 * t, 2 * t), 2 * t)

    def save(y):
        return pltpu.make_async_copy(
            hidden_ref.at[rows_of(y)], hidden_out.at[rows_of(y)], save_sem.at[y]
        )

    def columns(i):
        at, more = i * span, units + i * span
        return pl.ds(pl.multiple_of(at, span), span), pl.ds(pl.multiple_of(more, span), span)

    def forward(y):
        rows = rows_of(y)

        def one(i, _):
            cols, more = columns(i)
            gate = jnp.dot(h2_ref[rows], w_ref[:, cols], preferred_element_type=f32)
            up = jnp.dot(h2_ref[rows], w_ref[:, more], preferred_element_type=f32)
            sigmoid = jax.nn.sigmoid(gate)
            silu = gate * sigmoid
            hidden_ref[rows, cols] = (silu * up).astype(low)
            grad_ref[rows, cols] = (up * (sigmoid * (1.0 + gate * (1.0 - sigmoid)))).astype(low)
            grad_ref[rows, more] = silu.astype(low)
            return 0

        lax.fori_loop(0, units // span, one, 0)
        save(y).start()

    def backward(rows):
        def one(i, _):
            cols, more = columns(i)
            grad = jnp.dot(g_ref[rows], red_ref[:, cols], preferred_element_type=f32)
            grad_ref[rows, cols] = (grad * grad_ref[rows, cols].astype(f32)).astype(low)
            grad_ref[rows, more] = (grad * grad_ref[rows, more].astype(f32)).astype(low)
            return 0

        lax.fori_loop(0, units // span, one, 0)
        return grad_ref.at[rows]

    from_side(z)
    local().wait()
    loaded(0)
    forward(z)
    loaded(1, 2)
    put_at(z, backward, w_ref)
    deep = 256
    turns = width // deep
    piece = dw_red.shape[2]
    run = dw_red.shape[1] * piece

    def reduce_grad(i, _):
        at = pl.ds(pl.multiple_of(i * deep, deep), deep)
        got = lax.dot_general(g_ref[:, at], hidden_ref[...], over_rows, preferred_element_type=f32)
        first = i * deep
        dw_red[first // run, pl.ds(lax.rem(first, run) // piece, deep // piece)] = (
            got.astype(low).reshape(deep // piece, piece, units)
        )
        return 0

    def make_reduce_grad():
        if dw_red.shape[0] == 4:
            tiles = turns // 8

            def make(slot, half):
                first = (slot * 2 + half) * tiles
                lax.fori_loop(first, first + tiles, reduce_grad, 0)

            start_red.as_made(make)
        else:
            lax.fori_loop(0, turns, reduce_grad, 0)
            start_red()

    def save_dw(i, half):
        at = pl.ds(pl.multiple_of(i * deep, deep), deep)
        return pltpu.make_async_copy(
            dw_ref.at[lax.rem(i, 2), half], (gate_out, up_out)[half].at[at], dw_sem.at[lax.rem(i, 2), half]
        )

    def expand_grad(i, _):
        at = pl.ds(pl.multiple_of(i * deep, deep), deep)
        for half in range(2):
            pl.when(i >= 2)(lambda: save_dw(i - 2, half).wait())
            dw_ref[lax.rem(i, 2), half] = lax.dot_general(
                h2_ref[:, at], grad_ref[:, half * units : (half + 1) * units], over_rows,
                preferred_element_type=f32,
            ).astype(low)
            save_dw(i, half).start()
        return 0

    last = 2 * chips - 3
    done = 0
    for turn in range(1, last + 1):
        if turn < chips:
            pass_on(turn)

            @pl.when(z - turn >= 0)
            def _():
                from_side(z - turn)
                forward(z - turn)
                put_at(z - turn, backward, w_ref)

            @pl.when(z + turn < chips)
            def _():
                from_side(z + turn)
                forward(z + turn)
                put_at(z + turn, backward, w_ref)

        hop_up(turn - z)
        hop_down(2 * (chips - 1) - z - turn)
        if turn == chips - 1:
            make_reduce_grad()
        elif turn >= chips:
            until = turns * (turn - chips + 1) // (last - chips + 1)
            lax.fori_loop(done, until, expand_grad, 0)
            done = until
    middle_red()
    finish()
    inverse = inverse_ref[...]
    middle_grad, gain = norm_backward(grad_out[...], x1_ref[...] * inverse, inverse, gain_ref[...])
    grad_x1 = cotangent_ref[...].astype(f32) + middle_grad
    grad_out[...] = grad_x1
    low_out[...] = grad_x1.astype(low)
    gain_out[...] = gain[None]
    wait_red()
    sent()
    for y in range(chips):
        save(y).wait()
    for i in range(max(0, turns - 2), turns):
        for half in range(2):
            save_dw(i, half).wait()


def feed_forward(
    cid, h2, x1, inverse, gain, cotangent, w_gu, w_red, g_all, cuts=2, tile=1024
):
    nr, nb = lax.axis_size("rows"), lax.axis_size("blk")
    seq, width = g_all.shape
    both = w_gu.shape[1]
    units = both // 2
    t = seq // nb
    piece = width // (nr * nb)
    dma, f32, bf16 = pltpu.SemaphoreType.DMA, jnp.float32, jnp.bfloat16
    half = jax.ShapeDtypeStruct((width, units), bf16)
    slots, sems = (5, 6) if nr == 4 else (nr, nr)
    return pl.pallas_call(
        functools.partial(feed_forward_kernel, nb // 2, cuts, tile),
        out_shape=[
            jax.ShapeDtypeStruct((t, width), f32),
            jax.ShapeDtypeStruct((t, width), bf16),
            jax.ShapeDtypeStruct((1, width), f32),
            jax.ShapeDtypeStruct((seq, units), bf16),
            half,
            half,
            jax.ShapeDtypeStruct((nb, piece, units), bf16),
        ],
        in_specs=[VMEM] * 5 + [ANY] * 3,
        out_specs=[VMEM] * 3 + [ANY] * 4,
        scratch_shapes=[
            pltpu.VMEM((seq, width), bf16),
            pltpu.VMEM((seq, units), bf16),
            pltpu.VMEM((seq, both), bf16),
            pltpu.VMEM((width, both), bf16),
            pltpu.VMEM((width, units), bf16),
            pltpu.VMEM((seq, width), bf16),
            pltpu.VMEM((nr, nb, piece, units), bf16),
            pltpu.VMEM((2, 2, 256, units), bf16),
            pltpu.VMEM((slots, nb, piece, units), bf16),
            dma((3,)),
            dma((nb // 2,)),
            dma((2, 2)),
            dma((4,)) if nr == 4 else dma,
            dma((sems,)),
            dma((sems,)),
        ]
        + gather_sems(nb, cuts)
        + scatter_scratch(nb // 2, cuts, t, width),
        compiler_params=params(cid),
        cost_estimate=cost(9 * seq * width * both),
    )(h2, x1, inverse, gain[None], cotangent, w_gu, w_red, g_all)


def attend_out_kernel(chips, cuts, tile, extras, a_ref, w_ref, x_ref, gain_ref, *refs):
    n = extras.n
    srcs, (x1_ref, inverse_ref, h2_ref), dsts, refs = (
        refs[:n], refs[n : n + 3], refs[3 + n : 3 + 2 * n], refs[3 + 2 * n :],
    )
    put, _, hop, finish = scatter_task(chips, cuts, tile, x1_ref, refs[:4], refs[4:10])
    start_swaps, start_rows, middle, wait_rows, wait_swaps = extras.tasks(srcs, dsts, refs[10:])
    greet(chips, False, extras.rows)
    start_rows()
    for s in range(chips):
        put(s, lambda rows: a_ref.at[rows], w_ref)
        if s < chips - 1:
            hop(s)
    middle()
    finish()
    x1 = x_ref[...].astype(jnp.float32) + x1_ref[...]
    x1_ref[...] = x1
    _, inverse_ref[...], h2_ref[...] = norm_forward(x1, gain_ref[...])
    wait_rows()


def norm_forward(values, gain_vector):
    inverse = lax.rsqrt(jnp.mean(values * values, axis=-1, keepdims=True) + norm_eps)
    unit_values = values * inverse
    return (unit_values, inverse, (unit_values * gain_vector).astype(jnp.bfloat16))


def norm_backward(grad_normed, unit_values, inverse, gain_vector):
    grad_unit = grad_normed * gain_vector
    grad_values = inverse * (
        grad_unit - unit_values * jnp.mean(grad_unit * unit_values, axis=-1, keepdims=True)
    )
    return (grad_values, jnp.sum(grad_normed * unit_values, axis=0))


def contract_last(left, right):
    return lax.dot_general(
        left, right, (((1,), (1,)), ((), ())), preferred_element_type=jnp.float32
    )


def adam_step(master, moment_one, moment_two, gradient):
    moment_one = beta_one * moment_one + (1.0 - beta_one) * gradient
    moment_two = beta_two * moment_two + (1.0 - beta_two) * gradient * gradient
    update = (
        moment_one
        / (1.0 - beta_one**step_count)
        / (jnp.sqrt(moment_two / (1.0 - beta_two**step_count)) + adam_eps)
    )
    return (master - learn_rate * (update + decay_rate * master), moment_one, moment_two)


def moment_step(moment_one, moment_two, gradient):
    moment_one = beta_one * moment_one + (1.0 - beta_one) * gradient
    moment_two = beta_two * moment_two + (1.0 - beta_two) * gradient * gradient
    return (moment_one, moment_two)


def once(*shape):
    return pl.BlockSpec(shape, lambda i: (0,) * len(shape), pipeline_mode=pl.Buffered(1))


def partner(values):
    width = values.shape[1]
    half = HEAD_DIM // 2
    feature = lax.broadcasted_iota(jnp.int32, values.shape, 1) % HEAD_DIM
    return jnp.where(
        feature < half, pltpu.roll(values, width - half, 1), pltpu.roll(values, half, 1)
    )


def spread_table(table, width):
    return jnp.concatenate([table] * (width // table.shape[1]), axis=1)


def head_lanes(shape):
    return lax.broadcasted_iota(jnp.int32, shape, 1) // HEAD_DIM


def attend_kernel(
    chips, cuts, tile_o, extras, h1_hbm, w_hbm, cos_ref, sin_ref, q_place, k_place, length_ref, g_ref,
    x_ref, gain_ref, w_out_ref, *refs
):
    n = extras.n
    srcs, refs = refs[:n], refs[n:]
    (o_ref, q_ref, k_ref, v_ref, p_out, g_all, x1_ref, inverse_ref, h2_ref), refs = refs[:9], refs[9:]
    dsts, (h1_ref, w_ref, p_ref, load_sem, p_sem), refs = refs[:n], refs[n : n + 5], refs[n + 5 :]
    load, loaded = mover([(w_hbm, w_ref), (h1_hbm, h1_ref)], load_sem)
    begin, pass_on, from_side, local, sent = gather_task(chips, cuts, g_ref, g_all, refs[:5])
    put, _, hop, finish = scatter_task(chips, cuts, tile_o, x1_ref, refs[5:9], refs[9:15])
    start_swaps, start_rows, middle, wait_rows, wait_swaps = extras.tasks(srcs, dsts, refs[15:])
    step, steps = pl.program_id(0), pl.num_programs(0)
    seq, width = o_ref.shape
    tile = seq // chips
    f32, bf16 = jnp.float32, jnp.bfloat16
    table = need_order(chips)
    _, z, _ = line_place()

    @pl.when(step == 0)
    def _():
        load()
        greet(chips, False, extras.rows)
        begin()
        start_rows()
        loaded()

        def one(i, _):
            rows = pl.ds(pl.multiple_of(i * tile, tile), tile)
            mixed = jnp.dot(h1_ref[rows], w_ref[...], preferred_element_type=f32)
            cosine, sine = spread_table(cos_ref[rows], width), spread_table(sin_ref[rows], width)
            for at, ref in enumerate((q_ref, k_ref)):
                got = mixed[:, at * width : (at + 1) * width]
                ref[rows] = (got * cosine + partner(got) * sine).astype(bf16)
            v_ref[rows] = mixed[:, 2 * width :].astype(bf16)
            return 0

        lax.fori_loop(0, steps, one, 0)

    pl.when(step == steps - 1)(middle)

    @pl.when(step > 0)
    def _():
        pass_on(step)

    def rows_at(s):
        return pl.ds(pl.multiple_of(pick(table, z, s) * tile, tile), tile)

    def save(s):
        slot = lax.rem(s, 2)
        return pltpu.make_async_copy(p_ref.at[slot], p_out.at[:, rows_at(s)], p_sem.at[slot])

    pl.when(step >= 2)(lambda: save(step - 2).wait())
    rows = rows_at(step)
    queries = q_ref[rows] * jnp.asarray(1.0 / math.sqrt(HEAD_DIM), bf16)
    lanes = head_lanes((tile, width))
    place = q_place[rows]
    allowed = k_place[...] <= place
    out = jnp.zeros((tile, width), f32)
    for head in range(width // HEAD_DIM):
        here = lanes == head
        one_head = jnp.where(here, queries, jnp.zeros((), bf16))
        scores = lax.dot_general(
            one_head, k_ref[...], (((1,), (1,)), ((), ())), preferred_element_type=f32
        )
        scores = jnp.where(allowed, scores, neg_large)
        weights = jnp.exp(scores - jnp.max(scores, axis=-1, keepdims=True))
        weights = weights * (1.0 / jnp.sum(weights, axis=-1, keepdims=True))
        low = weights.astype(bf16)
        p_ref[lax.rem(step, 2), head] = low
        out = jnp.where(here, jnp.dot(low, v_ref[...], preferred_element_type=f32), out)
    save(step).start()
    o_ref[rows] = jnp.where(place < length_ref[0], out, 0.0).astype(bf16)
    put(step, lambda rows: o_ref.at[rows], w_out_ref)
    pl.when(step < steps - 1)(lambda: hop(step))

    @pl.when(step == steps - 1)
    def _():
        finish()
        x1 = x_ref[...].astype(f32) + x1_ref[...]
        x1_ref[...] = x1
        _, inverse_ref[...], h2_ref[...] = norm_forward(x1, gain_ref[...])
        for s in range(max(0, chips - 2), chips):
            save(s).wait()
        local().wait()
        for y in range(chips):
            from_side(y)
        sent()
        wait_rows()


def attend(
    cid, h1_all, w_in, cosine, sine, place, live_place, length, g, x, gain, w_out, extras, cuts=2, tile_o=1024
):
    seq, wide = h1_all.shape
    width = w_in.shape[1] // 3
    heads = width // HEAD_DIM
    nb = lax.axis_size("blk")
    chips = nb // 2
    tile = seq // chips
    t = x.shape[0]
    full = jax.ShapeDtypeStruct((seq, width), jnp.bfloat16)
    return pl.pallas_call(
        functools.partial(attend_kernel, chips, cuts, tile_o, extras),
        grid=(chips,),
        in_specs=[
            ANY, ANY, once(seq, 2 * HEAD_DIM), once(seq, 2 * HEAD_DIM), once(seq, 1), once(1, seq),
            pl.BlockSpec(memory_space=pltpu.SMEM),
            once(*g.shape), once(t, wide), once(1, wide), once(wide, width),
        ]
        + extras.specs,
        out_specs=[once(seq, width)] * 4
        + [ANY, ANY, once(t, wide), once(t, 1), once(t, wide)]
        + extras.specs,
        out_shape=[full] * 4
        + [
            jax.ShapeDtypeStruct((heads, seq, seq), jnp.bfloat16),
            jax.ShapeDtypeStruct((seq, g.shape[1]), g.dtype),
            jax.ShapeDtypeStruct((t, wide), jnp.float32),
            jax.ShapeDtypeStruct((t, 1), jnp.float32),
            jax.ShapeDtypeStruct((t, wide), jnp.bfloat16),
        ]
        + extras.shapes,
        scratch_shapes=[
            pltpu.VMEM(h1_all.shape, h1_all.dtype),
            pltpu.VMEM(w_in.shape, w_in.dtype),
            pltpu.VMEM((2, heads, tile, seq), jnp.bfloat16),
            pltpu.SemaphoreType.DMA((2,)),
            pltpu.SemaphoreType.DMA((2,)),
        ]
        + gather_sems(nb, cuts)
        + scatter_scratch(chips, cuts, t, wide)
        + extras.scratch,
        compiler_params=params(cid),
        cost_estimate=cost(4 * seq * seq * width + 6 * seq * wide * width),
    )(
        h1_all, w_in, cosine, sine, place, live_place, length.reshape(1), g, x, gain[None], w_out,
        *extras.operands,
    )


def attend_back_kernel(
    chips, cuts, tile_y, extras, q_ref, k_ref, v_ref, o_all, cos_ref, sin_ref, q_place, length_ref, x_ref,
    w_out_ref, p_hbm, hidden_hbm, red_hbm, h1_hbm, *refs
):
    n = extras.n
    srcs, (mixed_ref, y_ref, dw_ref), dsts = refs[:n], refs[n : n + 3], refs[n + 3 : 2 * n + 3]
    refs = refs[2 * n + 3 :]
    (
        branch_ref, p_ref, ds_ref, qm_ref, gm_ref, dk_acc, dv_acc, hidden_ref, red_ref, h1_ref, load_sem, p_sem,
    ), refs = refs[:12], refs[12:]
    begin, pass_on, from_side, local, sent = gather_task(chips, cuts, x_ref, branch_ref, refs[:5])
    put, _, hop, finish = scatter_task(chips, cuts, tile_y, y_ref, refs[5:9], refs[9:15])
    start_swaps, start_rows, middle, wait_rows, wait_swaps = extras.tasks(srcs, dsts, refs[15:])
    one_buffer = h1_ref.shape != branch_ref.shape
    h1_ref = branch_ref if one_buffer else h1_ref
    load, loaded = mover([(red_hbm, red_ref), (hidden_hbm, hidden_ref), (h1_hbm, h1_ref)], load_sem)
    step, steps = pl.program_id(0), pl.num_programs(0)
    seq, width = q_ref.shape
    tile = seq // chips
    f32, bf16 = jnp.float32, jnp.bfloat16
    factor = 1.0 / math.sqrt(HEAD_DIM)
    over_rows = (((0,), (0,)), ((), ()))
    table = arrival_order(chips)
    _, z, _ = line_place()

    def rows_at(s):
        return pl.ds(pl.multiple_of(pick(table, z, s) * tile, tile), tile)

    def p_load(s):
        slot = lax.rem(s, 2)
        return pltpu.make_async_copy(p_hbm.at[:, rows_at(s)], p_ref.at[slot], p_sem.at[slot])

    @pl.when(step == 0)
    def _():
        p_load(step).start()
        load(0, 1)
        if not one_buffer:
            load(2)
        greet(chips, True, extras.rows)
        begin()
        start_rows()
        dk_acc[...] = jnp.zeros_like(dk_acc)
        dv_acc[...] = jnp.zeros_like(dv_acc)
        loaded(0, 1)
        local().wait()

    pl.when(step < steps - 1)(lambda: p_load(step + 1).start())
    put(step, lambda rows: hidden_ref.at[rows], red_ref)

    @pl.when(step > 0)
    def _():
        pass_on(step)

    pl.when(step == steps // 2)(start_swaps)
    pl.when(step == steps - 1)(middle)
    from_side(pick(table, z, step))
    rows = rows_at(step)
    lanes = head_lanes((tile, width))
    nothing = jnp.zeros((), bf16)
    grad = jnp.dot(branch_ref[rows], w_out_ref[...], preferred_element_type=f32).astype(bf16)
    grad = jnp.where(q_place[rows] < length_ref[0], grad, nothing)
    both = grad.astype(f32) * o_all[rows].astype(f32)
    queries = q_ref[rows]
    grad_q = jnp.zeros((tile, width), f32)
    p_load(step).wait()
    low = p_ref.at[lax.rem(step, 2)]
    heads = width // HEAD_DIM
    for head in range(heads):
        here = lanes == head
        block = pl.ds(head * tile, tile)
        delta = jnp.sum(jnp.where(here, both, 0.0), axis=-1, keepdims=True)
        one_grad = jnp.where(here, grad, nothing)
        gm_ref[block] = one_grad
        qm_ref[block] = jnp.where(here, queries, nothing)
        grad_p = lax.dot_general(
            one_grad, v_ref[...], (((1,), (1,)), ((), ())), preferred_element_type=f32
        )
        grad_s = (low[head].astype(f32) * (grad_p - delta)).astype(bf16)
        ds_ref[block] = grad_s
        grad_q = jnp.where(here, jnp.dot(grad_s, k_ref[...], preferred_element_type=f32), grad_q)
    dv_acc[...] += lax.dot_general(
        low[...].reshape(heads * tile, seq), gm_ref[...], over_rows, preferred_element_type=f32
    )
    dk_acc[...] += lax.dot_general(ds_ref[...], qm_ref[...], over_rows, preferred_element_type=f32)

    def back(value, cosine, sine):
        value = (value * factor).astype(bf16).astype(f32)
        cosine, sine = spread_table(cosine, width), spread_table(sine, width)
        return (value * cosine - partner(value) * sine).astype(bf16)

    mixed_ref[rows, :width] = back(grad_q, cos_ref[rows], sin_ref[rows])
    pl.when(step < steps - 1)(lambda: hop(step))

    @pl.when(step == steps - 1)
    def _():
        mixed_ref[:, width : 2 * width] = back(dk_acc[...], cos_ref[...], sin_ref[...])
        mixed_ref[:, 2 * width :] = dv_acc[...].astype(bf16)
        deep = 256

        def out_grad(i, _):
            at = pl.ds(pl.multiple_of(i * deep, deep), deep)
            dw_ref[at, 3 * width :] = lax.dot_general(
                branch_ref[:, at], o_all[...], over_rows, preferred_element_type=f32
            ).astype(bf16)
            return 0

        def in_grad(i, _):
            at = pl.ds(pl.multiple_of(i * deep, deep), deep)
            dw_ref[at, : 3 * width] = lax.dot_general(
                h1_ref[:, at], mixed_ref[...], over_rows, preferred_element_type=f32
            ).astype(bf16)
            return 0

        turns = dw_ref.shape[0] // deep
        lax.fori_loop(0, turns, out_grad, 0)
        if one_buffer:
            sent()
            load(2)
        loaded(2)
        lax.fori_loop(0, turns, in_grad, 0)
        wait_rows()
        finish()
        if not one_buffer:
            sent()
        wait_swaps()


def attend_back(
    cid, q, k, v, o, p, cosine, sine, place, length, branch, w_out, hidden, w_red, h1_all, extras, cuts=2
):
    seq, width = q.shape
    heads = width // HEAD_DIM
    nb = lax.axis_size("blk")
    chips = nb // 2
    tile = seq // chips
    wide, units = w_red.shape
    t = seq // nb
    full = once(seq, width)
    f32, bf16 = jnp.float32, jnp.bfloat16
    loads = (hidden, w_red, h1_all)
    dma = pltpu.SemaphoreType.DMA
    return pl.pallas_call(
        functools.partial(attend_back_kernel, chips, cuts, 1024, extras),
        grid=(chips,),
        in_specs=[
            full, full, full, full, once(seq, 2 * HEAD_DIM), once(seq, 2 * HEAD_DIM), once(seq, 1),
            pl.BlockSpec(memory_space=pltpu.SMEM), once(t, wide), once(wide, width),
        ]
        + [ANY] * 4
        + extras.specs,
        out_specs=[once(seq, 3 * width), once(t, wide), once(wide, 4 * width)] + extras.specs,
        out_shape=[
            jax.ShapeDtypeStruct((seq, 3 * width), bf16),
            jax.ShapeDtypeStruct((t, wide), f32),
            jax.ShapeDtypeStruct((wide, 4 * width), bf16),
        ]
        + extras.shapes,
        scratch_shapes=[
            pltpu.VMEM((seq, wide), bf16),
            pltpu.VMEM((2, heads, tile, seq), bf16),
            pltpu.VMEM((heads * tile, seq), bf16),
            pltpu.VMEM((heads * tile, width), bf16),
            pltpu.VMEM((heads * tile, width), bf16),
            pltpu.VMEM((seq, width), f32),
            pltpu.VMEM((seq, width), f32),
        ]
        + [pltpu.VMEM(value.shape, value.dtype) for value in loads[:2]]
        + [pltpu.VMEM(h1_all.shape if seq <= 1024 else (16, 128), bf16)]
        + [dma((3,)), dma((2,))]
        + gather_sems(nb, cuts)
        + scatter_scratch(chips, cuts, t, wide)
        + extras.scratch,
        compiler_params=params(cid),
        cost_estimate=cost(10 * seq * seq * width),
    )(q, k, v, o, cosine, sine, place, length.reshape(1), branch, w_out, p, *loads, *extras.operands)


def arrange(weight, out, parts):
    nb, _, wide = out.shape
    span = wide // parts
    for j in range(nb):
        for part in range(parts):
            at = (part * nb + j) * span
            out[j, :, part * span : (part + 1) * span] = weight[:, at : at + span].astype(out.dtype)


def first_kernel(chips, cuts, parts, map_ref, tokens_ref, gain_ref, frequency_ref, *refs):
    n = len(parts)
    refs = list(refs)

    def take(count):
        return [refs.pop(0) for _ in range(count)]

    sources, h1_all, swapped, gathered = take(n), take(1)[0], take(n), take(n - 1)
    inverse_ref, place_ref, cos_ref, sin_ref = take(4)
    weights, held, (h1_ref, load_sem) = take(n), take(n), take(2)
    swaps = [swap_task(a, b, *take(3)) for a, b in zip(held, swapped)]
    task = square_gather if gathered[0].shape[0] == 4 else direct_gather
    rows = [task(a, b, *take(4)) for a, b in zip(swapped, gathered)]
    begin, pass_on, from_side, local, sent = gather_task(chips, cuts, h1_ref, h1_all, refs)
    load, loaded = mover(list(zip(sources, weights)), load_sem)
    load()
    greet(chips, True, True)
    for i in range(n - 1):
        loaded(i)
        arrange(weights[i], held[i], parts[i])
        swaps[i][0]()
    _, inverse_ref[...], h1_ref[...] = norm_forward(
        tokens_ref[...].astype(jnp.float32), gain_ref[...]
    )
    loaded(n - 1)
    arrange(weights[n - 1], held[n - 1], parts[n - 1])
    blocks = map_ref.shape[1]
    block = place_ref.shape[0] // blocks
    lanes = cos_ref.shape[1]
    front = lax.broadcasted_iota(jnp.int32, (block, lanes), 1) % HEAD_DIM < HEAD_DIM // 2
    for j in range(blocks):
        at = slice(j * block, (j + 1) * block)
        place = map_ref[0, j] * block + lax.broadcasted_iota(jnp.int32, (block, lanes), 0)
        place_ref[at] = place[:, :1]
        angle = place.astype(jnp.float32) * frequency_ref[...]
        cos_ref[at] = jnp.cos(angle)
        sine = jnp.sin(angle)
        sin_ref[at] = jnp.where(front, -sine, sine)
    for i in range(n - 2):
        swaps[i][1]()
        rows[i][0]()
    swaps[n - 2][1]()
    rows[n - 2][0]()
    begin()
    for k in range(1, chips):
        if k == min(3, chips - 1):
            swaps[n - 1][0]()
        pass_on(k)
    for _, middle, _ in rows:
        middle()
    local().wait()
    for y in range(chips):
        from_side(y)
    sent()
    for _, _, wait in rows:
        wait()
    swaps[n - 1][1]()


def first(cid, block_map, tokens, gain, weights, parts, cuts=4):
    nr, nb = lax.axis_size("rows"), lax.axis_size("blk")
    shapes = [(nb, value.shape[0], value.shape[1] // nb) for value in weights]
    n = len(weights)
    t, width = tokens.shape
    half = HEAD_DIM // 2
    frequency = jnp.exp(
        -jnp.arange(half, dtype=jnp.float32) * (2.0 / HEAD_DIM) * math.log(theta_base)
    )
    dma, f32, bf16 = pltpu.SemaphoreType.DMA, jnp.float32, jnp.bfloat16
    table = jax.ShapeDtypeStruct((nb * t, 2 * HEAD_DIM), f32)
    sems = 6 if nr == 4 else nr
    scratch = [pltpu.VMEM(value.shape, value.dtype) for value in weights]
    scratch += [pltpu.VMEM(shape, bf16) for shape in shapes]
    scratch += [pltpu.VMEM((t, width), bf16), dma((n,))]
    scratch += [dma, dma((nb,)), dma((nb,))] * n
    for shape in shapes[:-1]:
        scratch += [pltpu.VMEM(shape, bf16), dma, dma((sems,)), dma((sems,))]
    return pl.pallas_call(
        functools.partial(first_kernel, nb // 2, cuts, parts),
        out_shape=[jax.ShapeDtypeStruct((nb * t, width), bf16)]
        + [jax.ShapeDtypeStruct(shape, bf16) for shape in shapes]
        + [jax.ShapeDtypeStruct((nr,) + shape, bf16) for shape in shapes[:-1]]
        + [
            jax.ShapeDtypeStruct((t, 1), f32),
            jax.ShapeDtypeStruct((nb * t, 1), jnp.int32),
            table,
            table,
        ],
        in_specs=[pl.BlockSpec(memory_space=pltpu.SMEM)] + [VMEM] * 3 + [ANY] * n,
        out_specs=[ANY] * (2 * n) + [VMEM] * 4,
        scratch_shapes=scratch + gather_sems(nb, cuts),
        compiler_params=params(cid),
        cost_estimate=cost(0),
    )(block_map, tokens, gain[None], jnp.tile(frequency, 4)[None], *weights)


def total_task(nr, nb, x_ref, o_ref, held, rows_held, send_one, recv_one, send_two, recv_two):
    r, b = lax.axis_index("rows"), lax.axis_index("blk")
    across = [lax.rem(b + k, nb) for k in range(1, nb)]
    along = [lax.rem(r + k, nr) for k in range(1, nr)]

    def first(other, slot):
        return pltpu.make_async_remote_copy(
            src_ref=rows_held.at[r], dst_ref=rows_held.at[slot], send_sem=send_two.at[other],
            recv_sem=recv_two.at[slot], device_id=(other, b), device_id_type=MESH,
        )

    def second(other, slot):
        return pltpu.make_async_remote_copy(
            src_ref=held.at[b], dst_ref=held.at[slot], send_sem=send_one.at[other],
            recv_sem=recv_one.at[slot], device_id=(r, other), device_id_type=MESH,
        )

    def start():
        rows_held[r] = x_ref[...]
        for other in along:
            first(other, r).start()

    def middle():
        for other in along:
            first(other, other).wait_recv()
        held[b] = jnp.sum(rows_held[...], axis=0)
        for other in across:
            second(other, b).start()

    def finish():
        for other in across:
            second(other, other).wait_recv()
        o_ref[...] = jnp.sum(held[...], axis=0)
        for other in along:
            first(other, r).wait_send()
        for other in across:
            second(other, b).wait_send()

    return start, middle, finish


def last_scatter_kernel(
    chips, nr, cuts, tile, extras, a_ref, w_ref, x_ref, inverse_ref, gain_ref, resid_ref, gain_two_ref, h1_hbm, *refs
):
    n = extras.n
    srcs, refs = refs[:n], refs[n:]
    o_ref, total_ref, dsts, refs = refs[0], refs[1], refs[2 : 2 + n], refs[2 + n :]
    sum_ref, part_ref, h1_ref, load_sem, refs = refs[0], refs[1], refs[2], refs[3], refs[4:]
    put, _, hop, finish = scatter_task(chips, cuts, tile, sum_ref, refs[:4], refs[4:10])
    start_total, middle_total, finish_total = total_task(
        nr, 2 * chips, part_ref, total_ref, *refs[10:16]
    )
    start_swaps, start_rows, middle, wait_rows, wait_swaps = extras.tasks(srcs, dsts, refs[16:])
    load, loaded = mover([(h1_hbm, h1_ref)], load_sem)
    load()
    greet(chips, True, True)
    start_swaps()
    start_rows()
    part_ref[0:1] = jnp.zeros_like(part_ref[0:1])
    part_ref[1:2] = gain_two_ref[...]
    loaded()

    def seen(rows, cols, got):
        part_ref[0:1, cols] += jnp.sum(got * h1_ref[rows, cols].astype(jnp.float32), axis=0)[None]

    for s in range(chips):
        put(s, lambda rows: a_ref.at[rows], w_ref, seen)
        if s < chips - 1:
            hop(s)
    part_ref[0:1] = part_ref[0:1] / gain_ref[...]
    start_total()
    middle()
    middle_total()
    wait_rows()
    finish()
    inverse = inverse_ref[...]
    unit = x_ref[...].astype(jnp.float32) * inverse
    o_ref[...] = resid_ref[...] + norm_backward(sum_ref[...], unit, inverse, gain_ref[...])[0]
    finish_total()
    wait_swaps()


def last_scatter(cid, a, w, x, inverse, gain, resid, gain_two, h1_all, extras, cuts=2, tile=1024):
    nr, nb = lax.axis_size("rows"), lax.axis_size("blk")
    t, width = x.shape
    pair = (2, width)
    dma, f32 = pltpu.SemaphoreType.DMA, jnp.float32
    return pl.pallas_call(
        functools.partial(last_scatter_kernel, nb // 2, nr, cuts, tile, extras),
        out_shape=[jax.ShapeDtypeStruct((t, width), f32), jax.ShapeDtypeStruct(pair, f32)]
        + extras.shapes,
        in_specs=[VMEM] * 7 + [ANY] + extras.specs,
        out_specs=[VMEM] * 2 + extras.specs,
        scratch_shapes=[
            pltpu.VMEM((t, width), f32),
            pltpu.VMEM(pair, f32),
            pltpu.VMEM(h1_all.shape, h1_all.dtype),
            dma((1,)),
        ]
        + scatter_scratch(nb // 2, cuts, t, width)
        + [pltpu.VMEM((nb,) + pair, f32), pltpu.VMEM((nr,) + pair, f32)]
        + [dma((nb,))] * 2 + [dma((nr,))] * 2
        + extras.scratch,
        compiler_params=params(cid),
        cost_estimate=cost(2 * a.shape[0] * width * w.shape[1]),
    )(a, w, x, inverse, gain[None], resid, gain_two, h1_all, *extras.operands)


def step_kernel(parts, one_array, *refs):
    count = 1 if one_array else parts
    grads, refs = refs[:count], refs[count:]
    outs = len(refs) // 2
    rule = adam_step if outs == 3 else moment_step

    def go(grad):
        wide = grad.shape[2]
        for j in range(grad.shape[0]):
            cols = slice(j * wide, (j + 1) * wide)
            gradient = grad[j].astype(jnp.float32)
            for ref, value in zip(
                refs[outs:], rule(*[ref[:, cols] for ref in refs[:outs]], gradient)
            ):
                ref[:, cols] = value

    if one_array:
        go(grads[0])
        return
    for part, grad in enumerate(grads):
        pl.when(pl.program_id(0) == part)(functools.partial(go, grad))


def step(pieces, parts, states, first=0):
    one_array = not isinstance(pieces, list)
    pieces = [pieces] if one_array else pieces
    nb = pieces[0].shape[0]
    rows, columns = states[0].shape
    tile = min(rows, 64 if parts > 1 else 32)
    span = columns // parts
    at = pl.BlockSpec((tile, span), lambda part, i: (i, part))
    block = (nb, tile, span // nb)
    if one_array:
        grads = [pl.BlockSpec(block, lambda part, i: (0, i, first + part))]
    else:
        grads = [pl.BlockSpec(block, lambda part, i: (0, i, 0))] * parts
    outs = len(states)
    return pl.pallas_call(
        functools.partial(step_kernel, parts, one_array),
        grid=(parts, rows // tile),
        in_specs=grads + [at] * outs,
        out_specs=[at] * outs,
        out_shape=[jax.ShapeDtypeStruct((rows, columns), jnp.float32)] * outs,
        compiler_params=pltpu.CompilerParams(vmem_limit_bytes=60 * MIB),
        cost_estimate=pl.CostEstimate(
            flops=0, bytes_accessed=(8 * outs + 2) * rows * columns, transcendentals=0
        ),
    )(*pieces, *states)


def after(value, *others):
    return lax.optimization_barrier((value,) + others)[0]


def over_tokens(left, right):
    return lax.dot_general(
        left, right, (((0,), (0,)), ((), ())), preferred_element_type=jnp.float32
    )


def shards(
    tokens, cotangent, lengths, block_map, gain_attend, gain_expand,
    attend_in, attend_out, expand_in, reduce_out,
    attend_in_first, attend_out_first, expand_in_first, reduce_out_first,
    attend_in_second, attend_out_second, expand_in_second, reduce_out_second,
):
    nb = lax.axis_size("blk")
    length = lengths[0]
    h1_all, _, _, _, swap_gu, w_in, w_out, w_red, inverse_one, place, cosine, sine = first(
        2, block_map, tokens[0], gain_attend,
        (attend_in, attend_out.T, reduce_out.T, expand_in), (3, 1, 1, 2),
    )
    block_rows = tokens.shape[1] // 2
    row_place = (block_map[0][:, None] * block_rows + jnp.arange(block_rows)[None, :]).reshape(1, -1)
    live_place = jnp.where(row_place < length, row_place, jnp.int32(1 << 30))
    nr = lax.axis_size("rows")
    deep = nb * attend_in.shape[0]
    wide = tokens.shape[2]

    def flat(pieces):
        return pieces.reshape(deep, pieces.shape[2])

    w_in, w_out, w_red = [value.reshape(wide, value.shape[3]) for value in (w_in, w_out, w_red)]
    attended, q, k, v, p, g_all, x1, inverse_two, h2, w_gu = attend(
        4, h1_all, w_in, cosine, sine, place, live_place, length, cotangent[0],
        tokens[0], gain_expand, w_out, Extras([], [(flat(swap_gu), 0, deep)]),
    )
    w_gu = w_gu.reshape(wide, -1)

    def by_rows(gradient):
        return gradient.reshape(nr, nb, deep // nb, gradient.shape[1])

    grad_x1, branch, gain_two, hidden, part_gate, part_up, rows_reduce = feed_forward(
        6, h2, x1, inverse_two, gain_expand, cotangent[0], w_gu, w_red, g_all
    )
    grad_mixed, y, part_both, own_reduce, rows_gate, rows_up = attend_back(
        10, q, k, v, attended, p, cosine, sine, place, length, branch, w_out, hidden, w_red, h1_all,
        Extras([rows_reduce], [], [by_rows(part_gate), by_rows(part_up)]),
    )
    y = x1 + y
    grad_input, gains, own_gate, own_up, rows_both = last_scatter(
        11, grad_mixed, w_in, tokens[0], inverse_one, gain_attend, grad_x1, gain_two, h1_all,
        Extras([rows_gate, rows_up], [], [by_rows(part_both)]),
    )
    both = lax.all_to_all(rows_both, "blk", 0, 0, tiled=True)
    set_four = step(own_reduce, 1, (reduce_out.T, reduce_out_first.T, reduce_out_second.T))
    set_three = step([own_gate, own_up], 2, (expand_in, expand_in_first, expand_in_second))
    both = after(both, set_three[2], set_four[2])
    set_one = step(both, 3, (attend_in, attend_in_first, attend_in_second))
    set_two = step(both, 1, (attend_out_first.T, attend_out_second.T), 3)
    return (
        y.astype(jnp.bfloat16).reshape(tokens.shape),
        grad_input.reshape(tokens.shape),
        gains[0],
        gains[1],
        *set_one,
        *[value.T for value in set_two],
        *set_three,
        *[value.T for value in set_four],
    )


def solution(mesh):
    placed = (
        P("rows", "blk", None),
        P("rows", "blk", None),
        P("rows"),
        P("rows", None),
        P(),
        P(),
        P(("rows", "blk"), None),
        P(None, ("rows", "blk")),
        P(("rows", "blk"), None),
        P(None, ("rows", "blk")),
        P(("rows", "blk"), None),
        P(None, ("rows", "blk")),
        P(("rows", "blk"), None),
        P(None, ("rows", "blk")),
        P(("rows", "blk"), None),
        P(None, ("rows", "blk")),
        P(("rows", "blk"), None),
        P(None, ("rows", "blk")),
    )
    return jax.shard_map(
        shards,
        mesh=mesh,
        in_specs=placed,
        out_specs=(
            P("rows", "blk", None),
            P("rows", "blk", None),
            P(),
            P(),
            P(("rows", "blk"), None),
            P(("rows", "blk"), None),
            P(("rows", "blk"), None),
            P(None, ("rows", "blk")),
            P(None, ("rows", "blk")),
            P(("rows", "blk"), None),
            P(("rows", "blk"), None),
            P(("rows", "blk"), None),
            P(None, ("rows", "blk")),
            P(None, ("rows", "blk")),
            P(None, ("rows", "blk")),
        ),
        check_vma=False,
    )
```
